32 devices in a mesh: dp: 8 (over z, x), mp: 4 (over y, core).
Axes of the slice: x: 2, y: 2, z: 4, core: 2. Of those that a mesh axis runs over, the one named last changes fastest.
Arguments:
- tokens: bfloat16 [16384, 768], P('dp'), may hold values from -6 to 6
- lengths: int32 [8, 3], P('dp'), may hold values from 1 to 1792, 2048 in all within a row
- norm_gain: bfloat16 [2, 2, 768], P(None, None, 'dp'), may hold values from 0.099609375 to 1.8984375
- w_value: bfloat16 [2, 768, 768], P(None, 'dp', 'mp'), may hold values from -0.21875 to 0.21875
- w_out: bfloat16 [2, 768, 768], P(None, 'mp', 'dp'), may hold values from -0.875 to 0.875
- w_up: bfloat16 [2, 768, 3072], P(None, 'dp', 'mp'), may hold values from -0.21875 to 0.21875
- w_down: bfloat16 [2, 3072, 768], P(None, 'mp', 'dp'), may hold values from -0.109375 to 0.109375
- synth_first: bfloat16 [768, 768], P('dp', 'mp'), may hold values from -0.21875 to 0.21875
- synth_second: bfloat16 [12, 64, 2048], P('mp', None, 'dp'), may hold values from -4 to 4
- random_table: bfloat16 [12, 2048, 2048], P('mp', 'dp'), may hold values from -9 to 9
- cotangent: bfloat16 [16384, 768], P('dp'), may hold values from -6 to 6
Outputs:
- layer_output: bfloat16 [16384, 768], P('dp')
- input_grad: bfloat16 [16384, 768], P('dp')
- gain_grad: float32 [2, 2, 768], P(None, None, 'dp')
- value_grad: float32 [2, 768, 768], P(None, 'dp', 'mp')
- out_grad: float32 [2, 768, 768], P(None, 'mp', 'dp')
- up_grad: float32 [2, 768, 3072], P(None, 'dp', 'mp')
- down_grad: float32 [2, 3072, 768], P(None, 'mp', 'dp')
- first_grad: float32 [768, 768], P('dp', 'mp')
- second_grad: float32 [12, 64, 2048], P('mp', None, 'dp')
- random_grad: float32 [12, 2048, 2048], P('mp', 'dp')
The draws below stay inside these ranges and needn't reach their ends.
Inputs may be any that keep to these rules, and one draw needn't show every extreme that they name: Each row lists the lengths of the 3 items of one slot; a row sums to 2048 and its longest item is 1792.
All inputs are finite; a program needn't handle non-finite values.
Results may differ from the reference program's by a relative error of at most 0.023.
Values may be sent and summed in bfloat16 or wider, within the bound.
A program may use at most 448 MiB of HBM per device.

```python
import math
from functools import partial
import jax
import jax.numpy as jnp
import numpy as np
from jax import lax

D = 768
HEADS = 12
HD = 64
FF = 3072
LMAX = 2048
ITEMS = 3
MOST = 1792
SLOTS = 8
TOKENS = 16384
N_MP = 4


def level_of(rng, shape, shards, smallest, high):
    factor_of, own = 1.0, jax.random.fold_in(rng, 6)
    for position, shards_of in shards:
        heights = jnp.exp(jax.random.uniform(jax.random.fold_in(own, position), (shards_of,), jnp.float32, smallest / len(shards), high / len(shards)))
        factor_of = factor_of * jnp.repeat(heights, shape[position] // shards_of).reshape([-1 if axis == position else 1 for axis in range(len(shape))])
    return factor_of


def split_up(number_of, total, reach, lean):
    portions = [(1 << 20) // math.isqrt(standing ** lean) + 1 for standing in range(2, number_of + 1)]
    rest, given = total - reach - (number_of - 1), [1] * (number_of - 1)
    while rest > 0:
        candidates = [i for i in range(number_of - 1) if given[i] < reach]
        whole, left = sum([portions[i] for i in candidates]), rest
        for i in candidates:
            extra = min(reach - given[i], max(1, left * portions[i] // whole), rest)
            given[i] = given[i] + extra
            rest = rest - extra
    return np.array([reach] + given)


def ragged(rng, amount, total, most, skew):
    if amount == 2:
        one = jax.random.randint(rng, (), max(1, total - most), min(most, total - 1) + 1)
        return jnp.stack([one, total - one])
    sizes = jnp.asarray(split_up(amount, total, most, skew), jnp.int32)
    twos = (amount - 1) // 2
    donor, sink = sizes[1:1 + 2 * twos:2], sizes[2:2 + 2 * twos:2]
    room = jnp.minimum(donor - 1, most - sink)
    moved = jax.random.randint(jax.random.fold_in(rng, 1), (twos,), 0, 1 << 20) % (room + 1)
    sizes = sizes.at[1:1 + 2 * twos:2].set(donor - moved).at[2:2 + 2 * twos:2].set(sink + moved)
    return sizes[jax.random.permutation(jax.random.fold_in(rng, 2), amount)]


def centred(key, dims, width, limit, shards=(), kind=jnp.bfloat16):
    entries = width * jax.random.normal(key, dims, jnp.float32)
    if shards:
        entries = entries * level_of(key, dims, shards, -0.22, 0.18)
    return jnp.clip(entries, -limit, limit).astype(kind)


def setup_inputs(seed: int = 0) -> dict:
    splits = jax.random.split(jax.random.key(seed), 12)
    return {
        "tokens": centred(splits[0], (TOKENS, D), 1.0, 6.0, ((0, 8),)),
        "lengths": jax.vmap(lambda own: ragged(own, ITEMS, LMAX, MOST, 2))(jax.random.split(splits[1], SLOTS)).reshape((SLOTS, ITEMS)).astype(jnp.int32),
        "norm_gain": jnp.clip(1.0 + 0.18 * jax.random.normal(splits[2], (2, 2, D), jnp.float32), 0.099609375, 1.8984375).astype(jnp.bfloat16),
        "w_value": centred(splits[3], (2, D, D), D ** -0.5, 0.21875, ((1, 8), (2, 4))),
        "w_out": centred(splits[4], (2, D, D), (D // 16) ** -0.5, 0.875, ((1, 4), (2, 8))),
        "w_up": centred(splits[5], (2, D, FF), D ** -0.5, 0.21875, ((1, 8), (2, 4))),
        "w_down": centred(splits[6], (2, FF, D), FF ** -0.5, 0.109375, ((1, 4), (2, 8))),
        "synth_first": centred(splits[7], (D, D), D ** -0.5, 0.21875, ((0, 8), (1, 4))),
        "synth_second": centred(splits[8], (HEADS, HD, LMAX), 0.3, 4.0, ((0, 4), (2, 8))),
        "random_table": centred(splits[9], (HEADS, LMAX, LMAX), 1.5, 9.0, ((0, 4), (1, 8))),
        "cotangent": centred(splits[10], (TOKENS, D), 1.0, 6.0, ((0, 8),)),
    }


eps = 1e-06

@jax.custom_vjp
def low(v):
    return lax.optimization_barrier(v.astype(jnp.bfloat16)).astype(jnp.float32)

@jax.custom_vjp
def low_back(v):
    return v

def low_keep(v):
    return (low(v), None)

def low_pass(kept, grad):
    return (grad,)

def back_keep(v):
    return (v, None)

def back_low(kept, grad):
    return (low(grad),)
low.defvjp(low_keep, low_pass)
low_back.defvjp(back_keep, back_low)

def normalize(inputs, gain):
    return inputs * lax.rsqrt(lax.optimization_barrier(jnp.mean(inputs * inputs, axis=-1, keepdims=True)) + eps) * gain

def product(former, latter):
    return jnp.dot(former, latter, precision=lax.Precision.HIGHEST)

def slot_layout(item_lengths):
    item_ends = jnp.cumsum(item_lengths).astype(jnp.int32)
    starts = (item_ends - item_lengths).astype(jnp.int32)
    places = jnp.arange(LMAX, dtype=jnp.int32)
    member = lax.optimization_barrier(jnp.sum((places[:, None] >= item_ends[None, :]).astype(jnp.int32), axis=1)).astype(jnp.int32)
    onehot = member[:, None] == jnp.arange(ITEMS, dtype=jnp.int32)[None, :]
    within = (places - lax.optimization_barrier(jnp.sum(jnp.where(onehot, starts[None, :], 0), axis=1))).astype(jnp.int32)
    return (member, within)

def attend(scores, member, values):
    same_item = member[:, None] == member[None, :]
    soft_weights = jax.nn.softmax(jnp.where(same_item[None], scores, -1000000000.0), axis=-1)
    return jnp.einsum('hij,jhd->ihd', low(soft_weights), values, precision=lax.Precision.HIGHEST)

def dense_slot(record, score_table):
    activations, values, item_lengths = record
    member, within = slot_layout(item_lengths)
    synth_rows = low_back(jnp.einsum('thd,hdp->htp', activations, score_table, precision=lax.Precision.HIGHEST))
    return attend(jnp.take(synth_rows, within, axis=2), member, values)

def random_slot(record, score_table):
    values, item_lengths = record
    member, within = slot_layout(item_lengths)
    scores = jnp.take(jnp.take(score_table, within, axis=1), within, axis=2)
    return attend(scores, member, values)

def residual_layer(inputs, gain_rows, w_value, w_out, w_up, w_down, lengths, synth_first, score_table):
    slots = lengths.shape[0]
    heads_here = HEADS // N_MP
    group_width = heads_here * HD
    hidden_width = FF // N_MP
    normed = low(normalize(inputs, gain_rows[0]))
    branch = jnp.zeros(inputs.shape, jnp.float32)
    for shard_rank in range(N_MP):
        group_input = low_back(normed)
        column_span = slice(shard_rank * group_width, (shard_rank + 1) * group_width)
        values = low(low_back(product(group_input, w_value[:, column_span])))
        values = values.reshape(slots, LMAX, heads_here, HD)
        table_part = score_table[shard_rank * heads_here:(shard_rank + 1) * heads_here]
        if synth_first is None:
            mixed_rows = lax.map(jax.checkpoint(partial(random_slot, score_table=table_part)), (values, lengths))
        else:
            activations = low(jax.nn.gelu(low_back(product(group_input, synth_first[:, column_span]))))
            activations = activations.reshape(slots, LMAX, heads_here, HD)
            mixed_rows = lax.map(jax.checkpoint(partial(dense_slot, score_table=table_part)), (activations, values, lengths))
        mixed_rows = low(low_back(mixed_rows.reshape(slots * LMAX, group_width)))
        branch = branch + low(product(mixed_rows, w_out[column_span, :]))
    middle = inputs + low_back(branch)
    normed_ffn = low(normalize(middle, gain_rows[1]))
    feed_branch = jnp.zeros(inputs.shape, jnp.float32)
    for shard_rank in range(N_MP):
        group_input = low_back(normed_ffn)
        column_span = slice(shard_rank * hidden_width, (shard_rank + 1) * hidden_width)
        hidden = low(jax.nn.gelu(low_back(product(group_input, w_up[:, column_span]))))
        feed_branch = feed_branch + low(product(hidden, w_down[column_span, :]))
    return middle + low_back(feed_branch)

def reference(tokens, lengths, norm_gain, w_value, w_out, w_up, w_down, synth_first, synth_second, random_table, cotangent):

    def forward(inputs, gain_rows, value_weights, out_weights, up_weights, down_weights, first_weights, second_weights, random_weights):
        between = residual_layer(inputs, gain_rows[0], value_weights[0], out_weights[0], up_weights[0], down_weights[0], lengths, first_weights, second_weights)
        return residual_layer(between, gain_rows[1], value_weights[1], out_weights[1], up_weights[1], down_weights[1], lengths, None, random_weights)
    floats = [argument.astype(jnp.float32) for argument in (tokens, norm_gain, w_value, w_out, w_up, w_down, synth_first, synth_second, random_table)]
    result, pullback = jax.vjp(forward, *floats)
    gradients = pullback(cotangent.astype(jnp.float32))
    return (result.astype(jnp.bfloat16), gradients[0].astype(jnp.bfloat16), gradients[1], gradients[2], gradients[3], gradients[4], gradients[5], gradients[6], gradients[7], gradients[8])
```

```python
from functools import partial

import jax
import jax.numpy as jnp
from jax import lax
from jax.experimental import pallas as pl
from jax.experimental.pallas import tpu as pltpu
from jax.sharding import PartitionSpec as P

F32, BF16 = jnp.float32, jnp.bfloat16
HD = 64
MOST = 1792
TILE = 256
VMEM = 58 * 1024 * 1024


def nn(a, b):
    return lax.dot_general(a, b, (((1,), (0,)), ((), ())), preferred_element_type=F32)


def nt(a, b):
    return lax.dot_general(a, b, (((1,), (1,)), ((), ())), preferred_element_type=F32)


def tn(a, b):
    return lax.dot_general(a, b, (((0,), (0,)), ((), ())), preferred_element_type=F32)


def small_masks(first, size):
    row = lax.broadcasted_iota(jnp.int32, (size, size), 0)
    col = lax.broadcasted_iota(jnp.int32, (size, size), 1)
    early = row < first
    inside = col < jnp.where(early, first, size - first)
    shift = jnp.where(col == row + first, 1.0, 0.0).astype(BF16)
    rows = jnp.where(col == jnp.where(early, row, row - first), 1.0, 0.0).astype(BF16)
    return early, inside, shift, rows


def masked_soft(scores, inside):
    masked = jnp.where(inside, scores, -1e30)
    powers = jnp.where(inside, jnp.exp(masked - jnp.max(masked, axis=1, keepdims=True)), 0.0)
    return powers / jnp.sum(powers, axis=1, keepdims=True)


def by_token(soft, early, shift):
    low = soft.astype(BF16)
    zero = jnp.zeros_like(low)
    late = nn(jnp.where(early, zero, low), shift).astype(BF16)
    return jnp.where(early, low, zero) + late


def dense_forward(first, acts, values, table):
    tokens, width = acts.shape
    heads = width // HD
    tiles = MOST // TILE
    size = tokens - MOST

    def kernel(first_ref, acts_ref, values_ref, table_ref, out_ref, lse_ref):
        tile = pl.program_id(0)
        lane = lax.broadcasted_iota(jnp.int32, (TILE, 128), 1)

        @pl.when(tile < tiles)
        def _():
            lse = jnp.zeros((TILE, 128), F32)
            parts = []
            for head in range(heads):
                span = slice(head * HD, (head + 1) * HD)
                scores = nn(acts_ref[:, span], table_ref[span, :])
                top = jnp.max(scores, axis=1, keepdims=True)
                powers = jnp.exp(scores - top)
                total = jnp.sum(powers, axis=1, keepdims=True)
                mixed = nn(powers.astype(BF16), values_ref[0:MOST, span])
                parts.append((mixed / total).astype(BF16))
                lse = jnp.where(lane == head, top + jnp.log(total), lse)
            out_ref[...] = jnp.concatenate(parts, axis=1)
            lse_ref[...] = lse

        @pl.when(tile == tiles)
        def _():
            early, inside, shift, _ = small_masks(first_ref[0, 0], size)
            parts = []
            for head in range(heads):
                span = slice(head * HD, (head + 1) * HD)
                scores = nn(acts_ref[:, span], table_ref[span, 0:size])
                soft = by_token(masked_soft(scores, inside), early, shift)
                parts.append(nn(soft, values_ref[MOST:tokens, span]).astype(BF16))
            out_ref[...] = jnp.concatenate(parts, axis=1)
            lse_ref[...] = jnp.zeros((TILE, 128), F32)

    return pl.pallas_call(
        kernel,
        grid=(tiles + 1,),
        in_specs=[
            pl.BlockSpec(memory_space=pltpu.SMEM),
            pl.BlockSpec((TILE, width), lambda t: (t, 0)),
            pl.BlockSpec((tokens, width), lambda t: (0, 0)),
            pl.BlockSpec((width, MOST), lambda t: (0, 0)),
        ],
        out_specs=[
            pl.BlockSpec((TILE, width), lambda t: (t, 0)),
            pl.BlockSpec((TILE, 128), lambda t: (t, 0)),
        ],
        out_shape=[
            jax.ShapeDtypeStruct((tokens, width), BF16),
            jax.ShapeDtypeStruct((tokens, 128), F32),
        ],
        compiler_params=pltpu.CompilerParams(vmem_limit_bytes=VMEM),
        name="dense_forward",
    )(first, acts, values, table)


def dense_backward(first, acts, acts_t, values_t, upstream, upstream_t, table, table_t, lse):
    tokens, width = acts.shape
    heads = width // HD
    tiles = MOST // TILE
    size = tokens - MOST

    def kernel(first_ref, acts_ref, acts_t_ref, values_t_ref, up_ref, up_t_ref, table_ref, table_t_ref,
               lse_ref, dacts_ref, dvalues_ref, dtable_ref, dv_acc):
        tile = pl.program_id(0)

        @pl.when(tile == 0)
        def _():
            dv_acc[...] = jnp.zeros_like(dv_acc)
            dtable_ref[...] = jnp.zeros_like(dtable_ref)

        @pl.when(tile < tiles)
        def _():
            parts = []
            for head in range(heads):
                span = slice(head * HD, (head + 1) * HD)
                scores = nn(acts_ref[:, span], table_ref[span, :])
                soft = jnp.exp(scores - lse_ref[:, head : head + 1])
                dsoft = nn(up_ref[:, span], values_t_ref[span, 0:MOST])
                dv_acc[span, :] += nn(up_t_ref[span, :], soft.astype(BF16))
                weighed = soft * dsoft
                centre = jnp.sum(weighed, axis=1, keepdims=True)
                dscores = (weighed - soft * centre).astype(BF16)
                dtable_ref[span, :] += nn(acts_t_ref[span, :], dscores)
                parts.append(nn(dscores, table_t_ref[:, span]))
            dacts_ref[...] = jnp.concatenate(parts, axis=1)

        @pl.when(tile == tiles)
        def _():
            early, inside, shift, _ = small_masks(first_ref[0, 0], size)
            parts = []
            for head in range(heads):
                span = slice(head * HD, (head + 1) * HD)
                scores = nn(acts_ref[:, span], table_ref[span, 0:size])
                soft = masked_soft(scores, inside)
                here = values_t_ref[span, MOST:tokens]
                moved = nt(here, shift).astype(BF16)
                dsoft = jnp.where(early, nn(up_ref[:, span], here), nn(up_ref[:, span], moved))
                dvalues_ref[span, MOST:tokens] = nn(up_t_ref[span, :], by_token(soft, early, shift)).astype(BF16)
                centre = jnp.sum(soft * dsoft, axis=1, keepdims=True)
                dscores = (soft * (dsoft - centre)).astype(BF16)
                dtable_ref[span, 0:size] += nn(acts_t_ref[span, :], dscores)
                parts.append(nn(dscores, table_t_ref[0:size, span]))
            dacts_ref[...] = jnp.concatenate(parts, axis=1)
            dvalues_ref[:, 0:MOST] = dv_acc[...].astype(BF16)

    whole = lambda t: (0, 0)
    return pl.pallas_call(
        kernel,
        grid=(tiles + 1,),
        in_specs=[
            pl.BlockSpec(memory_space=pltpu.SMEM),
            pl.BlockSpec((TILE, width), lambda t: (t, 0)),
            pl.BlockSpec((width, TILE), lambda t: (0, t)),
            pl.BlockSpec((width, tokens), whole),
            pl.BlockSpec((TILE, width), lambda t: (t, 0)),
            pl.BlockSpec((width, TILE), lambda t: (0, t)),
            pl.BlockSpec((width, MOST), whole),
            pl.BlockSpec((MOST, width), whole),
            pl.BlockSpec((TILE, 128), lambda t: (t, 0)),
        ],
        out_specs=[
            pl.BlockSpec((TILE, width), lambda t: (t, 0)),
            pl.BlockSpec((width, tokens), whole),
            pl.BlockSpec((width, MOST), whole),
        ],
        out_shape=[
            jax.ShapeDtypeStruct((tokens, width), F32),
            jax.ShapeDtypeStruct((width, tokens), BF16),
            jax.ShapeDtypeStruct((width, MOST), F32),
        ],
        scratch_shapes=[pltpu.VMEM((width, MOST), F32)],
        compiler_params=pltpu.CompilerParams(vmem_limit_bytes=VMEM),
        name="dense_backward",
    )(first, acts, acts_t, values_t, upstream, upstream_t, table, table_t, lse)


def random_forward(table, values_t):
    heads, rows, _ = table.shape
    slots, width, _ = values_t.shape

    def kernel(table_ref, values_ref, out_ref, lse_ref):
        scores = table_ref[0, :, 0:MOST].astype(F32)
        top = jnp.max(scores, axis=1, keepdims=True)
        powers = jnp.exp(scores - top)
        total = jnp.sum(powers, axis=1, keepdims=True)
        soft = (powers / total).astype(BF16)
        values = values_ref[...].reshape(slots * HD, MOST)
        out_ref[...] = nt(values, soft).astype(BF16).reshape(slots, HD, rows)
        lse_ref[...] = jnp.broadcast_to(top + jnp.log(total), (1, rows, 128))

    return pl.pallas_call(
        kernel,
        grid=(heads,),
        in_specs=[
            pl.BlockSpec((1, rows, table.shape[2]), lambda h: (h, 0, 0)),
            pl.BlockSpec((slots, HD, MOST), lambda h: (0, h, 0)),
        ],
        out_specs=[
            pl.BlockSpec((slots, HD, rows), lambda h: (0, h, 0)),
            pl.BlockSpec((1, rows, 128), lambda h: (h, 0, 0)),
        ],
        out_shape=[
            jax.ShapeDtypeStruct((slots, width, rows), BF16),
            jax.ShapeDtypeStruct((heads, rows, 128), F32),
        ],
        compiler_params=pltpu.CompilerParams(vmem_limit_bytes=VMEM),
        name="random_forward",
    )(table, values_t)


def random_backward(valid, table, lse, values_t, upstream_t):
    heads, rows, columns = table.shape
    slots, width, _ = values_t.shape
    buffers = pl.Buffered(2 if slots <= 16 else 1)

    def kernel(valid_ref, table_ref, lse_ref, values_ref, up_ref, dtable_ref, dvalues_ref):
        soft = jnp.exp(table_ref[0, :, 0:MOST].astype(F32) - lse_ref[0, :, 0:1])
        up = up_ref[...].reshape(slots * HD, rows) * valid_ref[0, 0].astype(BF16)
        values = values_ref[...].reshape(slots * HD, MOST)
        dsoft = tn(up, values)
        weighed = soft * dsoft
        centre = jnp.sum(weighed, axis=1, keepdims=True)
        dtable_ref[0, :, 0:MOST] = weighed - soft * centre
        dtable_ref[0, :, MOST:columns] = jnp.zeros((rows, columns - MOST), F32)
        dvalues_ref[...] = nn(up, soft.astype(BF16)).astype(BF16).reshape(slots, HD, MOST)

    return pl.pallas_call(
        kernel,
        grid=(heads,),
        in_specs=[
            pl.BlockSpec(memory_space=pltpu.SMEM),
            pl.BlockSpec((1, rows, columns), lambda h: (h, 0, 0)),
            pl.BlockSpec((1, rows, 128), lambda h: (h, 0, 0)),
            pl.BlockSpec((slots, HD, MOST), lambda h: (0, h, 0), pipeline_mode=buffers),
            pl.BlockSpec((slots, HD, rows), lambda h: (0, h, 0)),
        ],
        out_specs=[
            pl.BlockSpec((1, rows, columns), lambda h: (h, 0, 0)),
            pl.BlockSpec((slots, HD, MOST), lambda h: (0, h, 0)),
        ],
        out_shape=[
            jax.ShapeDtypeStruct((heads, rows, columns), F32),
            jax.ShapeDtypeStruct((slots, width, MOST), BF16),
        ],
        compiler_params=pltpu.CompilerParams(vmem_limit_bytes=VMEM),
        name="random_backward",
    )(valid, table, lse, values_t, upstream_t)


def short_forward(first, corner, values_t):
    heads, size, _ = corner.shape
    width = values_t.shape[0]

    def kernel(first_ref, corner_ref, values_ref, out_ref):
        early, inside, shift, rows = small_masks(first_ref[0, 0], size)
        for head in range(heads):
            span = slice(head * HD, (head + 1) * HD)
            soft = by_token(masked_soft(nn(rows, corner_ref[head]), inside), early, shift)
            out_ref[span, :] = nt(values_ref[span, :], soft).astype(BF16)

    return pl.pallas_call(
        kernel,
        in_specs=[
            pl.BlockSpec(memory_space=pltpu.SMEM),
            pl.BlockSpec(memory_space=pltpu.VMEM),
            pl.BlockSpec(memory_space=pltpu.VMEM),
        ],
        out_specs=pl.BlockSpec(memory_space=pltpu.VMEM),
        out_shape=jax.ShapeDtypeStruct((width, size), BF16),
        name="short_forward",
    )(first, corner, values_t)


def short_backward(first, corner, values_t, upstream_t):
    heads, size, _ = corner.shape
    width = values_t.shape[0]

    def kernel(first_ref, corner_ref, values_ref, up_ref, dcorner_ref, dvalues_ref):
        early, inside, shift, rows = small_masks(first_ref[0, 0], size)
        for head in range(heads):
            span = slice(head * HD, (head + 1) * HD)
            soft = masked_soft(nn(rows, corner_ref[head]), inside)
            here, up = values_ref[span, :], up_ref[span, :]
            moved = nt(here, shift).astype(BF16)
            dsoft = jnp.where(early, tn(up, here), tn(up, moved))
            dvalues_ref[span, :] = nn(up, by_token(soft, early, shift)).astype(BF16)
            centre = jnp.sum(soft * dsoft, axis=1, keepdims=True)
            dscores = (soft * (dsoft - centre)).astype(BF16)
            dcorner_ref[head] = tn(rows, dscores).astype(BF16)

    return pl.pallas_call(
        kernel,
        in_specs=[
            pl.BlockSpec(memory_space=pltpu.SMEM),
            pl.BlockSpec(memory_space=pltpu.VMEM),
            pl.BlockSpec(memory_space=pltpu.VMEM),
            pl.BlockSpec(memory_space=pltpu.VMEM),
        ],
        out_specs=[
            pl.BlockSpec(memory_space=pltpu.VMEM),
            pl.BlockSpec(memory_space=pltpu.VMEM),
        ],
        out_shape=[
            jax.ShapeDtypeStruct((heads, size, size), BF16),
            jax.ShapeDtypeStruct((width, size), BF16),
        ],
        name="short_backward",
    )(first, corner, values_t, upstream_t)


EPS = 1e-06


def root(x):
    return lax.rsqrt(jnp.mean(x * x, axis=-1, keepdims=True) + EPS)


def normalize(x, gain):
    return (x * root(x) * gain).astype(BF16)


def normalize_back(x, gain, grad):
    scale = root(x)
    weighed = grad * gain
    pull = jnp.mean(weighed * x, axis=-1, keepdims=True)
    return scale * weighed - x * (scale * scale * scale * pull), jnp.sum(grad * x * scale, axis=0)


def feed_forward(middle, gain, up, down_t):
    normed = normalize(middle, gain)
    out, kept = middle, []
    for group in range(up.shape[0]):
        pre = nn(normed, up[group])
        hidden = jax.nn.gelu(pre).astype(BF16)
        out = out + nt(hidden, down_t[group])
        kept.append((pre, hidden))
    return out, (normed, kept)


def feed_backward(middle, gain, up, down_t, record, grad):
    normed, kept = record
    low = grad.astype(BF16)
    up_grads, down_grads, dnormed = [], [], 0.0
    for group in range(up.shape[0]):
        pre, hidden = kept[group]
        down_grads.append(tn(low, hidden).astype(BF16))
        dpre = jax.vjp(jax.nn.gelu, pre)[1](nn(low, down_t[group]))[0].astype(BF16)
        up_grads.append(tn(normed, dpre).astype(BF16))
        dnormed = dnormed + nt(dpre, up[group])
    dmiddle, gain_grad = normalize_back(middle, gain, dnormed)
    return grad + dmiddle, gain_grad, jnp.stack(up_grads), jnp.stack(down_grads)


def heads_out(parts, chunks):
    got = lax.all_to_all(parts, "mp", 0, 0, tiled=True)
    return got.transpose(1, 0, 2).reshape(parts.shape[1], chunks * parts.shape[2])


def heads_in(whole, chunks):
    width, tokens = whole.shape
    parts = whole.reshape(width, chunks, tokens // chunks).transpose(1, 0, 2)
    return lax.all_to_all(parts, "mp", 0, 0, tiled=True)


def per_device(
    n_dp,
    n_mp,
    tokens,
    lengths,
    norm_gain,
    w_value,
    w_out,
    w_up,
    w_down,
    synth_first,
    synth_second,
    random_table,
    cotangent,
):
    both = ("mp", "dp")
    place, rank = lax.axis_index("dp"), lax.axis_index("mp")
    total, model = tokens.shape
    share = total // n_mp
    size = total - MOST
    depth, width = w_value.shape[1], w_value.shape[2]
    hidden = w_up.shape[2]
    heads, rows, columns = random_table.shape

    item_lengths = lengths[0]
    longest = jnp.argmax(item_lengths)
    start = (jnp.cumsum(item_lengths) - item_lengths)[longest]
    first = item_lengths[(longest + 1) % item_lengths.shape[0]].astype(jnp.int32).reshape(1, 1)

    def turned(x, by):
        return lax.dynamic_slice_in_dim(jnp.concatenate([x, x]), by, total)

    def mine(x):
        return lax.dynamic_slice_in_dim(x, rank * share, share)

    gains = jnp.pad(norm_gain.reshape(4, depth).T, ((0, 0), (0, 124)))
    pack = jnp.concatenate([w_value[0], synth_first, synth_second.reshape(depth, -1), gains], axis=1)
    pack = lax.all_gather(pack, "dp")
    spot = 2 * width + synth_second.size // depth
    value_one = pack[:, :, :width].reshape(model, width)
    first_one = pack[:, :, width : 2 * width].reshape(model, width)
    table = pack[:, :, 2 * width : spot].reshape(n_dp, width, total // n_dp)
    table = table.transpose(1, 0, 2).reshape(width, total)[:, :MOST]
    gain = pack[:, :, spot : spot + 4].reshape(model, 4).T.astype(F32)

    def whole(parts):
        joined = lax.all_gather(jnp.concatenate(parts, axis=1), both)
        return joined.reshape(n_mp, model, -1)

    def cut(joined, widths):
        out, spot = [], 0
        for each in widths:
            out.append(joined[:, :, spot : spot + each])
            spot += each
        return out

    out_one, up_one, down_one, value_two = cut(
        whole([w_out[0].T, w_up[0], w_down[0].T, w_value[1]]), (width, hidden, hidden, width)
    )
    out_two, up_two, down_two, value_all, first_all = cut(
        whole([w_out[1].T, w_up[1], w_down[1].T, w_value[0], synth_first]),
        (width, hidden, hidden, width, width),
    )

    begin = jnp.minimum(place * rows, size - rows) if rows < size else 0
    inside = (place * rows < size).astype(BF16)
    corner = jnp.zeros((heads, size, size), BF16)
    corner = lax.dynamic_update_slice(corner, random_table[:, :, :size] * inside, (0, begin, 0))
    corner = lax.psum(corner, "dp")

    inputs = turned(tokens, start).astype(F32)
    normed_one = normalize(inputs, gain[0])
    pre_one = nn(normed_one, first_one)
    acts = jax.nn.gelu(pre_one).astype(BF16)
    values = nn(normed_one, value_one).astype(BF16)
    mixed, lse = dense_forward(first, acts, values, table)
    mixed_one = lax.all_to_all(mixed, "mp", 0, 1, tiled=True)
    inputs_here = mine(inputs)
    middle_one = inputs_here + jnp.einsum(
        "tgw,gdw->td", mixed_one.reshape(share, n_mp, width), out_one, preferred_element_type=F32
    )
    between, feed_one = feed_forward(middle_one, gain[1], up_one, down_one)

    normed_two = normalize(between, gain[2])
    parts = jnp.einsum("gdw,td->gwt", value_two, normed_two, preferred_element_type=F32)
    values_two = heads_out(parts.astype(BF16), n_mp)
    values_all = lax.all_gather(values_two[:, :MOST], "dp")
    mixed, table_lse = random_forward(random_table, values_all)
    mixed = lax.all_to_all(mixed, "dp", 0, 0, tiled=True).transpose(1, 0, 2).reshape(width, total)
    short = short_forward(first, corner, values_two[:, MOST:])
    mixed_two = heads_in(jnp.concatenate([mixed[:, :MOST], short], axis=1), n_mp)
    middle_two = between + jnp.einsum(
        "gwt,gdw->td", mixed_two, out_two, preferred_element_type=F32
    )
    result, feed_two = feed_forward(middle_two, gain[3], up_two, down_two)
    result = lax.all_gather(result.astype(BF16), "mp", tiled=True)
    result = turned(result, total - start)

    grad = mine(turned(cotangent, start)).astype(F32)
    dmiddle, gain_3, up_grad_two, down_grad_two = feed_backward(
        middle_two, gain[3], up_two, down_two, feed_two, grad
    )
    feed_grads = lax.psum_scatter(
        jnp.concatenate([up_grad_two, down_grad_two], axis=2).reshape(n_mp * n_dp, depth, -1),
        both,
        scatter_dimension=0,
    )
    low = dmiddle.astype(BF16)
    out_grad_two = jnp.einsum("td,gwt->gdw", low, mixed_two, preferred_element_type=F32)
    parts = jnp.einsum("gdw,td->gwt", out_two, low, preferred_element_type=F32)
    upstream = heads_out(parts.astype(BF16), n_mp)
    dcorner, dshort = short_backward(first, corner, values_two[:, MOST:], upstream[:, MOST:])
    dcorner = lax.psum(dcorner, "dp")
    upstream = upstream.reshape(width, n_dp, rows).transpose(1, 0, 2)
    upstream = lax.all_to_all(upstream, "dp", 0, 0, tiled=True)
    valid = (place * rows < MOST).astype(F32).reshape(1, 1)
    dtable, dvalues = random_backward(valid, random_table, table_lse, values_all, upstream)
    dvalues = lax.psum_scatter(dvalues, "dp", scatter_dimension=0)
    dvalues = heads_in(jnp.concatenate([dvalues, dshort], axis=1), n_mp)
    value_grad_two = jnp.einsum("td,gwt->gdw", normed_two, dvalues, preferred_element_type=F32)
    dnormed = jnp.einsum("gwt,gdw->td", dvalues, value_two, preferred_element_type=F32)
    dbetween, gain_2 = normalize_back(between, gain[2], dnormed)
    grad = dmiddle + dbetween

    dmiddle, gain_1, up_grad_one, down_grad_one = feed_backward(
        middle_one, gain[1], up_one, down_one, feed_one, grad
    )
    low = dmiddle.astype(BF16)
    out_grad_one = jnp.einsum(
        "td,tgw->gdw", low, mixed_one.reshape(share, n_mp, width), preferred_element_type=F32
    )
    more_grads = lax.psum_scatter(
        jnp.concatenate(
            [
                up_grad_one,
                down_grad_one,
                out_grad_one.astype(BF16),
                out_grad_two.astype(BF16),
                value_grad_two.astype(BF16),
            ],
            axis=2,
        ).reshape(n_mp * n_dp, depth, -1),
        both,
        scatter_dimension=0,
    )
    upstream = jnp.einsum("td,gdw->tgw", low, out_one, preferred_element_type=F32)
    upstream = lax.all_to_all(
        upstream.astype(BF16).reshape(share, n_mp * width), "mp", 1, 0, tiled=True
    )
    dacts, dvalues_t, dsecond = dense_backward(
        first, acts, acts.T, values.T, upstream, upstream.T, table, table.T, lse
    )
    dpre = jax.vjp(jax.nn.gelu, pre_one)[1](dacts)[0].astype(BF16)
    dvalues = dvalues_t.T
    value_grad_one = tn(normed_one, dvalues)
    first_grad = tn(normed_one, dpre)
    dsecond = jnp.pad(dsecond, ((0, 0), (0, size))).reshape(width, n_dp, total // n_dp)
    last_grads = lax.psum_scatter(
        jnp.concatenate(
            [
                value_grad_one.reshape(n_dp, depth, width),
                first_grad.reshape(n_dp, depth, width),
                dsecond.transpose(1, 0, 2).reshape(n_dp, depth, -1),
            ],
            axis=2,
        ).astype(BF16),
        "dp",
        scatter_dimension=0,
    ).astype(F32)
    back = jnp.concatenate([dvalues, dpre], axis=1).reshape(n_mp, share, 2 * width)
    back = lax.all_to_all(back, "mp", 0, 0, tiled=True)
    dnormed = jnp.einsum(
        "gtw,gdw->td", back, jnp.concatenate([value_all, first_all], axis=2), preferred_element_type=F32
    )
    dinputs, gain_0 = normalize_back(inputs_here, gain[0], dnormed)
    input_grad = lax.all_gather((dmiddle + dinputs).astype(BF16), "mp", tiled=True)
    input_grad = turned(input_grad, total - start)

    gain_grad = lax.psum(jnp.stack([gain_0, gain_1, gain_2, gain_3]), both)
    gain_grad = lax.dynamic_slice_in_dim(gain_grad, place * depth, depth, axis=1)
    up_two_g, down_two_g = cut(feed_grads[None], (hidden, hidden))
    up_one_g, down_one_g, out_one_g, out_two_g, value_two_g = cut(
        more_grads[None], (hidden, hidden, width, width, width)
    )
    begin = jnp.minimum(place * rows, size - rows) if rows < size else 0
    dcorner = lax.dynamic_slice(dcorner, (0, begin, 0), (heads, rows, size)) * inside
    random_grad = dtable.at[:, :, :size].add(dcorner.astype(F32))
    swap = lambda x: x[0].T.astype(F32)
    return (
        result,
        input_grad,
        gain_grad.reshape(2, 2, depth),
        jnp.stack([last_grads[:, :width], value_two_g[0].astype(F32)]),
        jnp.stack([swap(out_one_g), swap(out_two_g)]),
        jnp.stack([up_one_g[0].astype(F32), up_two_g[0].astype(F32)]),
        jnp.stack([swap(down_one_g), swap(down_two_g)]),
        last_grads[:, width : 2 * width],
        last_grads[:, 2 * width :].reshape(heads, HD, -1),
        random_grad,
    )


def solution(mesh):
    in_specs = (
        P("dp", None),
        P("dp", None),
        P(None, None, "dp"),
        P(None, "dp", "mp"),
        P(None, "mp", "dp"),
        P(None, "dp", "mp"),
        P(None, "mp", "dp"),
        P("dp", "mp"),
        P("mp", None, "dp"),
        P("mp", "dp", None),
        P("dp", None),
    )
    out_specs = (
        P("dp", None),
        P("dp", None),
        P(None, None, "dp"),
        P(None, "dp", "mp"),
        P(None, "mp", "dp"),
        P(None, "dp", "mp"),
        P(None, "mp", "dp"),
        P("dp", "mp"),
        P("mp", None, "dp"),
        P("mp", "dp", None),
    )
    return jax.shard_map(
        partial(per_device, mesh.shape["dp"], mesh.shape["mp"]),
        mesh=mesh,
        in_specs=in_specs,
        out_specs=out_specs,
        check_vma=False,
    )
```

```python
from functools import partial

import jax
import jax.numpy as jnp
from jax import lax
from jax.experimental import pallas as pl
from jax.experimental.pallas import tpu as pltpu
from jax.sharding import PartitionSpec as P

F32, BF16 = jnp.float32, jnp.bfloat16
HD = 64
MOST = 1792
TILE = 256
VMEM = 58 * 1024 * 1024


def nn(a, b):
    return lax.dot_general(a, b, (((1,), (0,)), ((), ())), preferred_element_type=F32)


def nt(a, b):
    return lax.dot_general(a, b, (((1,), (1,)), ((), ())), preferred_element_type=F32)


def tn(a, b):
    return lax.dot_general(a, b, (((0,), (0,)), ((), ())), preferred_element_type=F32)


def small_masks(first, size):
    row = lax.broadcasted_iota(jnp.int32, (size, size), 0)
    col = lax.broadcasted_iota(jnp.int32, (size, size), 1)
    early = row < first
    inside = col < jnp.where(early, first, size - first)
    shift = jnp.where(col == row + first, 1.0, 0.0).astype(BF16)
    rows = jnp.where(col == jnp.where(early, row, row - first), 1.0, 0.0).astype(BF16)
    return early, inside, shift, rows


def masked_soft(scores, inside):
    masked = jnp.where(inside, scores, -1e30)
    powers = jnp.where(inside, jnp.exp(masked - jnp.max(masked, axis=1, keepdims=True)), 0.0)
    return powers / jnp.sum(powers, axis=1, keepdims=True)


def by_token(soft, early, shift):
    low = soft.astype(BF16)
    zero = jnp.zeros_like(low)
    late = nn(jnp.where(early, zero, low), shift).astype(BF16)
    return jnp.where(early, low, zero) + late


def dense_forward(first, acts, values, table):
    tokens, width = acts.shape
    heads = width // HD
    tiles = MOST // TILE
    size = tokens - MOST

    def kernel(first_ref, acts_ref, values_ref, table_ref, out_ref, lse_ref):
        tile = pl.program_id(0)
        lane = lax.broadcasted_iota(jnp.int32, (TILE, 128), 1)

        @pl.when(tile < tiles)
        def _():
            lse = jnp.zeros((TILE, 128), F32)
            parts = []
            for head in range(heads):
                span = slice(head * HD, (head + 1) * HD)
                scores = nn(acts_ref[:, span], table_ref[span, :])
                top = jnp.max(scores, axis=1, keepdims=True)
                powers = jnp.exp(scores - top)
                total = jnp.sum(powers, axis=1, keepdims=True)
                mixed = nn(powers.astype(BF16), values_ref[0:MOST, span])
                parts.append((mixed / total).astype(BF16))
                lse = jnp.where(lane == head, top + jnp.log(total), lse)
            out_ref[...] = jnp.concatenate(parts, axis=1)
            lse_ref[...] = lse

        @pl.when(tile == tiles)
        def _():
            early, inside, shift, _ = small_masks(first_ref[0, 0], size)
            parts = []
            for head in range(heads):
                span = slice(head * HD, (head + 1) * HD)
                scores = nn(acts_ref[:, span], table_ref[span, 0:size])
                soft = by_token(masked_soft(scores, inside), early, shift)
                parts.append(nn(soft, values_ref[MOST:tokens, span]).astype(BF16))
            out_ref[...] = jnp.concatenate(parts, axis=1)
            lse_ref[...] = jnp.zeros((TILE, 128), F32)

    return pl.pallas_call(
        kernel,
        grid=(tiles + 1,),
        in_specs=[
            pl.BlockSpec(memory_space=pltpu.SMEM),
            pl.BlockSpec((TILE, width), lambda t: (t, 0)),
            pl.BlockSpec((tokens, width), lambda t: (0, 0)),
            pl.BlockSpec((width, MOST), lambda t: (0, 0)),
        ],
        out_specs=[
            pl.BlockSpec((TILE, width), lambda t: (t, 0)),
            pl.BlockSpec((TILE, 128), lambda t: (t, 0)),
        ],
        out_shape=[
            jax.ShapeDtypeStruct((tokens, width), BF16),
            jax.ShapeDtypeStruct((tokens, 128), F32),
        ],
        compiler_params=pltpu.CompilerParams(vmem_limit_bytes=VMEM),
        name="dense_forward",
    )(first, acts, values, table)


def dense_backward(first, acts, acts_t, values_t, upstream, upstream_t, table, table_t, lse):
    tokens, width = acts.shape
    heads = width // HD
    tiles = MOST // TILE
    size = tokens - MOST

    def kernel(first_ref, acts_ref, acts_t_ref, values_t_ref, up_ref, up_t_ref, table_ref, table_t_ref,
               lse_ref, dacts_ref, dvalues_ref, dtable_ref, dv_acc):
        tile = pl.program_id(0)

        @pl.when(tile == 0)
        def _():
            dv_acc[...] = jnp.zeros_like(dv_acc)
            dtable_ref[...] = jnp.zeros_like(dtable_ref)

        @pl.when(tile < tiles)
        def _():
            parts = []
            for head in range(heads):
                span = slice(head * HD, (head + 1) * HD)
                scores = nn(acts_ref[:, span], table_ref[span, :])
                soft = jnp.exp(scores - lse_ref[:, head : head + 1])
                dsoft = nn(up_ref[:, span], values_t_ref[span, 0:MOST])
                dv_acc[span, :] += nn(up_t_ref[span, :], soft.astype(BF16))
                weighed = soft * dsoft
                centre = jnp.sum(weighed, axis=1, keepdims=True)
                dscores = (weighed - soft * centre).astype(BF16)
                dtable_ref[span, :] += nn(acts_t_ref[span, :], dscores)
                parts.append(nn(dscores, table_t_ref[:, span]))
            dacts_ref[...] = jnp.concatenate(parts, axis=1)

        @pl.when(tile == tiles)
        def _():
            early, inside, shift, _ = small_masks(first_ref[0, 0], size)
            parts = []
            for head in range(heads):
                span = slice(head * HD, (head + 1) * HD)
                scores = nn(acts_ref[:, span], table_ref[span, 0:size])
                soft = masked_soft(scores, inside)
                here = values_t_ref[span, MOST:tokens]
                moved = nt(here, shift).astype(BF16)
                dsoft = jnp.where(early, nn(up_ref[:, span], here), nn(up_ref[:, span], moved))
                dvalues_ref[span, MOST:tokens] = nn(up_t_ref[span, :], by_token(soft, early, shift)).astype(BF16)
                centre = jnp.sum(soft * dsoft, axis=1, keepdims=True)
                dscores = (soft * (dsoft - centre)).astype(BF16)
                dtable_ref[span, 0:size] += nn(acts_t_ref[span, :], dscores)
                parts.append(nn(dscores, table_t_ref[0:size, span]))
            dacts_ref[...] = jnp.concatenate(parts, axis=1)
            dvalues_ref[:, 0:MOST] = dv_acc[...].astype(BF16)

    whole = lambda t: (0, 0)
    return pl.pallas_call(
        kernel,
        grid=(tiles + 1,),
        in_specs=[
            pl.BlockSpec(memory_space=pltpu.SMEM),
            pl.BlockSpec((TILE, width), lambda t: (t, 0)),
            pl.BlockSpec((width, TILE), lambda t: (0, t)),
            pl.BlockSpec((width, tokens), whole),
            pl.BlockSpec((TILE, width), lambda t: (t, 0)),
            pl.BlockSpec((width, TILE), lambda t: (0, t)),
            pl.BlockSpec((width, MOST), whole),
            pl.BlockSpec((MOST, width), whole),
            pl.BlockSpec((TILE, 128), lambda t: (t, 0)),
        ],
        out_specs=[
            pl.BlockSpec((TILE, width), lambda t: (t, 0)),
            pl.BlockSpec((width, tokens), whole),
            pl.BlockSpec((width, MOST), whole),
        ],
        out_shape=[
            jax.ShapeDtypeStruct((tokens, width), F32),
            jax.ShapeDtypeStruct((width, tokens), BF16),
            jax.ShapeDtypeStruct((width, MOST), F32),
        ],
        scratch_shapes=[pltpu.VMEM((width, MOST), F32)],
        compiler_params=pltpu.CompilerParams(vmem_limit_bytes=VMEM),
        name="dense_backward",
    )(first, acts, acts_t, values_t, upstream, upstream_t, table, table_t, lse)


def random_forward(table, values_t):
    heads, rows, _ = table.shape
    slots, width, _ = values_t.shape

    def kernel(table_ref, values_ref, out_ref, lse_ref):
        scores = table_ref[0, :, 0:MOST].astype(F32)
        top = jnp.max(scores, axis=1, keepdims=True)
        powers = jnp.exp(scores - top)
        total = jnp.sum(powers, axis=1, keepdims=True)
        soft = (powers / total).astype(BF16)
        values = values_ref[...].reshape(slots * HD, MOST)
        out_ref[...] = nt(values, soft).astype(BF16).reshape(slots, HD, rows)
        lse_ref[...] = jnp.broadcast_to(top + jnp.log(total), (1, rows, 128))

    return pl.pallas_call(
        kernel,
        grid=(heads,),
        in_specs=[
            pl.BlockSpec((1, rows, table.shape[2]), lambda h: (h, 0, 0)),
            pl.BlockSpec((slots, HD, MOST), lambda h: (0, h, 0)),
        ],
        out_specs=[
            pl.BlockSpec((slots, HD, rows), lambda h: (0, h, 0)),
            pl.BlockSpec((1, rows, 128), lambda h: (h, 0, 0)),
        ],
        out_shape=[
            jax.ShapeDtypeStruct((slots, width, rows), BF16),
            jax.ShapeDtypeStruct((heads, rows, 128), F32),
        ],
        compiler_params=pltpu.CompilerParams(vmem_limit_bytes=VMEM),
        name="random_forward",
    )(table, values_t)


def random_backward(valid, table, lse, values_t, upstream_t):
    heads, rows, columns = table.shape
    slots, width, _ = values_t.shape
    buffers = pl.Buffered(2 if slots <= 16 else 1)

    def kernel(valid_ref, table_ref, lse_ref, values_ref, up_ref, dtable_ref, dvalues_ref):
        soft = jnp.exp(table_ref[0, :, 0:MOST].astype(F32) - lse_ref[0, :, 0:1])
        up = up_ref[...].reshape(slots * HD, rows) * valid_ref[0, 0].astype(BF16)
        values = values_ref[...].reshape(slots * HD, MOST)
        dsoft = tn(up, values)
        weighed = soft * dsoft
        centre = jnp.sum(weighed, axis=1, keepdims=True)
        dtable_ref[0, :, 0:MOST] = weighed - soft * centre
        dtable_ref[0, :, MOST:columns] = jnp.zeros((rows, columns - MOST), F32)
        dvalues_ref[...] = nn(up, soft.astype(BF16)).astype(BF16).reshape(slots, HD, MOST)

    return pl.pallas_call(
        kernel,
        grid=(heads,),
        in_specs=[
            pl.BlockSpec(memory_space=pltpu.SMEM),
            pl.BlockSpec((1, rows, columns), lambda h: (h, 0, 0)),
            pl.BlockSpec((1, rows, 128), lambda h: (h, 0, 0)),
            pl.BlockSpec((slots, HD, MOST), lambda h: (0, h, 0), pipeline_mode=buffers),
            pl.BlockSpec((slots, HD, rows), lambda h: (0, h, 0)),
        ],
        out_specs=[
            pl.BlockSpec((1, rows, columns), lambda h: (h, 0, 0)),
            pl.BlockSpec((slots, HD, MOST), lambda h: (0, h, 0)),
        ],
        out_shape=[
            jax.ShapeDtypeStruct((heads, rows, columns), F32),
            jax.ShapeDtypeStruct((slots, width, MOST), BF16),
        ],
        compiler_params=pltpu.CompilerParams(vmem_limit_bytes=VMEM),
        name="random_backward",
    )(valid, table, lse, values_t, upstream_t)


def short_forward(first, corner, values_t):
    heads, size, _ = corner.shape
    width = values_t.shape[0]

    def kernel(first_ref, corner_ref, values_ref, out_ref):
        early, inside, shift, rows = small_masks(first_ref[0, 0], size)
        for head in range(heads):
            span = slice(head * HD, (head + 1) * HD)
            soft = by_token(masked_soft(nn(rows, corner_ref[head]), inside), early, shift)
            out_ref[span, :] = nt(values_ref[span, :], soft).astype(BF16)

    return pl.pallas_call(
        kernel,
        in_specs=[
            pl.BlockSpec(memory_space=pltpu.SMEM),
            pl.BlockSpec(memory_space=pltpu.VMEM),
            pl.BlockSpec(memory_space=pltpu.VMEM),
        ],
        out_specs=pl.BlockSpec(memory_space=pltpu.VMEM),
        out_shape=jax.ShapeDtypeStruct((width, size), BF16),
        name="short_forward",
    )(first, corner, values_t)


def short_backward(first, corner, values_t, upstream_t):
    heads, size, _ = corner.shape
    width = values_t.shape[0]

    def kernel(first_ref, corner_ref, values_ref, up_ref, dcorner_ref, dvalues_ref):
        early, inside, shift, rows = small_masks(first_ref[0, 0], size)
        for head in range(heads):
            span = slice(head * HD, (head + 1) * HD)
            soft = masked_soft(nn(rows, corner_ref[head]), inside)
            here, up = values_ref[span, :], up_ref[span, :]
            moved = nt(here, shift).astype(BF16)
            dsoft = jnp.where(early, tn(up, here), tn(up, moved))
            dvalues_ref[span, :] = nn(up, by_token(soft, early, shift)).astype(BF16)
            centre = jnp.sum(soft * dsoft, axis=1, keepdims=True)
            dscores = (soft * (dsoft - centre)).astype(BF16)
            dcorner_ref[head] = tn(rows, dscores).astype(BF16)

    return pl.pallas_call(
        kernel,
        in_specs=[
            pl.BlockSpec(memory_space=pltpu.SMEM),
            pl.BlockSpec(memory_space=pltpu.VMEM),
            pl.BlockSpec(memory_space=pltpu.VMEM),
            pl.BlockSpec(memory_space=pltpu.VMEM),
        ],
        out_specs=[
            pl.BlockSpec(memory_space=pltpu.VMEM),
            pl.BlockSpec(memory_space=pltpu.VMEM),
        ],
        out_shape=[
            jax.ShapeDtypeStruct((heads, size, size), BF16),
            jax.ShapeDtypeStruct((width, size), BF16),
        ],
        name="short_backward",
    )(first, corner, values_t, upstream_t)


MESH = pl.DeviceIdType.MESH
ANY = pl.BlockSpec(memory_space=pl.ANY)
INTO = pl.BlockSpec(memory_space=pltpu.VMEM)
SCALAR = pl.BlockSpec(memory_space=pltpu.SMEM)
DMA = pltpu.SemaphoreType.DMA


def remote(source, target, send, recv, axis, index):
    return pltpu.make_async_remote_copy(
        src_ref=source, dst_ref=target, send_sem=send, recv_sem=recv, device_id={axis: index}, device_id_type=MESH
    )


def greet(groups):
    barrier = pltpu.get_barrier_semaphore()
    for axis, size in groups:
        me = lax.axis_index(axis)
        for step in range(1, size):
            pl.semaphore_signal(
                barrier, inc=1, device_id={axis: lax.rem(me + step, size)}, device_id_type=MESH
            )
    pl.semaphore_wait(barrier, sum(size - 1 for _, size in groups))


def comm_params(number):
    return pltpu.CompilerParams(collective_id=number, has_side_effects=True, vmem_limit_bytes=VMEM)


class Line:
    def __init__(self, size):
        self.size, self.length = size, size // 2
        self.place = lax.axis_index("dp")
        self.at, self.side = self.place // 2, lax.rem(self.place, 2)
        self.partner = self.at * 2 + 1 - self.side
        self.right, self.left = self.place + 2, self.place - 2
        self.has_right, self.has_left = self.at + 1 < self.length, self.at > 0


def line_gather(line, own, slots, send_x, send_z, recv, begin, use):
    length, at, side = line.length, line.at, line.side

    def push(source, s, send, to):
        remote(source, slots.at[s], send, recv.at[s], "dp", to).start()

    def landed(s):
        remote(own, slots.at[s], send_x.at[0], recv.at[s], "dp", line.partner).wait_recv()

    push(own, line.place, send_x.at[at], line.partner)

    @pl.when(line.has_right)
    def _():
        push(own, line.place, send_z.at[0, at], line.right)

    @pl.when(line.has_left)
    def _():
        push(own, line.place, send_z.at[1, at], line.left)

    def arrive(a, way):
        s = a * 2 + side
        landed(s)
        on, to = ((line.has_right, line.right), (line.has_left, line.left))[way]

        @pl.when(on)
        def _():
            push(slots.at[s], s, send_z.at[way, a], to)

        push(slots.at[s], s, send_x.at[a], line.partner)

    def across(a):
        s = a * 2 + 1 - side
        landed(s)
        use(s)

    begin()
    across(at)

    @pl.loop(1, length)
    def _(k):
        @pl.when(at - k >= 0)
        def _():
            arrive(at - k, 0)

        @pl.when(at + k < length)
        def _():
            arrive(at + k, 1)

        @pl.when(at - k >= 0)
        def _():
            use((at - k) * 2 + side)
            across(at - k)

        @pl.when(at + k < length)
        def _():
            use((at + k) * 2 + side)
            across(at + k)

    @pl.loop(0, length)
    def _(a):
        def sent(send):
            remote(own, slots.at[0], send, recv.at[0], "dp", line.partner).wait_send()

        sent(send_x.at[a])

        @pl.when(jnp.logical_and(line.has_right, a <= at))
        def _():
            sent(send_z.at[0, a])

        @pl.when(jnp.logical_and(line.has_left, a >= at))
        def _():
            sent(send_z.at[1, a])


def line_scatter(line, make, middle, out, x_out, x_in, z_out, l_in, r_in, sems):
    length, at, side = line.length, line.at, line.side
    send_x, recv_x, send_z, recv_l, recv_r = sems

    def cross(a):
        x_out[a] = make(a * 2 + 1 - side).astype(BF16)
        remote(x_out.at[a], x_in.at[a], send_x.at[a], recv_x.at[a], "dp", line.partner).start()

    def crossed(a):
        remote(x_out.at[a], x_in.at[a], send_x.at[a], recv_x.at[a], "dp", line.partner).wait_recv()

    def from_left(a, to=line.partner):
        return remote(z_out.at[a], l_in.at[a], send_z.at[a], recv_l.at[a], "dp", to)

    def from_right(a, to=line.partner):
        return remote(z_out.at[a], r_in.at[a], send_z.at[a], recv_r.at[a], "dp", to)

    @pl.loop(0, length - 1)
    def _(step):
        k = length - 1 - step

        @pl.when(at + k < length)
        def _():
            cross(at + k)

        @pl.when(at - k >= 0)
        def _():
            cross(at - k)

    cross(at)
    middle()

    def relay(a, behind, copy):
        total = make(a * 2 + side)
        crossed(a)
        z_out[a] = (total + x_in[a].astype(F32)).astype(BF16)

        @pl.when(behind)
        def _():
            copy(a).wait_recv()
            into = l_in if copy is from_left else r_in
            z_out[a] = (z_out[a].astype(F32) + into[a].astype(F32)).astype(BF16)

        copy(a, line.right if copy is from_left else line.left).start()

    @pl.loop(0, length - 1)
    def _(step):
        k = length - 1 - step

        @pl.when(at + k < length)
        def _():
            relay(at + k, line.has_left, from_left)

        @pl.when(at - k >= 0)
        def _():
            relay(at - k, line.has_right, from_right)

    total = make(line.place)
    crossed(at)
    out[...] = total + x_in[at].astype(F32)

    @pl.when(line.has_left)
    def _():
        from_left(at).wait_recv()
        out[...] += l_in[at].astype(F32)

    @pl.when(line.has_right)
    def _():
        from_right(at).wait_recv()
        out[...] += r_in[at].astype(F32)

    @pl.loop(0, length)
    def _(a):
        remote(x_out.at[a], x_in.at[a], send_x.at[a], recv_x.at[a], "dp", line.partner).wait_send()

        @pl.when(a != at)
        def _():
            from_left(a).wait_send()


def scatter_scratch(length, shape):
    return [pltpu.VMEM((length,) + shape, BF16)] * 5 + [DMA((length,))] * 5


def gather_weights(pack, corner, n):
    def kernel(pack_ref, corner_ref, all_ref, got_ref, send_x, send_z, recv, c_send, c_recv, own_sem):
        line = Line(n)
        greet([("dp", n)])
        own = pltpu.make_async_copy(pack_ref, all_ref.at[line.place], own_sem.at[0])
        own.start()
        keep = pltpu.make_async_copy(corner_ref, got_ref, own_sem.at[1])

        def across(source):
            return remote(source, got_ref, c_send.at[0], c_recv, "dp", line.partner)

        def along(source, to=line.partner):
            return remote(source, got_ref, c_send.at[1], c_recv, "dp", to)

        @pl.when(line.place == 0)
        def _():
            keep.start()
            across(corner_ref).start()
            along(corner_ref, line.right).start()

        line_gather(line, pack_ref, all_ref, send_x, send_z, recv, lambda: None, lambda s: None)

        @pl.when(line.place > 0)
        def _():
            across(got_ref).wait_recv()

        @pl.when(jnp.logical_and(line.side == 0, line.place > 0))
        def _():
            across(got_ref).start()

            @pl.when(line.has_right)
            def _():
                along(got_ref, line.right).start()

        @pl.when(line.side == 0)
        def _():
            across(got_ref).wait_send()

            @pl.when(line.has_right)
            def _():
                along(got_ref).wait_send()

        @pl.when(line.place == 0)
        def _():
            keep.wait()

        own.wait()

    return pl.pallas_call(
        kernel,
        in_specs=[ANY, ANY],
        out_specs=[ANY, ANY],
        out_shape=[
            jax.ShapeDtypeStruct((n,) + pack.shape, BF16),
            jax.ShapeDtypeStruct(corner.shape, BF16),
        ],
        scratch_shapes=[DMA((n // 2,)), DMA((2, n // 2)), DMA((n,)), DMA((2,)), DMA, DMA((2,))],
        compiler_params=comm_params(0),
        name="gather_weights",
    )(pack, corner)


def swap(x, n, number, lanes_in=False, lanes_out=False):
    if lanes_in:
        block = (x.shape[0], x.shape[1] // n)
    else:
        block = x.shape[1:]
    shape = (block[0], n * block[1]) if lanes_out else (n,) + block

    def at(ref, lanes, j):
        if lanes:
            return ref.at[:, pl.ds(pl.multiple_of(j * block[1], block[1]), block[1])]
        return ref.at[j]

    def kernel(x_ref, out_ref, send, recv, own_sem):
        me = lax.axis_index("mp")
        greet([("mp", n)])
        copies = []
        for step in range(1, n):
            peer = lax.rem(me + step, n)
            copies.append(
                remote(at(x_ref, lanes_in, peer), at(out_ref, lanes_out, me), send.at[step], recv.at[step], "mp", peer)
            )
            copies[-1].start()
        own = pltpu.make_async_copy(at(x_ref, lanes_in, me), at(out_ref, lanes_out, me), own_sem)
        own.start()
        own.wait()
        for copy in copies:
            copy.wait()

    return pl.pallas_call(
        kernel,
        in_specs=[ANY],
        out_specs=ANY,
        out_shape=jax.ShapeDtypeStruct(shape, x.dtype),
        scratch_shapes=[DMA((n,)), DMA((n,)), DMA],
        compiler_params=comm_params(number),
        name="swap",
    )(x)


def table_forward(first, table, corner, values_t, n):
    heads, rows, columns = table.shape
    width, tokens = values_t.shape
    size = tokens - MOST
    owners = MOST // rows

    def kernel(first_ref, table_ref, corner_ref, own_ref, values_ref, mixed_ref, lse_ref,
               soft, sums, send_x, send_z, recv, send_m, recv_m):
        line = Line(n)
        place = line.place
        values_ref[place] = own_ref[:, 0:MOST]
        greet([("dp", n)])
        owner = place < owners

        def prepare():
            for head in range(heads):
                scores = table_ref[head, :, 0:MOST].astype(F32)
                top = jnp.max(scores, axis=1, keepdims=True)
                powers = jnp.exp(scores - top)
                total = jnp.sum(powers, axis=1, keepdims=True)
                soft[head] = (powers / total).astype(BF16)
                lse_ref[head] = jnp.broadcast_to(top + jnp.log(total), (rows, 128))
            early, inside, shift, at = small_masks(first_ref[0, 0], size)
            for head in range(heads):
                span = slice(head * HD, (head + 1) * HD)
                weights = by_token(masked_soft(nn(at, corner_ref[head]), inside), early, shift)
                mixed_ref[owners, span, :] = nt(own_ref[span, MOST:tokens], weights).astype(BF16)

        def back(s):
            return remote(sums.at[s], mixed_ref.at[place], send_m.at[s], recv_m.at[place], "dp", s)

        def product(s, head):
            span = slice(head * HD, (head + 1) * HD)
            return nt(values_ref[s, span, :], soft[head]).astype(BF16)

        def begin():
            prepare()

            @pl.when(owner)
            def _():
                for head in range(heads):
                    mixed_ref[place, head * HD : (head + 1) * HD, :] = product(place, head)

        def use(s):
            @pl.when(owner)
            def _():
                for head in range(heads):
                    sums[s, head * HD : (head + 1) * HD, :] = product(s, head)
                back(s).start()

        line_gather(line, values_ref.at[place], values_ref, send_x, send_z, recv, begin, use)

        @pl.loop(0, n)
        def _(s):
            @pl.when(jnp.logical_and(owner, s != place))
            def _():
                back(s).wait_send()

            @pl.when(jnp.logical_and(s < owners, s != place))
            def _():
                remote(sums.at[0], mixed_ref.at[s], send_m.at[0], recv_m.at[s], "dp", s).wait_recv()

    return pl.pallas_call(
        kernel,
        in_specs=[SCALAR, INTO, INTO, INTO],
        out_specs=[INTO, INTO, INTO],
        out_shape=[
            jax.ShapeDtypeStruct((n, width, MOST), BF16),
            jax.ShapeDtypeStruct((n, width, rows), BF16),
            jax.ShapeDtypeStruct((heads, rows, 128), F32),
        ],
        scratch_shapes=[
            pltpu.VMEM((heads, rows, MOST), BF16),
            pltpu.VMEM((n, width, rows), BF16),
            DMA((n // 2,)),
            DMA((2, n // 2)),
            DMA((n,)),
            DMA((n,)),
            DMA((n,)),
        ],
        compiler_params=comm_params(1),
        name="table_forward",
    )(first, table, corner, values_t)


def table_backward(first, table, corner, lse, values, short_t, upstream, n):
    heads, rows, columns = table.shape
    width, size = short_t.shape
    owners = MOST // rows
    length = n // 2

    def kernel(first_ref, table_ref, corner_ref, lse_ref, values_ref, short_ref, up_ref, dtable_ref, dvalues_ref,
               ups, total, soft, dcorner, c_x, c_z, send_u, recv_u, c_send, c_recv, *rest):
        line = Line(n)
        place = line.place
        greet([("dp", n)])
        owner = place < owners

        def hand(s):
            return remote(up_ref.at[s], ups.at[place], send_u.at[s], recv_u.at[place], "dp", s)

        @pl.loop(0, owners)
        def _(s):
            @pl.when(s != place)
            def _():
                hand(s).start()

        early, inside, shift, at = small_masks(first_ref[0, 0], size)
        for head in range(heads):
            span = slice(head * HD, (head + 1) * HD)
            weights = masked_soft(nn(at, corner_ref[head]), inside)
            here, up = short_ref[span, :], up_ref[n - 1, span, :]
            moved = nt(here, shift).astype(BF16)
            dsoft = jnp.where(early, tn(up, here), tn(up, moved))
            dvalues_ref[span, MOST : MOST + size] = nn(up, by_token(weights, early, shift)).astype(BF16)
            centre = jnp.sum(weights * dsoft, axis=1, keepdims=True)
            dcorner[head] = tn(at, (weights * (dsoft - centre)).astype(BF16)).astype(BF16)

        def corner_across():
            return remote(dcorner, c_x, c_send.at[0], c_recv.at[0], "dp", line.partner)

        def corner_along(to=line.partner):
            return remote(dcorner, c_z, c_send.at[1], c_recv.at[1], "dp", to)

        @pl.when(line.side == 1)
        def _():
            corner_across().start()

        for head in range(heads):
            soft[head] = jnp.exp(table_ref[head, :, 0:MOST].astype(F32) - lse_ref[head, :, 0:1]).astype(BF16)

        @pl.when(owner)
        def _():
            ups[place] = up_ref[place]

            @pl.loop(0, n)
            def _(s):
                @pl.when(s != place)
                def _():
                    remote(up_ref.at[0], ups.at[s], send_u.at[0], recv_u.at[s], "dp", s).wait_recv()

        @pl.when(jnp.logical_not(owner))
        def _():
            ups[...] = jnp.zeros_like(ups)

        def make(s):
            return jnp.concatenate(
                [nn(ups[s, head * HD : (head + 1) * HD, :], soft[head]) for head in range(heads)], axis=0
            )

        def middle():
            for head in range(heads):
                span = slice(head * HD, (head + 1) * HD)
                up = ups[:, span, :].reshape(n * HD, rows)
                dsoft = tn(up, values_ref[:, span, :].reshape(n * HD, MOST))
                weights = jnp.exp(table_ref[head, :, 0:MOST].astype(F32) - lse_ref[head, :, 0:1])
                weighed = weights * dsoft
                centre = jnp.sum(weighed, axis=1, keepdims=True)
                dtable_ref[head, :, 0:MOST] = weighed - weights * centre
                dtable_ref[head, :, MOST:columns] = jnp.zeros((rows, columns - MOST), F32)

        line_scatter(line, make, middle, total, *rest[:5], rest[5:])
        dvalues_ref[:, 0:MOST] = total[...].astype(BF16)

        @pl.when(line.side == 1)
        def _():
            corner_across().wait_send()

        @pl.when(line.side == 0)
        def _():
            corner_across().wait_recv()
            dcorner[...] = (dcorner[...].astype(F32) + c_x[...].astype(F32)).astype(BF16)

            @pl.when(line.has_right)
            def _():
                corner_along().wait_recv()
                dcorner[...] = (dcorner[...].astype(F32) + c_z[...].astype(F32)).astype(BF16)

            @pl.when(line.has_left)
            def _():
                corner_along(line.left).start()
                corner_along().wait_send()

            @pl.when(place == 0)
            def _():
                dtable_ref[:, :, 0:size] += dcorner[...].astype(F32)

        @pl.loop(0, owners)
        def _(s):
            @pl.when(s != place)
            def _():
                hand(s).wait_send()

    return pl.pallas_call(
        kernel,
        in_specs=[SCALAR] + [INTO] * 6,
        out_specs=[INTO] * 2,
        out_shape=[
            jax.ShapeDtypeStruct((heads, rows, columns), F32),
            jax.ShapeDtypeStruct((width, MOST + size), BF16),
        ],
        scratch_shapes=[
            pltpu.VMEM((n, width, rows), BF16),
            pltpu.VMEM((width, MOST), F32),
            pltpu.VMEM((heads, rows, MOST), BF16),
            pltpu.VMEM((heads, size, size), BF16),
            pltpu.VMEM((heads, size, size), BF16),
            pltpu.VMEM((heads, size, size), BF16),
            DMA((n,)),
            DMA((n,)),
            DMA((2,)),
            DMA((2,)),
        ]
        + scatter_scratch(length, (width, MOST)),
        compiler_params=comm_params(2),
        name="table_backward",
    )(first, table, corner, lse, values, short_t, upstream)


def last_exchange(back, grads, n, n_mp):
    def kernel(back_ref, grads_ref, got_ref, out_ref, send, recv, own_sem, *rest):
        line = Line(n)
        me = lax.axis_index("mp")
        greet([("dp", n), ("mp", n_mp)])
        copies = []
        for step in range(1, n_mp):
            peer = lax.rem(me + step, n_mp)
            copies.append(
                remote(back_ref.at[peer], got_ref.at[me], send.at[step], recv.at[step], "mp", peer)
            )
            copies[-1].start()
        own = pltpu.make_async_copy(back_ref.at[me], got_ref.at[me], own_sem)
        own.start()
        line_scatter(
            line, lambda s: grads_ref[s].astype(F32), lambda: None, out_ref, *rest[:5], rest[5:]
        )
        own.wait()
        for copy in copies:
            copy.wait()

    return pl.pallas_call(
        kernel,
        in_specs=[ANY, INTO],
        out_specs=[ANY, INTO],
        out_shape=[
            jax.ShapeDtypeStruct(back.shape, BF16),
            jax.ShapeDtypeStruct(grads.shape[1:], F32),
        ],
        scratch_shapes=[DMA((n_mp,)), DMA((n_mp,)), DMA] + scatter_scratch(n // 2, grads.shape[1:]),
        compiler_params=comm_params(3),
        name="last_exchange",
    )(back, grads)


def finish(x, gains, n, n_mp):
    pairs = n_mp // 2

    def kernel(x_ref, gains_ref, all_ref, sum_ref, one, two, send, recv, own_sem, g_send, g_recv, h_send, h_recv):
        me, place = lax.axis_index("mp"), lax.axis_index("dp")
        pair, core = me // 2, lax.rem(me, 2)
        twin = pair * 2 + 1 - core
        greet([("dp", n), ("mp", n_mp)])
        own = pltpu.make_async_copy(x_ref, all_ref.at[me], own_sem)
        far = []
        for step in range(1, pairs):
            to = lax.rem(pair + step, pairs) * 2 + core
            far.append(remote(x_ref, all_ref.at[me], send.at[step], recv.at[step], "mp", to))
            far[-1].start()
        near = [remote(x_ref, all_ref.at[me], send.at[0], recv.at[0], "mp", twin)]
        near[0].start()
        own.start()
        one[me] = gains_ref[...]
        firsts = []
        for step in range(1, n_mp):
            to = lax.rem(me + step, n_mp)
            firsts.append(remote(gains_ref, one.at[me], g_send.at[step], g_recv.at[step], "mp", to))
            firsts[-1].start()
        for copy in firsts:
            copy.wait()
        total = one[0]
        for j in range(1, n_mp):
            total += one[j]
        two[place] = total

        def spread(step, there):
            return remote(two.at[place], two.at[there], h_send.at[step], h_recv.at[step], "dp", lax.rem(place + step, n))

        @pl.loop(1, n)
        def _(step):
            spread(step, place).start()

        for step in range(1, pairs):
            far[step - 1].wait_recv()
            source = lax.rem(pair + pairs - step, pairs) * 2 + core
            near.append(
                remote(all_ref.at[source], all_ref.at[source], send.at[pairs + step], recv.at[pairs + step], "mp", twin)
            )
            near[-1].start()

        @pl.loop(1, n)
        def _(step):
            spread(step, place).wait_send()
            spread(step, lax.rem(place + n - step, n)).wait_recv()

        total = two[0]
        for j in range(1, n):
            total += two[j]
        sum_ref[...] = total
        for copy in far:
            copy.wait_send()
        for copy in near:
            copy.wait()
        own.wait()

    return pl.pallas_call(
        kernel,
        in_specs=[ANY, INTO],
        out_specs=[ANY, INTO],
        out_shape=[
            jax.ShapeDtypeStruct((n_mp,) + x.shape, x.dtype),
            jax.ShapeDtypeStruct(gains.shape, F32),
        ],
        scratch_shapes=[
            pltpu.VMEM((n_mp,) + gains.shape, F32),
            pltpu.VMEM((n,) + gains.shape, F32),
            DMA((2 * pairs,)),
            DMA((2 * pairs,)),
            DMA,
            DMA((n_mp,)),
            DMA((n_mp,)),
            DMA((n,)),
            DMA((n,)),
        ],
        compiler_params=comm_params(4),
        name="finish",
    )(x, gains)


EPS = 1e-06


def root(x):
    return lax.rsqrt(jnp.mean(x * x, axis=-1, keepdims=True) + EPS)


def normalize(x, gain):
    return (x * root(x) * gain).astype(BF16)


def normalize_back(x, gain, grad):
    scale = root(x)
    weighed = grad * gain
    pull = jnp.mean(weighed * x, axis=-1, keepdims=True)
    return scale * weighed - x * (scale * scale * scale * pull), jnp.sum(grad * x * scale, axis=0)


def feed_forward(middle, gain, up, down_t):
    normed = normalize(middle, gain)
    out, kept = middle, []
    for group in range(up.shape[0]):
        pre = nn(normed, up[group])
        hidden = jax.nn.gelu(pre).astype(BF16)
        out = out + nt(hidden, down_t[group])
        kept.append((pre, hidden))
    return out, (normed, kept)


def feed_backward(middle, gain, up, down_t, record, grad):
    normed, kept = record
    low = grad.astype(BF16)
    up_grads, down_grads, dnormed = [], [], 0.0
    for group in range(up.shape[0]):
        pre, hidden = kept[group]
        down_grads.append(tn(low, hidden).astype(BF16))
        dpre = jax.vjp(jax.nn.gelu, pre)[1](nn(low, down_t[group]))[0].astype(BF16)
        up_grads.append(tn(normed, dpre).astype(BF16))
        dnormed = dnormed + nt(dpre, up[group])
    dmiddle, gain_grad = normalize_back(middle, gain, dnormed)
    return grad + dmiddle, gain_grad, jnp.stack(up_grads), jnp.stack(down_grads)


def per_device(
    n_dp,
    n_mp,
    tokens,
    lengths,
    norm_gain,
    w_value,
    w_out,
    w_up,
    w_down,
    synth_first,
    synth_second,
    random_table,
    cotangent,
):
    both = ("mp", "dp")
    place, rank = lax.axis_index("dp"), lax.axis_index("mp")
    total, model = tokens.shape
    share = total // n_mp
    size = total - MOST
    depth, width = w_value.shape[1], w_value.shape[2]
    hidden = w_up.shape[2]
    heads, rows, columns = random_table.shape

    item_lengths = lengths[0]
    longest = jnp.argmax(item_lengths)
    start = (jnp.cumsum(item_lengths) - item_lengths)[longest]
    first = item_lengths[(longest + 1) % item_lengths.shape[0]].astype(jnp.int32).reshape(1, 1)

    def turned(x, by):
        return lax.dynamic_slice_in_dim(jnp.concatenate([x, x]), by, total)

    def mine(x):
        return lax.dynamic_slice_in_dim(x, rank * share, share)

    gains = jnp.pad(norm_gain.reshape(4, depth).T, ((0, 0), (0, 124)))
    pack = jnp.concatenate([w_value[0], synth_first, synth_second.reshape(depth, -1), gains], axis=1)
    near = rows == size and n_dp % 2 == 0 and n_dp * width * MOST <= 4 << 20
    if near:
        pack, corner = gather_weights(pack, random_table[:, :, :size], n_dp)
    else:
        pack = lax.all_gather(pack, "dp")
    spot = 2 * width + synth_second.size // depth
    value_one = pack[:, :, :width].reshape(model, width)
    first_one = pack[:, :, width : 2 * width].reshape(model, width)
    table = pack[:, :, 2 * width : spot].reshape(n_dp, width, total // n_dp)
    table = table.transpose(1, 0, 2).reshape(width, total)[:, :MOST]
    gain = pack[:, :, spot : spot + 4].reshape(model, 4).T.astype(F32)

    def whole(parts):
        joined = lax.all_gather(jnp.concatenate(parts, axis=1), both)
        return joined.reshape(n_mp, model, -1)

    def cut(joined, widths):
        out, spot = [], 0
        for each in widths:
            out.append(joined[:, :, spot : spot + each])
            spot += each
        return out

    out_one, up_one, down_one, value_two = cut(
        whole([w_out[0].T, w_up[0], w_down[0].T, w_value[1]]), (width, hidden, hidden, width)
    )
    out_two, up_two, down_two, value_all, first_all = cut(
        whole([w_out[1].T, w_up[1], w_down[1].T, w_value[0], synth_first]),
        (width, hidden, hidden, width, width),
    )

    if not near:
        begin = jnp.minimum(place * rows, size - rows)
        inside = (place * rows < size).astype(BF16)
        corner = jnp.zeros((heads, size, size), BF16)
        corner = lax.dynamic_update_slice(corner, random_table[:, :, :size] * inside, (0, begin, 0))
        corner = lax.psum(corner, "dp")

    inputs = turned(tokens, start).astype(F32)
    normed_one = normalize(inputs, gain[0])
    pre_one = nn(normed_one, first_one)
    acts = jax.nn.gelu(pre_one).astype(BF16)
    values = nn(normed_one, value_one).astype(BF16)
    mixed, lse = dense_forward(first, acts, values, table)
    mixed_one = swap(mixed.reshape(n_mp, share, width), n_mp, 5)
    inputs_here = mine(inputs)
    middle_one = inputs_here + jnp.einsum("gtw,gdw->td", mixed_one, out_one, preferred_element_type=F32)
    between, feed_one = feed_forward(middle_one, gain[1], up_one, down_one)

    normed_two = normalize(between, gain[2])
    parts = jnp.einsum("gdw,td->gwt", value_two, normed_two, preferred_element_type=F32)
    values_two = swap(parts.astype(BF16), n_mp, 6, lanes_out=True)
    if near:
        values_all, mixed, table_lse = table_forward(first, random_table, corner, values_two, n_dp)
        mixed_two = swap(mixed.reshape(n_mp, -1, width, rows), n_mp, 7)
    else:
        values_all = lax.all_gather(values_two[:, :MOST], "dp")
        mixed, table_lse = random_forward(random_table, values_all)
        mixed = lax.all_to_all(mixed, "dp", 0, 0, tiled=True).transpose(1, 0, 2).reshape(width, total)
        short = short_forward(first, corner, values_two[:, MOST:])
        mixed_two = swap(jnp.concatenate([mixed[:, :MOST], short], axis=1), n_mp, 7, lanes_in=True)[:, None]
    middle_two = between + jnp.einsum(
        "gcwt,gdw->ctd", mixed_two, out_two, preferred_element_type=F32
    ).reshape(share, model)
    result, feed_two = feed_forward(middle_two, gain[3], up_two, down_two)
    result = lax.all_gather(result.astype(BF16), "mp", tiled=True)
    result = turned(result, total - start)

    grad = mine(turned(cotangent, start)).astype(F32)
    dmiddle, gain_3, up_grad_two, down_grad_two = feed_backward(
        middle_two, gain[3], up_two, down_two, feed_two, grad
    )
    feed_grads = lax.psum_scatter(
        jnp.concatenate([up_grad_two, down_grad_two], axis=2).reshape(n_mp * n_dp, depth, -1),
        both,
        scatter_dimension=0,
    )
    low = dmiddle.astype(BF16)
    blocks = low.reshape(mixed_two.shape[1], -1, model)
    out_grad_two = jnp.einsum("ctd,gcwt->gdw", blocks, mixed_two, preferred_element_type=F32)
    parts = jnp.einsum("gdw,ctd->gcwt", out_two, blocks, preferred_element_type=F32).astype(BF16)
    if near:
        upstream = swap(parts, n_mp, 8).reshape(n_dp, width, rows)
        dtable, dvalues = table_backward(
            first, random_table, corner, table_lse, values_all, values_two[:, MOST:], upstream, n_dp
        )
    else:
        upstream = swap(parts[:, 0], n_mp, 8, lanes_out=True)
        dcorner, dshort = short_backward(first, corner, values_two[:, MOST:], upstream[:, MOST:])
        dcorner = lax.psum(dcorner, "dp")
        upstream = upstream.reshape(width, n_dp, rows).transpose(1, 0, 2)
        upstream = lax.all_to_all(upstream, "dp", 0, 0, tiled=True)
        valid = (place * rows < MOST).astype(F32).reshape(1, 1)
        dtable, dvalues = random_backward(valid, random_table, table_lse, values_all, upstream)
        dvalues = lax.psum_scatter(dvalues, "dp", scatter_dimension=0)
        dvalues = jnp.concatenate([dvalues, dshort], axis=1)
    dvalues = swap(dvalues, n_mp, 9, lanes_in=True)
    value_grad_two = jnp.einsum("td,gwt->gdw", normed_two, dvalues, preferred_element_type=F32)
    dnormed = jnp.einsum("gwt,gdw->td", dvalues, value_two, preferred_element_type=F32)
    dbetween, gain_2 = normalize_back(between, gain[2], dnormed)
    grad = dmiddle + dbetween

    dmiddle, gain_1, up_grad_one, down_grad_one = feed_backward(
        middle_one, gain[1], up_one, down_one, feed_one, grad
    )
    low = dmiddle.astype(BF16)
    out_grad_one = jnp.einsum("td,gtw->gdw", low, mixed_one, preferred_element_type=F32)
    more_grads = lax.psum_scatter(
        jnp.concatenate(
            [
                up_grad_one,
                down_grad_one,
                out_grad_one.astype(BF16),
                out_grad_two.astype(BF16),
                value_grad_two.astype(BF16),
            ],
            axis=2,
        ).reshape(n_mp * n_dp, depth, -1),
        both,
        scatter_dimension=0,
    )
    upstream = jnp.einsum("td,gdw->gtw", low, out_one, preferred_element_type=F32)
    upstream = swap(upstream.astype(BF16), n_mp, 10).reshape(total, width)
    dacts, dvalues_t, dsecond = dense_backward(
        first, acts, acts.T, values.T, upstream, upstream.T, table, table.T, lse
    )
    dpre = jax.vjp(jax.nn.gelu, pre_one)[1](dacts)[0].astype(BF16)
    dvalues = dvalues_t.T
    value_grad_one = tn(normed_one, dvalues)
    first_grad = tn(normed_one, dpre)
    dsecond = jnp.pad(dsecond, ((0, 0), (0, size))).reshape(width, n_dp, total // n_dp)
    last_grads = jnp.concatenate(
        [
            value_grad_one.reshape(n_dp, depth, width),
            first_grad.reshape(n_dp, depth, width),
            dsecond.transpose(1, 0, 2).reshape(n_dp, depth, -1),
        ],
        axis=2,
    ).astype(BF16)
    back = jnp.concatenate([dvalues, dpre], axis=1).reshape(n_mp, share, 2 * width)
    if near:
        back, last_grads = last_exchange(back, last_grads, n_dp, n_mp)
    else:
        back = swap(back, n_mp, 11)
        last_grads = lax.psum_scatter(last_grads, "dp", scatter_dimension=0).astype(F32)
    dnormed = jnp.einsum(
        "gtw,gdw->td", back, jnp.concatenate([value_all, first_all], axis=2), preferred_element_type=F32
    )
    dinputs, gain_0 = normalize_back(inputs_here, gain[0], dnormed)
    gain_grad = jnp.pad(jnp.stack([gain_0, gain_1, gain_2, gain_3]), ((0, 4), (0, 0)))
    input_grad, gain_grad = finish((dmiddle + dinputs).astype(BF16), gain_grad, n_dp, n_mp)
    input_grad = turned(input_grad.reshape(total, model), total - start)

    gain_grad = lax.dynamic_slice_in_dim(gain_grad[:4], place * depth, depth, axis=1)
    up_two_g, down_two_g = cut(feed_grads[None], (hidden, hidden))
    up_one_g, down_one_g, out_one_g, out_two_g, value_two_g = cut(
        more_grads[None], (hidden, hidden, width, width, width)
    )
    if not near:
        dcorner = lax.dynamic_slice(dcorner, (0, begin, 0), (heads, rows, size)) * inside
        dtable = dtable.at[:, :, :size].add(dcorner.astype(F32))
    flip = lambda x: x[0].T.astype(F32)
    return (
        result,
        input_grad,
        gain_grad.reshape(2, 2, depth),
        jnp.stack([last_grads[:, :width], value_two_g[0].astype(F32)]),
        jnp.stack([flip(out_one_g), flip(out_two_g)]),
        jnp.stack([up_one_g[0].astype(F32), up_two_g[0].astype(F32)]),
        jnp.stack([flip(down_one_g), flip(down_two_g)]),
        last_grads[:, width : 2 * width],
        last_grads[:, 2 * width :].reshape(heads, HD, -1),
        dtable,
    )


def solution(mesh):
    in_specs = (
        P("dp", None),
        P("dp", None),
        P(None, None, "dp"),
        P(None, "dp", "mp"),
        P(None, "mp", "dp"),
        P(None, "dp", "mp"),
        P(None, "mp", "dp"),
        P("dp", "mp"),
        P("mp", None, "dp"),
        P("mp", "dp", None),
        P("dp", None),
    )
    out_specs = (
        P("dp", None),
        P("dp", None),
        P(None, None, "dp"),
        P(None, "dp", "mp"),
        P(None, "mp", "dp"),
        P(None, "dp", "mp"),
        P(None, "mp", "dp"),
        P("dp", "mp"),
        P("mp", None, "dp"),
        P("mp", "dp", None),
    )
    return jax.shard_map(
        partial(per_device, mesh.shape["dp"], mesh.shape["mp"]),
        mesh=mesh,
        in_specs=in_specs,
        out_specs=out_specs,
        check_vma=False,
    )
```

```python
from functools import partial

import jax
import jax.numpy as jnp
from jax import lax
from jax.experimental import pallas as pl
from jax.experimental.pallas import tpu as pltpu
from jax.sharding import PartitionSpec as P

F32, BF16 = jnp.float32, jnp.bfloat16
HD = 64
MOST = 1792
TILE = 256
VMEM = 58 * 1024 * 1024


def nn(a, b):
    return lax.dot_general(a, b, (((1,), (0,)), ((), ())), preferred_element_type=F32)


def nt(a, b):
    return lax.dot_general(a, b, (((1,), (1,)), ((), ())), preferred_element_type=F32)


def tn(a, b):
    return lax.dot_general(a, b, (((0,), (0,)), ((), ())), preferred_element_type=F32)


def small_masks(first, size):
    row = lax.broadcasted_iota(jnp.int32, (size, size), 0)
    col = lax.broadcasted_iota(jnp.int32, (size, size), 1)
    early = row < first
    inside = col < jnp.where(early, first, size - first)
    shift = jnp.where(col == row + first, 1.0, 0.0).astype(BF16)
    rows = jnp.where(col == jnp.where(early, row, row - first), 1.0, 0.0).astype(BF16)
    return early, inside, shift, rows


def masked_soft(scores, inside):
    masked = jnp.where(inside, scores, -1e30)
    powers = jnp.where(inside, jnp.exp(masked - jnp.max(masked, axis=1, keepdims=True)), 0.0)
    return powers / jnp.sum(powers, axis=1, keepdims=True)


def by_token(soft, early, shift):
    low = soft.astype(BF16)
    zero = jnp.zeros_like(low)
    late = nn(jnp.where(early, zero, low), shift).astype(BF16)
    return jnp.where(early, low, zero) + late


def dense_forward(first, acts, values, table):
    tokens, width = acts.shape
    heads = width // HD
    tiles = MOST // TILE
    size = tokens - MOST
    columns = table.shape[2]
    blocks = MOST // columns

    def kernel(first_ref, acts_ref, values_ref, table_ref, out_ref, lse_ref):
        tile = pl.program_id(0)
        lane = lax.broadcasted_iota(jnp.int32, (TILE, 128), 1)

        def scored(span, number):
            parts = [nn(acts_ref[:, span], table_ref[b, span, :]) for b in range(number)]
            return jnp.concatenate(parts, axis=1)

        @pl.when(tile < tiles)
        def _():
            lse = jnp.zeros((TILE, 128), F32)
            parts = []
            for head in range(heads):
                span = slice(head * HD, (head + 1) * HD)
                scores = scored(span, blocks)
                top = jnp.max(scores, axis=1, keepdims=True)
                powers = jnp.exp(scores - top)
                total = jnp.sum(powers, axis=1, keepdims=True)
                mixed = nn(powers.astype(BF16), values_ref[0:MOST, span])
                parts.append((mixed / total).astype(BF16))
                lse = jnp.where(lane == head, top + jnp.log(total), lse)
            out_ref[...] = jnp.concatenate(parts, axis=1)
            lse_ref[...] = lse

        @pl.when(tile == tiles)
        def _():
            early, inside, shift, _ = small_masks(first_ref[0, 0], size)
            parts = []
            for head in range(heads):
                span = slice(head * HD, (head + 1) * HD)
                soft = by_token(masked_soft(scored(span, size // columns), inside), early, shift)
                parts.append(nn(soft, values_ref[MOST:tokens, span]).astype(BF16))
            out_ref[...] = jnp.concatenate(parts, axis=1)
            lse_ref[...] = jnp.zeros((TILE, 128), F32)

    return pl.pallas_call(
        kernel,
        grid=(tiles + 1,),
        in_specs=[
            pl.BlockSpec(memory_space=pltpu.SMEM),
            pl.BlockSpec((TILE, width), lambda t: (t, 0)),
            pl.BlockSpec((tokens, width), lambda t: (0, 0)),
            pl.BlockSpec(table.shape, lambda t: (0, 0, 0)),
        ],
        out_specs=[
            pl.BlockSpec((TILE, width), lambda t: (t, 0)),
            pl.BlockSpec((TILE, 128), lambda t: (t, 0)),
        ],
        out_shape=[
            jax.ShapeDtypeStruct((tokens, width), BF16),
            jax.ShapeDtypeStruct((tokens, 128), F32),
        ],
        compiler_params=pltpu.CompilerParams(vmem_limit_bytes=VMEM),
        cost_estimate=pl.CostEstimate(flops=12 * tokens * tokens * width, bytes_accessed=8 * tokens * width, transcendentals=0),
        name="dense_forward",
    )(first, acts, values, table)


def dense_backward(first, acts, acts_t, values_t, upstream, table, lse, slope, normed):
    tokens, width = acts.shape
    model = normed.shape[1]
    heads = width // HD
    tiles = MOST // TILE
    size = tokens - MOST
    columns = table.shape[2]
    blocks = MOST // columns

    def kernel(first_ref, acts_ref, acts_t_ref, values_t_ref, up_ref, table_ref, lse_ref, slope_ref, normed_ref,
               back_ref, dweights_ref, dtable_ref, dv_acc, dt_acc, dpre):
        tile = pl.program_id(0)

        @pl.when(tile == 0)
        def _():
            dv_acc[...] = jnp.zeros_like(dv_acc)
            dt_acc[...] = jnp.zeros_like(dt_acc)

        def scored(span, number):
            parts = [nn(acts_ref[:, span], table_ref[b, span, :]) for b in range(number)]
            return jnp.concatenate(parts, axis=1)

        def spread(span, dscores, number):
            total = 0.0
            for b in range(number):
                part = dscores[:, b * columns : (b + 1) * columns]
                dt_acc[b, span, :] += nn(acts_t_ref[span, :], part)
                total += nt(part, table_ref[b, span, :])
            return total

        def keep(parts):
            slopes = slope_ref[...].astype(F32)
            rows = pl.ds(pl.multiple_of(tile * TILE, TILE), TILE)
            dpre[rows, :] = (slopes * jnp.concatenate(parts, axis=1)).astype(BF16)

        @pl.when(tile < tiles)
        def _():
            parts = []
            up_t = up_ref[...].T
            for head in range(heads):
                span = slice(head * HD, (head + 1) * HD)
                soft = jnp.exp(scored(span, blocks) - lse_ref[:, head : head + 1])
                dsoft = nn(up_ref[:, span], values_t_ref[span, 0:MOST])
                dv_acc[span, 0:MOST] += nn(up_t[span, :], soft.astype(BF16))
                weighed = soft * dsoft
                centre = jnp.sum(weighed, axis=1, keepdims=True)
                parts.append(spread(span, (weighed - soft * centre).astype(BF16), blocks))
            keep(parts)

        @pl.when(tile == tiles)
        def _():
            early, inside, shift, _ = small_masks(first_ref[0, 0], size)
            parts = []
            up_t = up_ref[...].T
            for head in range(heads):
                span = slice(head * HD, (head + 1) * HD)
                soft = masked_soft(scored(span, size // columns), inside)
                here = values_t_ref[span, MOST:tokens]
                moved = nt(here, shift).astype(BF16)
                dsoft = jnp.where(early, nn(up_ref[:, span], here), nn(up_ref[:, span], moved))
                dv_acc[span, MOST:tokens] = nn(up_t[span, :], by_token(soft, early, shift))
                centre = jnp.sum(soft * dsoft, axis=1, keepdims=True)
                parts.append(spread(span, (soft * (dsoft - centre)).astype(BF16), size // columns))
            keep(parts)
            dvalues_t = dv_acc[...].astype(BF16)
            back_ref[:, 0:width] = dvalues_t.T
            back_ref[:, width:] = dpre[...]
            value_grad = nn(dvalues_t, normed_ref[...])
            first_grad = nn(dpre[...].T, normed_ref[...])
            dweights_ref[:, 0:width] = value_grad.T.astype(BF16)
            dweights_ref[:, width:] = first_grad.T.astype(BF16)
            dtable_ref[...] = dt_acc[...].astype(BF16)

    whole = lambda t: (0, 0)
    rows = lambda t: (t, 0)
    return pl.pallas_call(
        kernel,
        grid=(tiles + 1,),
        in_specs=[
            pl.BlockSpec(memory_space=pltpu.SMEM),
            pl.BlockSpec((TILE, width), rows),
            pl.BlockSpec((width, TILE), lambda t: (0, t)),
            pl.BlockSpec((width, tokens), whole),
            pl.BlockSpec((TILE, width), rows),
            pl.BlockSpec(table.shape, lambda t: (0, 0, 0)),
            pl.BlockSpec((TILE, 128), rows),
            pl.BlockSpec((TILE, width), rows),
            pl.BlockSpec((tokens, model), whole),
        ],
        out_specs=[
            pl.BlockSpec((tokens, 2 * width), whole),
            pl.BlockSpec((model, 2 * width), whole),
            pl.BlockSpec(table.shape, lambda t: (0, 0, 0)),
        ],
        out_shape=[
            jax.ShapeDtypeStruct((tokens, 2 * width), BF16),
            jax.ShapeDtypeStruct((model, 2 * width), BF16),
            jax.ShapeDtypeStruct(table.shape, BF16),
        ],
        scratch_shapes=[
            pltpu.VMEM((width, tokens), F32),
            pltpu.VMEM(table.shape, F32),
            pltpu.VMEM((tokens, width), BF16),
        ],
        compiler_params=pltpu.CompilerParams(vmem_limit_bytes=VMEM),
        cost_estimate=pl.CostEstimate(flops=24 * tokens * tokens * width, bytes_accessed=16 * tokens * width, transcendentals=0),
        name="dense_backward",
    )(first, acts, acts_t, values_t, upstream, table, lse, slope, normed)


def random_forward(table, values_t):
    heads, rows, _ = table.shape
    slots, width, _ = values_t.shape

    def kernel(table_ref, values_ref, out_ref, lse_ref):
        scores = table_ref[0, :, 0:MOST].astype(F32)
        top = jnp.max(scores, axis=1, keepdims=True)
        powers = jnp.exp(scores - top)
        total = jnp.sum(powers, axis=1, keepdims=True)
        soft = (powers / total).astype(BF16)
        values = values_ref[...].reshape(slots * HD, MOST)
        out_ref[...] = nt(values, soft).astype(BF16).reshape(slots, HD, rows)
        lse_ref[...] = jnp.broadcast_to(top + jnp.log(total), (1, rows, 128))

    return pl.pallas_call(
        kernel,
        grid=(heads,),
        in_specs=[
            pl.BlockSpec((1, rows, table.shape[2]), lambda h: (h, 0, 0)),
            pl.BlockSpec((slots, HD, MOST), lambda h: (0, h, 0)),
        ],
        out_specs=[
            pl.BlockSpec((slots, HD, rows), lambda h: (0, h, 0)),
            pl.BlockSpec((1, rows, 128), lambda h: (h, 0, 0)),
        ],
        out_shape=[
            jax.ShapeDtypeStruct((slots, width, rows), BF16),
            jax.ShapeDtypeStruct((heads, rows, 128), F32),
        ],
        compiler_params=pltpu.CompilerParams(vmem_limit_bytes=VMEM),
        name="random_forward",
    )(table, values_t)


def random_backward(valid, table, lse, values_t, upstream_t):
    heads, rows, columns = table.shape
    slots, width, _ = values_t.shape
    buffers = pl.Buffered(2 if slots <= 16 else 1)

    def kernel(valid_ref, table_ref, lse_ref, values_ref, up_ref, dtable_ref, dvalues_ref):
        soft = jnp.exp(table_ref[0, :, 0:MOST].astype(F32) - lse_ref[0, :, 0:1])
        up = up_ref[...].reshape(slots * HD, rows) * valid_ref[0, 0].astype(BF16)
        values = values_ref[...].reshape(slots * HD, MOST)
        dsoft = tn(up, values)
        weighed = soft * dsoft
        centre = jnp.sum(weighed, axis=1, keepdims=True)
        dtable_ref[0, :, 0:MOST] = weighed - soft * centre
        dtable_ref[0, :, MOST:columns] = jnp.zeros((rows, columns - MOST), F32)
        dvalues_ref[...] = nn(up, soft.astype(BF16)).astype(BF16).reshape(slots, HD, MOST)

    return pl.pallas_call(
        kernel,
        grid=(heads,),
        in_specs=[
            pl.BlockSpec(memory_space=pltpu.SMEM),
            pl.BlockSpec((1, rows, columns), lambda h: (h, 0, 0)),
            pl.BlockSpec((1, rows, 128), lambda h: (h, 0, 0)),
            pl.BlockSpec((slots, HD, MOST), lambda h: (0, h, 0), pipeline_mode=buffers),
            pl.BlockSpec((slots, HD, rows), lambda h: (0, h, 0)),
        ],
        out_specs=[
            pl.BlockSpec((1, rows, columns), lambda h: (h, 0, 0)),
            pl.BlockSpec((slots, HD, MOST), lambda h: (0, h, 0)),
        ],
        out_shape=[
            jax.ShapeDtypeStruct((heads, rows, columns), F32),
            jax.ShapeDtypeStruct((slots, width, MOST), BF16),
        ],
        compiler_params=pltpu.CompilerParams(vmem_limit_bytes=VMEM),
        name="random_backward",
    )(valid, table, lse, values_t, upstream_t)


def short_forward(first, corner, values_t):
    heads, size, _ = corner.shape
    width = values_t.shape[0]

    def kernel(first_ref, corner_ref, values_ref, out_ref):
        early, inside, shift, rows = small_masks(first_ref[0, 0], size)
        for head in range(heads):
            span = slice(head * HD, (head + 1) * HD)
            soft = by_token(masked_soft(nn(rows, corner_ref[head]), inside), early, shift)
            out_ref[span, :] = nt(values_ref[span, :], soft).astype(BF16)

    return pl.pallas_call(
        kernel,
        in_specs=[
            pl.BlockSpec(memory_space=pltpu.SMEM),
            pl.BlockSpec(memory_space=pltpu.VMEM),
            pl.BlockSpec(memory_space=pltpu.VMEM),
        ],
        out_specs=pl.BlockSpec(memory_space=pltpu.VMEM),
        out_shape=jax.ShapeDtypeStruct((width, size), BF16),
        name="short_forward",
    )(first, corner, values_t)


def short_backward(first, corner, values_t, upstream_t):
    heads, size, _ = corner.shape
    width = values_t.shape[0]

    def kernel(first_ref, corner_ref, values_ref, up_ref, dcorner_ref, dvalues_ref):
        early, inside, shift, rows = small_masks(first_ref[0, 0], size)
        for head in range(heads):
            span = slice(head * HD, (head + 1) * HD)
            soft = masked_soft(nn(rows, corner_ref[head]), inside)
            here, up = values_ref[span, :], up_ref[span, :]
            moved = nt(here, shift).astype(BF16)
            dsoft = jnp.where(early, tn(up, here), tn(up, moved))
            dvalues_ref[span, :] = nn(up, by_token(soft, early, shift)).astype(BF16)
            centre = jnp.sum(soft * dsoft, axis=1, keepdims=True)
            dscores = (soft * (dsoft - centre)).astype(BF16)
            dcorner_ref[head] = tn(rows, dscores).astype(BF16)

    return pl.pallas_call(
        kernel,
        in_specs=[
            pl.BlockSpec(memory_space=pltpu.SMEM),
            pl.BlockSpec(memory_space=pltpu.VMEM),
            pl.BlockSpec(memory_space=pltpu.VMEM),
            pl.BlockSpec(memory_space=pltpu.VMEM),
        ],
        out_specs=[
            pl.BlockSpec(memory_space=pltpu.VMEM),
            pl.BlockSpec(memory_space=pltpu.VMEM),
        ],
        out_shape=[
            jax.ShapeDtypeStruct((heads, size, size), BF16),
            jax.ShapeDtypeStruct((width, size), BF16),
        ],
        name="short_backward",
    )(first, corner, values_t, upstream_t)


def table_grad(table, lse, values_t, upstream_t, corner):
    heads, rows, columns = table.shape
    slots, size = values_t.shape[0], corner.shape[2]

    def kernel(table_ref, lse_ref, values_ref, up_ref, corner_ref, out_ref):
        weights = jnp.exp(table_ref[0, :, 0:MOST].astype(F32) - lse_ref[0, :, 0:1])
        up = up_ref[...].reshape(slots * HD, rows)
        dsoft = tn(up, values_ref[...].reshape(slots * HD, MOST))
        weighed = weights * dsoft
        centre = jnp.sum(weighed, axis=1, keepdims=True)
        out_ref[0, :, 0:MOST] = weighed - weights * centre
        out_ref[0, :, MOST:columns] = jnp.zeros((rows, columns - MOST), F32)
        out_ref[0, :, 0:size] += corner_ref[0].astype(F32)

    return pl.pallas_call(
        kernel,
        grid=(heads,),
        in_specs=[
            pl.BlockSpec((1, rows, columns), lambda h: (h, 0, 0)),
            pl.BlockSpec((1, rows, 128), lambda h: (h, 0, 0)),
            pl.BlockSpec((slots, HD, MOST), lambda h: (0, h, 0)),
            pl.BlockSpec((slots, HD, rows), lambda h: (0, h, 0)),
            pl.BlockSpec((1, rows, size), lambda h: (h, 0, 0)),
        ],
        out_specs=pl.BlockSpec((1, rows, columns), lambda h: (h, 0, 0)),
        out_shape=jax.ShapeDtypeStruct((heads, rows, columns), F32),
        compiler_params=pltpu.CompilerParams(vmem_limit_bytes=VMEM),
        name="table_grad",
    )(table, lse, values_t, upstream_t, corner)


MESH = pl.DeviceIdType.MESH
ANY = pl.BlockSpec(memory_space=pl.ANY)
INTO = pl.BlockSpec(memory_space=pltpu.VMEM)
SCALAR = pl.BlockSpec(memory_space=pltpu.SMEM)
DMA = pltpu.SemaphoreType.DMA


def remote(source, target, send, recv, axis, index):
    return pltpu.make_async_remote_copy(
        src_ref=source, dst_ref=target, send_sem=send, recv_sem=recv, device_id={axis: index}, device_id_type=MESH
    )


def greet(groups):
    barrier = pltpu.get_barrier_semaphore()
    for axis, size in groups:
        me = lax.axis_index(axis)
        for step in range(1, size):
            pl.semaphore_signal(
                barrier, inc=1, device_id={axis: lax.rem(me + step, size)}, device_id_type=MESH
            )
    pl.semaphore_wait(barrier, sum(size - 1 for _, size in groups))


def comm_params(number):
    return pltpu.CompilerParams(collective_id=number, has_side_effects=True, vmem_limit_bytes=VMEM)


class Line:
    def __init__(self, size):
        self.size, self.length = size, size // 2
        self.place = lax.axis_index("dp")
        self.at, self.side = self.place // 2, lax.rem(self.place, 2)
        self.partner = self.at * 2 + 1 - self.side
        self.right, self.left = self.place + 2, self.place - 2
        self.has_right, self.has_left = self.at + 1 < self.length, self.at > 0


def line_gather(line, pieces, begin, use):
    length, at, side = line.length, line.at, line.side

    def push(s, to, across=False, way=0, fresh=False):
        for own, slots, send_x, send_z, recv in pieces:
            a = s // 2
            send = send_x.at[a] if across else send_z.at[way, a]
            remote(own if fresh else slots.at[s], slots.at[s], send, recv.at[s], "dp", to).start()

    def landed(s):
        for own, slots, send_x, send_z, recv in pieces:
            remote(own, slots.at[s], send_x.at[0], recv.at[s], "dp", line.partner).wait_recv()

    def sent(which):
        for own, slots, send_x, send_z, recv in pieces:
            remote(own, slots.at[0], which(send_x, send_z), recv.at[0], "dp", line.partner).wait_send()

    @pl.when(line.has_right)
    def _():
        push(line.place, line.right, way=0, fresh=True)

    @pl.when(line.has_left)
    def _():
        push(line.place, line.left, way=1, fresh=True)

    push(line.place, line.partner, across=True, fresh=True)

    def arrive(a, way):
        s = a * 2 + side
        landed(s)
        on, to = ((line.has_right, line.right), (line.has_left, line.left))[way]

        @pl.when(on)
        def _():
            push(s, to, way=way)

        push(s, line.partner, across=True)

    def crossed(a):
        s = a * 2 + 1 - side
        landed(s)
        use(s)

    begin()

    @pl.loop(1, length + 1)
    def _(k):
        low, high = at - k, at + k

        @pl.when(low >= 0)
        def _():
            arrive(low, 0)

        @pl.when(high < length)
        def _():
            arrive(high, 1)

        @pl.when(low >= 0)
        def _():
            use(low * 2 + side)

        @pl.when(high < length)
        def _():
            use(high * 2 + side)

        @pl.when(low + 1 >= 0)
        def _():
            crossed(low + 1)

        @pl.when(jnp.logical_and(k > 1, high - 1 < length))
        def _():
            crossed(high - 1)

    @pl.loop(0, length)
    def _(a):
        sent(lambda x, z: x.at[a])

        @pl.when(jnp.logical_and(line.has_right, a <= at))
        def _():
            sent(lambda x, z: z.at[0, a])

        @pl.when(jnp.logical_and(line.has_left, a >= at))
        def _():
            sent(lambda x, z: z.at[1, a])


def gather_scratch(n):
    return [DMA((n // 2,)), DMA((2, n // 2)), DMA((n,))]


def line_scatter(line, items, middle):
    length, at, side = line.length, line.at, line.side

    def over_x(item, a):
        _, _, x_out, x_in, _, _, _, send_x, recv_x = item[:9]
        return remote(x_out.at[a], x_in.at[a], send_x.at[a], recv_x.at[a], "dp", line.partner)

    def over_z(item, a, way, to=line.partner):
        z_out, into, send, recv = item[4], item[5 + way], item[9], item[10 + way]
        return remote(z_out.at[a], into.at[a], send.at[a], recv.at[a], "dp", to)

    def cross(a):
        for item in items:
            item[2][a] = item[0](a * 2 + 1 - side).astype(BF16)
            over_x(item, a).start()

    @pl.loop(0, length - 1)
    def _(step):
        k = length - 1 - step

        @pl.when(at + k < length)
        def _():
            cross(at + k)

        @pl.when(at - k >= 0)
        def _():
            cross(at - k)

    cross(at)
    middle()

    def relay(a, way, behind, to):
        for item in items:
            make, _, _, x_in, z_out = item[:5]
            total = make(a * 2 + side)
            over_x(item, a).wait_recv()
            z_out[a] = (total + x_in[a].astype(F32)).astype(BF16)

            @pl.when(behind)
            def _():
                over_z(item, a, way).wait_recv()
                z_out[a] = (z_out[a].astype(F32) + item[5 + way][a].astype(F32)).astype(BF16)

            over_z(item, a, way, to).start()

    @pl.loop(0, length - 1)
    def _(step):
        k = length - 1 - step

        @pl.when(at + k < length)
        def _():
            relay(at + k, 0, line.has_left, line.right)

        @pl.when(at - k >= 0)
        def _():
            relay(at - k, 1, line.has_right, line.left)

    for item in items:
        make, out, _, x_in, _, l_in, r_in = item[:7]
        total = make(line.place)
        over_x(item, at).wait_recv()
        out[...] = total + x_in[at].astype(F32)

        @pl.when(line.has_left)
        def _():
            over_z(item, at, 0).wait_recv()
            out[...] += l_in[at].astype(F32)

        @pl.when(line.has_right)
        def _():
            over_z(item, at, 1).wait_recv()
            out[...] += r_in[at].astype(F32)

    @pl.loop(0, length)
    def _(a):
        for item in items:
            over_x(item, a).wait_send()

        @pl.when(a != at)
        def _():
            for item in items:
                over_z(item, a, 0).wait_send()


def scatter_scratch(n, shape):
    return [pltpu.VMEM((n // 2,) + shape, BF16)] * 5 + [DMA((n // 2,))] * 5


def gather_weights(arrays, n):
    count = len(arrays)

    def kernel(*refs):
        owns, alls, rest = refs[:count], refs[count : 2 * count], refs[2 * count :]
        line = Line(n)
        greet([("dp", n)])
        kept = [
            pltpu.make_async_copy(owns[i], alls[i].at[line.place], rest[-1].at[i]) for i in range(count)
        ]
        pieces = [(owns[i], alls[i], *rest[3 * i : 3 * i + 3]) for i in range(count)]

        def begin():
            for copy in kept:
                copy.start()

        line_gather(line, pieces, begin, lambda s: None)
        for copy in kept:
            copy.wait()

    return pl.pallas_call(
        kernel,
        in_specs=[ANY] * count,
        out_specs=[ANY] * count,
        out_shape=[jax.ShapeDtypeStruct((n,) + a.shape, a.dtype) for a in arrays],
        scratch_shapes=gather_scratch(n) * count + [DMA((count,))],
        compiler_params=comm_params(0),
        name="gather_weights",
    )(*arrays)


def swap(x, n, number, lanes_in=False, lanes_out=False):
    if lanes_in:
        block = (x.shape[0], x.shape[1] // n)
    else:
        block = x.shape[1:]
    shape = (block[0], n * block[1]) if lanes_out else (n,) + block

    def at(ref, lanes, j):
        if lanes:
            return ref.at[:, pl.ds(pl.multiple_of(j * block[1], block[1]), block[1])]
        return ref.at[j]

    def kernel(x_ref, out_ref, send, recv, own_sem):
        me = lax.axis_index("mp")
        greet([("mp", n)])
        copies = []
        for step in range(1, n):
            peer = lax.rem(me + step, n)
            copies.append(
                remote(at(x_ref, lanes_in, peer), at(out_ref, lanes_out, me), send.at[step], recv.at[step], "mp", peer)
            )
            copies[-1].start()
        own = pltpu.make_async_copy(at(x_ref, lanes_in, me), at(out_ref, lanes_out, me), own_sem)
        own.start()
        own.wait()
        for copy in copies:
            copy.wait()

    return pl.pallas_call(
        kernel,
        in_specs=[ANY],
        out_specs=ANY,
        out_shape=jax.ShapeDtypeStruct(shape, x.dtype),
        scratch_shapes=[DMA((n,)), DMA((n,)), DMA],
        compiler_params=comm_params(number),
        name="swap",
    )(x)


def table_forward(first, table, corner, values_t, n):
    heads, rows, columns = table.shape
    width, tokens = values_t.shape
    size = tokens - MOST
    owners = MOST // rows

    def kernel(first_ref, table_ref, corner_ref, own_ref, values_ref, mixed_ref, lse_ref,
               soft, sums, send_x, send_z, recv, send_m, recv_m):
        line = Line(n)
        place = line.place
        values_ref[place] = own_ref[:, 0:MOST]
        greet([("dp", n)])
        owner = place < owners

        def prepare():
            for head in range(heads):
                scores = table_ref[head, :, 0:MOST].astype(F32)
                top = jnp.max(scores, axis=1, keepdims=True)
                powers = jnp.exp(scores - top)
                total = jnp.sum(powers, axis=1, keepdims=True)
                soft[head] = (powers / total).astype(BF16)
                lse_ref[head] = jnp.broadcast_to(top + jnp.log(total), (rows, 128))
            early, inside, shift, at = small_masks(first_ref[0, 0], size)
            for head in range(heads):
                span = slice(head * HD, (head + 1) * HD)
                weights = by_token(masked_soft(nn(at, corner_ref[head]), inside), early, shift)
                mixed_ref[owners, span, :] = nt(own_ref[span, MOST:tokens], weights).astype(BF16)

        def back(s):
            return remote(sums.at[s], mixed_ref.at[place], send_m.at[s], recv_m.at[place], "dp", s)

        def product(s, head):
            span = slice(head * HD, (head + 1) * HD)
            return nt(values_ref[s, span, :], soft[head]).astype(BF16)

        def begin():
            prepare()

            @pl.when(owner)
            def _():
                for head in range(heads):
                    mixed_ref[place, head * HD : (head + 1) * HD, :] = product(place, head)

        def use(s):
            @pl.when(owner)
            def _():
                for head in range(heads):
                    sums[s, head * HD : (head + 1) * HD, :] = product(s, head)
                back(s).start()

        line_gather(line, [(values_ref.at[place], values_ref, send_x, send_z, recv)], begin, use)

        @pl.loop(0, n)
        def _(s):
            @pl.when(jnp.logical_and(owner, s != place))
            def _():
                back(s).wait_send()

            @pl.when(jnp.logical_and(s < owners, s != place))
            def _():
                remote(sums.at[0], mixed_ref.at[s], send_m.at[0], recv_m.at[s], "dp", s).wait_recv()

    return pl.pallas_call(
        kernel,
        in_specs=[SCALAR, INTO, INTO, INTO],
        out_specs=[INTO, INTO, INTO],
        out_shape=[
            jax.ShapeDtypeStruct((n, width, MOST), BF16),
            jax.ShapeDtypeStruct((n, width, rows), BF16),
            jax.ShapeDtypeStruct((heads, rows, 128), F32),
        ],
        scratch_shapes=[
            pltpu.VMEM((heads, rows, MOST), BF16),
            pltpu.VMEM((n, width, rows), BF16),
            *gather_scratch(n),
            DMA((n,)),
            DMA((n,)),
        ],
        compiler_params=comm_params(1),
        name="table_forward",
    )(first, table, corner, values_t)


def spread_mp(x_ref, all_ref, send, recv, own_sem, n):
    me, pairs = lax.axis_index("mp"), n // 2
    pair, core = me // 2, lax.rem(me, 2)
    twin = pair * 2 + 1 - core
    own = pltpu.make_async_copy(x_ref, all_ref.at[me], own_sem)
    far = []
    for step in range(1, pairs):
        to = lax.rem(pair + step, pairs) * 2 + core
        far.append(remote(x_ref, all_ref.at[me], send.at[step], recv.at[step], "mp", to))
        far[-1].start()
    near = [remote(x_ref, all_ref.at[me], send.at[0], recv.at[0], "mp", twin)]
    near[0].start()
    own.start()

    def relay():
        for step in range(1, pairs):
            far[step - 1].wait_recv()
            source = lax.rem(pair + pairs - step, pairs) * 2 + core
            near.append(
                remote(all_ref.at[source], all_ref.at[source], send.at[pairs + step], recv.at[pairs + step], "mp", twin)
            )
            near[-1].start()

    def end():
        for copy in far:
            copy.wait_send()
        for copy in near:
            copy.wait()
        own.wait()

    return relay, end


def blend_mp(x_ref, out_ref, kept, twins, others, local, near_send, near_recv, far_send, far_recv, n):
    me, pairs = lax.axis_index("mp"), n // 2
    pair, core = me // 2, lax.rem(me, 2)
    twin = pair * 2 + 1 - core
    rows = x_ref.shape[1]
    chunk = rows // 6

    def keep(p):
        return pltpu.make_async_copy(x_ref.at[p * 2 + core], kept.at[p], local.at[p])

    def give(p):
        return remote(x_ref.at[p * 2 + 1 - core], twins.at[p], near_send.at[p], near_recv.at[p], "mp", twin)

    def pass_on(step):
        to = lax.rem(pair + step, pairs)
        return remote(
            kept.at[to], others.at[step - 1], far_send.at[step], far_recv.at[step], "mp", to * 2 + core
        )

    def over_rows(body):
        @pl.loop(0, rows // chunk)
        def _(i):
            body(pl.ds(pl.multiple_of(i * chunk, chunk), chunk))

    def start():
        for step in range(1, pairs + 1):
            p = lax.rem(pair + step, pairs)
            give(p).start()
            keep(p).start()

    def go_on():
        for step in range(1, pairs):
            p = lax.rem(pair + step, pairs)
            keep(p).wait()
            give(p).wait_recv()

            def body(at):
                kept[p, at, :] = (kept[p, at, :].astype(F32) + twins[p, at, :].astype(F32)).astype(BF16)

            over_rows(body)
            pass_on(step).start()

    def end():
        keep(pair).wait()
        give(pair).wait_recv()
        for step in range(1, pairs):
            pass_on(step).wait_recv()

        def body(at):
            total = kept[pair, at, :].astype(F32) + twins[pair, at, :].astype(F32)
            for j in range(pairs - 1):
                total += others[j, at, :].astype(F32)
            out_ref[at, :] = total.astype(BF16)

        over_rows(body)
        for p in range(pairs):
            give(p).wait_send()
        for step in range(1, pairs):
            pass_on(step).wait_send()

    return start, go_on, end


def blend_scratch(n, shape):
    pairs = n // 2
    return [
        pltpu.VMEM((pairs,) + shape, BF16),
        pltpu.VMEM((pairs,) + shape, BF16),
        pltpu.VMEM((pairs - 1,) + shape, BF16),
    ] + [DMA((pairs,))] * 5


def table_backward(first, table, corner, lse, short_t, upstream, result, grads, n, n_mp):
    heads, rows, columns = table.shape
    width, size = short_t.shape
    owners = MOST // rows

    def kernel(first_ref, table_ref, corner_ref, lse_ref, short_ref, up_ref, result_ref, grads_ref, ups, dvalues_ref,
               dcorner_ref, results_ref, blended_ref, total, soft, send_u, recv_u, send_r, recv_r, own_sem, *rest):
        line = Line(n)
        place = line.place
        greet([("dp", n), ("mp", n_mp)])
        owner = place < owners

        def hand(s):
            return remote(up_ref.at[s], ups.at[place], send_u.at[s], recv_u.at[place], "dp", s)

        @pl.loop(0, owners)
        def _(s):
            @pl.when(s != place)
            def _():
                hand(s).start()

        blend, go_on, blended = blend_mp(grads_ref, blended_ref, *rest[10:], n_mp)
        blend()
        relay, end = spread_mp(result_ref, results_ref, send_r, recv_r, own_sem, n_mp)

        early, inside, shift, at = small_masks(first_ref[0, 0], size)
        for head in range(heads):
            span = slice(head * HD, (head + 1) * HD)
            weights = masked_soft(nn(at, corner_ref[head]), inside)
            here, up = short_ref[span, :], up_ref[n - 1, span, :]
            moved = nt(here, shift).astype(BF16)
            dsoft = jnp.where(early, tn(up, here), tn(up, moved))
            dvalues_ref[span, MOST : MOST + size] = nn(up, by_token(weights, early, shift)).astype(BF16)
            centre = jnp.sum(weights * dsoft, axis=1, keepdims=True)
            dcorner_ref[head] = tn(at, (weights * (dsoft - centre)).astype(BF16)).astype(BF16)

        for head in range(heads):
            soft[head] = jnp.exp(table_ref[head, :, 0:MOST].astype(F32) - lse_ref[head, :, 0:1]).astype(BF16)

        go_on()

        @pl.when(owner)
        def _():
            ups[place] = up_ref[place]

            @pl.loop(0, n)
            def _(s):
                @pl.when(s != place)
                def _():
                    remote(up_ref.at[0], ups.at[s], send_u.at[0], recv_u.at[s], "dp", s).wait_recv()

        @pl.when(jnp.logical_not(owner))
        def _():
            ups[...] = jnp.zeros_like(ups)

        def make(s):
            return jnp.concatenate(
                [nn(ups[s, head * HD : (head + 1) * HD, :], soft[head]) for head in range(heads)], axis=0
            )

        line_scatter(line, [(make, total, *rest[:10])], relay)
        dvalues_ref[:, 0:MOST] = total[...].astype(BF16)
        end()
        blended()

        @pl.loop(0, owners)
        def _(s):
            @pl.when(s != place)
            def _():
                hand(s).wait_send()

    return pl.pallas_call(
        kernel,
        in_specs=[SCALAR] + [INTO] * 5 + [ANY] * 2,
        out_specs=[INTO] * 3 + [ANY, INTO],
        out_shape=[
            jax.ShapeDtypeStruct((n, width, rows), BF16),
            jax.ShapeDtypeStruct((width, MOST + size), BF16),
            jax.ShapeDtypeStruct((heads, size, size), BF16),
            jax.ShapeDtypeStruct((n_mp,) + result.shape, result.dtype),
            jax.ShapeDtypeStruct(grads.shape[1:], BF16),
        ],
        scratch_shapes=[
            pltpu.VMEM((width, MOST), F32),
            pltpu.VMEM((heads, rows, MOST), BF16),
            DMA((n,)),
            DMA((n,)),
            DMA((n_mp,)),
            DMA((n_mp,)),
            DMA,
        ]
        + scatter_scratch(n, (width, MOST))
        + blend_scratch(n_mp, grads.shape[1:]),
        compiler_params=comm_params(2),
        name="table_backward",
    )(first, table, corner, lse, short_t, upstream, result, grads)


def last_exchange(back, grads, n, n_mp):
    count = len(grads)

    def kernel(*refs):
        back_ref, grad_refs = refs[0], refs[1 : 1 + count]
        got_ref, out_refs = refs[1 + count], refs[2 + count : 2 + 2 * count]
        send, recv, own_sem = refs[2 + 2 * count : 5 + 2 * count]
        rest = refs[5 + 2 * count :]
        line = Line(n)
        me = lax.axis_index("mp")
        greet([("dp", n), ("mp", n_mp)])
        copies = []
        for step in range(1, n_mp):
            peer = lax.rem(me + step, n_mp)
            copies.append(
                remote(back_ref.at[peer], got_ref.at[me], send.at[step], recv.at[step], "mp", peer)
            )
            copies[-1].start()
        own = pltpu.make_async_copy(back_ref.at[me], got_ref.at[me], own_sem)
        own.start()
        items = [
            (lambda s, ref=grad_refs[i]: ref[s].astype(F32), out_refs[i], *rest[10 * i : 10 * i + 10])
            for i in range(count)
        ]
        line_scatter(line, items, lambda: None)
        own.wait()
        for copy in copies:
            copy.wait()

    return pl.pallas_call(
        kernel,
        in_specs=[ANY] + [INTO] * count,
        out_specs=[ANY] + [INTO] * count,
        out_shape=[jax.ShapeDtypeStruct(back.shape, BF16)]
        + [jax.ShapeDtypeStruct(g.shape[1:], F32) for g in grads],
        scratch_shapes=[DMA((n_mp,)), DMA((n_mp,)), DMA]
        + [each for g in grads for each in scatter_scratch(n, g.shape[1:])],
        compiler_params=comm_params(3),
        name="last_exchange",
    )(back, *grads)


def finish(x, gains, n, n_mp):
    def kernel(x_ref, gains_ref, all_ref, sum_ref, one, two, send, recv, own_sem, g_send, g_recv, h_send, h_recv):
        me, place = lax.axis_index("mp"), lax.axis_index("dp")
        greet([("dp", n), ("mp", n_mp)])
        relay, end = spread_mp(x_ref, all_ref, send, recv, own_sem, n_mp)
        one[me] = gains_ref[...]
        firsts = []
        for step in range(1, n_mp):
            to = lax.rem(me + step, n_mp)
            firsts.append(remote(gains_ref, one.at[me], g_send.at[step], g_recv.at[step], "mp", to))
            firsts[-1].start()
        for copy in firsts:
            copy.wait()
        total = one[0]
        for j in range(1, n_mp):
            total += one[j]
        two[place] = total

        def spread(step, there):
            return remote(two.at[place], two.at[there], h_send.at[step], h_recv.at[step], "dp", lax.rem(place + step, n))

        @pl.loop(1, n)
        def _(step):
            spread(step, place).start()

        relay()

        @pl.loop(1, n)
        def _(step):
            spread(step, place).wait_send()
            spread(step, lax.rem(place + n - step, n)).wait_recv()

        total = two[0]
        for j in range(1, n):
            total += two[j]
        sum_ref[...] = total
        end()

    return pl.pallas_call(
        kernel,
        in_specs=[ANY, INTO],
        out_specs=[ANY, INTO],
        out_shape=[
            jax.ShapeDtypeStruct((n_mp,) + x.shape, x.dtype),
            jax.ShapeDtypeStruct(gains.shape, F32),
        ],
        scratch_shapes=[
            pltpu.VMEM((n_mp,) + gains.shape, F32),
            pltpu.VMEM((n,) + gains.shape, F32),
            DMA((n_mp,)),
            DMA((n_mp,)),
            DMA,
            DMA((n_mp,)),
            DMA((n_mp,)),
            DMA((n,)),
            DMA((n,)),
        ],
        compiler_params=comm_params(4),
        name="finish",
    )(x, gains)


EPS = 1e-06
CURVE = 0.7978845608028654


def root(x):
    return lax.rsqrt(jnp.mean(x * x, axis=-1, keepdims=True) + EPS)


def normalize(x, gain):
    return (x * root(x) * gain).astype(BF16)


def normalize_back(x, gain, grad):
    scale = root(x)
    weighed = grad * gain
    pull = jnp.mean(weighed * x, axis=-1, keepdims=True)
    return scale * weighed - x * (scale * scale * scale * pull), jnp.sum(grad * x * scale, axis=0, keepdims=True)


def gelu(x):
    square = x * x
    bend = jnp.tanh(CURVE * x * (1.0 + 0.044715 * square))
    half = 0.5 * (1.0 + bend)
    slope = half + 0.5 * x * (1.0 - bend * bend) * (CURVE * (1.0 + 3 * 0.044715 * square))
    return x * half, slope


def begin(inputs, weights, gain):
    total, model = inputs.shape
    width = weights.shape[1] // 2
    tile = 256

    def kernel(x_ref, w_ref, gain_ref, normed_ref, values_ref, values_t_ref, acts_ref, acts_t_ref, slope_ref):
        normed = normalize(x_ref[...].astype(F32), gain_ref[0:1, :])
        normed_ref[...] = normed
        both = nn(normed, w_ref[...])
        acts, slope = gelu(both[:, width:])
        values = both[:, :width]
        values_ref[...] = values.astype(BF16)
        values_t_ref[...] = values.T.astype(BF16)
        acts_ref[...] = acts.astype(BF16)
        acts_t_ref[...] = acts.T.astype(BF16)
        slope_ref[...] = slope.astype(BF16)

    rows = lambda i: (i, 0)
    columns = lambda i: (0, i)
    return pl.pallas_call(
        kernel,
        grid=(total // tile,),
        in_specs=[
            pl.BlockSpec((tile, model), rows),
            pl.BlockSpec(weights.shape, lambda i: (0, 0)),
            pl.BlockSpec(gain.shape, lambda i: (0, 0)),
        ],
        out_specs=[
            pl.BlockSpec((tile, model), rows),
            pl.BlockSpec((tile, width), rows),
            pl.BlockSpec((width, tile), columns),
            pl.BlockSpec((tile, width), rows),
            pl.BlockSpec((width, tile), columns),
            pl.BlockSpec((tile, width), rows),
        ],
        out_shape=[
            jax.ShapeDtypeStruct((total, model), BF16),
            jax.ShapeDtypeStruct((total, width), BF16),
            jax.ShapeDtypeStruct((width, total), BF16),
            jax.ShapeDtypeStruct((total, width), BF16),
            jax.ShapeDtypeStruct((width, total), BF16),
            jax.ShapeDtypeStruct((total, width), BF16),
        ],
        compiler_params=pltpu.CompilerParams(vmem_limit_bytes=VMEM),
        cost_estimate=pl.CostEstimate(flops=2 * total * model * 2 * width, bytes_accessed=6 * total * model, transcendentals=0),
        name="begin",
    )(inputs, weights, gain)


def by_rows(mixed):
    if len(mixed.shape) == 2:
        return mixed.T
    return jnp.concatenate([mixed[c].T for c in range(mixed.shape[0])], axis=0)


def ends(x, mixed, flat, weights, width, gain, row, more):
    share, model = x.shape
    groups = weights.shape[0]
    hidden = (weights.shape[2] - 2 * width) // 2

    def kernel(*refs):
        x_ref, mixed_ref, gain_ref, up_ref, down_ref, side_ref = refs[:6]
        refs = refs[6:]
        middle_ref, normed_ref, hidden_ref, slope_ref, y_ref = refs[:5]
        acc = refs[-1]
        group = pl.program_id(0)

        @pl.when(group == 0)
        def _():
            total = x_ref[...].astype(F32)
            for j in range(groups):
                block = mixed_ref[j] if flat else by_rows(mixed_ref[j])
                total += nt(block, side_ref[j, :, 0:width])
            middle_ref[...] = total
            normed_ref[...] = normalize(total, gain_ref[row : row + 1, :])
            acc[...] = total

        value_of, slope = gelu(nn(normed_ref[...], up_ref[0]))
        low = value_of.astype(BF16)
        hidden_ref[0] = low
        slope_ref[0] = slope.astype(BF16)
        acc[...] += nt(low, down_ref[0])

        @pl.when(group == groups - 1)
        def _():
            y = acc[...]
            y_ref[...] = y.astype(y_ref.dtype)
            if more:
                normed = normalize(y, gain_ref[row + 1 : row + 2, :])
                refs[5][...] = normed
                for j in range(groups):
                    refs[6][j] = nn(normed, side_ref[j, :, width : 2 * width]).T.astype(BF16)

    whole2, whole3 = (lambda g: (0, 0)), (lambda g: (0, 0, 0))
    in_specs = [
        pl.BlockSpec(x.shape, whole2),
        pl.BlockSpec(mixed.shape, lambda g: (0,) * mixed.ndim),
        pl.BlockSpec(gain.shape, whole2),
        pl.BlockSpec((1, model, hidden), lambda g: (g, 0, 0)),
        pl.BlockSpec((1, model, hidden), lambda g: (g, 0, 1)),
        pl.BlockSpec((groups, model, 2 * width), lambda g: (0, 0, hidden // width)),
    ]
    out_specs = [
        pl.BlockSpec((share, model), whole2),
        pl.BlockSpec((share, model), whole2),
        pl.BlockSpec((1, share, hidden), lambda g: (g, 0, 0)),
        pl.BlockSpec((1, share, hidden), lambda g: (g, 0, 0)),
        pl.BlockSpec((share, model), whole2),
    ]
    out_shape = [
        jax.ShapeDtypeStruct((share, model), F32),
        jax.ShapeDtypeStruct((share, model), BF16),
        jax.ShapeDtypeStruct((groups, share, hidden), BF16),
        jax.ShapeDtypeStruct((groups, share, hidden), BF16),
        jax.ShapeDtypeStruct((share, model), F32 if more else BF16),
    ]
    if more:
        out_specs += [pl.BlockSpec((share, model), whole2), pl.BlockSpec((groups, width, share), whole3)]
        out_shape += [
            jax.ShapeDtypeStruct((share, model), BF16),
            jax.ShapeDtypeStruct((groups, width, share), BF16),
        ]
    return pl.pallas_call(
        kernel,
        grid=(groups,),
        in_specs=in_specs,
        out_specs=out_specs,
        out_shape=out_shape,
        scratch_shapes=[pltpu.VMEM((share, model), F32)],
        compiler_params=pltpu.CompilerParams(vmem_limit_bytes=VMEM),
        cost_estimate=pl.CostEstimate(flops=4 * share * model * groups * hidden, bytes_accessed=4 * groups * model * hidden, transcendentals=0),
        name="ends",
    )(x, mixed, gain, weights, weights, weights)


def ends_back(grad, mixed, flat, weights, width, gain, row, record, after=None):
    middle, normed, hid, slope = record
    share, model = middle.shape
    groups = weights.shape[0]
    hidden = hid.shape[2]
    more = after is not None
    columns = 2 * hidden + (2 if more else 1) * width

    def kernel(*refs):
        grad_ref, mixed_ref, gain_ref, up_ref, down_ref, side_ref, middle_ref, normed_ref, hidden_ref, slope_ref = refs[:10]
        refs = refs[10:]
        if more:
            next_ref, next_normed_ref, dvalues_ref = refs[:3]
            refs = refs[3:]
        grads_ref, dmiddle_ref, dmixed_ref, dgain_ref, total, low, low_t, normed_t, dnormed = refs
        group = pl.program_id(0)

        @pl.when(group == 0)
        def _():
            g = grad_ref[...].astype(F32)
            dgain_ref[...] = jnp.zeros_like(dgain_ref)
            if more:
                pull = jnp.zeros((share, model), F32)
                next_t = next_normed_ref[...].T
                for j in range(groups):
                    dvalues = dvalues_ref[j].T
                    grads_ref[j, :, 2 * hidden + width : columns] = nn(next_t, dvalues).astype(BF16)
                    pull += nt(dvalues, side_ref[j, :, width : 2 * width])
                dx, dg = normalize_back(next_ref[...], gain_ref[row + 1 : row + 2, :], pull)
                g += dx
                dgain_ref[1:2, :] = dg
            total[...] = g
            low[...] = g.astype(BF16)
            low_t[...] = g.astype(BF16).T
            normed_t[...] = normed_ref[...].T
            dnormed[...] = jnp.zeros_like(dnormed)

        dpre = (slope_ref[0].astype(F32) * nn(low[...], down_ref[0])).astype(BF16)
        grads_ref[group, :, 0:hidden] = nn(normed_t[...], dpre).astype(BF16)
        grads_ref[group, :, hidden : 2 * hidden] = nn(low_t[...], hidden_ref[0]).astype(BF16)
        dnormed[...] += nt(dpre, up_ref[0])

        @pl.when(group == groups - 1)
        def _():
            dx, dg = normalize_back(middle_ref[...], gain_ref[row : row + 1, :], dnormed[...])
            dmiddle = total[...] + dx
            dgain_ref[0:1, :] = dg
            dmiddle_ref[...] = dmiddle
            down = dmiddle.astype(BF16)
            down_t = down.T
            for j in range(groups):
                block = mixed_ref[j] if flat else by_rows(mixed_ref[j])
                grads_ref[j, :, 2 * hidden : 2 * hidden + width] = nn(down_t, block).astype(BF16)
                dmixed = nn(down, side_ref[j, :, 0:width])
                if flat:
                    dmixed_ref[j] = dmixed.astype(BF16)
                elif len(mixed.shape) == 3:
                    dmixed_ref[j] = dmixed.T.astype(BF16)
                else:
                    rows = mixed.shape[3]
                    for c in range(mixed.shape[1]):
                        dmixed_ref[j, c] = dmixed[c * rows : (c + 1) * rows].T.astype(BF16)

    whole2, whole3 = (lambda g: (0, 0)), (lambda g: (0, 0, 0))
    whole = lambda a: pl.BlockSpec(a.shape, lambda g: (0,) * a.ndim)
    in_specs = [
        whole(grad),
        whole(mixed),
        whole(gain),
        pl.BlockSpec((1, model, hidden), lambda g: (g, 0, 0)),
        pl.BlockSpec((1, model, hidden), lambda g: (g, 0, 1)),
        pl.BlockSpec((groups, model, 2 * width), lambda g: (0, 0, hidden // width)),
        whole(middle),
        whole(normed),
        pl.BlockSpec((1, share, hidden), lambda g: (g, 0, 0)),
        pl.BlockSpec((1, share, hidden), lambda g: (g, 0, 0)),
    ]
    operands = [grad, mixed, gain, weights, weights, weights, middle, normed, hid, slope]
    if more:
        in_specs += [whole(a) for a in after]
        operands += list(after)
    return pl.pallas_call(
        kernel,
        grid=(groups,),
        in_specs=in_specs,
        out_specs=[
            pl.BlockSpec(memory_space=pltpu.VMEM),
            pl.BlockSpec((share, model), whole2),
            whole(mixed),
            pl.BlockSpec((8, model), whole2),
        ],
        out_shape=[
            jax.ShapeDtypeStruct((groups, model, columns), BF16),
            jax.ShapeDtypeStruct((share, model), F32),
            jax.ShapeDtypeStruct(mixed.shape, BF16),
            jax.ShapeDtypeStruct((8, model), F32),
        ],
        scratch_shapes=[
            pltpu.VMEM((share, model), F32),
            pltpu.VMEM((share, model), BF16),
            pltpu.VMEM((model, share), BF16),
            pltpu.VMEM((model, share), BF16),
            pltpu.VMEM((share, model), F32),
        ],
        compiler_params=pltpu.CompilerParams(vmem_limit_bytes=VMEM),
        cost_estimate=pl.CostEstimate(flops=8 * share * model * groups * hidden, bytes_accessed=8 * groups * model * hidden, transcendentals=0),
        name="ends_back",
    )(*operands)


def close(back, weights, first, x, gain, dmiddle):
    groups, share, both = back.shape
    model, width = first.shape[1:]
    spot = weights.shape[2] // (2 * width) - 1

    def kernel(back_ref, side_ref, first_ref, x_ref, gain_ref, dmiddle_ref, out_ref, dgain_ref):
        pull = jnp.zeros((share, model), F32)
        for j in range(groups):
            pull += nt(back_ref[j, :, 0:width], side_ref[j, :, width : 2 * width])
            pull += nt(back_ref[j, :, width:both], first_ref[j])
        dx, dg = normalize_back(x_ref[...].astype(F32), gain_ref[0:1, :], pull)
        out_ref[...] = (dmiddle_ref[...] + dx).astype(BF16)
        dgain_ref[...] = jnp.concatenate([dg, jnp.zeros((7, model), F32)], axis=0)

    return pl.pallas_call(
        kernel,
        grid=(1,),
        in_specs=[
            pl.BlockSpec(back.shape, lambda i: (0, 0, 0)),
            pl.BlockSpec((groups, model, 2 * width), lambda i: (0, 0, spot)),
            pl.BlockSpec(first.shape, lambda i: (0, 0, 0)),
            pl.BlockSpec(x.shape, lambda i: (0, 0)),
            pl.BlockSpec(gain.shape, lambda i: (0, 0)),
            pl.BlockSpec(dmiddle.shape, lambda i: (0, 0)),
        ],
        out_specs=[pl.BlockSpec((share, model), lambda i: (0, 0)), pl.BlockSpec((8, model), lambda i: (0, 0))],
        out_shape=[
            jax.ShapeDtypeStruct((share, model), BF16),
            jax.ShapeDtypeStruct((8, model), F32),
        ],
        compiler_params=pltpu.CompilerParams(vmem_limit_bytes=VMEM),
        name="close",
    )(back, weights, first, x, gain, dmiddle)


def gather_corner(table, rows, n):
    size = table.shape[2]
    place = lax.axis_index("dp")
    if rows == size and n & (n - 1) == 0:
        corner, step = jnp.where(place == 0, table, 0), n // 2
        while step:
            got = lax.ppermute(corner, "dp", [(i, i + step) for i in range(0, n, 2 * step)])
            corner = jnp.where(lax.rem(place, 2 * step) == step, got, corner)
            step //= 2
        return corner
    inside = (place * rows < size).astype(BF16)
    corner = jnp.zeros((table.shape[0], size, size), BF16)
    start = jnp.minimum(place * rows, size - rows)
    return lax.psum(lax.dynamic_update_slice(corner, table * inside, (0, start, 0)), "dp")


def scatter_corner(corner, rows, n):
    size = corner.shape[1]
    place = lax.axis_index("dp")
    if rows == size and n & (n - 1) == 0:
        step = 1
        while step < n:
            got = lax.ppermute(corner, "dp", [(i + step, i) for i in range(0, n, 2 * step)])
            corner = (corner.astype(F32) + got.astype(F32)).astype(BF16)
            step *= 2
        return jnp.where(place == 0, corner, 0)
    inside = (place * rows < size).astype(BF16)
    start = jnp.minimum(place * rows, size - rows)
    return lax.dynamic_slice_in_dim(lax.psum(corner, "dp"), start, rows, axis=1) * inside


def per_device(
    n_dp,
    n_mp,
    tokens,
    lengths,
    norm_gain,
    w_value,
    w_out,
    w_up,
    w_down,
    synth_first,
    synth_second,
    random_table,
    cotangent,
):
    both = ("mp", "dp")
    place, rank = lax.axis_index("dp"), lax.axis_index("mp")
    total, model = tokens.shape
    share = total // n_mp
    size = total - MOST
    depth, width = w_value.shape[1], w_value.shape[2]
    hidden = w_up.shape[2]
    heads, rows, columns = random_table.shape
    near = rows == size and n_dp % 2 == 0 and n_dp * width * MOST <= 4 << 20

    item_lengths = lengths[0]
    longest = jnp.argmax(item_lengths)
    start = (jnp.cumsum(item_lengths) - item_lengths)[longest]
    first = item_lengths[(longest + 1) % item_lengths.shape[0]].astype(jnp.int32).reshape(1, 1)

    def turned(x, by):
        return lax.dynamic_slice_in_dim(jnp.concatenate([x, x]), by, total)

    def mine(x):
        return lax.dynamic_slice_in_dim(x, rank * share, share)

    gains = jnp.pad(norm_gain.reshape(4, depth).T, ((0, 0), (0, 124)))
    pack = jnp.concatenate([w_value[0], synth_first, gains], axis=1)
    table = synth_second.reshape(width, -1)
    if near:
        pack, table = gather_weights([pack, table], n_dp)
    else:
        pack, table = lax.all_gather(pack, "dp"), lax.all_gather(table, "dp")
        table = table.transpose(1, 0, 2).reshape(width, total // size, size).transpose(1, 0, 2)
    pack = pack.reshape(model, -1)
    gain = jnp.pad(pack[:, 2 * width : 2 * width + 4].T.astype(F32), ((0, 4), (0, 0)))

    def whole(parts):
        joined = lax.all_gather(jnp.concatenate(parts, axis=1), both)
        return joined.reshape(n_mp, model, -1)

    weights_one = whole([w_up[0], w_down[0].T, w_out[0].T, w_value[1]])
    weights_two = whole([w_up[1], w_down[1].T, w_out[1].T, w_value[0]])
    own_corner, pack = lax.optimization_barrier((random_table[:, :, :size], pack))
    corner = gather_corner(own_corner, rows, n_dp)

    inputs = turned(tokens, start)
    normed_one, values, values_t, acts, acts_t, slope = begin(inputs, pack[:, : 2 * width], gain)
    mixed, lse = dense_forward(first, acts, values, table)
    mixed_one = swap(mixed.reshape(n_mp, share, width), n_mp, 5)
    inputs = mine(inputs)
    *record_one, between, normed_two, parts = ends(
        inputs, mixed_one, True, weights_one, width, gain, 1, True
    )

    values_two = swap(parts, n_mp, 6, lanes_out=True)
    if near:
        values_all, mixed, table_lse = table_forward(first, random_table, corner, values_two, n_dp)
        mixed_two = swap(mixed.reshape(n_mp, -1, width, rows), n_mp, 7)
    else:
        values_all = lax.all_gather(values_two[:, :MOST], "dp")
        mixed, table_lse = random_forward(random_table, values_all)
        mixed = lax.all_to_all(mixed, "dp", 0, 0, tiled=True).transpose(1, 0, 2).reshape(width, total)
        short = short_forward(first, corner, values_two[:, MOST:])
        mixed_two = swap(jnp.concatenate([mixed[:, :MOST], short], axis=1), n_mp, 7, lanes_in=True)
    *record_two, result = ends(between, mixed_two, False, weights_two, width, gain, 3, False)
    early_first, _ = lax.optimization_barrier((synth_first, mixed_two))
    first_all = whole([early_first])

    grads_two, dmiddle, parts, dgain_two = ends_back(
        mine(turned(cotangent, start)), mixed_two, False, weights_two, width, gain, 3, record_two
    )

    def scattered(grads, axes):
        grads = grads.reshape(-1, depth, grads.shape[-1])
        return lax.psum_scatter(grads, axes, scatter_dimension=0).astype(F32)

    if near:
        upstream = swap(parts, n_mp, 8).reshape(n_dp, width, rows)
        rows_upstream, dvalues, dcorner, result, grads_two = table_backward(
            first, random_table, corner, table_lse, values_two[:, MOST:], upstream, result, grads_two, n_dp, n_mp
        )
        grads_two = scattered(grads_two, "dp")
    else:
        upstream = swap(parts, n_mp, 8, lanes_out=True)
        dcorner, dshort = short_backward(first, corner, values_two[:, MOST:], upstream[:, MOST:])
        upstream = upstream.reshape(width, n_dp, rows).transpose(1, 0, 2)
        upstream = lax.all_to_all(upstream, "dp", 0, 0, tiled=True)
        valid = (place * rows < MOST).astype(F32).reshape(1, 1)
        dtable, dvalues = random_backward(valid, random_table, table_lse, values_all, upstream)
        dvalues = lax.psum_scatter(dvalues, "dp", scatter_dimension=0)
        dvalues = jnp.concatenate([dvalues, dshort], axis=1)
        result = lax.all_gather(result, "mp")
        grads_two = scattered(grads_two, both)
    dcorner = scatter_corner(dcorner, rows, n_dp)
    result = turned(result.reshape(total, model), total - start)
    dvalues = swap(dvalues, n_mp, 9, lanes_in=True)

    grads_one, dmiddle, parts, dgain_one = ends_back(
        dmiddle, mixed_one, True, weights_one, width, gain, 1, record_one, (between, normed_two, dvalues)
    )
    grads_one = scattered(grads_one, both)
    upstream = swap(parts, n_mp, 10).reshape(total, width)
    back, entry_grad, second_grad = dense_backward(
        first, acts, acts_t, values_t, upstream, table, lse, slope, normed_one
    )
    back = back.reshape(n_mp, share, 2 * width)
    entry_grad = entry_grad.reshape(n_dp, depth, 2 * width)
    if near:
        back, entry_grad, second_grad = last_exchange(back, [entry_grad, second_grad], n_dp, n_mp)
    else:
        back = swap(back, n_mp, 11)
        entry_grad = lax.psum_scatter(entry_grad, "dp", scatter_dimension=0).astype(F32)
        second_grad = second_grad.transpose(1, 0, 2).reshape(width, n_dp, -1).transpose(1, 0, 2)
        second_grad = lax.psum_scatter(second_grad, "dp", scatter_dimension=0).astype(F32)
    input_grad, dgain = close(back, weights_two, first_all, inputs, gain, dmiddle)
    gain_grad = jnp.concatenate([dgain[:1], dgain_one[:2], dgain_two[:1], jnp.zeros((4, model), F32)])
    input_grad, gain_grad = finish(input_grad, gain_grad, n_dp, n_mp)
    input_grad = turned(input_grad.reshape(total, model), total - start)
    if near:
        upstream_last, _ = lax.optimization_barrier((rows_upstream, gain_grad))
        dtable = table_grad(random_table, table_lse, values_all, upstream_last, dcorner)
    else:
        dtable = dtable.at[:, :, :size].add(dcorner.astype(F32))

    gain_grad = lax.dynamic_slice_in_dim(gain_grad[:4], place * depth, depth, axis=1)
    out_at = slice(2 * hidden, 2 * hidden + width)
    return (
        result,
        input_grad,
        gain_grad.reshape(2, 2, depth),
        jnp.stack([entry_grad[:, :width], grads_one[:, 2 * hidden + width :]]),
        jnp.stack([grads_one[:, out_at].T, grads_two[:, out_at].T]),
        jnp.stack([grads_one[:, :hidden], grads_two[:, :hidden]]),
        jnp.stack([grads_one[:, hidden : 2 * hidden].T, grads_two[:, hidden : 2 * hidden].T]),
        entry_grad[:, width:],
        second_grad.reshape(heads, HD, -1),
        dtable,
    )


def solution(mesh):
    in_specs = (
        P("dp", None),
        P("dp", None),
        P(None, None, "dp"),
        P(None, "dp", "mp"),
        P(None, "mp", "dp"),
        P(None, "dp", "mp"),
        P(None, "mp", "dp"),
        P("dp", "mp"),
        P("mp", None, "dp"),
        P("mp", "dp", None),
        P("dp", None),
    )
    out_specs = (
        P("dp", None),
        P("dp", None),
        P(None, None, "dp"),
        P(None, "dp", "mp"),
        P(None, "mp", "dp"),
        P(None, "dp", "mp"),
        P(None, "mp", "dp"),
        P("dp", "mp"),
        P("mp", None, "dp"),
        P("mp", "dp", None),
    )
    return jax.shard_map(
        partial(per_device, mesh.shape["dp"], mesh.shape["mp"]),
        mesh=mesh,
        in_specs=in_specs,
        out_specs=out_specs,
        check_vma=False,
    )
```

```python
from functools import partial

import jax
import jax.numpy as jnp
from jax import lax
from jax.experimental import pallas as pl
from jax.experimental.pallas import tpu as pltpu
from jax.sharding import PartitionSpec as P

F32, BF16 = jnp.float32, jnp.bfloat16
HD = 64
MOST = 1792
TILE = 256
VMEM = 58 * 1024 * 1024


MESH = pl.DeviceIdType.MESH
ANY = pl.BlockSpec(memory_space=pl.ANY)
INTO = pl.BlockSpec(memory_space=pltpu.VMEM)
SCALAR = pl.BlockSpec(memory_space=pltpu.SMEM)
DMA = pltpu.SemaphoreType.DMA


def remote(source, target, send, recv, axis, index):
    return pltpu.make_async_remote_copy(
        src_ref=source, dst_ref=target, send_sem=send, recv_sem=recv, device_id={axis: index}, device_id_type=MESH
    )


def greet(groups):
    barrier = pltpu.get_barrier_semaphore()
    for axis, size in groups:
        me = lax.axis_index(axis)
        for step in range(1, size):
            pl.semaphore_signal(
                barrier, inc=1, device_id={axis: lax.rem(me + step, size)}, device_id_type=MESH
            )
    pl.semaphore_wait(barrier, sum(size - 1 for _, size in groups))


def greet_all(n, n_mp):
    barrier = pltpu.get_barrier_semaphore()
    me = lax.axis_index("dp") * n_mp + lax.axis_index("mp")

    @pl.loop(1, n * n_mp)
    def _(step):
        there = lax.rem(me + step, n * n_mp)
        where = {"dp": there // n_mp, "mp": lax.rem(there, n_mp)}
        pl.semaphore_signal(barrier, inc=1, device_id=where, device_id_type=MESH)

    pl.semaphore_wait(barrier, n * n_mp - 1)


def remote_to(source, target, send, recv, place, rank):
    return pltpu.make_async_remote_copy(
        src_ref=source,
        dst_ref=target,
        send_sem=send,
        recv_sem=recv,
        device_id={"dp": place, "mp": rank},
        device_id_type=MESH,
    )


def comm_params(number):
    return pltpu.CompilerParams(collective_id=number, has_side_effects=True, vmem_limit_bytes=VMEM)


class Line:
    def __init__(self, size):
        self.size, self.length = size, size // 2
        self.place = lax.axis_index("dp")
        self.at, self.side = self.place // 2, lax.rem(self.place, 2)
        self.partner = self.at * 2 + 1 - self.side
        self.right, self.left = self.place + 2, self.place - 2
        self.has_right, self.has_left = self.at + 1 < self.length, self.at > 0


def line_gather(line, early, late, begin, more, use):
    length, at, side = line.length, line.at, line.side
    pieces = early + late

    def push(piece, s, to, across=False, way=0, fresh=False):
        own, slots, send_x, send_z, recv, _ = piece
        a = s // 2
        send = send_x.at[a] if across else send_z.at[way, a]
        remote(own if fresh else slots.at[s], slots.at[s], send, recv.at[s], "dp", to).start()

    def arrived(piece, s):
        own, slots, send_x, send_z, recv, _ = piece
        remote(own, slots.at[s], send_x.at[0], recv.at[s], "dp", line.partner).wait_recv()

    def sent(which):
        for own, slots, send_x, send_z, recv, _ in pieces:
            remote(own, slots.at[0], which(send_x, send_z), recv.at[0], "dp", line.partner).wait_send()

    def start(piece):
        @pl.when(line.has_right)
        def _():
            push(piece, line.place, line.right, way=0, fresh=True)

        @pl.when(line.has_left)
        def _():
            push(piece, line.place, line.left, way=1, fresh=True)

        push(piece, line.place, line.partner, across=True, fresh=True)

    def arrive(a, way):
        s = a * 2 + side
        on, to = ((line.has_right, line.right), (line.has_left, line.left))[way]
        for piece in pieces:
            arrived(piece, s)

            @pl.when(on)
            def _():
                push(piece, s, to, way=way)

            push(piece, s, line.partner, across=True)
            piece[5](s)

    def crossed(a):
        s = a * 2 + 1 - side
        for piece in pieces:
            arrived(piece, s)
            piece[5](s)
        use(s)

    for piece in early:
        start(piece)
    begin()
    for piece in late:
        start(piece)
    more()

    @pl.loop(1, length + 1)
    def _(k):
        low, high = at - k, at + k

        @pl.when(low >= 0)
        def _():
            arrive(low, 0)

        @pl.when(high < length)
        def _():
            arrive(high, 1)

        @pl.when(low >= 0)
        def _():
            use(low * 2 + side)

        @pl.when(high < length)
        def _():
            use(high * 2 + side)

        @pl.when(low + 1 >= 0)
        def _():
            crossed(low + 1)

        @pl.when(jnp.logical_and(k > 1, high - 1 < length))
        def _():
            crossed(high - 1)

    @pl.loop(0, length)
    def _(a):
        sent(lambda x, z: x.at[a])

        @pl.when(jnp.logical_and(line.has_right, a <= at))
        def _():
            sent(lambda x, z: z.at[0, a])

        @pl.when(jnp.logical_and(line.has_left, a >= at))
        def _():
            sent(lambda x, z: z.at[1, a])


def nothing(*_):
    pass


def gather_scratch(n):
    return [DMA((n // 2,)), DMA((2, n // 2)), DMA((n,))]


class Scatter:
    def __init__(self, line, items):
        self.line, self.items = line, items

    def over_x(self, item, a):
        _, _, x_out, x_in, _, _, _, send_x, recv_x = item[:9]
        return remote(x_out.at[a], x_in.at[a], send_x.at[a], recv_x.at[a], "dp", self.line.partner)

    def over_z(self, item, a, way, to=None):
        z_out, into, send, recv = item[4], item[5 + way], item[9], item[10 + way]
        return remote(z_out.at[a], into.at[a], send.at[a], recv.at[a], "dp", self.line.partner if to is None else to)

    def cross(self):
        length, at, side = self.line.length, self.line.at, self.line.side

        def one(a):
            for item in self.items:
                item[2][a] = item[0](a * 2 + 1 - side).astype(BF16)
                self.over_x(item, a).start()

        @pl.loop(0, length - 1)
        def _(step):
            k = length - 1 - step

            @pl.when(at + k < length)
            def _():
                one(at + k)

            @pl.when(at - k >= 0)
            def _():
                one(at - k)

        one(at)

    def relay(self, k):
        line = self.line
        length, at, side = line.length, line.at, line.side

        def one(a, way, behind, to):
            for item in self.items:
                make, _, _, x_in, z_out = item[:5]
                total = make(a * 2 + side)
                self.over_x(item, a).wait_recv()
                z_out[a] = (total + x_in[a].astype(F32)).astype(BF16)

                @pl.when(behind)
                def _():
                    self.over_z(item, a, way).wait_recv()
                    z_out[a] = (z_out[a].astype(F32) + item[5 + way][a].astype(F32)).astype(BF16)

                self.over_z(item, a, way, to).start()

        @pl.when(at + k < length)
        def _():
            one(at + k, 0, line.has_left, line.right)

        @pl.when(at - k >= 0)
        def _():
            one(at - k, 1, line.has_right, line.left)

    def end(self):
        line = self.line
        at = line.at
        for item in self.items:
            make, out, _, x_in, _, l_in, r_in = item[:7]
            total = make(line.place)
            self.over_x(item, at).wait_recv()
            out[...] = total + x_in[at].astype(F32)

            @pl.when(line.has_left)
            def _():
                self.over_z(item, at, 0).wait_recv()
                out[...] += l_in[at].astype(F32)

            @pl.when(line.has_right)
            def _():
                self.over_z(item, at, 1).wait_recv()
                out[...] += r_in[at].astype(F32)

        @pl.loop(0, line.length)
        def _(a):
            for item in self.items:
                self.over_x(item, a).wait_send()

            @pl.when(a != at)
            def _():
                for item in self.items:
                    self.over_z(item, a, 0).wait_send()


def line_scatter(line, items, middle):
    scatter = Scatter(line, items)
    scatter.cross()
    middle()

    @pl.loop(0, line.length - 1)
    def _(step):
        scatter.relay(line.length - 1 - step)

    scatter.end()


def scatter_scratch(n, shape):
    return [pltpu.VMEM((n // 2,) + shape, BF16)] * 5 + [DMA((n // 2,))] * 5


def gather_weights(arrays, corner, n):
    count = len(arrays)

    def kernel(*refs):
        owns, corner_ref, alls, part_ref = refs[:count], refs[count], refs[count + 1 : 2 * count + 1], refs[2 * count + 1]
        send, recv, kept_sem = refs[2 * count + 2 : 2 * count + 5]
        rest = refs[2 * count + 5 :]
        line = Line(n)
        place = line.place
        greet([("dp", n)])
        kept = [pltpu.make_async_copy(owns[i], alls[i].at[place], kept_sem.at[i]) for i in range(count)]

        def deal(s):
            return remote(corner_ref.at[s], part_ref, send.at[s], recv, "dp", s)

        def begin():
            for copy in kept:
                copy.start()

            @pl.when(place == 0)
            def _():
                @pl.loop(1, n)
                def _(s):
                    deal(s).start()

                part_ref[...] = corner_ref[0]

        pieces = [(owns[i], alls[i], *rest[3 * i : 3 * i + 3], nothing) for i in range(count)]
        line_gather(line, pieces, [], begin, nothing, nothing)
        for copy in kept:
            copy.wait()

        @pl.when(place != 0)
        def _():
            deal(0).wait_recv()

        @pl.when(place == 0)
        def _():
            @pl.loop(1, n)
            def _(s):
                deal(s).wait_send()

    return pl.pallas_call(
        kernel,
        in_specs=[ANY] * count + [INTO],
        out_specs=[ANY] * count + [INTO],
        out_shape=[jax.ShapeDtypeStruct((n,) + a.shape, a.dtype) for a in arrays]
        + [jax.ShapeDtypeStruct(corner.shape[1:], corner.dtype)],
        scratch_shapes=[DMA((n,)), DMA, DMA((count,))] + gather_scratch(n) * count,
        compiler_params=comm_params(0),
        name="gather_weights",
    )(*arrays, corner)


def swap(x, n, number, lanes_in=False, lanes_out=False, part=None, n_dp=None):
    if lanes_in:
        block = (x.shape[0], x.shape[1] // n)
    else:
        block = x.shape[1:]
    shape = (block[0], n * block[1]) if lanes_out else (n,) + block

    def at(ref, lanes, j):
        if lanes:
            return ref.at[:, pl.ds(pl.multiple_of(j * block[1], block[1]), block[1])]
        return ref.at[j]

    def kernel(x_ref, *refs):
        if part is not None:
            part_ref, out_ref, all_ref, send, recv, own_sem, *rest = refs
            greet([("mp", n), ("dp", n_dp)])
        else:
            out_ref, send, recv, own_sem = refs
            greet([("mp", n)])
        me = lax.axis_index("mp")
        copies = []
        for step in range(1, n):
            peer = lax.rem(me + step, n)
            copies.append(
                remote(at(x_ref, lanes_in, peer), at(out_ref, lanes_out, me), send.at[step], recv.at[step], "mp", peer)
            )
            copies[-1].start()
        own = pltpu.make_async_copy(at(x_ref, lanes_in, me), at(out_ref, lanes_out, me), own_sem)
        own.start()
        if part is not None:
            line = Line(n_dp)
            all_ref[line.place] = part_ref[...]
            line_gather(line, [(part_ref, all_ref, *rest, nothing)], [], nothing, nothing, nothing)
        own.wait()
        for copy in copies:
            copy.wait()

    more = part is not None
    return pl.pallas_call(
        kernel,
        in_specs=[ANY] + [INTO] * more,
        out_specs=[ANY, INTO] if more else ANY,
        out_shape=[
            jax.ShapeDtypeStruct(shape, x.dtype),
            jax.ShapeDtypeStruct((n_dp,) + part.shape, part.dtype),
        ]
        if more
        else jax.ShapeDtypeStruct(shape, x.dtype),
        scratch_shapes=[DMA((n,)), DMA((n,)), DMA] + (gather_scratch(n_dp) if more else []),
        compiler_params=comm_params(number),
        name="swap",
    )(*([x, part] if more else [x]))


def table_forward(first, table, corner, parts, weights, n, n_mp):
    heads, rows, columns = table.shape
    _, width, share = parts.shape
    tokens = share * n_mp
    size = tokens - MOST
    owners = MOST // rows
    chunks = share // rows
    pairs = n_mp // 2

    def kernel(first_ref, table_ref, corner_ref, parts_ref, weights_ref, values_ref, mixed_ref, short_ref, lse_ref,
               all_ref, own, soft, sums, short_sum, v_send, v_recv, send_x, send_z, recv, send_m, recv_m, send_s,
               w_send_x, w_send_z, w_recv, w_own, far_send, far_recv, near_send, near_recv, on_send, on_recv):
        line = Line(n)
        place, me = line.place, lax.axis_index("mp")
        pair, core = me // 2, lax.rem(me, 2)
        twin = pair * 2 + 1 - core
        owner = place < owners
        greet_all(n, n_mp)

        def lanes(j):
            return own.at[:, pl.ds(pl.multiple_of(j * share, share), share)]

        gets = []
        for step in range(1, n_mp):
            peer = lax.rem(me + step, n_mp)
            gets.append(remote(parts_ref.at[peer], lanes(me), v_send.at[step], v_recv.at[step], "mp", peer))
        keep = pltpu.make_async_copy(weights_ref, all_ref.at[me, place], w_own)

        def prepare():
            offer(place, weights_ref)
            keep.start()
            own[:, pl.ds(pl.multiple_of(me * share, share), share)] = parts_ref[me]
            for head in range(heads):
                scores = table_ref[head, :, 0:MOST].astype(F32)
                top = jnp.max(scores, axis=1, keepdims=True)
                powers = jnp.exp(scores - top)
                total = jnp.sum(powers, axis=1, keepdims=True)
                soft[head] = (powers / total).astype(BF16)
                lse_ref[head] = jnp.broadcast_to(top + jnp.log(total), (rows, 128))
            for copy in gets:
                copy.wait()
            values_ref[place] = own[:, 0:MOST]
            short_ref[...] = own[:, MOST:tokens]

        def over(step, s, source):
            to = lax.rem(pair + step, pairs) * 2 + core
            return remote(source, all_ref.at[me, s], far_send.at[step, s], far_recv.at[step, s], "mp", to)

        def across(s, source):
            return remote(source, all_ref.at[me, s], near_send.at[s], near_recv.at[s], "mp", twin)

        def onward(step, s):
            block = lax.rem(pair + pairs - step, pairs) * 2 + core
            return remote(
                all_ref.at[block, s], all_ref.at[block, s], on_send.at[step, s], on_recv.at[step, s], "mp", twin
            )

        def offer(s, source):
            for step in range(1, pairs):
                over(step, s, source).start()
            across(s, source).start()

        def product(s):
            for head in range(heads):
                span = slice(head * HD, (head + 1) * HD)
                sums[s, span, :] = nt(values_ref[s, span, :], soft[head]).astype(BF16)

        here = jnp.logical_and(owner, place // chunks == me)

        def back(s):
            return remote_to(
                sums.at[s],
                mixed_ref.at[me, lax.rem(place, chunks)],
                send_m.at[s],
                recv_m.at[me, lax.rem(place, chunks)],
                s,
                place // chunks,
            )

        def short_back():
            return remote(
                short_sum,
                mixed_ref.at[me, owners % chunks],
                send_s,
                recv_m.at[me, owners % chunks],
                "mp",
                owners // chunks,
            )

        def begin():
            early, inside, shift, at = small_masks(first_ref[0, 0], size)
            for head in range(heads):
                span = slice(head * HD, (head + 1) * HD)
                weighed = by_token(masked_soft(nn(at, corner_ref[head]), inside), early, shift)
                short_sum[span, :] = nt(own[span, MOST:tokens], weighed).astype(BF16)

            @pl.when(me == owners // chunks)
            def _():
                mixed_ref[me, owners % chunks] = short_sum[...]

            @pl.when(me != owners // chunks)
            def _():
                short_back().start()

            @pl.when(owner)
            def _():
                product(place)

            @pl.when(here)
            def _():
                mixed_ref[me, lax.rem(place, chunks)] = sums[place]

            @pl.when(jnp.logical_and(owner, jnp.logical_not(here)))
            def _():
                back(place).start()

        def use(s):
            @pl.when(owner)
            def _():
                product(s)
                back(s).start()

        for copy in gets:
            copy.start()
        line_gather(
            line,
            [(weights_ref, all_ref.at[me], w_send_x, w_send_z, w_recv, lambda s: offer(s, all_ref.at[me, s]))],
            [(values_ref.at[place], values_ref, send_x, send_z, recv, nothing)],
            prepare,
            begin,
            use,
        )

        @pl.loop(0, n)
        def _(s):
            for step in range(1, pairs):
                over(step, s, weights_ref).wait_recv()
                onward(step, s).start()

        @pl.loop(0, n)
        def _(s):
            @pl.when(jnp.logical_and(owner, jnp.logical_or(s != place, jnp.logical_not(here))))
            def _():
                back(s).wait_send()

            across(s, weights_ref).wait()
            for step in range(1, pairs):
                over(step, s, weights_ref).wait_send()
                onward(step, s).wait()

        @pl.when(me != owners // chunks)
        def _():
            short_back().wait_send()

        for c in range(chunks):
            d = me * chunks + c
            for g in range(n_mp):
                source = jnp.where(d < owners, d, place)

                @pl.when(jnp.logical_not(jnp.logical_and(source == place, g == me)))
                def _():
                    remote(short_sum, mixed_ref.at[g, c], send_s, recv_m.at[g, c], "mp", twin).wait_recv()

        keep.wait()

    return pl.pallas_call(
        kernel,
        in_specs=[SCALAR, INTO, INTO, INTO, ANY],
        out_specs=[INTO, INTO, INTO, INTO, ANY],
        out_shape=[
            jax.ShapeDtypeStruct((n, width, MOST), BF16),
            jax.ShapeDtypeStruct((n_mp, chunks, width, rows), BF16),
            jax.ShapeDtypeStruct((width, size), BF16),
            jax.ShapeDtypeStruct((heads, rows, 128), F32),
            jax.ShapeDtypeStruct((n_mp, n) + weights.shape, BF16),
        ],
        scratch_shapes=[
            pltpu.VMEM((width, tokens), BF16),
            pltpu.VMEM((heads, rows, MOST), BF16),
            pltpu.VMEM((n, width, rows), BF16),
            pltpu.VMEM((width, rows), BF16),
            DMA((n_mp,)),
            DMA((n_mp,)),
            *gather_scratch(n),
            DMA((n,)),
            DMA((n_mp, chunks)),
            DMA,
            *gather_scratch(n),
            DMA,
            DMA((pairs, n)),
            DMA((pairs, n)),
            DMA((n,)),
            DMA((n,)),
            DMA((pairs, n)),
            DMA((pairs, n)),
        ],
        compiler_params=comm_params(1),
        name="table_forward",
    )(first, table, corner, parts, weights)


def spread_mp(x_ref, all_ref, send, recv, own_sem, n):
    me, pairs = lax.axis_index("mp"), n // 2
    pair, core = me // 2, lax.rem(me, 2)
    twin = pair * 2 + 1 - core
    own = pltpu.make_async_copy(x_ref, all_ref.at[me], own_sem)
    near = remote(x_ref, all_ref.at[me], send.at[0], recv.at[0], "mp", twin)

    def far(step):
        to = lax.rem(pair + step, pairs) * 2 + core
        return remote(x_ref, all_ref.at[me], send.at[step], recv.at[step], "mp", to)

    def onward(step):
        source = lax.rem(pair + pairs - step, pairs) * 2 + core
        return remote(
            all_ref.at[source], all_ref.at[source], send.at[pairs + step], recv.at[pairs + step], "mp", twin
        )

    def start():
        for step in range(1, pairs):
            far(step).start()
        near.start()
        own.start()

    def relay():
        for step in range(1, pairs):
            far(step).wait_recv()
            onward(step).start()

    def end():
        for step in range(1, pairs):
            far(step).wait_send()
            onward(step).wait()
        near.wait()
        own.wait()

    return start, relay, end


def blend_mp(x_ref, out_refs, kept, twins, others, local, near_send, near_recv, far_send, far_recv, n):
    me, pairs = lax.axis_index("mp"), n // 2
    pair, core = me // 2, lax.rem(me, 2)
    twin = pair * 2 + 1 - core
    rows = x_ref.shape[1]
    chunk = rows // 6

    def keep(p):
        return pltpu.make_async_copy(x_ref.at[p * 2 + core], kept.at[p], local.at[p])

    def give(p):
        return remote(x_ref.at[p * 2 + 1 - core], twins.at[p], near_send.at[p], near_recv.at[p], "mp", twin)

    def pass_on(step):
        to = lax.rem(pair + step, pairs)
        return remote(
            kept.at[to], others.at[step - 1], far_send.at[step], far_recv.at[step], "mp", to * 2 + core
        )

    def over_rows(body):
        @pl.loop(0, rows // chunk)
        def _(i):
            body(pl.ds(pl.multiple_of(i * chunk, chunk), chunk))

    def start():
        for step in range(1, pairs + 1):
            p = lax.rem(pair + step, pairs)
            give(p).start()
            keep(p).start()

    def go_on():
        for step in range(1, pairs):
            p = lax.rem(pair + step, pairs)
            keep(p).wait()
            give(p).wait_recv()

            def body(at):
                kept[p, at, :] = (kept[p, at, :].astype(F32) + twins[p, at, :].astype(F32)).astype(BF16)

            over_rows(body)
            pass_on(step).start()

    def end():
        keep(pair).wait()
        give(pair).wait_recv()
        for step in range(1, pairs):
            pass_on(step).wait_recv()

        def body(at):
            total = kept[pair, at, :].astype(F32) + twins[pair, at, :].astype(F32)
            for j in range(pairs - 1):
                total += others[j, at, :].astype(F32)
            spot = 0
            for ref in out_refs:
                ref[at, :] = total[:, spot : spot + ref.shape[1]].astype(BF16)
                spot += ref.shape[1]

        over_rows(body)
        for p in range(pairs):
            give(p).wait_send()
        for step in range(1, pairs):
            pass_on(step).wait_send()

    return start, go_on, end


def blend_scratch(n, shape):
    pairs = n // 2
    return [
        pltpu.VMEM((pairs,) + shape, BF16),
        pltpu.VMEM((pairs,) + shape, BF16),
        pltpu.VMEM((pairs - 1,) + shape, BF16),
    ] + [DMA((pairs,))] * 5


def table_backward(first, table, corner, lse, short_t, parts, grads, n, n_mp):
    heads, rows, columns = table.shape
    width, size = short_t.shape
    owners = MOST // rows
    _, chunks, _, _ = parts.shape
    share = chunks * rows

    def kernel(first_ref, table_ref, corner_ref, lse_ref, short_ref, parts_ref, grads_ref, ups, got_ref, dcorner_ref,
               blended_ref, full, short_up, total, soft, send_u, recv_u, recv_s, v_send, v_recv, *rest):
        line = Line(n)
        place, me = line.place, lax.axis_index("mp")
        owner = place < owners
        greet_all(n, n_mp)
        blend, go_on, blended = blend_mp(grads_ref, [blended_ref], *rest[10:], n_mp)

        def hand(g, c):
            return remote_to(
                parts_ref.at[g, c], ups.at[place], send_u.at[g, c], recv_u.at[place], me * chunks + c, g
            )

        def hand_short(g, c):
            return remote_to(parts_ref.at[g, c], short_up, send_u.at[g, c], recv_s, place, g)

        def each_hand(act):
            for c in range(chunks):
                d = me * chunks + c
                for g in range(n_mp):
                    @pl.when(jnp.logical_and(d < owners, jnp.logical_not(jnp.logical_and(d == place, g == me))))
                    def _():
                        act(hand(g, c))

                    @pl.when(jnp.logical_and(d == owners, g != me))
                    def _():
                        act(hand_short(g, c))

        each_hand(lambda copy: copy.start())
        blend()

        @pl.when(jnp.logical_and(owner, place // chunks == me))
        def _():
            ups[place] = parts_ref[me, lax.rem(place, chunks)]

        @pl.when(me == owners // chunks)
        def _():
            short_up[...] = parts_ref[me, owners % chunks]

        for head in range(heads):
            soft[head] = jnp.exp(table_ref[head, :, 0:MOST].astype(F32) - lse_ref[head, :, 0:1]).astype(BF16)

        @pl.when(me != owners // chunks)
        def _():
            hand_short(0, 0).wait_recv()

        early, inside, shift, at = small_masks(first_ref[0, 0], size)
        for head in range(heads):
            span = slice(head * HD, (head + 1) * HD)
            weights = masked_soft(nn(at, corner_ref[head]), inside)
            here, up = short_ref[span, :], short_up[span, :]
            moved = nt(here, shift).astype(BF16)
            dsoft = jnp.where(early, tn(up, here), tn(up, moved))
            full[span, MOST : MOST + size] = nn(up, by_token(weights, early, shift)).astype(BF16)
            centre = jnp.sum(weights * dsoft, axis=1, keepdims=True)
            dcorner_ref[head] = tn(at, (weights * (dsoft - centre)).astype(BF16)).astype(BF16)

        def make(s):
            @pl.when(jnp.logical_and(owner, jnp.logical_not(jnp.logical_and(s == place, place // chunks == me))))
            def _():
                remote(short_up, ups.at[s], send_u.at[0, 0], recv_u.at[s], "dp", line.partner).wait_recv()

            @pl.when(jnp.logical_not(owner))
            def _():
                ups[s] = jnp.zeros((width, rows), BF16)

            return jnp.concatenate(
                [nn(ups[s, head * HD : (head + 1) * HD, :], soft[head]) for head in range(heads)], axis=0
            )

        line_scatter(line, [(make, total, *rest[:10])], go_on)
        full[:, 0:MOST] = total[...].astype(BF16)

        def lanes(j):
            return full.at[:, pl.ds(pl.multiple_of(j * share, share), share)]

        gives = []
        for step in range(1, n_mp):
            peer = lax.rem(me + step, n_mp)
            gives.append(remote(lanes(peer), got_ref.at[me], v_send.at[step], v_recv.at[step], "mp", peer))
            gives[-1].start()
        got_ref[me] = full[:, pl.ds(pl.multiple_of(me * share, share), share)]
        blended()
        each_hand(lambda copy: copy.wait_send())
        for copy in gives:
            copy.wait()

    return pl.pallas_call(
        kernel,
        in_specs=[SCALAR] + [INTO] * 5 + [ANY],
        out_specs=[INTO] * 4,
        out_shape=[
            jax.ShapeDtypeStruct((n, width, rows), BF16),
            jax.ShapeDtypeStruct((n_mp, width, share), BF16),
            jax.ShapeDtypeStruct((heads, size, size), BF16),
            jax.ShapeDtypeStruct(grads.shape[1:], BF16),
        ],
        scratch_shapes=[
            pltpu.VMEM((width, share * n_mp), BF16),
            pltpu.VMEM((width, rows), BF16),
            pltpu.VMEM((width, MOST), F32),
            pltpu.VMEM((heads, rows, MOST), BF16),
            DMA((n_mp, chunks)),
            DMA((n,)),
            DMA,
            DMA((n_mp,)),
            DMA((n_mp,)),
        ]
        + scatter_scratch(n, (width, MOST))
        + blend_scratch(n_mp, grads.shape[1:]),
        compiler_params=comm_params(2),
        name="table_backward",
    )(first, table, corner, lse, short_t, parts, grads)


def last_exchange(back, grads, n, n_mp):
    count = len(grads)

    def kernel(*refs):
        back_ref, grad_refs = refs[0], refs[1 : 1 + count]
        got_ref, out_refs = refs[1 + count], refs[2 + count : 2 + 2 * count]
        send, recv, own_sem, part, part_send, part_recv, last = refs[2 + 2 * count : 9 + 2 * count]
        rest = refs[9 + 2 * count :]
        line = Line(n)
        place, me = line.place, lax.axis_index("mp")
        greet([("dp", n), ("mp", n_mp)])
        copies = []
        for step in range(1, n_mp):
            peer = lax.rem(me + step, n_mp)
            copies.append(
                remote(back_ref.at[peer], got_ref.at[me], send.at[step], recv.at[step], "mp", peer)
            )
            copies[-1].start()
        own = pltpu.make_async_copy(back_ref.at[me], got_ref.at[me], own_sem)
        own.start()
        outs = [*out_refs[: count - 1], last]
        items = [
            (lambda s, ref=grad_refs[i]: ref[s].astype(F32), outs[i], *rest[10 * i : 10 * i + 10])
            for i in range(count)
        ]
        line_scatter(line, items, nothing)
        part[...] = last[...].astype(BF16)

        def hand(s):
            return remote(part, out_refs[-1].at[s], part_send, part_recv.at[s], "dp", 0)

        @pl.when(place != 0)
        def _():
            hand(place).start()
            hand(place).wait_send()

        @pl.when(place == 0)
        def _():
            out_refs[-1][0] = part[...]

            @pl.loop(1, n)
            def _(s):
                hand(s).wait_recv()

        @pl.when(place != 0)
        def _():
            out_refs[-1][...] = jnp.zeros_like(out_refs[-1])

        own.wait()
        for copy in copies:
            copy.wait()

    return pl.pallas_call(
        kernel,
        in_specs=[ANY] + [INTO] * count,
        out_specs=[ANY] + [INTO] * count,
        out_shape=[jax.ShapeDtypeStruct(back.shape, BF16)]
        + [jax.ShapeDtypeStruct(g.shape[1:], F32) for g in grads[:-1]]
        + [jax.ShapeDtypeStruct(grads[-1].shape, BF16)],
        scratch_shapes=[DMA((n_mp,)), DMA((n_mp,)), DMA]
        + [pltpu.VMEM(grads[-1].shape[1:], BF16), DMA, DMA((n,)), pltpu.VMEM(grads[-1].shape[1:], F32)]
        + [each for g in grads for each in scatter_scratch(n, g.shape[1:])],
        compiler_params=comm_params(3),
        name="last_exchange",
    )(back, *grads)


def nn(a, b):
    return lax.dot_general(a, b, (((1,), (0,)), ((), ())), preferred_element_type=F32)


def nt(a, b):
    return lax.dot_general(a, b, (((1,), (1,)), ((), ())), preferred_element_type=F32)


def tn(a, b):
    return lax.dot_general(a, b, (((0,), (0,)), ((), ())), preferred_element_type=F32)


def small_masks(first, size):
    row = lax.broadcasted_iota(jnp.int32, (size, size), 0)
    col = lax.broadcasted_iota(jnp.int32, (size, size), 1)
    early = row < first
    inside = col < jnp.where(early, first, size - first)
    shift = jnp.where(col == row + first, 1.0, 0.0).astype(BF16)
    rows = jnp.where(col == jnp.where(early, row, row - first), 1.0, 0.0).astype(BF16)
    return early, inside, shift, rows


def masked_soft(scores, inside):
    masked = jnp.where(inside, scores, -1e30)
    powers = jnp.where(inside, jnp.exp(masked - jnp.max(masked, axis=1, keepdims=True)), 0.0)
    return powers / jnp.sum(powers, axis=1, keepdims=True)


def by_token(soft, early, shift):
    low = soft.astype(BF16)
    zero = jnp.zeros_like(low)
    late = nn(jnp.where(early, zero, low), shift).astype(BF16)
    return jnp.where(early, low, zero) + late


def dense_forward(first, acts, values, table):
    tokens, width = acts.shape
    heads = width // HD
    tiles = MOST // TILE
    size = tokens - MOST
    columns = table.shape[2]
    blocks = MOST // columns

    def kernel(first_ref, acts_ref, values_ref, table_ref, out_ref, lse_ref):
        tile = pl.program_id(0)
        lane = lax.broadcasted_iota(jnp.int32, (TILE, 128), 1)

        def scored(span, number):
            parts = [nn(acts_ref[:, span], table_ref[b, span, :]) for b in range(number)]
            return jnp.concatenate(parts, axis=1)

        @pl.when(tile < tiles)
        def _():
            lse = jnp.zeros((TILE, 128), F32)
            parts = []
            for head in range(heads):
                span = slice(head * HD, (head + 1) * HD)
                scores = scored(span, blocks)
                top = jnp.max(scores, axis=1, keepdims=True)
                powers = jnp.exp(scores - top)
                total = jnp.sum(powers, axis=1, keepdims=True)
                mixed = nn(powers.astype(BF16), values_ref[0:MOST, span])
                parts.append((mixed / total).astype(BF16))
                lse = jnp.where(lane == head, top + jnp.log(total), lse)
            out_ref[...] = jnp.concatenate(parts, axis=1)
            lse_ref[...] = lse

        @pl.when(tile == tiles)
        def _():
            early, inside, shift, _ = small_masks(first_ref[0, 0], size)
            parts = []
            for head in range(heads):
                span = slice(head * HD, (head + 1) * HD)
                soft = by_token(masked_soft(scored(span, size // columns), inside), early, shift)
                parts.append(nn(soft, values_ref[MOST:tokens, span]).astype(BF16))
            out_ref[...] = jnp.concatenate(parts, axis=1)
            lse_ref[...] = jnp.zeros((TILE, 128), F32)

    return pl.pallas_call(
        kernel,
        grid=(tiles + 1,),
        in_specs=[
            pl.BlockSpec(memory_space=pltpu.SMEM),
            pl.BlockSpec((TILE, width), lambda t: (t, 0)),
            pl.BlockSpec((tokens, width), lambda t: (0, 0)),
            pl.BlockSpec(table.shape, lambda t: (0, 0, 0)),
        ],
        out_specs=[
            pl.BlockSpec((TILE, width), lambda t: (t, 0)),
            pl.BlockSpec((TILE, 128), lambda t: (t, 0)),
        ],
        out_shape=[
            jax.ShapeDtypeStruct((tokens, width), BF16),
            jax.ShapeDtypeStruct((tokens, 128), F32),
        ],
        compiler_params=pltpu.CompilerParams(vmem_limit_bytes=VMEM),
        cost_estimate=pl.CostEstimate(flops=12 * tokens * tokens * width, bytes_accessed=8 * tokens * width, transcendentals=0),
        name="dense_forward",
    )(first, acts, values, table)


def dense_backward(first, acts, acts_t, values_t, upstream, table, lse, slope, normed, parts=None, give=None, n=None, n_mp=None):
    busy = parts is not None
    tokens, width = acts.shape
    model = normed.shape[1]
    heads = width // HD
    tiles = MOST // TILE
    size = tokens - MOST
    columns = table.shape[2]
    blocks = MOST // columns

    def kernel(first_ref, acts_ref, acts_t_ref, values_t_ref, up_ref, table_ref, lse_ref, slope_ref, normed_ref, *refs):
        tile = pl.program_id(0)
        if busy:
            parts_ref, give_ref, back_ref, dweights_ref, dtable_ref, part_ref, all_ref = refs[:7]
            dv_acc, dt_acc, dpre, send, recv, own_sem, *rest = refs[7:]
            line = Line(n)
            scatter = Scatter(line, [(lambda s: parts_ref[s].astype(F32), part_ref, *rest)])
            start, relay, end = spread_mp(give_ref, all_ref, send, recv, own_sem, n_mp)

            @pl.when(tile == 0)
            def _():
                greet([("dp", n), ("mp", n_mp)])
                start()
                scatter.cross()

            for k in range(line.length - 1, 0, -1):
                @pl.when(tile == 2 * (line.length - k))
                def _():
                    scatter.relay(k)

            @pl.when(tile == 5)
            def _():
                relay()
        else:
            back_ref, dweights_ref, dtable_ref, dv_acc, dt_acc, dpre = refs

        @pl.when(tile == 0)
        def _():
            dv_acc[...] = jnp.zeros_like(dv_acc)
            dt_acc[...] = jnp.zeros_like(dt_acc)

        def scored(span, number):
            parts = [nn(acts_ref[:, span], table_ref[b, span, :]) for b in range(number)]
            return jnp.concatenate(parts, axis=1)

        def spread(span, dscores, number):
            total = 0.0
            for b in range(number):
                part = dscores[:, b * columns : (b + 1) * columns]
                dt_acc[b, span, :] += nn(acts_t_ref[span, :], part)
                total += nt(part, table_ref[b, span, :])
            return total

        def keep(parts):
            slopes = slope_ref[...].astype(F32)
            rows = pl.ds(pl.multiple_of(tile * TILE, TILE), TILE)
            dpre[rows, :] = (slopes * jnp.concatenate(parts, axis=1)).astype(BF16)

        @pl.when(tile < tiles)
        def _():
            parts = []
            up_t = up_ref[...].T
            for head in range(heads):
                span = slice(head * HD, (head + 1) * HD)
                soft = jnp.exp(scored(span, blocks) - lse_ref[:, head : head + 1])
                dsoft = nn(up_ref[:, span], values_t_ref[span, 0:MOST])
                dv_acc[span, 0:MOST] += nn(up_t[span, :], soft.astype(BF16))
                weighed = soft * dsoft
                centre = jnp.sum(weighed, axis=1, keepdims=True)
                parts.append(spread(span, (weighed - soft * centre).astype(BF16), blocks))
            keep(parts)

        @pl.when(tile == tiles)
        def _():
            early, inside, shift, _ = small_masks(first_ref[0, 0], size)
            parts = []
            up_t = up_ref[...].T
            for head in range(heads):
                span = slice(head * HD, (head + 1) * HD)
                soft = masked_soft(scored(span, size // columns), inside)
                here = values_t_ref[span, MOST:tokens]
                moved = nt(here, shift).astype(BF16)
                dsoft = jnp.where(early, nn(up_ref[:, span], here), nn(up_ref[:, span], moved))
                dv_acc[span, MOST:tokens] = nn(up_t[span, :], by_token(soft, early, shift))
                centre = jnp.sum(soft * dsoft, axis=1, keepdims=True)
                parts.append(spread(span, (soft * (dsoft - centre)).astype(BF16), size // columns))
            keep(parts)
            dvalues_t = dv_acc[...].astype(BF16)
            back_ref[:, 0:width] = dvalues_t.T
            back_ref[:, width:] = dpre[...]
            value_grad = nn(dvalues_t, normed_ref[...])
            first_grad = nn(dpre[...].T, normed_ref[...])
            dweights_ref[:, 0:width] = value_grad.T.astype(BF16)
            dweights_ref[:, width:] = first_grad.T.astype(BF16)
            dtable_ref[...] = dt_acc[...].astype(BF16)
            if busy:
                scatter.end()
                end()

    whole = lambda t: (0, 0)
    rows = lambda t: (t, 0)
    return pl.pallas_call(
        kernel,
        grid=(tiles + 1,),
        in_specs=[
            pl.BlockSpec(memory_space=pltpu.SMEM),
            pl.BlockSpec((TILE, width), rows),
            pl.BlockSpec((width, TILE), lambda t: (0, t)),
            pl.BlockSpec((width, tokens), whole),
            pl.BlockSpec((TILE, width), rows),
            pl.BlockSpec(table.shape, lambda t: (0, 0, 0)),
            pl.BlockSpec((TILE, 128), rows),
            pl.BlockSpec((TILE, width), rows),
            pl.BlockSpec((tokens, model), whole),
        ]
        + [INTO, ANY] * busy,
        out_specs=[
            pl.BlockSpec((tokens, 2 * width), whole),
            pl.BlockSpec((model, 2 * width), whole),
            pl.BlockSpec(table.shape, lambda t: (0, 0, 0)),
        ]
        + [INTO, ANY] * busy,
        out_shape=[
            jax.ShapeDtypeStruct((tokens, 2 * width), BF16),
            jax.ShapeDtypeStruct((model, 2 * width), BF16),
            jax.ShapeDtypeStruct(table.shape, BF16),
        ]
        + (
            [
                jax.ShapeDtypeStruct(parts.shape[1:], F32),
                jax.ShapeDtypeStruct((n_mp,) + give.shape, give.dtype),
            ]
            if busy
            else []
        ),
        scratch_shapes=[
            pltpu.VMEM((width, tokens), F32),
            pltpu.VMEM(table.shape, F32),
            pltpu.VMEM((tokens, width), BF16),
        ]
        + ([DMA((n_mp,)), DMA((n_mp,)), DMA] + scatter_scratch(n, parts.shape[1:]) if busy else []),
        compiler_params=comm_params(9) if busy else pltpu.CompilerParams(vmem_limit_bytes=VMEM),
        cost_estimate=pl.CostEstimate(flops=24 * tokens * tokens * width, bytes_accessed=16 * tokens * width, transcendentals=0),
        name="dense_backward",
    )(first, acts, acts_t, values_t, upstream, table, lse, slope, normed, *([parts, give] if busy else []))


def random_forward(table, values_t):
    heads, rows, _ = table.shape
    slots, width, _ = values_t.shape

    def kernel(table_ref, values_ref, out_ref, lse_ref):
        scores = table_ref[0, :, 0:MOST].astype(F32)
        top = jnp.max(scores, axis=1, keepdims=True)
        powers = jnp.exp(scores - top)
        total = jnp.sum(powers, axis=1, keepdims=True)
        soft = (powers / total).astype(BF16)
        values = values_ref[...].reshape(slots * HD, MOST)
        out_ref[...] = nt(values, soft).astype(BF16).reshape(slots, HD, rows)
        lse_ref[...] = jnp.broadcast_to(top + jnp.log(total), (1, rows, 128))

    return pl.pallas_call(
        kernel,
        grid=(heads,),
        in_specs=[
            pl.BlockSpec((1, rows, table.shape[2]), lambda h: (h, 0, 0)),
            pl.BlockSpec((slots, HD, MOST), lambda h: (0, h, 0)),
        ],
        out_specs=[
            pl.BlockSpec((slots, HD, rows), lambda h: (0, h, 0)),
            pl.BlockSpec((1, rows, 128), lambda h: (h, 0, 0)),
        ],
        out_shape=[
            jax.ShapeDtypeStruct((slots, width, rows), BF16),
            jax.ShapeDtypeStruct((heads, rows, 128), F32),
        ],
        compiler_params=pltpu.CompilerParams(vmem_limit_bytes=VMEM),
        name="random_forward",
    )(table, values_t)


def random_backward(valid, table, lse, values_t, upstream_t):
    heads, rows, columns = table.shape
    slots, width, _ = values_t.shape
    buffers = pl.Buffered(2 if slots <= 16 else 1)

    def kernel(valid_ref, table_ref, lse_ref, values_ref, up_ref, dtable_ref, dvalues_ref):
        soft = jnp.exp(table_ref[0, :, 0:MOST].astype(F32) - lse_ref[0, :, 0:1])
        up = up_ref[...].reshape(slots * HD, rows) * valid_ref[0, 0].astype(BF16)
        values = values_ref[...].reshape(slots * HD, MOST)
        dsoft = tn(up, values)
        weighed = soft * dsoft
        centre = jnp.sum(weighed, axis=1, keepdims=True)
        dtable_ref[0, :, 0:MOST] = weighed - soft * centre
        dtable_ref[0, :, MOST:columns] = jnp.zeros((rows, columns - MOST), F32)
        dvalues_ref[...] = nn(up, soft.astype(BF16)).astype(BF16).reshape(slots, HD, MOST)

    return pl.pallas_call(
        kernel,
        grid=(heads,),
        in_specs=[
            pl.BlockSpec(memory_space=pltpu.SMEM),
            pl.BlockSpec((1, rows, columns), lambda h: (h, 0, 0)),
            pl.BlockSpec((1, rows, 128), lambda h: (h, 0, 0)),
            pl.BlockSpec((slots, HD, MOST), lambda h: (0, h, 0), pipeline_mode=buffers),
            pl.BlockSpec((slots, HD, rows), lambda h: (0, h, 0)),
        ],
        out_specs=[
            pl.BlockSpec((1, rows, columns), lambda h: (h, 0, 0)),
            pl.BlockSpec((slots, HD, MOST), lambda h: (0, h, 0)),
        ],
        out_shape=[
            jax.ShapeDtypeStruct((heads, rows, columns), F32),
            jax.ShapeDtypeStruct((slots, width, MOST), BF16),
        ],
        compiler_params=pltpu.CompilerParams(vmem_limit_bytes=VMEM),
        name="random_backward",
    )(valid, table, lse, values_t, upstream_t)


def short_forward(first, corner, values_t):
    heads, size, _ = corner.shape
    width = values_t.shape[0]

    def kernel(first_ref, corner_ref, values_ref, out_ref):
        early, inside, shift, rows = small_masks(first_ref[0, 0], size)
        for head in range(heads):
            span = slice(head * HD, (head + 1) * HD)
            soft = by_token(masked_soft(nn(rows, corner_ref[head]), inside), early, shift)
            out_ref[span, :] = nt(values_ref[span, :], soft).astype(BF16)

    return pl.pallas_call(
        kernel,
        in_specs=[
            pl.BlockSpec(memory_space=pltpu.SMEM),
            pl.BlockSpec(memory_space=pltpu.VMEM),
            pl.BlockSpec(memory_space=pltpu.VMEM),
        ],
        out_specs=pl.BlockSpec(memory_space=pltpu.VMEM),
        out_shape=jax.ShapeDtypeStruct((width, size), BF16),
        name="short_forward",
    )(first, corner, values_t)


def short_backward(first, corner, values_t, upstream_t):
    heads, size, _ = corner.shape
    width = values_t.shape[0]

    def kernel(first_ref, corner_ref, values_ref, up_ref, dcorner_ref, dvalues_ref):
        early, inside, shift, rows = small_masks(first_ref[0, 0], size)
        for head in range(heads):
            span = slice(head * HD, (head + 1) * HD)
            soft = masked_soft(nn(rows, corner_ref[head]), inside)
            here, up = values_ref[span, :], up_ref[span, :]
            moved = nt(here, shift).astype(BF16)
            dsoft = jnp.where(early, tn(up, here), tn(up, moved))
            dvalues_ref[span, :] = nn(up, by_token(soft, early, shift)).astype(BF16)
            centre = jnp.sum(soft * dsoft, axis=1, keepdims=True)
            dscores = (soft * (dsoft - centre)).astype(BF16)
            dcorner_ref[head] = tn(rows, dscores).astype(BF16)

    return pl.pallas_call(
        kernel,
        in_specs=[
            pl.BlockSpec(memory_space=pltpu.SMEM),
            pl.BlockSpec(memory_space=pltpu.VMEM),
            pl.BlockSpec(memory_space=pltpu.VMEM),
            pl.BlockSpec(memory_space=pltpu.VMEM),
        ],
        out_specs=[
            pl.BlockSpec(memory_space=pltpu.VMEM),
            pl.BlockSpec(memory_space=pltpu.VMEM),
        ],
        out_shape=[
            jax.ShapeDtypeStruct((heads, size, size), BF16),
            jax.ShapeDtypeStruct((width, size), BF16),
        ],
        name="short_backward",
    )(first, corner, values_t, upstream_t)


def table_grad(table, lse, values_t, upstream_t, corner):
    heads, rows, columns = table.shape
    slots, size = values_t.shape[0], corner.shape[2]

    def kernel(table_ref, lse_ref, values_ref, up_ref, corner_ref, out_ref):
        weights = jnp.exp(table_ref[0, :, 0:MOST].astype(F32) - lse_ref[0, :, 0:1])
        up = up_ref[...].reshape(slots * HD, rows)
        dsoft = tn(up, values_ref[...].reshape(slots * HD, MOST))
        weighed = weights * dsoft
        centre = jnp.sum(weighed, axis=1, keepdims=True)
        out_ref[0, :, 0:MOST] = weighed - weights * centre
        out_ref[0, :, MOST:columns] = jnp.zeros((rows, columns - MOST), F32)
        out_ref[0, :, 0:size] += corner_ref[0].astype(F32)

    return pl.pallas_call(
        kernel,
        grid=(heads,),
        in_specs=[
            pl.BlockSpec((1, rows, columns), lambda h: (h, 0, 0)),
            pl.BlockSpec((1, rows, 128), lambda h: (h, 0, 0)),
            pl.BlockSpec((slots, HD, MOST), lambda h: (0, h, 0)),
            pl.BlockSpec((slots, HD, rows), lambda h: (0, h, 0)),
            pl.BlockSpec((1, rows, size), lambda h: (h, 0, 0)),
        ],
        out_specs=pl.BlockSpec((1, rows, columns), lambda h: (h, 0, 0)),
        out_shape=jax.ShapeDtypeStruct((heads, rows, columns), F32),
        compiler_params=pltpu.CompilerParams(vmem_limit_bytes=VMEM),
        name="table_grad",
    )(table, lse, values_t, upstream_t, corner)


EPS = 1e-06
CURVE = 0.7978845608028654


def root(x):
    return lax.rsqrt(jnp.mean(x * x, axis=-1, keepdims=True) + EPS)


def normalize(x, gain):
    return (x * root(x) * gain).astype(BF16)


def normalize_back(x, gain, grad):
    scale = root(x)
    weighed = grad * gain
    pull = jnp.mean(weighed * x, axis=-1, keepdims=True)
    return scale * weighed - x * (scale * scale * scale * pull), jnp.sum(grad * x * scale, axis=0, keepdims=True)


def gelu(x):
    square = x * x
    bend = jnp.tanh(CURVE * x * (1.0 + 0.044715 * square))
    half = 0.5 * (1.0 + bend)
    slope = half + 0.5 * x * (1.0 - bend * bend) * (CURVE * (1.0 + 3 * 0.044715 * square))
    return x * half, slope


def begin(inputs, weights, gain):
    total, model = inputs.shape
    width = weights.shape[1] // 2
    tile = 256

    def kernel(x_ref, w_ref, gain_ref, normed_ref, values_ref, values_t_ref, acts_ref, acts_t_ref, slope_ref):
        normed = normalize(x_ref[...].astype(F32), gain_ref[0:1, :])
        normed_ref[...] = normed
        both = nn(normed, w_ref[...])
        acts, slope = gelu(both[:, width:])
        values = both[:, :width]
        values_ref[...] = values.astype(BF16)
        values_t_ref[...] = values.T.astype(BF16)
        acts_ref[...] = acts.astype(BF16)
        acts_t_ref[...] = acts.T.astype(BF16)
        slope_ref[...] = slope.astype(BF16)

    rows = lambda i: (i, 0)
    columns = lambda i: (0, i)
    return pl.pallas_call(
        kernel,
        grid=(total // tile,),
        in_specs=[
            pl.BlockSpec((tile, model), rows),
            pl.BlockSpec(weights.shape, lambda i: (0, 0)),
            pl.BlockSpec(gain.shape, lambda i: (0, 0)),
        ],
        out_specs=[
            pl.BlockSpec((tile, model), rows),
            pl.BlockSpec((tile, width), rows),
            pl.BlockSpec((width, tile), columns),
            pl.BlockSpec((tile, width), rows),
            pl.BlockSpec((width, tile), columns),
            pl.BlockSpec((tile, width), rows),
        ],
        out_shape=[
            jax.ShapeDtypeStruct((total, model), BF16),
            jax.ShapeDtypeStruct((total, width), BF16),
            jax.ShapeDtypeStruct((width, total), BF16),
            jax.ShapeDtypeStruct((total, width), BF16),
            jax.ShapeDtypeStruct((width, total), BF16),
            jax.ShapeDtypeStruct((total, width), BF16),
        ],
        compiler_params=pltpu.CompilerParams(vmem_limit_bytes=VMEM),
        cost_estimate=pl.CostEstimate(flops=2 * total * model * 2 * width, bytes_accessed=6 * total * model, transcendentals=0),
        name="begin",
    )(inputs, weights, gain)


def by_rows(mixed):
    if len(mixed.shape) == 2:
        return mixed.T
    return jnp.concatenate([mixed[c].T for c in range(mixed.shape[0])], axis=0)


def ends(x, mixed, flat, weights, width, gain, row, more):
    share, model = x.shape
    groups = weights.shape[0]
    hidden = (weights.shape[2] - 2 * width) // 2

    def kernel(*refs):
        x_ref, mixed_ref, gain_ref, up_ref, down_ref, side_ref = refs[:6]
        refs = refs[6:]
        middle_ref, normed_ref, hidden_ref, slope_ref, y_ref = refs[:5]
        acc = refs[-1]
        group = pl.program_id(0)

        @pl.when(group == 0)
        def _():
            total = x_ref[...].astype(F32)
            for j in range(groups):
                block = mixed_ref[j] if flat else by_rows(mixed_ref[j])
                total += nt(block, side_ref[j, :, 0:width])
            middle_ref[...] = total
            normed_ref[...] = normalize(total, gain_ref[row : row + 1, :])
            acc[...] = total

        value_of, slope = gelu(nn(normed_ref[...], up_ref[0]))
        low = value_of.astype(BF16)
        hidden_ref[0] = low
        slope_ref[0] = slope.astype(BF16)
        acc[...] += nt(low, down_ref[0])

        @pl.when(group == groups - 1)
        def _():
            y = acc[...]
            y_ref[...] = y.astype(y_ref.dtype)
            if more:
                normed = normalize(y, gain_ref[row + 1 : row + 2, :])
                refs[5][...] = normed
                for j in range(groups):
                    refs[6][j] = nn(normed, side_ref[j, :, width : 2 * width]).T.astype(BF16)

    whole2, whole3 = (lambda g: (0, 0)), (lambda g: (0, 0, 0))
    in_specs = [
        pl.BlockSpec(x.shape, whole2),
        pl.BlockSpec(mixed.shape, lambda g: (0,) * mixed.ndim),
        pl.BlockSpec(gain.shape, whole2),
        pl.BlockSpec((1, model, hidden), lambda g: (g, 0, 0)),
        pl.BlockSpec((1, model, hidden), lambda g: (g, 0, 1)),
        pl.BlockSpec((groups, model, 2 * width), lambda g: (0, 0, hidden // width)),
    ]
    out_specs = [
        pl.BlockSpec((share, model), whole2),
        pl.BlockSpec((share, model), whole2),
        pl.BlockSpec((1, share, hidden), lambda g: (g, 0, 0)),
        pl.BlockSpec((1, share, hidden), lambda g: (g, 0, 0)),
        pl.BlockSpec((share, model), whole2),
    ]
    out_shape = [
        jax.ShapeDtypeStruct((share, model), F32),
        jax.ShapeDtypeStruct((share, model), BF16),
        jax.ShapeDtypeStruct((groups, share, hidden), BF16),
        jax.ShapeDtypeStruct((groups, share, hidden), BF16),
        jax.ShapeDtypeStruct((share, model), F32 if more else BF16),
    ]
    if more:
        out_specs += [pl.BlockSpec((share, model), whole2), pl.BlockSpec((groups, width, share), whole3)]
        out_shape += [
            jax.ShapeDtypeStruct((share, model), BF16),
            jax.ShapeDtypeStruct((groups, width, share), BF16),
        ]
    return pl.pallas_call(
        kernel,
        grid=(groups,),
        in_specs=in_specs,
        out_specs=out_specs,
        out_shape=out_shape,
        scratch_shapes=[pltpu.VMEM((share, model), F32)],
        compiler_params=pltpu.CompilerParams(vmem_limit_bytes=VMEM),
        cost_estimate=pl.CostEstimate(flops=4 * share * model * groups * hidden, bytes_accessed=4 * groups * model * hidden, transcendentals=0),
        name="ends",
    )(x, mixed, gain, weights, weights, weights)


def ends_back(grad, mixed, flat, weights, width, gain, row, record, after=None):
    middle, normed, hid, slope = record
    share, model = middle.shape
    groups = weights.shape[0]
    hidden = hid.shape[2]
    more = after is not None
    columns = 2 * hidden + (2 if more else 1) * width

    def kernel(*refs):
        grad_ref, mixed_ref, gain_ref, up_ref, down_ref, side_ref, middle_ref, normed_ref, hidden_ref, slope_ref = refs[:10]
        refs = refs[10:]
        if more:
            next_ref, next_normed_ref, dvalues_ref = refs[:3]
            refs = refs[3:]
        grads_ref, dmiddle_ref, dmixed_ref, dgain_ref, total, low, low_t, normed_t, dnormed = refs
        group = pl.program_id(0)

        @pl.when(group == 0)
        def _():
            g = grad_ref[...].astype(F32)
            dgain_ref[...] = jnp.zeros_like(dgain_ref)
            if more:
                pull = jnp.zeros((share, model), F32)
                next_t = next_normed_ref[...].T
                for j in range(groups):
                    dvalues = dvalues_ref[j].T
                    grads_ref[j, :, 2 * hidden + width : columns] = nn(next_t, dvalues).astype(BF16)
                    pull += nt(dvalues, side_ref[j, :, width : 2 * width])
                dx, dg = normalize_back(next_ref[...], gain_ref[row + 1 : row + 2, :], pull)
                g += dx
                dgain_ref[1:2, :] = dg
            total[...] = g
            low[...] = g.astype(BF16)
            low_t[...] = g.astype(BF16).T
            normed_t[...] = normed_ref[...].T
            dnormed[...] = jnp.zeros_like(dnormed)

        dpre = (slope_ref[0].astype(F32) * nn(low[...], down_ref[0])).astype(BF16)
        grads_ref[group, :, 0:hidden] = nn(normed_t[...], dpre).astype(BF16)
        grads_ref[group, :, hidden : 2 * hidden] = nn(low_t[...], hidden_ref[0]).astype(BF16)
        dnormed[...] += nt(dpre, up_ref[0])

        @pl.when(group == groups - 1)
        def _():
            dx, dg = normalize_back(middle_ref[...], gain_ref[row : row + 1, :], dnormed[...])
            dmiddle = total[...] + dx
            dgain_ref[0:1, :] = dg
            dmiddle_ref[...] = dmiddle
            down = dmiddle.astype(BF16)
            down_t = down.T
            for j in range(groups):
                block = mixed_ref[j] if flat else by_rows(mixed_ref[j])
                grads_ref[j, :, 2 * hidden : 2 * hidden + width] = nn(down_t, block).astype(BF16)
                dmixed = nn(down, side_ref[j, :, 0:width])
                if flat:
                    dmixed_ref[j] = dmixed.astype(BF16)
                elif len(mixed.shape) == 3:
                    dmixed_ref[j] = dmixed.T.astype(BF16)
                else:
                    rows = mixed.shape[3]
                    for c in range(mixed.shape[1]):
                        dmixed_ref[j, c] = dmixed[c * rows : (c + 1) * rows].T.astype(BF16)

    whole2, whole3 = (lambda g: (0, 0)), (lambda g: (0, 0, 0))
    whole = lambda a: pl.BlockSpec(a.shape, lambda g: (0,) * a.ndim)
    in_specs = [
        whole(grad),
        whole(mixed),
        whole(gain),
        pl.BlockSpec((1, model, hidden), lambda g: (g, 0, 0)),
        pl.BlockSpec((1, model, hidden), lambda g: (g, 0, 1)),
        pl.BlockSpec((groups, model, 2 * width), lambda g: (0, 0, hidden // width)),
        whole(middle),
        whole(normed),
        pl.BlockSpec((1, share, hidden), lambda g: (g, 0, 0)),
        pl.BlockSpec((1, share, hidden), lambda g: (g, 0, 0)),
    ]
    operands = [grad, mixed, gain, weights, weights, weights, middle, normed, hid, slope]
    if more:
        in_specs += [whole(a) for a in after]
        operands += list(after)
    out_specs = [
        pl.BlockSpec(memory_space=pltpu.VMEM),
        pl.BlockSpec((share, model), whole2),
        whole(mixed),
        pl.BlockSpec((8, model), whole2),
    ]
    out_shape = [
        jax.ShapeDtypeStruct((groups, model, columns), BF16),
        jax.ShapeDtypeStruct((share, model), F32),
        jax.ShapeDtypeStruct(mixed.shape, BF16),
        jax.ShapeDtypeStruct((8, model), F32),
    ]
    scratch = [
        pltpu.VMEM((share, model), F32),
        pltpu.VMEM((share, model), BF16),
        pltpu.VMEM((model, share), BF16),
        pltpu.VMEM((model, share), BF16),
        pltpu.VMEM((share, model), F32),
    ]
    return pl.pallas_call(
        kernel,
        grid=(groups,),
        in_specs=in_specs,
        out_specs=out_specs,
        out_shape=out_shape,
        scratch_shapes=scratch,
        compiler_params=pltpu.CompilerParams(vmem_limit_bytes=VMEM),
        cost_estimate=pl.CostEstimate(flops=8 * share * model * groups * hidden, bytes_accessed=8 * groups * model * hidden, transcendentals=0),
        name="ends_back",
    )(*operands)


def finish(back, weights, first, x, gain, dmiddle, gains, n, n_mp):
    groups, share, both = back.shape
    model, width = first.shape[1:]
    spot = weights.shape[2] // (2 * width) - 1
    pairs = n_mp // 2
    chunks = 4
    tall = share // chunks

    def kernel(back_ref, side_ref, first_ref, x_ref, gain_ref, dmiddle_ref, gains_ref, all_ref, sum_ref, out, here, one,
               two, far_send, far_recv, near_send, near_recv, on_send, on_recv, own_sem, g_send, g_recv, h_send, h_recv):
        me, place = lax.axis_index("mp"), lax.axis_index("dp")
        pair, core = me // 2, lax.rem(me, 2)
        twin = pair * 2 + 1 - core
        greet([("dp", n), ("mp", n_mp)])

        def rows(c):
            return pl.ds(c * tall, tall)

        def far(step, c):
            to = lax.rem(pair + step, pairs) * 2 + core
            return remote(
                out.at[rows(c)], all_ref.at[me, rows(c)], far_send.at[step, c], far_recv.at[step, c], "mp", to
            )

        def near(c):
            return remote(out.at[rows(c)], all_ref.at[me, rows(c)], near_send.at[c], near_recv.at[c], "mp", twin)

        def onward(step, c):
            source = lax.rem(pair + pairs - step, pairs) * 2 + core
            block = all_ref.at[source, rows(c)]
            return remote(block, block, on_send.at[step, c], on_recv.at[step, c], "mp", twin)

        total = jnp.zeros((1, model), F32)
        for c in range(chunks):
            span = slice(c * tall, (c + 1) * tall)
            pull = jnp.zeros((tall, model), F32)
            for j in range(groups):
                pull += nt(back_ref[j, span, 0:width], side_ref[j, :, width : 2 * width])
                pull += nt(back_ref[j, span, width:both], first_ref[j])
            dx, dg = normalize_back(x_ref[span, :].astype(F32), gain_ref[0:1, :], pull)
            out[span, :] = (dmiddle_ref[span, :] + dx).astype(BF16)
            total += dg
            for step in range(1, pairs):
                far(step, c).start()
            near(c).start()
        own = pltpu.make_async_copy(out, all_ref.at[me], own_sem)
        own.start()
        here[...] = gains_ref[...]
        here[0:1, :] = total
        one[me] = here[...]
        firsts = []
        for step in range(1, n_mp):
            to = lax.rem(me + step, n_mp)
            firsts.append(remote(here, one.at[me], g_send.at[step], g_recv.at[step], "mp", to))
            firsts[-1].start()
        for copy in firsts:
            copy.wait()
        total = one[0]
        for j in range(1, n_mp):
            total += one[j]
        two[place] = total

        def spread(step, there):
            return remote(two.at[place], two.at[there], h_send.at[step], h_recv.at[step], "dp", lax.rem(place + step, n))

        @pl.loop(1, n)
        def _(step):
            spread(step, place).start()

        for c in range(chunks):
            for step in range(1, pairs):
                far(step, c).wait_recv()
                onward(step, c).start()

        @pl.loop(1, n)
        def _(step):
            spread(step, place).wait_send()
            spread(step, lax.rem(place + n - step, n)).wait_recv()

        total = two[0]
        for j in range(1, n):
            total += two[j]
        sum_ref[...] = total
        for c in range(chunks):
            near(c).wait()
            for step in range(1, pairs):
                far(step, c).wait_send()
                onward(step, c).wait()
        own.wait()

    return pl.pallas_call(
        kernel,
        grid=(1,),
        in_specs=[
            pl.BlockSpec(back.shape, lambda i: (0, 0, 0)),
            pl.BlockSpec((groups, model, 2 * width), lambda i: (0, 0, spot)),
            pl.BlockSpec(first.shape, lambda i: (0, 0, 0)),
            pl.BlockSpec(x.shape, lambda i: (0, 0)),
            pl.BlockSpec(gain.shape, lambda i: (0, 0)),
            pl.BlockSpec(dmiddle.shape, lambda i: (0, 0)),
            pl.BlockSpec(gains.shape, lambda i: (0, 0)),
        ],
        out_specs=[ANY, pl.BlockSpec(gains.shape, lambda i: (0, 0))],
        out_shape=[
            jax.ShapeDtypeStruct((n_mp, share, model), BF16),
            jax.ShapeDtypeStruct(gains.shape, F32),
        ],
        scratch_shapes=[
            pltpu.VMEM((share, model), BF16),
            pltpu.VMEM(gains.shape, F32),
            pltpu.VMEM((n_mp,) + gains.shape, F32),
            pltpu.VMEM((n,) + gains.shape, F32),
            DMA((pairs, chunks)),
            DMA((pairs, chunks)),
            DMA((chunks,)),
            DMA((chunks,)),
            DMA((pairs, chunks)),
            DMA((pairs, chunks)),
            DMA,
            DMA((n_mp,)),
            DMA((n_mp,)),
            DMA((n,)),
            DMA((n,)),
        ],
        compiler_params=comm_params(4),
        name="finish",
    )(back, weights, first, x, gain, dmiddle, gains)


def per_device(
    n_dp,
    n_mp,
    tokens,
    lengths,
    norm_gain,
    w_value,
    w_out,
    w_up,
    w_down,
    synth_first,
    synth_second,
    random_table,
    cotangent,
):
    both = ("mp", "dp")
    place, rank = lax.axis_index("dp"), lax.axis_index("mp")
    total, model = tokens.shape
    share = total // n_mp
    size = total - MOST
    depth, width = w_value.shape[1], w_value.shape[2]
    hidden = w_up.shape[2]
    heads, rows, columns = random_table.shape
    near = rows == size and share % rows == 0 and n_dp in (2, 4, 6, 8)

    item_lengths = lengths[0]
    longest = jnp.argmax(item_lengths)
    start = (jnp.cumsum(item_lengths) - item_lengths)[longest]
    first = item_lengths[(longest + 1) % item_lengths.shape[0]].astype(jnp.int32).reshape(1, 1)

    def turned(x, by):
        return lax.dynamic_slice_in_dim(jnp.concatenate([x, x]), by, total)

    def mine(x):
        return lax.dynamic_slice_in_dim(x, rank * share, share)

    gains = jnp.pad(norm_gain.reshape(4, depth).T, ((0, 0), (0, 124)))
    pack = jnp.concatenate([w_value[0], synth_first, gains], axis=1)
    table = synth_second.reshape(width, -1)
    corner = random_table[:, :, :size]
    if near:
        pack, table, corner = gather_weights([pack, table], corner.reshape(n_dp, -1, size), n_dp)
    else:
        begins = jnp.minimum(place * rows, size - rows)
        inside = (place * rows < size).astype(BF16)
        corner = lax.dynamic_update_slice(jnp.zeros((heads, size, size), BF16), corner * inside, (0, begins, 0))
        corner = lax.psum(corner, "dp")
        pack, table = lax.all_gather(pack, "dp"), lax.all_gather(table, "dp")
        table = table.transpose(1, 0, 2).reshape(width, total // size, size).transpose(1, 0, 2)
    pack = pack.reshape(model, -1)
    gain = jnp.pad(pack[:, 2 * width : 2 * width + 4].T.astype(F32), ((0, 4), (0, 0)))

    def whole(parts):
        joined = lax.all_gather(jnp.concatenate(parts, axis=1), both)
        return joined.reshape(n_mp, model, -1)

    weights_one = whole([w_up[0], w_down[0].T, w_out[0].T, w_value[1]])
    weights_two = [w_up[1], w_down[1].T, w_out[1].T, w_value[0]]

    inputs = turned(tokens, start)
    normed_one, values, values_t, acts, acts_t, slope = begin(inputs, pack[:, : 2 * width], gain)
    mixed, lse = dense_forward(first, acts, values, table)
    mixed = mixed.reshape(n_mp, share, width)
    if near:
        mixed_one, corner = swap(mixed, n_mp, 5, part=corner, n_dp=n_dp)
        corner = corner.reshape(heads, size, size)
    else:
        mixed_one = swap(mixed, n_mp, 5)
    inputs = mine(inputs)
    *record_one, between, normed_two, parts = ends(
        inputs, mixed_one, True, weights_one, width, gain, 1, True
    )

    if near:
        values_all, mixed_two, short_t, table_lse, weights_two = table_forward(
            first, random_table, corner, parts, jnp.concatenate(weights_two, axis=1), n_dp, n_mp
        )
        weights_two = weights_two.reshape(n_mp, model, -1)
    else:
        weights_two = whole(weights_two)
        values_two = swap(parts, n_mp, 6, lanes_out=True)
        short_t = values_two[:, MOST:]
        values_all = lax.all_gather(values_two[:, :MOST], "dp")
        mixed, table_lse = random_forward(random_table, values_all)
        mixed = lax.all_to_all(mixed, "dp", 0, 0, tiled=True).transpose(1, 0, 2).reshape(width, total)
        mixed = jnp.concatenate([mixed[:, :MOST], short_forward(first, corner, short_t)], axis=1)
        mixed_two = swap(mixed, n_mp, 7, lanes_in=True)
    *record_two, result = ends(between, mixed_two, False, weights_two, width, gain, 3, False)
    early_first, _ = lax.optimization_barrier((synth_first, mixed_two))
    first_all = whole([early_first])

    grads_two, dmiddle, parts, dgain_two = ends_back(
        mine(turned(cotangent, start)), mixed_two, False, weights_two, width, gain, 3, record_two
    )

    def scattered(grads, axes):
        grads = grads.reshape(-1, depth, grads.shape[-1])
        return lax.psum_scatter(grads, axes, scatter_dimension=0).astype(F32)

    if near:
        rows_upstream, dvalues, dcorner, grads_two = table_backward(
            first, random_table, corner, table_lse, short_t, parts, grads_two, n_dp, n_mp
        )
    else:
        upstream = swap(parts, n_mp, 8, lanes_out=True)
        dcorner, dshort = short_backward(first, corner, short_t, upstream[:, MOST:])
        dcorner = lax.dynamic_slice_in_dim(lax.psum(dcorner, "dp"), begins, rows, axis=1) * inside
        upstream = upstream.reshape(width, n_dp, rows).transpose(1, 0, 2)
        upstream = lax.all_to_all(upstream, "dp", 0, 0, tiled=True)
        valid = (place * rows < MOST).astype(F32).reshape(1, 1)
        dtable, dvalues = random_backward(valid, random_table, table_lse, values_all, upstream)
        dvalues = lax.psum_scatter(dvalues, "dp", scatter_dimension=0)
        dvalues = swap(jnp.concatenate([dvalues, dshort], axis=1), n_mp, 9, lanes_in=True)
        result = lax.all_gather(result, "mp")
        grads_two = scattered(grads_two, both)

    grads_one, dmiddle, parts, dgain_one = ends_back(
        dmiddle, mixed_one, True, weights_one, width, gain, 1, record_one, (between, normed_two, dvalues)
    )
    grads_one = scattered(grads_one, both)
    upstream = swap(parts, n_mp, 10).reshape(total, width)
    back_one = partial(dense_backward, first, acts, acts_t, values_t, upstream, table, lse, slope, normed_one)
    if near:
        back, entry_grad, second_grad, grads_two, result = back_one(
            grads_two.reshape(n_dp, depth, -1), result, n_dp, n_mp
        )
    else:
        back, entry_grad, second_grad = back_one()
    result = turned(result.reshape(total, model), total - start)
    back = back.reshape(n_mp, share, 2 * width)
    entry_grad = entry_grad.reshape(n_dp, depth, 2 * width)
    if near:
        back, entry_grad, second_grad, dcorner = last_exchange(
            back, [entry_grad, second_grad, dcorner.reshape(n_dp, -1, size)], n_dp, n_mp
        )
        dcorner = dcorner.reshape(heads, size, size)
    else:
        back = swap(back, n_mp, 11)
        entry_grad = lax.psum_scatter(entry_grad, "dp", scatter_dimension=0).astype(F32)
        second_grad = second_grad.transpose(1, 0, 2).reshape(width, n_dp, -1).transpose(1, 0, 2)
        second_grad = lax.psum_scatter(second_grad, "dp", scatter_dimension=0).astype(F32)
    gain_grad = jnp.concatenate([dgain_one[:1], dgain_one[:2], dgain_two[:1], jnp.zeros((4, model), F32)])
    input_grad, gain_grad = finish(back, weights_two, first_all, inputs, gain, dmiddle, gain_grad, n_dp, n_mp)
    input_grad = turned(input_grad.reshape(total, model), total - start)
    if near:
        upstream_last, _ = lax.optimization_barrier((rows_upstream, gain_grad))
        dtable = table_grad(random_table, table_lse, values_all, upstream_last, dcorner)
    else:
        dtable = dtable.at[:, :, :size].add(dcorner.astype(F32))

    gain_grad = lax.dynamic_slice_in_dim(gain_grad[:4], place * depth, depth, axis=1)
    out_at = slice(2 * hidden, 2 * hidden + width)
    return (
        result,
        input_grad,
        gain_grad.reshape(2, 2, depth),
        jnp.stack([entry_grad[:, :width], grads_one[:, 2 * hidden + width :]]),
        jnp.stack([grads_one[:, out_at].T, grads_two[:, out_at].T]),
        jnp.stack([grads_one[:, :hidden], grads_two[:, :hidden]]),
        jnp.stack([grads_one[:, hidden : 2 * hidden].T, grads_two[:, hidden : 2 * hidden].T]),
        entry_grad[:, width:],
        second_grad.reshape(heads, HD, -1),
        dtable,
    )


def solution(mesh):
    in_specs = (
        P("dp", None),
        P("dp", None),
        P(None, None, "dp"),
        P(None, "dp", "mp"),
        P(None, "mp", "dp"),
        P(None, "dp", "mp"),
        P(None, "mp", "dp"),
        P("dp", "mp"),
        P("mp", None, "dp"),
        P("mp", "dp", None),
        P("dp", None),
    )
    out_specs = (
        P("dp", None),
        P("dp", None),
        P(None, None, "dp"),
        P(None, "dp", "mp"),
        P(None, "mp", "dp"),
        P(None, "dp", "mp"),
        P(None, "mp", "dp"),
        P("dp", "mp"),
        P("mp", None, "dp"),
        P("mp", "dp", None),
    )
    return jax.shard_map(
        partial(per_device, mesh.shape["dp"], mesh.shape["mp"]),
        mesh=mesh,
        in_specs=in_specs,
        out_specs=out_specs,
        check_vma=False,
    )
```

```python
from functools import partial

import jax
import jax.numpy as jnp
from jax import lax
from jax.experimental import pallas as pl
from jax.experimental.pallas import tpu as pltpu
from jax.sharding import PartitionSpec as P

F32, BF16 = jnp.float32, jnp.bfloat16
HD = 64
MOST = 1792
TILE = 256
VMEM = 58 * 1024 * 1024


MESH = pl.DeviceIdType.MESH
ANY = pl.BlockSpec(memory_space=pl.ANY)
INTO = pl.BlockSpec(memory_space=pltpu.VMEM)
SCALAR = pl.BlockSpec(memory_space=pltpu.SMEM)
DMA = pltpu.SemaphoreType.DMA


def remote(source, target, send, recv, axis, index):
    return pltpu.make_async_remote_copy(
        src_ref=source, dst_ref=target, send_sem=send, recv_sem=recv, device_id={axis: index}, device_id_type=MESH
    )


def greet(groups):
    barrier = pltpu.get_barrier_semaphore()
    for axis, size in groups:
        me = lax.axis_index(axis)
        for step in range(1, size):
            pl.semaphore_signal(
                barrier, inc=1, device_id={axis: lax.rem(me + step, size)}, device_id_type=MESH
            )
    pl.semaphore_wait(barrier, sum(size - 1 for _, size in groups))


def greet_all(n, n_mp):
    barrier = pltpu.get_barrier_semaphore()
    me = lax.axis_index("dp") * n_mp + lax.axis_index("mp")

    @pl.loop(1, n * n_mp)
    def _(step):
        there = lax.rem(me + step, n * n_mp)
        where = {"dp": there // n_mp, "mp": lax.rem(there, n_mp)}
        pl.semaphore_signal(barrier, inc=1, device_id=where, device_id_type=MESH)

    pl.semaphore_wait(barrier, n * n_mp - 1)


def remote_to(source, target, send, recv, place, rank):
    return pltpu.make_async_remote_copy(
        src_ref=source,
        dst_ref=target,
        send_sem=send,
        recv_sem=recv,
        device_id={"dp": place, "mp": rank},
        device_id_type=MESH,
    )


def comm_params(number):
    return pltpu.CompilerParams(collective_id=number, has_side_effects=True, vmem_limit_bytes=VMEM)


class Line:
    def __init__(self, size):
        self.size, self.length = size, size // 2
        self.place = lax.axis_index("dp")
        self.at, self.side = self.place // 2, lax.rem(self.place, 2)
        self.partner = self.at * 2 + 1 - self.side
        self.right, self.left = self.place + 2, self.place - 2
        self.has_right, self.has_left = self.at + 1 < self.length, self.at > 0


class Gather:
    def __init__(self, line, pieces, use, even=False):
        self.line, self.pieces, self.use = line, pieces, use
        self.even = even and line.length == 4

    def block(self, slots, s, half=None):
        if half is None:
            return slots.at[s]
        rows = slots.shape[1] // 2
        return slots.at[s, pl.ds(half * rows, rows)]

    def push(self, piece, s, to, send, fresh=False, half=None, recv=None):
        own, slots = piece[:2]
        target = self.block(slots, s, half)
        remote(own if fresh else target, target, send, piece[4].at[s] if recv is None else recv, "dp", to).start()

    def arrived(self, piece, s, half=None, recv=None):
        target = self.block(piece[1], s, half)
        recv = piece[4].at[s] if recv is None else recv
        remote(target, target, piece[2].at[0], recv, "dp", self.line.partner).wait_recv()

    def sent(self, which, half=None):
        for piece in self.pieces:
            target = self.block(piece[1], 0, half)
            remote(target, target, which(piece), piece[4].at[0], "dp", self.line.partner).wait_send()

    def start(self, piece):
        line = self.line

        @pl.when(line.has_right)
        def _():
            self.push(piece, line.place, line.right, piece[3].at[0, line.at], fresh=True)

        @pl.when(line.has_left)
        def _():
            self.push(piece, line.place, line.left, piece[3].at[1, line.at], fresh=True)

        self.push(piece, line.place, line.partner, piece[2].at[line.at], fresh=True)

    def spared(self, a):
        at = self.line.at
        half = jnp.logical_or(jnp.logical_and(at == 0, a == 3), jnp.logical_and(at == 3, a == 0))
        none = jnp.logical_or(jnp.logical_and(at == 1, a == 0), jnp.logical_and(at == 2, a == 3))
        return jnp.logical_not(jnp.logical_or(half, none)), half

    def arrive(self, a, way):
        line = self.line
        s = a * 2 + line.side
        on, to = ((line.has_right, line.right), (line.has_left, line.left))[way]
        for piece in self.pieces:
            self.arrived(piece, s)

            @pl.when(on)
            def _():
                self.push(piece, s, to, piece[3].at[way, a])

            if self.even:
                whole, half = self.spared(a)

                @pl.when(whole)
                def _():
                    self.push(piece, s, line.partner, piece[2].at[a])

                @pl.when(half)
                def _():
                    self.push(piece, s, line.partner, piece[2].at[a], half=0)
            else:
                self.push(piece, s, line.partner, piece[2].at[a])
            piece[6](s)

    def crossed(self, a):
        line = self.line
        at = line.at
        s = a * 2 + 1 - line.side
        for piece in self.pieces:
            if self.even:
                _, half = self.spared(a)
                send, recv = piece[5].at[0], piece[5].at[1]

                @pl.when(half)
                def _():
                    self.arrived(piece, s, half=0)
                    self.arrived(piece, s, half=1, recv=recv)

                @pl.when(jnp.logical_not(half))
                def _():
                    self.arrived(piece, s)

                @pl.when(jnp.logical_and(at == 0, a == 0))
                def _():
                    self.push(piece, s, line.right, send)

                @pl.when(jnp.logical_and(at == 3, a == 3))
                def _():
                    self.push(piece, s, line.left, send)

                @pl.when(jnp.logical_and(at == 1, a == 3))
                def _():
                    self.push(piece, s, line.left, send, half=1, recv=recv)

                @pl.when(jnp.logical_and(at == 2, a == 0))
                def _():
                    self.push(piece, s, line.right, send, half=1, recv=recv)
            else:
                self.arrived(piece, s)
            piece[6](s)
        self.use(s)

    def step(self, k):
        line = self.line
        low, high = line.at - k, line.at + k

        @pl.when(low >= 0)
        def _():
            self.arrive(low, 0)

        @pl.when(high < line.length)
        def _():
            self.arrive(high, 1)

        @pl.when(low >= 0)
        def _():
            self.use(low * 2 + line.side)

        @pl.when(high < line.length)
        def _():
            self.use(high * 2 + line.side)

        @pl.when(low + 1 >= 0)
        def _():
            self.crossed(low + 1)

        @pl.when(jnp.logical_and(k > 1, high - 1 < line.length))
        def _():
            self.crossed(high - 1)

    def end(self):
        line = self.line

        @pl.loop(0, line.length)
        def _(a):
            if self.even:
                whole, half = self.spared(a)

                @pl.when(whole)
                def _():
                    self.sent(lambda piece: piece[2].at[a])

                @pl.when(half)
                def _():
                    self.sent(lambda piece: piece[2].at[a], half=0)
            else:
                self.sent(lambda piece: piece[2].at[a])

            @pl.when(jnp.logical_and(line.has_right, a <= line.at))
            def _():
                self.sent(lambda piece: piece[3].at[0, a])

            @pl.when(jnp.logical_and(line.has_left, a >= line.at))
            def _():
                self.sent(lambda piece: piece[3].at[1, a])

        if self.even:
            outer = jnp.logical_or(line.at == 0, line.at == 3)

            @pl.when(outer)
            def _():
                self.sent(lambda piece: piece[5].at[0])

            @pl.when(jnp.logical_not(outer))
            def _():
                self.sent(lambda piece: piece[5].at[0], half=1)


def line_gather(line, early, late, begin, more, use, even=False):
    gather = Gather(line, early + late, use, even)
    for piece in early:
        gather.start(piece)
    begin()
    for piece in late:
        gather.start(piece)
    more()

    @pl.loop(1, line.length + 1)
    def _(k):
        gather.step(k)

    gather.end()


def nothing(*_):
    pass


def gather_scratch(n):
    return [DMA((n // 2,)), DMA((2, n // 2)), DMA((n,)), DMA((2,))]


class Scatter:
    def __init__(self, line, items):
        self.line, self.items = line, items

    def over_x(self, item, a):
        _, _, x_out, x_in, _, _, _, send_x, recv_x = item[:9]
        return remote(x_out.at[a], x_in.at[a], send_x.at[a], recv_x.at[a], "dp", self.line.partner)

    def over_z(self, item, a, way, to=None):
        z_out, into, send, recv = item[4], item[5 + way], item[9], item[10 + way]
        return remote(z_out.at[a], into.at[a], send.at[a], recv.at[a], "dp", self.line.partner if to is None else to)

    def cross(self):
        length, at, side = self.line.length, self.line.at, self.line.side

        def one(a):
            for item in self.items:
                item[2][a] = item[0](a * 2 + 1 - side).astype(BF16)
                self.over_x(item, a).start()

        @pl.loop(0, length - 1)
        def _(step):
            k = length - 1 - step

            @pl.when(at + k < length)
            def _():
                one(at + k)

            @pl.when(at - k >= 0)
            def _():
                one(at - k)

        one(at)

    def relay(self, k):
        line = self.line
        length, at, side = line.length, line.at, line.side

        def one(a, way, behind, to):
            for item in self.items:
                make, _, _, x_in, z_out = item[:5]
                total = make(a * 2 + side)
                self.over_x(item, a).wait_recv()
                z_out[a] = (total + x_in[a].astype(F32)).astype(BF16)

                @pl.when(behind)
                def _():
                    self.over_z(item, a, way).wait_recv()
                    z_out[a] = (z_out[a].astype(F32) + item[5 + way][a].astype(F32)).astype(BF16)

                self.over_z(item, a, way, to).start()

        @pl.when(at + k < length)
        def _():
            one(at + k, 0, line.has_left, line.right)

        @pl.when(at - k >= 0)
        def _():
            one(at - k, 1, line.has_right, line.left)

    def end(self):
        line = self.line
        at = line.at
        for item in self.items:
            make, out, _, x_in, _, l_in, r_in = item[:7]
            total = make(line.place)
            self.over_x(item, at).wait_recv()
            out[...] = total + x_in[at].astype(F32)

            @pl.when(line.has_left)
            def _():
                self.over_z(item, at, 0).wait_recv()
                out[...] += l_in[at].astype(F32)

            @pl.when(line.has_right)
            def _():
                self.over_z(item, at, 1).wait_recv()
                out[...] += r_in[at].astype(F32)

        @pl.loop(0, line.length)
        def _(a):
            for item in self.items:
                self.over_x(item, a).wait_send()

            @pl.when(a != at)
            def _():
                for item in self.items:
                    self.over_z(item, a, 0).wait_send()


def line_scatter(line, items, middle):
    scatter = Scatter(line, items)
    scatter.cross()
    middle()

    @pl.loop(0, line.length - 1)
    def _(step):
        scatter.relay(line.length - 1 - step)

    scatter.end()


def scatter_scratch(n, shape):
    return [pltpu.VMEM((n // 2,) + shape, BF16)] * 5 + [DMA((n // 2,))] * 5


def gather_weights(arrays, corner, n):
    count = len(arrays)

    def kernel(*refs):
        owns, corner_ref, alls, part_ref = refs[:count], refs[count], refs[count + 1 : 2 * count + 1], refs[2 * count + 1]
        send, recv, kept_sem = refs[2 * count + 2 : 2 * count + 5]
        rest = refs[2 * count + 5 :]
        line = Line(n)
        place = line.place
        greet([("dp", n)])
        kept = [pltpu.make_async_copy(owns[i], alls[i].at[place], kept_sem.at[i]) for i in range(count)]

        def deal(s):
            return remote(corner_ref.at[s], part_ref, send.at[s], recv, "dp", s)

        def begin():
            for copy in kept:
                copy.start()

            @pl.when(place == 0)
            def _():
                @pl.loop(1, n)
                def _(s):
                    deal(s).start()

                part_ref[...] = corner_ref[0]

        pieces = [(owns[i], alls[i], *rest[4 * i : 4 * i + 4], nothing) for i in range(count)]
        line_gather(line, pieces, [], begin, nothing, nothing)
        for copy in kept:
            copy.wait()

        @pl.when(place != 0)
        def _():
            deal(0).wait_recv()

        @pl.when(place == 0)
        def _():
            @pl.loop(1, n)
            def _(s):
                deal(s).wait_send()

    return pl.pallas_call(
        kernel,
        in_specs=[ANY] * count + [INTO],
        out_specs=[ANY] * count + [INTO],
        out_shape=[jax.ShapeDtypeStruct((n,) + a.shape, a.dtype) for a in arrays]
        + [jax.ShapeDtypeStruct(corner.shape[1:], corner.dtype)],
        scratch_shapes=[DMA((n,)), DMA, DMA((count,))] + gather_scratch(n) * count,
        compiler_params=comm_params(0),
        name="gather_weights",
    )(*arrays, corner)


def swap(x, n, number, lanes_in=False, lanes_out=False):
    if lanes_in:
        block = (x.shape[0], x.shape[1] // n)
    else:
        block = x.shape[1:]
    shape = (block[0], n * block[1]) if lanes_out else (n,) + block

    def at(ref, lanes, j):
        if lanes:
            return ref.at[:, pl.ds(pl.multiple_of(j * block[1], block[1]), block[1])]
        return ref.at[j]

    def kernel(x_ref, out_ref, send, recv, own_sem):
        greet([("mp", n)])
        me = lax.axis_index("mp")
        copies = []
        for step in range(1, n):
            peer = lax.rem(me + step, n)
            copies.append(
                remote(at(x_ref, lanes_in, peer), at(out_ref, lanes_out, me), send.at[step], recv.at[step], "mp", peer)
            )
            copies[-1].start()
        own = pltpu.make_async_copy(at(x_ref, lanes_in, me), at(out_ref, lanes_out, me), own_sem)
        own.start()
        own.wait()
        for copy in copies:
            copy.wait()

    return pl.pallas_call(
        kernel,
        in_specs=[ANY],
        out_specs=ANY,
        out_shape=jax.ShapeDtypeStruct(shape, x.dtype),
        scratch_shapes=[DMA((n,)), DMA((n,)), DMA],
        compiler_params=comm_params(number),
        name="swap",
    )(x)


def table_forward(first, table, corner, parts, weights, n, n_mp):
    heads, rows, columns = table.shape
    _, width, share = parts.shape
    tokens = share * n_mp
    size = tokens - MOST
    owners = MOST // rows
    chunks = share // rows
    pairs = n_mp // 2

    def kernel(first_ref, table_ref, corner_ref, parts_ref, weights_ref, values_ref, mixed_ref, short_ref, lse_ref,
               all_ref, own, soft, sums, short_sum, v_send, v_recv, send_x, send_z, recv, more, send_m, recv_m, send_s,
               w_send_x, w_send_z, w_recv, w_more, w_own, far_send, far_recv, near_send, near_recv, on_send, on_recv):
        line = Line(n)
        place, me = line.place, lax.axis_index("mp")
        pair, core = me // 2, lax.rem(me, 2)
        twin = pair * 2 + 1 - core
        owner = place < owners
        greet_all(n, n_mp)

        def lanes(j):
            return own.at[:, pl.ds(pl.multiple_of(j * share, share), share)]

        gets = []
        for step in range(1, n_mp):
            peer = lax.rem(me + step, n_mp)
            gets.append(remote(parts_ref.at[peer], lanes(me), v_send.at[step], v_recv.at[step], "mp", peer))
        keep = pltpu.make_async_copy(weights_ref, all_ref.at[me, place], w_own)

        def prepare():
            offer(place, weights_ref)
            keep.start()
            own[:, pl.ds(pl.multiple_of(me * share, share), share)] = parts_ref[me]
            for copy in gets:
                copy.wait()
            values_ref[place] = own[:, 0:MOST]

        def over(step, s, source):
            to = lax.rem(pair + step, pairs) * 2 + core
            return remote(source, all_ref.at[me, s], far_send.at[step, s], far_recv.at[step, s], "mp", to)

        def across(s, source):
            return remote(source, all_ref.at[me, s], near_send.at[s], near_recv.at[s], "mp", twin)

        def onward(step, s):
            block = lax.rem(pair + pairs - step, pairs) * 2 + core
            return remote(
                all_ref.at[block, s], all_ref.at[block, s], on_send.at[step, s], on_recv.at[step, s], "mp", twin
            )

        def offer(s, source):
            for step in range(1, pairs):
                over(step, s, source).start()
            across(s, source).start()

        def product(s):
            for head in range(heads):
                span = slice(head * HD, (head + 1) * HD)
                sums[s, span, :] = nt(values_ref[s, span, :], soft[head]).astype(BF16)

        here = jnp.logical_and(owner, place // chunks == me)

        def back(s):
            return remote_to(
                sums.at[s],
                mixed_ref.at[me, lax.rem(place, chunks)],
                send_m.at[s],
                recv_m.at[me, lax.rem(place, chunks)],
                s,
                place // chunks,
            )

        def short_back():
            return remote(
                short_sum,
                mixed_ref.at[me, owners % chunks],
                send_s,
                recv_m.at[me, owners % chunks],
                "mp",
                owners // chunks,
            )

        def begin():
            short_ref[...] = own[:, MOST:tokens]
            for head in range(heads):
                scores = table_ref[head, :, 0:MOST].astype(F32)
                top = jnp.max(scores, axis=1, keepdims=True)
                powers = jnp.exp(scores - top)
                total = jnp.sum(powers, axis=1, keepdims=True)
                soft[head] = (powers / total).astype(BF16)
                lse_ref[head] = jnp.broadcast_to(top + jnp.log(total), (rows, 128))
            early, inside, shift, at = small_masks(first_ref[0, 0], size)
            for head in range(heads):
                span = slice(head * HD, (head + 1) * HD)
                weighed = by_token(masked_soft(nn(at, corner_ref[head]), inside), early, shift)
                short_sum[span, :] = nt(own[span, MOST:tokens], weighed).astype(BF16)

            @pl.when(me == owners // chunks)
            def _():
                mixed_ref[me, owners % chunks] = short_sum[...]

            @pl.when(me != owners // chunks)
            def _():
                short_back().start()

            @pl.when(owner)
            def _():
                product(place)

            @pl.when(here)
            def _():
                mixed_ref[me, lax.rem(place, chunks)] = sums[place]

            @pl.when(jnp.logical_and(owner, jnp.logical_not(here)))
            def _():
                back(place).start()

        def use(s):
            @pl.when(owner)
            def _():
                product(s)
                back(s).start()

        for copy in gets:
            copy.start()
        line_gather(
            line,
            [(weights_ref, all_ref.at[me], w_send_x, w_send_z, w_recv, w_more, lambda s: offer(s, all_ref.at[me, s]))],
            [(values_ref.at[place], values_ref, send_x, send_z, recv, more, nothing)],
            prepare,
            begin,
            use,
            even=True,
        )

        @pl.loop(0, n)
        def _(s):
            for step in range(1, pairs):
                over(step, s, weights_ref).wait_recv()
                onward(step, s).start()

        @pl.loop(0, n)
        def _(s):
            @pl.when(jnp.logical_and(owner, jnp.logical_or(s != place, jnp.logical_not(here))))
            def _():
                back(s).wait_send()

            across(s, weights_ref).wait()
            for step in range(1, pairs):
                over(step, s, weights_ref).wait_send()
                onward(step, s).wait()

        @pl.when(me != owners // chunks)
        def _():
            short_back().wait_send()

        for c in range(chunks):
            d = me * chunks + c
            for g in range(n_mp):
                source = jnp.where(d < owners, d, place)

                @pl.when(jnp.logical_not(jnp.logical_and(source == place, g == me)))
                def _():
                    remote(short_sum, mixed_ref.at[g, c], send_s, recv_m.at[g, c], "mp", twin).wait_recv()

        keep.wait()

    return pl.pallas_call(
        kernel,
        in_specs=[SCALAR, INTO, INTO, INTO, ANY],
        out_specs=[INTO, INTO, INTO, INTO, ANY],
        out_shape=[
            jax.ShapeDtypeStruct((n, width, MOST), BF16),
            jax.ShapeDtypeStruct((n_mp, chunks, width, rows), BF16),
            jax.ShapeDtypeStruct((width, size), BF16),
            jax.ShapeDtypeStruct((heads, rows, 128), F32),
            jax.ShapeDtypeStruct((n_mp, n) + weights.shape, BF16),
        ],
        scratch_shapes=[
            pltpu.VMEM((width, tokens), BF16),
            pltpu.VMEM((heads, rows, MOST), BF16),
            pltpu.VMEM((n, width, rows), BF16),
            pltpu.VMEM((width, rows), BF16),
            DMA((n_mp,)),
            DMA((n_mp,)),
            *gather_scratch(n),
            DMA((n,)),
            DMA((n_mp, chunks)),
            DMA,
            *gather_scratch(n),
            DMA,
            DMA((pairs, n)),
            DMA((pairs, n)),
            DMA((n,)),
            DMA((n,)),
            DMA((pairs, n)),
            DMA((pairs, n)),
        ],
        compiler_params=comm_params(1),
        name="table_forward",
    )(first, table, corner, parts, weights)


def spread_mp(x_ref, all_ref, send, recv, own_sem, n):
    me, pairs = lax.axis_index("mp"), n // 2
    pair, core = me // 2, lax.rem(me, 2)
    twin = pair * 2 + 1 - core
    own = pltpu.make_async_copy(x_ref, all_ref.at[me], own_sem)
    near = remote(x_ref, all_ref.at[me], send.at[0], recv.at[0], "mp", twin)

    def far(step):
        to = lax.rem(pair + step, pairs) * 2 + core
        return remote(x_ref, all_ref.at[me], send.at[step], recv.at[step], "mp", to)

    def onward(step):
        source = lax.rem(pair + pairs - step, pairs) * 2 + core
        return remote(
            all_ref.at[source], all_ref.at[source], send.at[pairs + step], recv.at[pairs + step], "mp", twin
        )

    def start():
        for step in range(1, pairs):
            far(step).start()
        near.start()
        own.start()

    def relay():
        for step in range(1, pairs):
            far(step).wait_recv()
            onward(step).start()

    def end():
        for step in range(1, pairs):
            far(step).wait_send()
            onward(step).wait()
        near.wait()
        own.wait()

    return start, relay, end


def blend_mp(x_ref, out_refs, kept, twins, others, local, near_send, near_recv, far_send, far_recv, n):
    me, pairs = lax.axis_index("mp"), n // 2
    pair, core = me // 2, lax.rem(me, 2)
    twin = pair * 2 + 1 - core
    rows = x_ref.shape[1]
    chunk = rows // 6

    def keep(p):
        return pltpu.make_async_copy(x_ref.at[p * 2 + core], kept.at[p], local.at[p])

    def give(p):
        return remote(x_ref.at[p * 2 + 1 - core], twins.at[p], near_send.at[p], near_recv.at[p], "mp", twin)

    def pass_on(step):
        to = lax.rem(pair + step, pairs)
        return remote(
            kept.at[to], others.at[step - 1], far_send.at[step], far_recv.at[step], "mp", to * 2 + core
        )

    def over_rows(body):
        @pl.loop(0, rows // chunk)
        def _(i):
            body(pl.ds(pl.multiple_of(i * chunk, chunk), chunk))

    def start():
        for step in range(1, pairs + 1):
            p = lax.rem(pair + step, pairs)
            give(p).start()
            keep(p).start()

    def go_on():
        for step in range(1, pairs):
            p = lax.rem(pair + step, pairs)
            keep(p).wait()
            give(p).wait_recv()

            def body(at):
                kept[p, at, :] = (kept[p, at, :].astype(F32) + twins[p, at, :].astype(F32)).astype(BF16)

            over_rows(body)
            pass_on(step).start()

    def end():
        keep(pair).wait()
        give(pair).wait_recv()
        for step in range(1, pairs):
            pass_on(step).wait_recv()

        def body(at):
            total = kept[pair, at, :].astype(F32) + twins[pair, at, :].astype(F32)
            for j in range(pairs - 1):
                total += others[j, at, :].astype(F32)
            spot = 0
            for ref in out_refs:
                ref[at, :] = total[:, spot : spot + ref.shape[1]].astype(BF16)
                spot += ref.shape[1]

        over_rows(body)
        for p in range(pairs):
            give(p).wait_send()
        for step in range(1, pairs):
            pass_on(step).wait_send()

    return start, go_on, end


def blend_scratch(n, shape):
    pairs = n // 2
    return [
        pltpu.VMEM((pairs,) + shape, BF16),
        pltpu.VMEM((pairs,) + shape, BF16),
        pltpu.VMEM((pairs - 1,) + shape, BF16),
    ] + [DMA((pairs,))] * 5


def table_backward(first, table, corner, lse, short_t, parts, grads, n, n_mp):
    heads, rows, columns = table.shape
    width, size = short_t.shape
    owners = MOST // rows
    _, chunks, _, _ = parts.shape
    share = chunks * rows

    def kernel(first_ref, table_ref, corner_ref, lse_ref, short_ref, parts_ref, grads_ref, ups, got_ref, dcorner_ref,
               blended_ref, full, short_up, total, soft, send_u, recv_u, recv_s, v_send, v_recv, *rest):
        line = Line(n)
        place, me = line.place, lax.axis_index("mp")
        owner = place < owners
        greet_all(n, n_mp)
        blend, go_on, blended = blend_mp(grads_ref, [blended_ref], *rest[10:], n_mp)

        def hand(g, c):
            return remote_to(
                parts_ref.at[g, c], ups.at[place], send_u.at[g, c], recv_u.at[place], me * chunks + c, g
            )

        def hand_short(g, c):
            return remote_to(parts_ref.at[g, c], short_up, send_u.at[g, c], recv_s, place, g)

        def each_hand(act):
            for c in range(chunks):
                d = me * chunks + c
                for g in range(n_mp):
                    @pl.when(jnp.logical_and(d < owners, jnp.logical_not(jnp.logical_and(d == place, g == me))))
                    def _():
                        act(hand(g, c))

                    @pl.when(jnp.logical_and(d == owners, g != me))
                    def _():
                        act(hand_short(g, c))

        each_hand(lambda copy: copy.start())
        blend()

        @pl.when(jnp.logical_and(owner, place // chunks == me))
        def _():
            ups[place] = parts_ref[me, lax.rem(place, chunks)]

        @pl.when(me == owners // chunks)
        def _():
            short_up[...] = parts_ref[me, owners % chunks]

        for head in range(heads):
            soft[head] = jnp.exp(table_ref[head, :, 0:MOST].astype(F32) - lse_ref[head, :, 0:1]).astype(BF16)

        @pl.when(me != owners // chunks)
        def _():
            hand_short(0, 0).wait_recv()

        early, inside, shift, at = small_masks(first_ref[0, 0], size)
        for head in range(heads):
            span = slice(head * HD, (head + 1) * HD)
            weights = masked_soft(nn(at, corner_ref[head]), inside)
            here, up = short_ref[span, :], short_up[span, :]
            moved = nt(here, shift).astype(BF16)
            dsoft = jnp.where(early, tn(up, here), tn(up, moved))
            full[span, MOST : MOST + size] = nn(up, by_token(weights, early, shift)).astype(BF16)
            centre = jnp.sum(weights * dsoft, axis=1, keepdims=True)
            dcorner_ref[head] = tn(at, (weights * (dsoft - centre)).astype(BF16)).astype(BF16)

        def make(s):
            @pl.when(jnp.logical_and(owner, jnp.logical_not(jnp.logical_and(s == place, place // chunks == me))))
            def _():
                remote(short_up, ups.at[s], send_u.at[0, 0], recv_u.at[s], "dp", line.partner).wait_recv()

            @pl.when(jnp.logical_not(owner))
            def _():
                ups[s] = jnp.zeros((width, rows), BF16)

            return jnp.concatenate(
                [nn(ups[s, head * HD : (head + 1) * HD, :], soft[head]) for head in range(heads)], axis=0
            )

        line_scatter(line, [(make, total, *rest[:10])], go_on)
        full[:, 0:MOST] = total[...].astype(BF16)

        def lanes(j):
            return full.at[:, pl.ds(pl.multiple_of(j * share, share), share)]

        gives = []
        for step in range(1, n_mp):
            peer = lax.rem(me + step, n_mp)
            gives.append(remote(lanes(peer), got_ref.at[me], v_send.at[step], v_recv.at[step], "mp", peer))
            gives[-1].start()
        got_ref[me] = full[:, pl.ds(pl.multiple_of(me * share, share), share)]
        blended()
        each_hand(lambda copy: copy.wait_send())
        for copy in gives:
            copy.wait()

    return pl.pallas_call(
        kernel,
        in_specs=[SCALAR] + [INTO] * 5 + [ANY],
        out_specs=[INTO] * 4,
        out_shape=[
            jax.ShapeDtypeStruct((n, width, rows), BF16),
            jax.ShapeDtypeStruct((n_mp, width, share), BF16),
            jax.ShapeDtypeStruct((heads, size, size), BF16),
            jax.ShapeDtypeStruct(grads.shape[1:], BF16),
        ],
        scratch_shapes=[
            pltpu.VMEM((width, share * n_mp), BF16),
            pltpu.VMEM((width, rows), BF16),
            pltpu.VMEM((width, MOST), F32),
            pltpu.VMEM((heads, rows, MOST), BF16),
            DMA((n_mp, chunks)),
            DMA((n,)),
            DMA,
            DMA((n_mp,)),
            DMA((n_mp,)),
        ]
        + scatter_scratch(n, (width, MOST))
        + blend_scratch(n_mp, grads.shape[1:]),
        compiler_params=comm_params(2),
        name="table_backward",
    )(first, table, corner, lse, short_t, parts, grads)


def last_exchange(back, grads, n, n_mp):
    count = len(grads)

    def kernel(*refs):
        back_ref, grad_refs = refs[0], refs[1 : 1 + count]
        got_ref, out_refs = refs[1 + count], refs[2 + count : 2 + 2 * count]
        send, recv, own_sem, part, part_send, part_recv, last = refs[2 + 2 * count : 9 + 2 * count]
        rest = refs[9 + 2 * count :]
        line = Line(n)
        place, me = line.place, lax.axis_index("mp")
        greet([("dp", n), ("mp", n_mp)])
        copies = []
        for step in range(1, n_mp):
            peer = lax.rem(me + step, n_mp)
            copies.append(
                remote(back_ref.at[peer], got_ref.at[me], send.at[step], recv.at[step], "mp", peer)
            )
            copies[-1].start()
        own = pltpu.make_async_copy(back_ref.at[me], got_ref.at[me], own_sem)
        own.start()
        outs = [*out_refs[: count - 1], last]
        items = [
            (lambda s, ref=grad_refs[i]: ref[s].astype(F32), outs[i], *rest[10 * i : 10 * i + 10])
            for i in range(count)
        ]
        line_scatter(line, items, nothing)
        part[...] = last[...].astype(BF16)

        def hand(s):
            return remote(part, out_refs[-1].at[s], part_send, part_recv.at[s], "dp", 0)

        @pl.when(place != 0)
        def _():
            hand(place).start()
            hand(place).wait_send()

        @pl.when(place == 0)
        def _():
            out_refs[-1][0] = part[...]

            @pl.loop(1, n)
            def _(s):
                hand(s).wait_recv()

        @pl.when(place != 0)
        def _():
            out_refs[-1][...] = jnp.zeros_like(out_refs[-1])

        own.wait()
        for copy in copies:
            copy.wait()

    return pl.pallas_call(
        kernel,
        in_specs=[ANY] + [INTO] * count,
        out_specs=[ANY] + [INTO] * count,
        out_shape=[jax.ShapeDtypeStruct(back.shape, BF16)]
        + [jax.ShapeDtypeStruct(g.shape[1:], F32) for g in grads[:-1]]
        + [jax.ShapeDtypeStruct(grads[-1].shape, BF16)],
        scratch_shapes=[DMA((n_mp,)), DMA((n_mp,)), DMA]
        + [pltpu.VMEM(grads[-1].shape[1:], BF16), DMA, DMA((n,)), pltpu.VMEM(grads[-1].shape[1:], F32)]
        + [each for g in grads for each in scatter_scratch(n, g.shape[1:])],
        compiler_params=comm_params(3),
        name="last_exchange",
    )(back, *grads)


def nn(a, b):
    return lax.dot_general(a, b, (((1,), (0,)), ((), ())), preferred_element_type=F32)


def nt(a, b):
    return lax.dot_general(a, b, (((1,), (1,)), ((), ())), preferred_element_type=F32)


def tn(a, b):
    return lax.dot_general(a, b, (((0,), (0,)), ((), ())), preferred_element_type=F32)


def small_masks(first, size):
    row = lax.broadcasted_iota(jnp.int32, (size, size), 0)
    col = lax.broadcasted_iota(jnp.int32, (size, size), 1)
    early = row < first
    inside = col < jnp.where(early, first, size - first)
    shift = jnp.where(col == row + first, 1.0, 0.0).astype(BF16)
    rows = jnp.where(col == jnp.where(early, row, row - first), 1.0, 0.0).astype(BF16)
    return early, inside, shift, rows


def masked_soft(scores, inside):
    masked = jnp.where(inside, scores, -1e30)
    powers = jnp.where(inside, jnp.exp(masked - jnp.max(masked, axis=1, keepdims=True)), 0.0)
    return powers / jnp.sum(powers, axis=1, keepdims=True)


def by_token(soft, early, shift):
    low = soft.astype(BF16)
    zero = jnp.zeros_like(low)
    late = nn(jnp.where(early, zero, low), shift).astype(BF16)
    return jnp.where(early, low, zero) + late


def dense_forward(first, acts, values, table, part=None, n=None, n_mp=None):
    busy = part is not None
    tokens, width = acts.shape
    heads = width // HD
    tiles = MOST // TILE
    size = tokens - MOST
    columns = table.shape[2]
    blocks = MOST // columns

    def kernel(first_ref, acts_ref, values_ref, table_ref, *refs):
        tile = pl.program_id(0)
        if busy:
            part_ref, got_ref, lse_ref, all_ref, out_ref, give_send, give_recv, own_sem, *rest = refs
            line = Line(n)
            me = lax.axis_index("mp")
            share = tokens // n_mp
            piece = (part_ref, all_ref, *rest, nothing)
            gather = Gather(line, [piece], nothing)

            @pl.when(tile == 0)
            def _():
                pltpu.make_async_copy(part_ref, all_ref.at[line.place], own_sem.at[0]).start()
                greet([("dp", n), ("mp", n_mp)])
                gather.start(piece)

            for k in range(1, line.length + 1):
                @pl.when(tile == min(2 * k, tiles))
                def _():
                    gather.step(k)

            def give(j):
                rows = out_ref.at[pl.ds(j * share, share)]
                return remote(rows, got_ref.at[me], give_send.at[j], give_recv.at[me], "mp", j)

            def keep():
                rows = out_ref.at[pl.ds(pl.multiple_of(me * share, share), share)]
                return pltpu.make_async_copy(rows, got_ref.at[me], own_sem.at[1])

            def put(rows):
                out_ref[pl.ds(pl.multiple_of(tile * TILE, TILE), TILE), :] = rows
                for j in range(n_mp):
                    done = tile == (j + 1) * share // TILE - 1

                    @pl.when(jnp.logical_and(done, me == j))
                    def _():
                        keep().start()

                    @pl.when(jnp.logical_and(done, me != j))
                    def _():
                        give(j).start()
        else:
            out_ref, lse_ref = refs

            def put(rows):
                out_ref[...] = rows
        lane = lax.broadcasted_iota(jnp.int32, (TILE, 128), 1)

        def scored(span, number):
            parts = [nn(acts_ref[:, span], table_ref[b, span, :]) for b in range(number)]
            return jnp.concatenate(parts, axis=1)

        @pl.when(tile < tiles)
        def _():
            lse = jnp.zeros((TILE, 128), F32)
            parts = []
            spans = [slice(head * HD, (head + 1) * HD) for head in range(heads)]
            ahead = scored(spans[0], blocks)
            for head in range(heads):
                scores = ahead
                if head + 1 < heads:
                    ahead = scored(spans[head + 1], blocks)
                top = jnp.max(scores, axis=1, keepdims=True)
                powers = jnp.exp(scores - top)
                total = jnp.sum(powers, axis=1, keepdims=True)
                mixed = nn(powers.astype(BF16), values_ref[0:MOST, spans[head]])
                parts.append((mixed / total).astype(BF16))
                lse = jnp.where(lane == head, top + jnp.log(total), lse)
            put(jnp.concatenate(parts, axis=1))
            lse_ref[...] = lse

        @pl.when(tile == tiles)
        def _():
            early, inside, shift, _ = small_masks(first_ref[0, 0], size)
            parts = []
            for head in range(heads):
                span = slice(head * HD, (head + 1) * HD)
                soft = by_token(masked_soft(scored(span, size // columns), inside), early, shift)
                parts.append(nn(soft, values_ref[MOST:tokens, span]).astype(BF16))
            put(jnp.concatenate(parts, axis=1))
            lse_ref[...] = jnp.zeros((TILE, 128), F32)
            if busy:
                gather.end()
                keep().wait()
                pltpu.make_async_copy(part_ref, all_ref.at[line.place], own_sem.at[0]).wait()
                for j in range(n_mp):
                    @pl.when(me != j)
                    def _():
                        give(j).wait_send()
                        remote(out_ref.at[0:share], got_ref.at[j], give_send.at[j], give_recv.at[j], "mp", j).wait_recv()

    return pl.pallas_call(
        kernel,
        grid=(tiles + 1,),
        in_specs=[
            pl.BlockSpec(memory_space=pltpu.SMEM),
            pl.BlockSpec((TILE, width), lambda t: (t, 0)),
            pl.BlockSpec((tokens, width), lambda t: (0, 0)),
            pl.BlockSpec(table.shape, lambda t: (0, 0, 0)),
        ]
        + [ANY] * busy,
        out_specs=[
            ANY if busy else pl.BlockSpec((TILE, width), lambda t: (t, 0)),
            pl.BlockSpec((TILE, 128), lambda t: (t, 0)),
        ]
        + [ANY] * busy,
        out_shape=[
            jax.ShapeDtypeStruct((n_mp, tokens // n_mp, width) if busy else (tokens, width), BF16),
            jax.ShapeDtypeStruct((tokens, 128), F32),
        ]
        + ([jax.ShapeDtypeStruct((n,) + part.shape, part.dtype)] if busy else []),
        scratch_shapes=[pltpu.VMEM((tokens, width), BF16), DMA((n_mp,)), DMA((n_mp,)), DMA((2,))] + gather_scratch(n) if busy else [],
        compiler_params=comm_params(8) if busy else pltpu.CompilerParams(vmem_limit_bytes=VMEM),
        cost_estimate=pl.CostEstimate(flops=12 * tokens * tokens * width, bytes_accessed=8 * tokens * width, transcendentals=0),
        name="dense_forward",
    )(first, acts, values, table, *([part] if busy else []))


def dense_backward(first, acts, acts_t, values_t, upstream, table, lse, slope, normed, parts=None, give=None, n=None, n_mp=None):
    busy = parts is not None
    tokens, width = acts.shape
    model = normed.shape[1]
    heads = width // HD
    tiles = MOST // TILE
    size = tokens - MOST
    columns = table.shape[2]
    blocks = MOST // columns

    def kernel(first_ref, acts_ref, acts_t_ref, values_t_ref, up_ref, table_ref, lse_ref, slope_ref, normed_ref, *refs):
        tile = pl.program_id(0)
        if busy:
            parts_ref, give_ref, back_ref, dweights_ref, dtable_ref, part_ref, all_ref = refs[:7]
            dv_acc, dt_acc, dpre, send, recv, own_sem, *rest = refs[7:]
            line = Line(n)
            scatter = Scatter(line, [(lambda s: parts_ref[s].astype(F32), part_ref, *rest)])
            start, relay, end = spread_mp(give_ref, all_ref, send, recv, own_sem, n_mp)

            @pl.when(tile == 0)
            def _():
                greet([("dp", n), ("mp", n_mp)])
                start()
                scatter.cross()

            for k in range(line.length - 1, 0, -1):
                @pl.when(tile == 2 * (line.length - k))
                def _():
                    scatter.relay(k)

            @pl.when(tile == 5)
            def _():
                relay()
        else:
            back_ref, dweights_ref, dtable_ref, dv_acc, dt_acc, dpre = refs

        @pl.when(tile == 0)
        def _():
            dv_acc[...] = jnp.zeros_like(dv_acc)
            dt_acc[...] = jnp.zeros_like(dt_acc)

        def scored(span, number):
            parts = [nn(acts_ref[:, span], table_ref[b, span, :]) for b in range(number)]
            return jnp.concatenate(parts, axis=1)

        def spread(span, dscores, number):
            total = 0.0
            for b in range(number):
                part = dscores[:, b * columns : (b + 1) * columns]
                dt_acc[b, span, :] += nn(acts_t_ref[span, :], part)
                total += nt(part, table_ref[b, span, :])
            return total

        def keep(parts):
            slopes = slope_ref[...].astype(F32)
            rows = pl.ds(pl.multiple_of(tile * TILE, TILE), TILE)
            dpre[rows, :] = (slopes * jnp.concatenate(parts, axis=1)).astype(BF16)

        @pl.when(tile < tiles)
        def _():
            parts = []
            up_t = up_ref[...].T
            spans = [slice(head * HD, (head + 1) * HD) for head in range(heads)]

            def made(span):
                return scored(span, blocks), nn(up_ref[:, span], values_t_ref[span, 0:MOST])

            ahead = made(spans[0])
            for head in range(heads):
                span = spans[head]
                scores, dsoft = ahead
                if head + 1 < heads:
                    ahead = made(spans[head + 1])
                soft = jnp.exp(scores - lse_ref[:, head : head + 1])
                dv_acc[span, 0:MOST] += nn(up_t[span, :], soft.astype(BF16))
                weighed = soft * dsoft
                centre = jnp.sum(weighed, axis=1, keepdims=True)
                parts.append(spread(span, (soft * (dsoft - centre)).astype(BF16), blocks))
            keep(parts)

        @pl.when(tile == tiles)
        def _():
            early, inside, shift, _ = small_masks(first_ref[0, 0], size)
            parts = []
            up_t = up_ref[...].T
            for head in range(heads):
                span = slice(head * HD, (head + 1) * HD)
                soft = masked_soft(scored(span, size // columns), inside)
                here = values_t_ref[span, MOST:tokens]
                moved = nt(here, shift).astype(BF16)
                dsoft = jnp.where(early, nn(up_ref[:, span], here), nn(up_ref[:, span], moved))
                dv_acc[span, MOST:tokens] = nn(up_t[span, :], by_token(soft, early, shift))
                centre = jnp.sum(soft * dsoft, axis=1, keepdims=True)
                parts.append(spread(span, (soft * (dsoft - centre)).astype(BF16), size // columns))
            keep(parts)
            dvalues_t = dv_acc[...].astype(BF16)
            back_ref[:, 0:width] = dvalues_t.T
            back_ref[:, width:] = dpre[...]
            value_grad = nn(dvalues_t, normed_ref[...])
            first_grad = nn(dpre[...].T, normed_ref[...])
            dweights_ref[:, 0:width] = value_grad.T.astype(BF16)
            dweights_ref[:, width:] = first_grad.T.astype(BF16)
            dtable_ref[...] = dt_acc[...].astype(BF16)
            if busy:
                scatter.end()
                end()

    whole = lambda t: (0, 0)
    rows = lambda t: (t, 0)
    return pl.pallas_call(
        kernel,
        grid=(tiles + 1,),
        in_specs=[
            pl.BlockSpec(memory_space=pltpu.SMEM),
            pl.BlockSpec((TILE, width), rows),
            pl.BlockSpec((width, TILE), lambda t: (0, t)),
            pl.BlockSpec((width, tokens), whole),
            pl.BlockSpec((TILE, width), rows),
            pl.BlockSpec(table.shape, lambda t: (0, 0, 0)),
            pl.BlockSpec((TILE, 128), rows),
            pl.BlockSpec((TILE, width), rows),
            pl.BlockSpec((tokens, model), whole),
        ]
        + [INTO, ANY] * busy,
        out_specs=[
            pl.BlockSpec((tokens, 2 * width), whole),
            pl.BlockSpec((model, 2 * width), whole),
            pl.BlockSpec(table.shape, lambda t: (0, 0, 0)),
        ]
        + [INTO, ANY] * busy,
        out_shape=[
            jax.ShapeDtypeStruct((tokens, 2 * width), BF16),
            jax.ShapeDtypeStruct((model, 2 * width), BF16),
            jax.ShapeDtypeStruct(table.shape, BF16),
        ]
        + (
            [
                jax.ShapeDtypeStruct(parts.shape[1:], F32),
                jax.ShapeDtypeStruct((n_mp,) + give.shape, give.dtype),
            ]
            if busy
            else []
        ),
        scratch_shapes=[
            pltpu.VMEM((width, tokens), F32),
            pltpu.VMEM(table.shape, F32),
            pltpu.VMEM((tokens, width), BF16),
        ]
        + ([DMA((n_mp,)), DMA((n_mp,)), DMA] + scatter_scratch(n, parts.shape[1:]) if busy else []),
        compiler_params=comm_params(9) if busy else pltpu.CompilerParams(vmem_limit_bytes=VMEM),
        cost_estimate=pl.CostEstimate(flops=24 * tokens * tokens * width, bytes_accessed=16 * tokens * width, transcendentals=0),
        name="dense_backward",
    )(first, acts, acts_t, values_t, upstream, table, lse, slope, normed, *([parts, give] if busy else []))


def random_forward(table, values_t):
    heads, rows, _ = table.shape
    slots, width, _ = values_t.shape

    def kernel(table_ref, values_ref, out_ref, lse_ref):
        scores = table_ref[0, :, 0:MOST].astype(F32)
        top = jnp.max(scores, axis=1, keepdims=True)
        powers = jnp.exp(scores - top)
        total = jnp.sum(powers, axis=1, keepdims=True)
        soft = (powers / total).astype(BF16)
        values = values_ref[...].reshape(slots * HD, MOST)
        out_ref[...] = nt(values, soft).astype(BF16).reshape(slots, HD, rows)
        lse_ref[...] = jnp.broadcast_to(top + jnp.log(total), (1, rows, 128))

    return pl.pallas_call(
        kernel,
        grid=(heads,),
        in_specs=[
            pl.BlockSpec((1, rows, table.shape[2]), lambda h: (h, 0, 0)),
            pl.BlockSpec((slots, HD, MOST), lambda h: (0, h, 0)),
        ],
        out_specs=[
            pl.BlockSpec((slots, HD, rows), lambda h: (0, h, 0)),
            pl.BlockSpec((1, rows, 128), lambda h: (h, 0, 0)),
        ],
        out_shape=[
            jax.ShapeDtypeStruct((slots, width, rows), BF16),
            jax.ShapeDtypeStruct((heads, rows, 128), F32),
        ],
        compiler_params=pltpu.CompilerParams(vmem_limit_bytes=VMEM),
        name="random_forward",
    )(table, values_t)


def random_backward(valid, table, lse, values_t, upstream_t):
    heads, rows, columns = table.shape
    slots, width, _ = values_t.shape
    buffers = pl.Buffered(2 if slots <= 16 else 1)

    def kernel(valid_ref, table_ref, lse_ref, values_ref, up_ref, dtable_ref, dvalues_ref):
        soft = jnp.exp(table_ref[0, :, 0:MOST].astype(F32) - lse_ref[0, :, 0:1])
        up = up_ref[...].reshape(slots * HD, rows) * valid_ref[0, 0].astype(BF16)
        values = values_ref[...].reshape(slots * HD, MOST)
        dsoft = tn(up, values)
        weighed = soft * dsoft
        centre = jnp.sum(weighed, axis=1, keepdims=True)
        dtable_ref[0, :, 0:MOST] = weighed - soft * centre
        dtable_ref[0, :, MOST:columns] = jnp.zeros((rows, columns - MOST), F32)
        dvalues_ref[...] = nn(up, soft.astype(BF16)).astype(BF16).reshape(slots, HD, MOST)

    return pl.pallas_call(
        kernel,
        grid=(heads,),
        in_specs=[
            pl.BlockSpec(memory_space=pltpu.SMEM),
            pl.BlockSpec((1, rows, columns), lambda h: (h, 0, 0)),
            pl.BlockSpec((1, rows, 128), lambda h: (h, 0, 0)),
            pl.BlockSpec((slots, HD, MOST), lambda h: (0, h, 0), pipeline_mode=buffers),
            pl.BlockSpec((slots, HD, rows), lambda h: (0, h, 0)),
        ],
        out_specs=[
            pl.BlockSpec((1, rows, columns), lambda h: (h, 0, 0)),
            pl.BlockSpec((slots, HD, MOST), lambda h: (0, h, 0)),
        ],
        out_shape=[
            jax.ShapeDtypeStruct((heads, rows, columns), F32),
            jax.ShapeDtypeStruct((slots, width, MOST), BF16),
        ],
        compiler_params=pltpu.CompilerParams(vmem_limit_bytes=VMEM),
        name="random_backward",
    )(valid, table, lse, values_t, upstream_t)


def short_forward(first, corner, values_t):
    heads, size, _ = corner.shape
    width = values_t.shape[0]

    def kernel(first_ref, corner_ref, values_ref, out_ref):
        early, inside, shift, rows = small_masks(first_ref[0, 0], size)
        for head in range(heads):
            span = slice(head * HD, (head + 1) * HD)
            soft = by_token(masked_soft(nn(rows, corner_ref[head]), inside), early, shift)
            out_ref[span, :] = nt(values_ref[span, :], soft).astype(BF16)

    return pl.pallas_call(
        kernel,
        in_specs=[
            pl.BlockSpec(memory_space=pltpu.SMEM),
            pl.BlockSpec(memory_space=pltpu.VMEM),
            pl.BlockSpec(memory_space=pltpu.VMEM),
        ],
        out_specs=pl.BlockSpec(memory_space=pltpu.VMEM),
        out_shape=jax.ShapeDtypeStruct((width, size), BF16),
        name="short_forward",
    )(first, corner, values_t)


def short_backward(first, corner, values_t, upstream_t):
    heads, size, _ = corner.shape
    width = values_t.shape[0]

    def kernel(first_ref, corner_ref, values_ref, up_ref, dcorner_ref, dvalues_ref):
        early, inside, shift, rows = small_masks(first_ref[0, 0], size)
        for head in range(heads):
            span = slice(head * HD, (head + 1) * HD)
            soft = masked_soft(nn(rows, corner_ref[head]), inside)
            here, up = values_ref[span, :], up_ref[span, :]
            moved = nt(here, shift).astype(BF16)
            dsoft = jnp.where(early, tn(up, here), tn(up, moved))
            dvalues_ref[span, :] = nn(up, by_token(soft, early, shift)).astype(BF16)
            centre = jnp.sum(soft * dsoft, axis=1, keepdims=True)
            dscores = (soft * (dsoft - centre)).astype(BF16)
            dcorner_ref[head] = tn(rows, dscores).astype(BF16)

    return pl.pallas_call(
        kernel,
        in_specs=[
            pl.BlockSpec(memory_space=pltpu.SMEM),
            pl.BlockSpec(memory_space=pltpu.VMEM),
            pl.BlockSpec(memory_space=pltpu.VMEM),
            pl.BlockSpec(memory_space=pltpu.VMEM),
        ],
        out_specs=[
            pl.BlockSpec(memory_space=pltpu.VMEM),
            pl.BlockSpec(memory_space=pltpu.VMEM),
        ],
        out_shape=[
            jax.ShapeDtypeStruct((heads, size, size), BF16),
            jax.ShapeDtypeStruct((width, size), BF16),
        ],
        name="short_backward",
    )(first, corner, values_t, upstream_t)


def table_grad(table, lse, values_t, upstream_t, corner):
    heads, rows, columns = table.shape
    slots, size = values_t.shape[0], corner.shape[2]

    def kernel(table_ref, lse_ref, values_ref, up_ref, corner_ref, out_ref):
        weights = jnp.exp(table_ref[0, :, 0:MOST].astype(F32) - lse_ref[0, :, 0:1])
        up = up_ref[...].reshape(slots * HD, rows)
        dsoft = tn(up, values_ref[...].reshape(slots * HD, MOST))
        weighed = weights * dsoft
        centre = jnp.sum(weighed, axis=1, keepdims=True)
        out_ref[0, :, 0:MOST] = weighed - weights * centre
        out_ref[0, :, MOST:columns] = jnp.zeros((rows, columns - MOST), F32)
        out_ref[0, :, 0:size] += corner_ref[0].astype(F32)

    return pl.pallas_call(
        kernel,
        grid=(heads,),
        in_specs=[
            pl.BlockSpec((1, rows, columns), lambda h: (h, 0, 0)),
            pl.BlockSpec((1, rows, 128), lambda h: (h, 0, 0)),
            pl.BlockSpec((slots, HD, MOST), lambda h: (0, h, 0)),
            pl.BlockSpec((slots, HD, rows), lambda h: (0, h, 0)),
            pl.BlockSpec((1, rows, size), lambda h: (h, 0, 0)),
        ],
        out_specs=pl.BlockSpec((1, rows, columns), lambda h: (h, 0, 0)),
        out_shape=jax.ShapeDtypeStruct((heads, rows, columns), F32),
        compiler_params=pltpu.CompilerParams(vmem_limit_bytes=VMEM),
        name="table_grad",
    )(table, lse, values_t, upstream_t, corner)


EPS = 1e-06
CURVE = 0.7978845608028654


def root(x):
    return lax.rsqrt(jnp.mean(x * x, axis=-1, keepdims=True) + EPS)


def normalize(x, gain):
    return (x * root(x) * gain).astype(BF16)


def normalize_back(x, gain, grad):
    scale = root(x)
    weighed = grad * gain
    pull = jnp.mean(weighed * x, axis=-1, keepdims=True)
    return scale * weighed - x * (scale * scale * scale * pull), jnp.sum(grad * x * scale, axis=0, keepdims=True)


def gelu(x):
    square = x * x
    bend = jnp.tanh(CURVE * x * (1.0 + 0.044715 * square))
    half = 0.5 * (1.0 + bend)
    slope = half + 0.5 * x * (1.0 - bend * bend) * (CURVE * (1.0 + 3 * 0.044715 * square))
    return x * half, slope


def turn(x, start, rows):
    total, model = x.shape

    def kernel(start_ref, x_ref, out_ref, wide):
        for i in range(model // 128):
            lanes = slice(i * 128, (i + 1) * 128)
            part = x_ref[:, lanes].astype(F32)
            wide[i % 2, 0:total] = part
            wide[i % 2, total : total + rows] = part[0:rows]
            out_ref[:, lanes] = wide[i % 2, pl.ds(start_ref[0, 0], rows), :].astype(x.dtype)

    return pl.pallas_call(
        kernel,
        in_specs=[SCALAR, INTO],
        out_specs=INTO,
        out_shape=jax.ShapeDtypeStruct((rows, model), x.dtype),
        scratch_shapes=[pltpu.VMEM((2, total + rows, 128), F32)],
        compiler_params=pltpu.CompilerParams(vmem_limit_bytes=VMEM),
        name="turn",
    )(start.astype(jnp.int32).reshape(1, 1), x)


def begin(inputs, weights, gain):
    total, model = inputs.shape
    width = weights.shape[1] // 2
    tile = 256

    def kernel(x_ref, w_ref, gain_ref, normed_ref, values_ref, values_t_ref, acts_ref, acts_t_ref, slope_ref):
        normed = normalize(x_ref[...].astype(F32), gain_ref[0:1, :])
        normed_ref[...] = normed
        both = nn(normed, w_ref[...])
        acts, slope = gelu(both[:, width:])
        values = both[:, :width]
        values_ref[...] = values.astype(BF16)
        values_t_ref[...] = values.T.astype(BF16)
        acts_ref[...] = acts.astype(BF16)
        acts_t_ref[...] = acts.T.astype(BF16)
        slope_ref[...] = slope.astype(BF16)

    rows = lambda i: (i, 0)
    columns = lambda i: (0, i)
    return pl.pallas_call(
        kernel,
        grid=(total // tile,),
        in_specs=[
            pl.BlockSpec((tile, model), rows),
            pl.BlockSpec(weights.shape, lambda i: (0, 0)),
            pl.BlockSpec(gain.shape, lambda i: (0, 0)),
        ],
        out_specs=[
            pl.BlockSpec((tile, model), rows),
            pl.BlockSpec((tile, width), rows),
            pl.BlockSpec((width, tile), columns),
            pl.BlockSpec((tile, width), rows),
            pl.BlockSpec((width, tile), columns),
            pl.BlockSpec((tile, width), rows),
        ],
        out_shape=[
            jax.ShapeDtypeStruct((total, model), BF16),
            jax.ShapeDtypeStruct((total, width), BF16),
            jax.ShapeDtypeStruct((width, total), BF16),
            jax.ShapeDtypeStruct((total, width), BF16),
            jax.ShapeDtypeStruct((width, total), BF16),
            jax.ShapeDtypeStruct((total, width), BF16),
        ],
        compiler_params=pltpu.CompilerParams(vmem_limit_bytes=VMEM),
        cost_estimate=pl.CostEstimate(flops=2 * total * model * 2 * width, bytes_accessed=6 * total * model, transcendentals=0),
        name="begin",
    )(inputs, weights, gain)


def by_rows(mixed):
    if len(mixed.shape) == 2:
        return mixed.T
    return jnp.concatenate([mixed[c].T for c in range(mixed.shape[0])], axis=0)


def ends(x, mixed, flat, weights, width, gain, row, more):
    share, model = x.shape
    groups = weights.shape[0]
    hidden = (weights.shape[2] - 2 * width) // 2

    def kernel(*refs):
        x_ref, mixed_ref, gain_ref, up_ref, down_ref, side_ref = refs[:6]
        refs = refs[6:]
        middle_ref, normed_ref, hidden_ref, slope_ref, y_ref = refs[:5]
        acc = refs[-1]
        group = pl.program_id(0)

        @pl.when(group == 0)
        def _():
            total = x_ref[...].astype(F32)
            for j in range(groups):
                block = mixed_ref[j] if flat else by_rows(mixed_ref[j])
                total += nt(block, side_ref[j, :, 0:width])
            middle_ref[...] = total
            normed_ref[...] = normalize(total, gain_ref[row : row + 1, :])
            acc[...] = total

        value_of, slope = gelu(nn(normed_ref[...], up_ref[0]))
        low = value_of.astype(BF16)
        hidden_ref[0] = low
        slope_ref[0] = slope.astype(BF16)
        acc[...] += nt(low, down_ref[0])

        @pl.when(group == groups - 1)
        def _():
            y = acc[...]
            y_ref[...] = y.astype(y_ref.dtype)
            if more:
                normed = normalize(y, gain_ref[row + 1 : row + 2, :])
                refs[5][...] = normed
                for j in range(groups):
                    refs[6][j] = nn(normed, side_ref[j, :, width : 2 * width]).T.astype(BF16)

    whole2, whole3 = (lambda g: (0, 0)), (lambda g: (0, 0, 0))
    in_specs = [
        pl.BlockSpec(x.shape, whole2),
        pl.BlockSpec(mixed.shape, lambda g: (0,) * mixed.ndim),
        pl.BlockSpec(gain.shape, whole2),
        pl.BlockSpec((1, model, hidden), lambda g: (g, 0, 0)),
        pl.BlockSpec((1, model, hidden), lambda g: (g, 0, 1)),
        pl.BlockSpec((groups, model, 2 * width), lambda g: (0, 0, hidden // width)),
    ]
    out_specs = [
        pl.BlockSpec((share, model), whole2),
        pl.BlockSpec((share, model), whole2),
        pl.BlockSpec((1, share, hidden), lambda g: (g, 0, 0)),
        pl.BlockSpec((1, share, hidden), lambda g: (g, 0, 0)),
        pl.BlockSpec((share, model), whole2),
    ]
    out_shape = [
        jax.ShapeDtypeStruct((share, model), F32),
        jax.ShapeDtypeStruct((share, model), BF16),
        jax.ShapeDtypeStruct((groups, share, hidden), BF16),
        jax.ShapeDtypeStruct((groups, share, hidden), BF16),
        jax.ShapeDtypeStruct((share, model), F32 if more else BF16),
    ]
    if more:
        out_specs += [pl.BlockSpec((share, model), whole2), pl.BlockSpec((groups, width, share), whole3)]
        out_shape += [
            jax.ShapeDtypeStruct((share, model), BF16),
            jax.ShapeDtypeStruct((groups, width, share), BF16),
        ]
    return pl.pallas_call(
        kernel,
        grid=(groups,),
        in_specs=in_specs,
        out_specs=out_specs,
        out_shape=out_shape,
        scratch_shapes=[pltpu.VMEM((share, model), F32)],
        compiler_params=pltpu.CompilerParams(vmem_limit_bytes=VMEM),
        cost_estimate=pl.CostEstimate(flops=4 * share * model * groups * hidden, bytes_accessed=4 * groups * model * hidden, transcendentals=0),
        name="ends",
    )(x, mixed, gain, weights, weights, weights)


def ends_back(grad, mixed, flat, weights, width, gain, row, record, after=None):
    middle, normed, hid, slope = record
    share, model = middle.shape
    groups = weights.shape[0]
    hidden = hid.shape[2]
    more = after is not None
    columns = 2 * hidden + (2 if more else 1) * width

    def kernel(*refs):
        grad_ref, mixed_ref, gain_ref, up_ref, down_ref, side_ref, middle_ref, normed_ref, hidden_ref, slope_ref = refs[:10]
        refs = refs[10:]
        if more:
            next_ref, next_normed_ref, dvalues_ref = refs[:3]
            refs = refs[3:]
        grads_ref, dmiddle_ref, dmixed_ref, dgain_ref, total, low, low_t, normed_t, dnormed = refs
        group = pl.program_id(0)

        @pl.when(group == 0)
        def _():
            g = grad_ref[...].astype(F32)
            dgain_ref[...] = jnp.zeros_like(dgain_ref)
            if more:
                pull = jnp.zeros((share, model), F32)
                next_t = next_normed_ref[...].T
                for j in range(groups):
                    dvalues = dvalues_ref[j].T
                    grads_ref[j, :, 2 * hidden + width : columns] = nn(next_t, dvalues).astype(BF16)
                    pull += nt(dvalues, side_ref[j, :, width : 2 * width])
                dx, dg = normalize_back(next_ref[...], gain_ref[row + 1 : row + 2, :], pull)
                g += dx
                dgain_ref[1:2, :] = dg
            total[...] = g
            low[...] = g.astype(BF16)
            low_t[...] = g.astype(BF16).T
            normed_t[...] = normed_ref[...].T
            dnormed[...] = jnp.zeros_like(dnormed)

        dpre = (slope_ref[0].astype(F32) * nn(low[...], down_ref[0])).astype(BF16)
        grads_ref[group, :, 0:hidden] = nn(normed_t[...], dpre).astype(BF16)
        grads_ref[group, :, hidden : 2 * hidden] = nn(low_t[...], hidden_ref[0]).astype(BF16)
        dnormed[...] += nt(dpre, up_ref[0])

        @pl.when(group == groups - 1)
        def _():
            dx, dg = normalize_back(middle_ref[...], gain_ref[row : row + 1, :], dnormed[...])
            dmiddle = total[...] + dx
            dgain_ref[0:1, :] = dg
            dmiddle_ref[...] = dmiddle
            down = dmiddle.astype(BF16)
            down_t = down.T
            for j in range(groups):
                block = mixed_ref[j] if flat else by_rows(mixed_ref[j])
                grads_ref[j, :, 2 * hidden : 2 * hidden + width] = nn(down_t, block).astype(BF16)
                dmixed = nn(down, side_ref[j, :, 0:width])
                if flat:
                    dmixed_ref[j] = dmixed.astype(BF16)
                elif len(mixed.shape) == 3:
                    dmixed_ref[j] = dmixed.T.astype(BF16)
                else:
                    rows = mixed.shape[3]
                    for c in range(mixed.shape[1]):
                        dmixed_ref[j, c] = dmixed[c * rows : (c + 1) * rows].T.astype(BF16)

    whole2, whole3 = (lambda g: (0, 0)), (lambda g: (0, 0, 0))
    whole = lambda a: pl.BlockSpec(a.shape, lambda g: (0,) * a.ndim)
    in_specs = [
        whole(grad),
        whole(mixed),
        whole(gain),
        pl.BlockSpec((1, model, hidden), lambda g: (g, 0, 0)),
        pl.BlockSpec((1, model, hidden), lambda g: (g, 0, 1)),
        pl.BlockSpec((groups, model, 2 * width), lambda g: (0, 0, hidden // width)),
        whole(middle),
        whole(normed),
        pl.BlockSpec((1, share, hidden), lambda g: (g, 0, 0)),
        pl.BlockSpec((1, share, hidden), lambda g: (g, 0, 0)),
    ]
    operands = [grad, mixed, gain, weights, weights, weights, middle, normed, hid, slope]
    if more:
        in_specs += [whole(a) for a in after]
        operands += list(after)
    out_specs = [
        pl.BlockSpec(memory_space=pltpu.VMEM),
        pl.BlockSpec((share, model), whole2),
        whole(mixed),
        pl.BlockSpec((8, model), whole2),
    ]
    out_shape = [
        jax.ShapeDtypeStruct((groups, model, columns), BF16),
        jax.ShapeDtypeStruct((share, model), F32),
        jax.ShapeDtypeStruct(mixed.shape, BF16),
        jax.ShapeDtypeStruct((8, model), F32),
    ]
    scratch = [
        pltpu.VMEM((share, model), F32),
        pltpu.VMEM((share, model), BF16),
        pltpu.VMEM((model, share), BF16),
        pltpu.VMEM((model, share), BF16),
        pltpu.VMEM((share, model), F32),
    ]
    return pl.pallas_call(
        kernel,
        grid=(groups,),
        in_specs=in_specs,
        out_specs=out_specs,
        out_shape=out_shape,
        scratch_shapes=scratch,
        compiler_params=pltpu.CompilerParams(vmem_limit_bytes=VMEM),
        cost_estimate=pl.CostEstimate(flops=8 * share * model * groups * hidden, bytes_accessed=8 * groups * model * hidden, transcendentals=0),
        name="ends_back",
    )(*operands)


def finish(back, weights, first, x, gain, dmiddle, gains, n, n_mp):
    groups, share, both = back.shape
    model, width = first.shape[1:]
    spot = weights.shape[2] // (2 * width) - 1
    pairs = n_mp // 2
    chunks = 4
    tall = share // chunks

    def kernel(back_ref, side_ref, first_ref, x_ref, gain_ref, dmiddle_ref, gains_ref, all_ref, sum_ref, out, here, one,
               two, far_send, far_recv, near_send, near_recv, on_send, on_recv, own_sem, g_send, g_recv, h_send, h_recv):
        me, place = lax.axis_index("mp"), lax.axis_index("dp")
        pair, core = me // 2, lax.rem(me, 2)
        twin = pair * 2 + 1 - core
        greet([("dp", n), ("mp", n_mp)])

        def rows(c):
            return pl.ds(c * tall, tall)

        def far(step, c):
            to = lax.rem(pair + step, pairs) * 2 + core
            return remote(
                out.at[rows(c)], all_ref.at[me, rows(c)], far_send.at[step, c], far_recv.at[step, c], "mp", to
            )

        def near(c):
            return remote(out.at[rows(c)], all_ref.at[me, rows(c)], near_send.at[c], near_recv.at[c], "mp", twin)

        def onward(step, c):
            source = lax.rem(pair + pairs - step, pairs) * 2 + core
            block = all_ref.at[source, rows(c)]
            return remote(block, block, on_send.at[step, c], on_recv.at[step, c], "mp", twin)

        total = jnp.zeros((1, model), F32)
        for c in range(chunks):
            span = slice(c * tall, (c + 1) * tall)
            pull = jnp.zeros((tall, model), F32)
            for j in range(groups):
                pull += nt(back_ref[j, span, 0:width], side_ref[j, :, width : 2 * width])
                pull += nt(back_ref[j, span, width:both], first_ref[j])
            dx, dg = normalize_back(x_ref[span, :].astype(F32), gain_ref[0:1, :], pull)
            out[span, :] = (dmiddle_ref[span, :] + dx).astype(BF16)
            total += dg
            for step in range(1, pairs):
                far(step, c).start()
            near(c).start()
        own = pltpu.make_async_copy(out, all_ref.at[me], own_sem)
        own.start()
        here[...] = gains_ref[...]
        here[0:1, :] = total
        one[me] = here[...]
        firsts = []
        for step in range(1, n_mp):
            to = lax.rem(me + step, n_mp)
            firsts.append(remote(here, one.at[me], g_send.at[step], g_recv.at[step], "mp", to))
            firsts[-1].start()
        for copy in firsts:
            copy.wait()
        total = one[0]
        for j in range(1, n_mp):
            total += one[j]
        two[place] = total

        def spread(step, there):
            return remote(two.at[place], two.at[there], h_send.at[step], h_recv.at[step], "dp", lax.rem(place + step, n))

        @pl.loop(1, n)
        def _(step):
            spread(step, place).start()

        for c in range(chunks):
            for step in range(1, pairs):
                far(step, c).wait_recv()
                onward(step, c).start()

        @pl.loop(1, n)
        def _(step):
            spread(step, place).wait_send()
            spread(step, lax.rem(place + n - step, n)).wait_recv()

        total = two[0]
        for j in range(1, n):
            total += two[j]
        sum_ref[...] = total
        for c in range(chunks):
            near(c).wait()
            for step in range(1, pairs):
                far(step, c).wait_send()
                onward(step, c).wait()
        own.wait()

    return pl.pallas_call(
        kernel,
        grid=(1,),
        in_specs=[
            pl.BlockSpec(back.shape, lambda i: (0, 0, 0)),
            pl.BlockSpec((groups, model, 2 * width), lambda i: (0, 0, spot)),
            pl.BlockSpec(first.shape, lambda i: (0, 0, 0)),
            pl.BlockSpec(x.shape, lambda i: (0, 0)),
            pl.BlockSpec(gain.shape, lambda i: (0, 0)),
            pl.BlockSpec(dmiddle.shape, lambda i: (0, 0)),
            pl.BlockSpec(gains.shape, lambda i: (0, 0)),
        ],
        out_specs=[ANY, pl.BlockSpec(gains.shape, lambda i: (0, 0))],
        out_shape=[
            jax.ShapeDtypeStruct((n_mp, share, model), BF16),
            jax.ShapeDtypeStruct(gains.shape, F32),
        ],
        scratch_shapes=[
            pltpu.VMEM((share, model), BF16),
            pltpu.VMEM(gains.shape, F32),
            pltpu.VMEM((n_mp,) + gains.shape, F32),
            pltpu.VMEM((n,) + gains.shape, F32),
            DMA((pairs, chunks)),
            DMA((pairs, chunks)),
            DMA((chunks,)),
            DMA((chunks,)),
            DMA((pairs, chunks)),
            DMA((pairs, chunks)),
            DMA,
            DMA((n_mp,)),
            DMA((n_mp,)),
            DMA((n,)),
            DMA((n,)),
        ],
        compiler_params=comm_params(4),
        name="finish",
    )(back, weights, first, x, gain, dmiddle, gains)


def per_device(
    n_dp,
    n_mp,
    tokens,
    lengths,
    norm_gain,
    w_value,
    w_out,
    w_up,
    w_down,
    synth_first,
    synth_second,
    random_table,
    cotangent,
):
    both = ("mp", "dp")
    place, rank = lax.axis_index("dp"), lax.axis_index("mp")
    total, model = tokens.shape
    share = total // n_mp
    size = total - MOST
    depth, width = w_value.shape[1], w_value.shape[2]
    hidden = w_up.shape[2]
    heads, rows, columns = random_table.shape
    near = rows == size and share % rows == 0 and n_dp in (2, 4, 6, 8)

    item_lengths = lengths[0]
    longest = jnp.argmax(item_lengths)
    start = (jnp.cumsum(item_lengths) - item_lengths)[longest]
    first = item_lengths[(longest + 1) % item_lengths.shape[0]].astype(jnp.int32).reshape(1, 1)

    gains = jnp.pad(norm_gain.reshape(4, depth).T, ((0, 0), (0, 124)))
    pack = jnp.concatenate([w_value[0], synth_first, gains], axis=1)
    table = synth_second.reshape(width, -1)
    corner = random_table[:, :, :size]
    if near:
        pack, table, corner = gather_weights([pack, table], corner.reshape(n_dp, -1, size), n_dp)
    else:
        begins = jnp.minimum(place * rows, size - rows)
        inside = (place * rows < size).astype(BF16)
        corner = lax.dynamic_update_slice(jnp.zeros((heads, size, size), BF16), corner * inside, (0, begins, 0))
        corner = lax.psum(corner, "dp")
        pack, table = lax.all_gather(pack, "dp"), lax.all_gather(table, "dp")
        table = table.transpose(1, 0, 2).reshape(width, total // size, size).transpose(1, 0, 2)
    pack = pack.reshape(model, -1)
    gain = jnp.pad(pack[:, 2 * width : 2 * width + 4].T.astype(F32), ((0, 4), (0, 0)))

    def whole(parts):
        joined = lax.all_gather(jnp.concatenate(parts, axis=1), both)
        return joined.reshape(n_mp, model, -1)

    weights_one = whole([w_up[0], w_down[0].T, w_out[0].T, w_value[1]])
    weights_two = [w_up[1], w_down[1].T, w_out[1].T, w_value[0]]

    inputs = turn(tokens, start, total)
    normed_one, values, values_t, acts, acts_t, slope = begin(inputs, pack[:, : 2 * width], gain)
    if near:
        mixed_one, lse, corner = dense_forward(first, acts, values, table, corner, n_dp, n_mp)
        corner = corner.reshape(heads, size, size)
    else:
        mixed, lse = dense_forward(first, acts, values, table)
        mixed_one = swap(mixed.reshape(n_mp, share, width), n_mp, 5)
    inputs = lax.dynamic_slice_in_dim(inputs, rank * share, share)
    *record_one, between, normed_two, parts = ends(
        inputs, mixed_one, True, weights_one, width, gain, 1, True
    )

    if near:
        values_all, mixed_two, short_t, table_lse, weights_two = table_forward(
            first, random_table, corner, parts, jnp.concatenate(weights_two, axis=1), n_dp, n_mp
        )
        weights_two = weights_two.reshape(n_mp, model, -1)
    else:
        weights_two = whole(weights_two)
        values_two = swap(parts, n_mp, 6, lanes_out=True)
        short_t = values_two[:, MOST:]
        values_all = lax.all_gather(values_two[:, :MOST], "dp")
        mixed, table_lse = random_forward(random_table, values_all)
        mixed = lax.all_to_all(mixed, "dp", 0, 0, tiled=True).transpose(1, 0, 2).reshape(width, total)
        mixed = jnp.concatenate([mixed[:, :MOST], short_forward(first, corner, short_t)], axis=1)
        mixed_two = swap(mixed, n_mp, 7, lanes_in=True)
    *record_two, result = ends(between, mixed_two, False, weights_two, width, gain, 3, False)
    early_first, _ = lax.optimization_barrier((synth_first, mixed_two))
    first_all = whole([early_first])

    grad = turn(cotangent, lax.rem(start + rank * share, total), share)
    grads_two, dmiddle, parts, dgain_two = ends_back(
        grad, mixed_two, False, weights_two, width, gain, 3, record_two
    )

    def scattered(grads, axes):
        grads = grads.reshape(-1, depth, grads.shape[-1])
        return lax.psum_scatter(grads, axes, scatter_dimension=0).astype(F32)

    if near:
        rows_upstream, dvalues, dcorner, grads_two = table_backward(
            first, random_table, corner, table_lse, short_t, parts, grads_two, n_dp, n_mp
        )
    else:
        upstream = swap(parts, n_mp, 8, lanes_out=True)
        dcorner, dshort = short_backward(first, corner, short_t, upstream[:, MOST:])
        dcorner = lax.dynamic_slice_in_dim(lax.psum(dcorner, "dp"), begins, rows, axis=1) * inside
        upstream = upstream.reshape(width, n_dp, rows).transpose(1, 0, 2)
        upstream = lax.all_to_all(upstream, "dp", 0, 0, tiled=True)
        valid = (place * rows < MOST).astype(F32).reshape(1, 1)
        dtable, dvalues = random_backward(valid, random_table, table_lse, values_all, upstream)
        dvalues = lax.psum_scatter(dvalues, "dp", scatter_dimension=0)
        dvalues = swap(jnp.concatenate([dvalues, dshort], axis=1), n_mp, 9, lanes_in=True)
        result = lax.all_gather(result, "mp")
        grads_two = scattered(grads_two, both)

    grads_one, dmiddle, parts, dgain_one = ends_back(
        dmiddle, mixed_one, True, weights_one, width, gain, 1, record_one, (between, normed_two, dvalues)
    )
    grads_one = scattered(grads_one, both)
    upstream = swap(parts, n_mp, 10).reshape(total, width)
    back_one = partial(dense_backward, first, acts, acts_t, values_t, upstream, table, lse, slope, normed_one)
    if near:
        back, entry_grad, second_grad, grads_two, result = back_one(
            grads_two.reshape(n_dp, depth, -1), result, n_dp, n_mp
        )
    else:
        back, entry_grad, second_grad = back_one()
    result = turn(result.reshape(total, model), total - start, total)
    back = back.reshape(n_mp, share, 2 * width)
    entry_grad = entry_grad.reshape(n_dp, depth, 2 * width)
    if near:
        back, entry_grad, second_grad, dcorner = last_exchange(
            back, [entry_grad, second_grad, dcorner.reshape(n_dp, -1, size)], n_dp, n_mp
        )
        dcorner = dcorner.reshape(heads, size, size)
    else:
        back = swap(back, n_mp, 11)
        entry_grad = lax.psum_scatter(entry_grad, "dp", scatter_dimension=0).astype(F32)
        second_grad = second_grad.transpose(1, 0, 2).reshape(width, n_dp, -1).transpose(1, 0, 2)
        second_grad = lax.psum_scatter(second_grad, "dp", scatter_dimension=0).astype(F32)
    gain_grad = jnp.concatenate([dgain_one[:1], dgain_one[:2], dgain_two[:1], jnp.zeros((4, model), F32)])
    input_grad, gain_grad = finish(back, weights_two, first_all, inputs, gain, dmiddle, gain_grad, n_dp, n_mp)
    input_grad = turn(input_grad.reshape(total, model), total - start, total)
    if near:
        upstream_last, _ = lax.optimization_barrier((rows_upstream, gain_grad))
        dtable = table_grad(random_table, table_lse, values_all, upstream_last, dcorner)
    else:
        dtable = dtable.at[:, :, :size].add(dcorner.astype(F32))

    gain_grad = lax.dynamic_slice_in_dim(gain_grad[:4], place * depth, depth, axis=1)
    out_at = slice(2 * hidden, 2 * hidden + width)
    return (
        result,
        input_grad,
        gain_grad.reshape(2, 2, depth),
        jnp.stack([entry_grad[:, :width], grads_one[:, 2 * hidden + width :]]),
        jnp.stack([grads_one[:, out_at].T, grads_two[:, out_at].T]),
        jnp.stack([grads_one[:, :hidden], grads_two[:, :hidden]]),
        jnp.stack([grads_one[:, hidden : 2 * hidden].T, grads_two[:, hidden : 2 * hidden].T]),
        entry_grad[:, width:],
        second_grad.reshape(heads, HD, -1),
        dtable,
    )


def solution(mesh):
    in_specs = (
        P("dp", None),
        P("dp", None),
        P(None, None, "dp"),
        P(None, "dp", "mp"),
        P(None, "mp", "dp"),
        P(None, "dp", "mp"),
        P(None, "mp", "dp"),
        P("dp", "mp"),
        P("mp", None, "dp"),
        P("mp", "dp", None),
        P("dp", None),
    )
    out_specs = (
        P("dp", None),
        P("dp", None),
        P(None, None, "dp"),
        P(None, "dp", "mp"),
        P(None, "mp", "dp"),
        P(None, "dp", "mp"),
        P(None, "mp", "dp"),
        P("dp", "mp"),
        P("mp", None, "dp"),
        P("mp", "dp", None),
    )
    return jax.shard_map(
        partial(per_device, mesh.shape["dp"], mesh.shape["mp"]),
        mesh=mesh,
        in_specs=in_specs,
        out_specs=out_specs,
        check_vma=False,
    )
```

```python
from functools import partial

import jax
import jax.numpy as jnp
from jax import lax
from jax.experimental import pallas as pl
from jax.experimental.pallas import tpu as pltpu
from jax.sharding import PartitionSpec as P

F32, BF16 = jnp.float32, jnp.bfloat16
HD = 64
MOST = 1792
TILE = 256
VMEM = 58 * 1024 * 1024


MESH = pl.DeviceIdType.MESH
ANY = pl.BlockSpec(memory_space=pl.ANY)
INTO = pl.BlockSpec(memory_space=pltpu.VMEM)
SCALAR = pl.BlockSpec(memory_space=pltpu.SMEM)
DMA = pltpu.SemaphoreType.DMA


def remote(source, target, send, recv, axis, index):
    return pltpu.make_async_remote_copy(
        src_ref=source, dst_ref=target, send_sem=send, recv_sem=recv, device_id={axis: index}, device_id_type=MESH
    )


def greet(groups):
    barrier = pltpu.get_barrier_semaphore()
    for axis, size in groups:
        me = lax.axis_index(axis)
        for step in range(1, size):
            pl.semaphore_signal(
                barrier, inc=1, device_id={axis: lax.rem(me + step, size)}, device_id_type=MESH
            )
    pl.semaphore_wait(barrier, sum(size - 1 for _, size in groups))


def greet_all(n, n_mp):
    barrier = pltpu.get_barrier_semaphore()
    me = lax.axis_index("dp") * n_mp + lax.axis_index("mp")

    @pl.loop(1, n * n_mp)
    def _(step):
        there = lax.rem(me + step, n * n_mp)
        where = {"dp": there // n_mp, "mp": lax.rem(there, n_mp)}
        pl.semaphore_signal(barrier, inc=1, device_id=where, device_id_type=MESH)

    pl.semaphore_wait(barrier, n * n_mp - 1)


def remote_to(source, target, send, recv, place, rank):
    return pltpu.make_async_remote_copy(
        src_ref=source,
        dst_ref=target,
        send_sem=send,
        recv_sem=recv,
        device_id={"dp": place, "mp": rank},
        device_id_type=MESH,
    )


def comm_params(number):
    return pltpu.CompilerParams(collective_id=number, has_side_effects=True, vmem_limit_bytes=VMEM)


class Line:
    def __init__(self, size):
        self.size, self.length = size, size // 2
        self.place = lax.axis_index("dp")
        self.at, self.side = self.place // 2, lax.rem(self.place, 2)
        self.partner = self.at * 2 + 1 - self.side
        self.right, self.left = self.place + 2, self.place - 2
        self.has_right, self.has_left = self.at + 1 < self.length, self.at > 0


class Gather:
    def __init__(self, line, pieces, use, even=False):
        self.line, self.pieces, self.use = line, pieces, use
        self.even = even and line.length == 4

    def block(self, slots, s, half=None):
        if half is None:
            return slots.at[s]
        rows = slots.shape[1] // 2
        return slots.at[s, pl.ds(half * rows, rows)]

    def push(self, piece, s, to, send, fresh=False, half=None, recv=None):
        own, slots = piece[:2]
        target = self.block(slots, s, half)
        remote(own if fresh else target, target, send, piece[4].at[s] if recv is None else recv, "dp", to).start()

    def arrived(self, piece, s, half=None, recv=None):
        target = self.block(piece[1], s, half)
        recv = piece[4].at[s] if recv is None else recv
        remote(target, target, piece[2].at[0], recv, "dp", self.line.partner).wait_recv()

    def sent(self, which, half=None):
        for piece in self.pieces:
            target = self.block(piece[1], 0, half)
            remote(target, target, which(piece), piece[4].at[0], "dp", self.line.partner).wait_send()

    def start(self, piece):
        line = self.line

        @pl.when(line.has_right)
        def _():
            self.push(piece, line.place, line.right, piece[3].at[0, line.at], fresh=True)

        @pl.when(line.has_left)
        def _():
            self.push(piece, line.place, line.left, piece[3].at[1, line.at], fresh=True)

        self.push(piece, line.place, line.partner, piece[2].at[line.at], fresh=True)

    def spared(self, a):
        at = self.line.at
        half = jnp.logical_or(jnp.logical_and(at == 0, a == 3), jnp.logical_and(at == 3, a == 0))
        none = jnp.logical_or(jnp.logical_and(at == 1, a == 0), jnp.logical_and(at == 2, a == 3))
        return jnp.logical_not(jnp.logical_or(half, none)), half

    def arrive(self, a, way):
        line = self.line
        s = a * 2 + line.side
        on, to = ((line.has_right, line.right), (line.has_left, line.left))[way]
        for piece in self.pieces:
            self.arrived(piece, s)

            @pl.when(on)
            def _():
                self.push(piece, s, to, piece[3].at[way, a])

            if self.even:
                whole, half = self.spared(a)

                @pl.when(whole)
                def _():
                    self.push(piece, s, line.partner, piece[2].at[a])

                @pl.when(half)
                def _():
                    self.push(piece, s, line.partner, piece[2].at[a], half=0)
            else:
                self.push(piece, s, line.partner, piece[2].at[a])
            piece[6](s)

    def crossed(self, a):
        line = self.line
        at = line.at
        s = a * 2 + 1 - line.side
        for piece in self.pieces:
            if self.even:
                _, half = self.spared(a)
                send, recv = piece[5].at[0], piece[5].at[1]

                @pl.when(half)
                def _():
                    self.arrived(piece, s, half=0)
                    self.arrived(piece, s, half=1, recv=recv)

                @pl.when(jnp.logical_not(half))
                def _():
                    self.arrived(piece, s)

                @pl.when(jnp.logical_and(at == 0, a == 0))
                def _():
                    self.push(piece, s, line.right, send)

                @pl.when(jnp.logical_and(at == 3, a == 3))
                def _():
                    self.push(piece, s, line.left, send)

                @pl.when(jnp.logical_and(at == 1, a == 3))
                def _():
                    self.push(piece, s, line.left, send, half=1, recv=recv)

                @pl.when(jnp.logical_and(at == 2, a == 0))
                def _():
                    self.push(piece, s, line.right, send, half=1, recv=recv)
            else:
                self.arrived(piece, s)
            piece[6](s)
        self.use(s)

    def step(self, k):
        line = self.line
        low, high = line.at - k, line.at + k

        @pl.when(low >= 0)
        def _():
            self.arrive(low, 0)

        @pl.when(high < line.length)
        def _():
            self.arrive(high, 1)

        @pl.when(low >= 0)
        def _():
            self.use(low * 2 + line.side)

        @pl.when(high < line.length)
        def _():
            self.use(high * 2 + line.side)

        @pl.when(low + 1 >= 0)
        def _():
            self.crossed(low + 1)

        @pl.when(jnp.logical_and(k > 1, high - 1 < line.length))
        def _():
            self.crossed(high - 1)

    def end(self):
        line = self.line

        @pl.loop(0, line.length)
        def _(a):
            if self.even:
                whole, half = self.spared(a)

                @pl.when(whole)
                def _():
                    self.sent(lambda piece: piece[2].at[a])

                @pl.when(half)
                def _():
                    self.sent(lambda piece: piece[2].at[a], half=0)
            else:
                self.sent(lambda piece: piece[2].at[a])

            @pl.when(jnp.logical_and(line.has_right, a <= line.at))
            def _():
                self.sent(lambda piece: piece[3].at[0, a])

            @pl.when(jnp.logical_and(line.has_left, a >= line.at))
            def _():
                self.sent(lambda piece: piece[3].at[1, a])

        if self.even:
            outer = jnp.logical_or(line.at == 0, line.at == 3)

            @pl.when(outer)
            def _():
                self.sent(lambda piece: piece[5].at[0])

            @pl.when(jnp.logical_not(outer))
            def _():
                self.sent(lambda piece: piece[5].at[0], half=1)


def line_gather(line, early, late, begin, more, use, even=False):
    gather = Gather(line, early + late, use, even)
    for piece in early:
        gather.start(piece)
    begin()
    for piece in late:
        gather.start(piece)
    more()

    @pl.loop(1, line.length + 1)
    def _(k):
        gather.step(k)

    gather.end()


def nothing(*_):
    pass


def gather_scratch(n):
    return [DMA((n // 2,)), DMA((2, n // 2)), DMA((n,)), DMA((2,))]


class Scatter:
    def __init__(self, line, items):
        self.line, self.items = line, items

    def over_x(self, item, a):
        _, _, x_out, x_in, _, _, _, send_x, recv_x = item[:9]
        return remote(x_out.at[a], x_in.at[a], send_x.at[a], recv_x.at[a], "dp", self.line.partner)

    def over_z(self, item, a, way, to=None):
        z_out, into, send, recv = item[4], item[5 + way], item[9], item[10 + way]
        return remote(z_out.at[a], into.at[a], send.at[a], recv.at[a], "dp", self.line.partner if to is None else to)

    def cross(self):
        length, at, side = self.line.length, self.line.at, self.line.side

        def one(a):
            for item in self.items:
                item[2][a] = item[0](a * 2 + 1 - side).astype(BF16)
                self.over_x(item, a).start()

        @pl.loop(0, length - 1)
        def _(step):
            k = length - 1 - step

            @pl.when(at + k < length)
            def _():
                one(at + k)

            @pl.when(at - k >= 0)
            def _():
                one(at - k)

        one(at)

    def relay(self, k):
        line = self.line
        length, at, side = line.length, line.at, line.side

        def one(a, way, behind, to):
            for item in self.items:
                make, _, _, x_in, z_out = item[:5]
                total = make(a * 2 + side)
                self.over_x(item, a).wait_recv()
                z_out[a] = (total + x_in[a].astype(F32)).astype(BF16)

                @pl.when(behind)
                def _():
                    self.over_z(item, a, way).wait_recv()
                    z_out[a] = (z_out[a].astype(F32) + item[5 + way][a].astype(F32)).astype(BF16)

                self.over_z(item, a, way, to).start()

        @pl.when(at + k < length)
        def _():
            one(at + k, 0, line.has_left, line.right)

        @pl.when(at - k >= 0)
        def _():
            one(at - k, 1, line.has_right, line.left)

    def end(self):
        line = self.line
        at = line.at
        for item in self.items:
            make, out, _, x_in, _, l_in, r_in = item[:7]
            total = make(line.place)
            self.over_x(item, at).wait_recv()
            out[...] = total + x_in[at].astype(F32)

            @pl.when(line.has_left)
            def _():
                self.over_z(item, at, 0).wait_recv()
                out[...] += l_in[at].astype(F32)

            @pl.when(line.has_right)
            def _():
                self.over_z(item, at, 1).wait_recv()
                out[...] += r_in[at].astype(F32)

        @pl.loop(0, line.length)
        def _(a):
            for item in self.items:
                self.over_x(item, a).wait_send()

            @pl.when(a != at)
            def _():
                for item in self.items:
                    self.over_z(item, a, 0).wait_send()


def line_scatter(line, items, middle):
    scatter = Scatter(line, items)
    scatter.cross()
    middle()

    @pl.loop(0, line.length - 1)
    def _(step):
        scatter.relay(line.length - 1 - step)

    scatter.end()


def scatter_scratch(n, shape):
    return [pltpu.VMEM((n // 2,) + shape, BF16)] * 5 + [DMA((n // 2,))] * 5


def gather_weights(arrays, corner, n):
    count = len(arrays)

    def kernel(*refs):
        owns, corner_ref, alls, part_ref = refs[:count], refs[count], refs[count + 1 : 2 * count + 1], refs[2 * count + 1]
        send, recv, kept_sem = refs[2 * count + 2 : 2 * count + 5]
        rest = refs[2 * count + 5 :]
        line = Line(n)
        place = line.place
        greet([("dp", n)])
        kept = [pltpu.make_async_copy(owns[i], alls[i].at[place], kept_sem.at[i]) for i in range(count)]

        def deal(s):
            return remote(corner_ref.at[s], part_ref, send.at[s], recv, "dp", s)

        def begin():
            for copy in kept:
                copy.start()

            @pl.when(place == 0)
            def _():
                @pl.loop(1, n)
                def _(s):
                    deal(s).start()

                part_ref[...] = corner_ref[0]

        pieces = [(owns[i], alls[i], *rest[4 * i : 4 * i + 4], nothing) for i in range(count)]
        line_gather(line, pieces, [], begin, nothing, nothing)
        for copy in kept:
            copy.wait()

        @pl.when(place != 0)
        def _():
            deal(0).wait_recv()

        @pl.when(place == 0)
        def _():
            @pl.loop(1, n)
            def _(s):
                deal(s).wait_send()

    return pl.pallas_call(
        kernel,
        in_specs=[ANY] * count + [INTO],
        out_specs=[ANY] * count + [INTO],
        out_shape=[jax.ShapeDtypeStruct((n,) + a.shape, a.dtype) for a in arrays]
        + [jax.ShapeDtypeStruct(corner.shape[1:], corner.dtype)],
        scratch_shapes=[DMA((n,)), DMA, DMA((count,))] + gather_scratch(n) * count,
        compiler_params=comm_params(0),
        name="gather_weights",
    )(*arrays, corner)


def swap(x, n, number, lanes_in=False, lanes_out=False):
    if lanes_in:
        block = (x.shape[0], x.shape[1] // n)
    else:
        block = x.shape[1:]
    shape = (block[0], n * block[1]) if lanes_out else (n,) + block

    def at(ref, lanes, j):
        if lanes:
            return ref.at[:, pl.ds(pl.multiple_of(j * block[1], block[1]), block[1])]
        return ref.at[j]

    def kernel(x_ref, out_ref, send, recv, own_sem):
        greet([("mp", n)])
        me = lax.axis_index("mp")
        copies = []
        for step in range(1, n):
            peer = lax.rem(me + step, n)
            copies.append(
                remote(at(x_ref, lanes_in, peer), at(out_ref, lanes_out, me), send.at[step], recv.at[step], "mp", peer)
            )
            copies[-1].start()
        own = pltpu.make_async_copy(at(x_ref, lanes_in, me), at(out_ref, lanes_out, me), own_sem)
        own.start()
        own.wait()
        for copy in copies:
            copy.wait()

    return pl.pallas_call(
        kernel,
        in_specs=[ANY],
        out_specs=ANY,
        out_shape=jax.ShapeDtypeStruct(shape, x.dtype),
        scratch_shapes=[DMA((n,)), DMA((n,)), DMA],
        compiler_params=comm_params(number),
        name="swap",
    )(x)


def table_forward(first, table, corner, parts, weights, n, n_mp):
    heads, rows, columns = table.shape
    _, width, share = parts.shape
    tokens = share * n_mp
    size = tokens - MOST
    owners = MOST // rows
    chunks = share // rows
    pairs = n_mp // 2

    def kernel(first_ref, table_ref, corner_ref, parts_ref, weights_ref, values_ref, mixed_ref, short_ref, lse_ref,
               all_ref, own, soft, sums, short_sum, v_send, v_recv, send_x, send_z, recv, more, send_m, recv_m, send_s,
               w_send_x, w_send_z, w_recv, w_more, w_own, far_send, far_recv, near_send, near_recv, on_send, on_recv):
        line = Line(n)
        place, me = line.place, lax.axis_index("mp")
        pair, core = me // 2, lax.rem(me, 2)
        twin = pair * 2 + 1 - core
        owner = place < owners
        greet_all(n, n_mp)

        def lanes(j):
            return own.at[:, pl.ds(pl.multiple_of(j * share, share), share)]

        gets = []
        for step in range(1, n_mp):
            peer = lax.rem(me + step, n_mp)
            gets.append(remote(parts_ref.at[peer], lanes(me), v_send.at[step], v_recv.at[step], "mp", peer))
        keep = pltpu.make_async_copy(weights_ref, all_ref.at[me, place], w_own)

        def prepare():
            offer(place, weights_ref)
            keep.start()
            own[:, pl.ds(pl.multiple_of(me * share, share), share)] = parts_ref[me]
            for copy in gets:
                copy.wait()
            values_ref[place] = own[:, 0:MOST]

        def over(step, s, source):
            to = lax.rem(pair + step, pairs) * 2 + core
            return remote(source, all_ref.at[me, s], far_send.at[step, s], far_recv.at[step, s], "mp", to)

        def across(s, source):
            return remote(source, all_ref.at[me, s], near_send.at[s], near_recv.at[s], "mp", twin)

        def onward(step, s):
            block = lax.rem(pair + pairs - step, pairs) * 2 + core
            return remote(
                all_ref.at[block, s], all_ref.at[block, s], on_send.at[step, s], on_recv.at[step, s], "mp", twin
            )

        def offer(s, source):
            for step in range(1, pairs):
                over(step, s, source).start()
            across(s, source).start()

        def product(s):
            for head in range(heads):
                span = slice(head * HD, (head + 1) * HD)
                sums[s, span, :] = nt(values_ref[s, span, :], soft[head]).astype(BF16)

        here = jnp.logical_and(owner, place // chunks == me)

        def back(s):
            return remote_to(
                sums.at[s],
                mixed_ref.at[me, lax.rem(place, chunks)],
                send_m.at[s],
                recv_m.at[me, lax.rem(place, chunks)],
                s,
                place // chunks,
            )

        def short_back():
            return remote(
                short_sum,
                mixed_ref.at[me, owners % chunks],
                send_s,
                recv_m.at[me, owners % chunks],
                "mp",
                owners // chunks,
            )

        def begin():
            short_ref[...] = own[:, MOST:tokens]
            for head in range(heads):
                scores = table_ref[head, :, 0:MOST].astype(F32)
                top = jnp.max(scores, axis=1, keepdims=True)
                powers = jnp.exp(scores - top)
                total = jnp.sum(powers, axis=1, keepdims=True)
                soft[head] = (powers / total).astype(BF16)
                lse_ref[head] = jnp.broadcast_to(top + jnp.log(total), (rows, 128))
            early, inside, shift, at = small_masks(first_ref[0, 0], size)
            for head in range(heads):
                span = slice(head * HD, (head + 1) * HD)
                weighed = by_token(masked_soft(nn(at, corner_ref[head]), inside), early, shift)
                short_sum[span, :] = nt(own[span, MOST:tokens], weighed).astype(BF16)

            @pl.when(me == owners // chunks)
            def _():
                mixed_ref[me, owners % chunks] = short_sum[...]

            @pl.when(me != owners // chunks)
            def _():
                short_back().start()

            @pl.when(owner)
            def _():
                product(place)

            @pl.when(here)
            def _():
                mixed_ref[me, lax.rem(place, chunks)] = sums[place]

            @pl.when(jnp.logical_and(owner, jnp.logical_not(here)))
            def _():
                back(place).start()

        def use(s):
            @pl.when(owner)
            def _():
                product(s)
                back(s).start()

        for copy in gets:
            copy.start()
        line_gather(
            line,
            [(weights_ref, all_ref.at[me], w_send_x, w_send_z, w_recv, w_more, lambda s: offer(s, all_ref.at[me, s]))],
            [(values_ref.at[place], values_ref, send_x, send_z, recv, more, nothing)],
            prepare,
            begin,
            use,
            even=True,
        )

        @pl.loop(0, n)
        def _(s):
            for step in range(1, pairs):
                over(step, s, weights_ref).wait_recv()
                onward(step, s).start()

        @pl.loop(0, n)
        def _(s):
            @pl.when(jnp.logical_and(owner, jnp.logical_or(s != place, jnp.logical_not(here))))
            def _():
                back(s).wait_send()

            across(s, weights_ref).wait()
            for step in range(1, pairs):
                over(step, s, weights_ref).wait_send()
                onward(step, s).wait()

        @pl.when(me != owners // chunks)
        def _():
            short_back().wait_send()

        for c in range(chunks):
            d = me * chunks + c
            for g in range(n_mp):
                source = jnp.where(d < owners, d, place)

                @pl.when(jnp.logical_not(jnp.logical_and(source == place, g == me)))
                def _():
                    remote(short_sum, mixed_ref.at[g, c], send_s, recv_m.at[g, c], "mp", twin).wait_recv()

        keep.wait()

    return pl.pallas_call(
        kernel,
        in_specs=[SCALAR, INTO, INTO, INTO, ANY],
        out_specs=[INTO, INTO, INTO, INTO, ANY],
        out_shape=[
            jax.ShapeDtypeStruct((n, width, MOST), BF16),
            jax.ShapeDtypeStruct((n_mp, chunks, width, rows), BF16),
            jax.ShapeDtypeStruct((width, size), BF16),
            jax.ShapeDtypeStruct((heads, rows, 128), F32),
            jax.ShapeDtypeStruct((n_mp, n) + weights.shape, BF16),
        ],
        scratch_shapes=[
            pltpu.VMEM((width, tokens), BF16),
            pltpu.VMEM((heads, rows, MOST), BF16),
            pltpu.VMEM((n, width, rows), BF16),
            pltpu.VMEM((width, rows), BF16),
            DMA((n_mp,)),
            DMA((n_mp,)),
            *gather_scratch(n),
            DMA((n,)),
            DMA((n_mp, chunks)),
            DMA,
            *gather_scratch(n),
            DMA,
            DMA((pairs, n)),
            DMA((pairs, n)),
            DMA((n,)),
            DMA((n,)),
            DMA((pairs, n)),
            DMA((pairs, n)),
        ],
        compiler_params=comm_params(1),
        name="table_forward",
    )(first, table, corner, parts, weights)


def spread_mp(x_ref, all_ref, send, recv, own_sem, n):
    me, pairs = lax.axis_index("mp"), n // 2
    pair, core = me // 2, lax.rem(me, 2)
    twin = pair * 2 + 1 - core
    own = pltpu.make_async_copy(x_ref, all_ref.at[me], own_sem)
    near = remote(x_ref, all_ref.at[me], send.at[0], recv.at[0], "mp", twin)

    def far(step):
        to = lax.rem(pair + step, pairs) * 2 + core
        return remote(x_ref, all_ref.at[me], send.at[step], recv.at[step], "mp", to)

    def onward(step):
        source = lax.rem(pair + pairs - step, pairs) * 2 + core
        return remote(
            all_ref.at[source], all_ref.at[source], send.at[pairs + step], recv.at[pairs + step], "mp", twin
        )

    def start():
        for step in range(1, pairs):
            far(step).start()
        near.start()
        own.start()

    def relay():
        for step in range(1, pairs):
            far(step).wait_recv()
            onward(step).start()

    def end():
        for step in range(1, pairs):
            far(step).wait_send()
            onward(step).wait()
        near.wait()
        own.wait()

    return start, relay, end


def blend_mp(x_ref, out_refs, kept, twins, others, local, near_send, near_recv, far_send, far_recv, n):
    me, pairs = lax.axis_index("mp"), n // 2
    pair, core = me // 2, lax.rem(me, 2)
    twin = pair * 2 + 1 - core
    rows = x_ref.shape[1]
    chunk = rows // 6

    def keep(p):
        return pltpu.make_async_copy(x_ref.at[p * 2 + core], kept.at[p], local.at[p])

    def give(p):
        return remote(x_ref.at[p * 2 + 1 - core], twins.at[p], near_send.at[p], near_recv.at[p], "mp", twin)

    def pass_on(step):
        to = lax.rem(pair + step, pairs)
        return remote(
            kept.at[to], others.at[step - 1], far_send.at[step], far_recv.at[step], "mp", to * 2 + core
        )

    def over_rows(body):
        @pl.loop(0, rows // chunk)
        def _(i):
            body(pl.ds(pl.multiple_of(i * chunk, chunk), chunk))

    def start():
        for step in range(1, pairs + 1):
            p = lax.rem(pair + step, pairs)
            give(p).start()
            keep(p).start()

    def go_on():
        for step in range(1, pairs):
            p = lax.rem(pair + step, pairs)
            keep(p).wait()
            give(p).wait_recv()

            def body(at):
                kept[p, at, :] = (kept[p, at, :].astype(F32) + twins[p, at, :].astype(F32)).astype(BF16)

            over_rows(body)
            pass_on(step).start()

    def end():
        keep(pair).wait()
        give(pair).wait_recv()
        for step in range(1, pairs):
            pass_on(step).wait_recv()

        def body(at):
            total = kept[pair, at, :].astype(F32) + twins[pair, at, :].astype(F32)
            for j in range(pairs - 1):
                total += others[j, at, :].astype(F32)
            spot = 0
            for ref in out_refs:
                ref[at, :] = total[:, spot : spot + ref.shape[1]].astype(BF16)
                spot += ref.shape[1]

        over_rows(body)
        for p in range(pairs):
            give(p).wait_send()
        for step in range(1, pairs):
            pass_on(step).wait_send()

    return start, go_on, end


def blend_scratch(n, shape):
    pairs = n // 2
    return [
        pltpu.VMEM((pairs,) + shape, BF16),
        pltpu.VMEM((pairs,) + shape, BF16),
        pltpu.VMEM((pairs - 1,) + shape, BF16),
    ] + [DMA((pairs,))] * 5


def table_backward(first, table, corner, lse, short_t, parts, grads, n, n_mp):
    heads, rows, columns = table.shape
    width, size = short_t.shape
    owners = MOST // rows
    _, chunks, _, _ = parts.shape
    share = chunks * rows

    def kernel(first_ref, table_ref, corner_ref, lse_ref, short_ref, parts_ref, grads_ref, ups, got_ref, dcorner_ref,
               blended_ref, full, short_up, total, soft, send_u, recv_u, recv_s, v_send, v_recv, *rest):
        line = Line(n)
        place, me = line.place, lax.axis_index("mp")
        owner = place < owners
        greet_all(n, n_mp)
        blend, go_on, blended = blend_mp(grads_ref, [blended_ref], *rest[10:], n_mp)

        def hand(g, c):
            return remote_to(
                parts_ref.at[g, c], ups.at[place], send_u.at[g, c], recv_u.at[place], me * chunks + c, g
            )

        def hand_short(g, c):
            return remote_to(parts_ref.at[g, c], short_up, send_u.at[g, c], recv_s, place, g)

        def each_hand(act):
            for c in range(chunks):
                d = me * chunks + c
                for g in range(n_mp):
                    @pl.when(jnp.logical_and(d < owners, jnp.logical_not(jnp.logical_and(d == place, g == me))))
                    def _():
                        act(hand(g, c))

                    @pl.when(jnp.logical_and(d == owners, g != me))
                    def _():
                        act(hand_short(g, c))

        each_hand(lambda copy: copy.start())
        blend()

        @pl.when(jnp.logical_and(owner, place // chunks == me))
        def _():
            ups[place] = parts_ref[me, lax.rem(place, chunks)]

        @pl.when(me == owners // chunks)
        def _():
            short_up[...] = parts_ref[me, owners % chunks]

        for head in range(heads):
            soft[head] = jnp.exp(table_ref[head, :, 0:MOST].astype(F32) - lse_ref[head, :, 0:1]).astype(BF16)

        @pl.when(me != owners // chunks)
        def _():
            hand_short(0, 0).wait_recv()

        early, inside, shift, at = small_masks(first_ref[0, 0], size)
        for head in range(heads):
            span = slice(head * HD, (head + 1) * HD)
            weights = masked_soft(nn(at, corner_ref[head]), inside)
            here, up = short_ref[span, :], short_up[span, :]
            moved = nt(here, shift).astype(BF16)
            dsoft = jnp.where(early, tn(up, here), tn(up, moved))
            full[span, MOST : MOST + size] = nn(up, by_token(weights, early, shift)).astype(BF16)
            centre = jnp.sum(weights * dsoft, axis=1, keepdims=True)
            dcorner_ref[head] = tn(at, (weights * (dsoft - centre)).astype(BF16)).astype(BF16)

        def make(s):
            @pl.when(jnp.logical_and(owner, jnp.logical_not(jnp.logical_and(s == place, place // chunks == me))))
            def _():
                remote(short_up, ups.at[s], send_u.at[0, 0], recv_u.at[s], "dp", line.partner).wait_recv()

            @pl.when(jnp.logical_not(owner))
            def _():
                ups[s] = jnp.zeros((width, rows), BF16)

            return jnp.concatenate(
                [nn(ups[s, head * HD : (head + 1) * HD, :], soft[head]) for head in range(heads)], axis=0
            )

        line_scatter(line, [(make, total, *rest[:10])], go_on)
        full[:, 0:MOST] = total[...].astype(BF16)

        def lanes(j):
            return full.at[:, pl.ds(pl.multiple_of(j * share, share), share)]

        gives = []
        for step in range(1, n_mp):
            peer = lax.rem(me + step, n_mp)
            gives.append(remote(lanes(peer), got_ref.at[me], v_send.at[step], v_recv.at[step], "mp", peer))
            gives[-1].start()
        got_ref[me] = full[:, pl.ds(pl.multiple_of(me * share, share), share)]
        blended()
        each_hand(lambda copy: copy.wait_send())
        for copy in gives:
            copy.wait()

    return pl.pallas_call(
        kernel,
        in_specs=[SCALAR] + [INTO] * 5 + [ANY],
        out_specs=[INTO] * 4,
        out_shape=[
            jax.ShapeDtypeStruct((n, width, rows), BF16),
            jax.ShapeDtypeStruct((n_mp, width, share), BF16),
            jax.ShapeDtypeStruct((heads, size, size), BF16),
            jax.ShapeDtypeStruct(grads.shape[1:], BF16),
        ],
        scratch_shapes=[
            pltpu.VMEM((width, share * n_mp), BF16),
            pltpu.VMEM((width, rows), BF16),
            pltpu.VMEM((width, MOST), F32),
            pltpu.VMEM((heads, rows, MOST), BF16),
            DMA((n_mp, chunks)),
            DMA((n,)),
            DMA,
            DMA((n_mp,)),
            DMA((n_mp,)),
        ]
        + scatter_scratch(n, (width, MOST))
        + blend_scratch(n_mp, grads.shape[1:]),
        compiler_params=comm_params(2),
        name="table_backward",
    )(first, table, corner, lse, short_t, parts, grads)


def last_exchange(back, grads, n, n_mp):
    count = len(grads)

    def kernel(*refs):
        back_ref, grad_refs = refs[0], refs[1 : 1 + count]
        got_ref, out_refs = refs[1 + count], refs[2 + count : 2 + 2 * count]
        send, recv, own_sem, part, part_send, part_recv, last = refs[2 + 2 * count : 9 + 2 * count]
        rest = refs[9 + 2 * count :]
        line = Line(n)
        place, me = line.place, lax.axis_index("mp")
        greet([("dp", n), ("mp", n_mp)])
        copies = []
        for step in range(1, n_mp):
            peer = lax.rem(me + step, n_mp)
            copies.append(
                remote(back_ref.at[peer], got_ref.at[me], send.at[step], recv.at[step], "mp", peer)
            )
            copies[-1].start()
        own = pltpu.make_async_copy(back_ref.at[me], got_ref.at[me], own_sem)
        own.start()
        outs = [*out_refs[: count - 1], last]
        items = [
            (lambda s, ref=grad_refs[i]: ref[s].astype(F32), outs[i], *rest[10 * i : 10 * i + 10])
            for i in range(count)
        ]
        line_scatter(line, items, nothing)
        part[...] = last[...].astype(BF16)

        def hand(s):
            return remote(part, out_refs[-1].at[s], part_send, part_recv.at[s], "dp", 0)

        @pl.when(place != 0)
        def _():
            hand(place).start()
            hand(place).wait_send()

        @pl.when(place == 0)
        def _():
            out_refs[-1][0] = part[...]

            @pl.loop(1, n)
            def _(s):
                hand(s).wait_recv()

        @pl.when(place != 0)
        def _():
            out_refs[-1][...] = jnp.zeros_like(out_refs[-1])

        own.wait()
        for copy in copies:
            copy.wait()

    return pl.pallas_call(
        kernel,
        in_specs=[ANY] + [INTO] * count,
        out_specs=[ANY] + [INTO] * count,
        out_shape=[jax.ShapeDtypeStruct(back.shape, BF16)]
        + [jax.ShapeDtypeStruct(g.shape[1:], F32) for g in grads[:-1]]
        + [jax.ShapeDtypeStruct(grads[-1].shape, BF16)],
        scratch_shapes=[DMA((n_mp,)), DMA((n_mp,)), DMA]
        + [pltpu.VMEM(grads[-1].shape[1:], BF16), DMA, DMA((n,)), pltpu.VMEM(grads[-1].shape[1:], F32)]
        + [each for g in grads for each in scatter_scratch(n, g.shape[1:])],
        compiler_params=comm_params(3),
        name="last_exchange",
    )(back, *grads)


def nn(a, b):
    return lax.dot_general(a, b, (((1,), (0,)), ((), ())), preferred_element_type=F32)


def nt(a, b):
    return lax.dot_general(a, b, (((1,), (1,)), ((), ())), preferred_element_type=F32)


def tn(a, b):
    return lax.dot_general(a, b, (((0,), (0,)), ((), ())), preferred_element_type=F32)


def small_masks(first, size):
    row = lax.broadcasted_iota(jnp.int32, (size, size), 0)
    col = lax.broadcasted_iota(jnp.int32, (size, size), 1)
    early = row < first
    inside = col < jnp.where(early, first, size - first)
    shift = jnp.where(col == row + first, 1.0, 0.0).astype(BF16)
    rows = jnp.where(col == jnp.where(early, row, row - first), 1.0, 0.0).astype(BF16)
    return early, inside, shift, rows


def masked_soft(scores, inside):
    masked = jnp.where(inside, scores, -1e30)
    powers = jnp.where(inside, jnp.exp(masked - jnp.max(masked, axis=1, keepdims=True)), 0.0)
    return powers / jnp.sum(powers, axis=1, keepdims=True)


def by_token(soft, early, shift):
    low = soft.astype(BF16)
    zero = jnp.zeros_like(low)
    late = nn(jnp.where(early, zero, low), shift).astype(BF16)
    return jnp.where(early, low, zero) + late


def dense_forward(first, acts, values, table, part=None, n=None, n_mp=None):
    busy = part is not None
    tokens, width = acts.shape
    heads = width // HD
    tiles = MOST // TILE
    size = tokens - MOST
    columns = table.shape[2]
    blocks = MOST // columns

    def kernel(first_ref, acts_ref, values_ref, table_ref, *refs):
        tile = pl.program_id(0)
        if busy:
            part_ref, got_ref, lse_ref, all_ref, out_ref, give_send, give_recv, own_sem, *rest = refs
            line = Line(n)
            me = lax.axis_index("mp")
            share = tokens // n_mp
            piece = (part_ref, all_ref, *rest, nothing)
            gather = Gather(line, [piece], nothing)

            @pl.when(tile == 0)
            def _():
                pltpu.make_async_copy(part_ref, all_ref.at[line.place], own_sem.at[0]).start()
                greet([("dp", n), ("mp", n_mp)])
                gather.start(piece)

            for k in range(1, line.length + 1):
                @pl.when(tile == min(2 * k, tiles))
                def _():
                    gather.step(k)

            def give(j):
                rows = out_ref.at[pl.ds(j * share, share)]
                return remote(rows, got_ref.at[me], give_send.at[j], give_recv.at[me], "mp", j)

            def keep():
                rows = out_ref.at[pl.ds(pl.multiple_of(me * share, share), share)]
                return pltpu.make_async_copy(rows, got_ref.at[me], own_sem.at[1])

            def put(rows):
                out_ref[pl.ds(pl.multiple_of(tile * TILE, TILE), TILE), :] = rows
                for j in range(n_mp):
                    done = tile == (j + 1) * share // TILE - 1

                    @pl.when(jnp.logical_and(done, me == j))
                    def _():
                        keep().start()

                    @pl.when(jnp.logical_and(done, me != j))
                    def _():
                        give(j).start()
        else:
            out_ref, lse_ref = refs

            def put(rows):
                out_ref[...] = rows
        lane = lax.broadcasted_iota(jnp.int32, (TILE, 128), 1)

        def scored(span, number):
            parts = [nn(acts_ref[:, span], table_ref[b, span, :]) for b in range(number)]
            return jnp.concatenate(parts, axis=1)

        @pl.when(tile < tiles)
        def _():
            lse = jnp.zeros((TILE, 128), F32)
            parts = []
            spans = [slice(head * HD, (head + 1) * HD) for head in range(heads)]
            ahead = scored(spans[0], blocks)
            for head in range(heads):
                scores = ahead
                if head + 1 < heads:
                    ahead = scored(spans[head + 1], blocks)
                top = jnp.max(scores, axis=1, keepdims=True)
                powers = jnp.exp(scores - top)
                total = jnp.sum(powers, axis=1, keepdims=True)
                mixed = nn(powers.astype(BF16), values_ref[0:MOST, spans[head]])
                parts.append((mixed / total).astype(BF16))
                lse = jnp.where(lane == head, top + jnp.log(total), lse)
            put(jnp.concatenate(parts, axis=1))
            lse_ref[...] = lse

        @pl.when(tile == tiles)
        def _():
            early, inside, shift, _ = small_masks(first_ref[0, 0], size)
            parts = []
            for head in range(heads):
                span = slice(head * HD, (head + 1) * HD)
                soft = by_token(masked_soft(scored(span, size // columns), inside), early, shift)
                parts.append(nn(soft, values_ref[MOST:tokens, span]).astype(BF16))
            put(jnp.concatenate(parts, axis=1))
            lse_ref[...] = jnp.zeros((TILE, 128), F32)
            if busy:
                gather.end()
                keep().wait()
                pltpu.make_async_copy(part_ref, all_ref.at[line.place], own_sem.at[0]).wait()
                for j in range(n_mp):
                    @pl.when(me != j)
                    def _():
                        give(j).wait_send()
                        remote(out_ref.at[0:share], got_ref.at[j], give_send.at[j], give_recv.at[j], "mp", j).wait_recv()

    return pl.pallas_call(
        kernel,
        grid=(tiles + 1,),
        in_specs=[
            pl.BlockSpec(memory_space=pltpu.SMEM),
            pl.BlockSpec((TILE, width), lambda t: (t, 0)),
            pl.BlockSpec((tokens, width), lambda t: (0, 0)),
            pl.BlockSpec(table.shape, lambda t: (0, 0, 0)),
        ]
        + [ANY] * busy,
        out_specs=[
            ANY if busy else pl.BlockSpec((TILE, width), lambda t: (t, 0)),
            pl.BlockSpec((TILE, 128), lambda t: (t, 0)),
        ]
        + [ANY] * busy,
        out_shape=[
            jax.ShapeDtypeStruct((n_mp, tokens // n_mp, width) if busy else (tokens, width), BF16),
            jax.ShapeDtypeStruct((tokens, 128), F32),
        ]
        + ([jax.ShapeDtypeStruct((n,) + part.shape, part.dtype)] if busy else []),
        scratch_shapes=[pltpu.VMEM((tokens, width), BF16), DMA((n_mp,)), DMA((n_mp,)), DMA((2,))] + gather_scratch(n) if busy else [],
        compiler_params=comm_params(8) if busy else pltpu.CompilerParams(vmem_limit_bytes=VMEM),
        cost_estimate=pl.CostEstimate(flops=12 * tokens * tokens * width, bytes_accessed=8 * tokens * width, transcendentals=0),
        name="dense_forward",
    )(first, acts, values, table, *([part] if busy else []))


def dense_backward(first, acts, acts_t, values_t, upstream, table, lse, slope, normed, parts=None, give=None, n=None, n_mp=None):
    busy = parts is not None
    tokens, width = acts.shape
    model = normed.shape[1]
    heads = width // HD
    tiles = MOST // TILE
    size = tokens - MOST
    columns = table.shape[2]
    blocks = MOST // columns

    def kernel(first_ref, acts_ref, acts_t_ref, values_t_ref, up_ref, table_ref, lse_ref, slope_ref, normed_ref, *refs):
        tile = pl.program_id(0)
        if busy:
            parts_ref, give_ref, back_ref, dweights_ref, dtable_ref, part_ref, all_ref = refs[:7]
            dv_acc, dt_acc, dpre, send, recv, own_sem, *rest = refs[7:]
            line = Line(n)
            scatter = Scatter(line, [(lambda s: parts_ref[s].astype(F32), part_ref, *rest)])
            start, relay, end = spread_mp(give_ref, all_ref, send, recv, own_sem, n_mp)

            @pl.when(tile == 0)
            def _():
                greet([("dp", n), ("mp", n_mp)])
                start()
                scatter.cross()

            for k in range(line.length - 1, 0, -1):
                @pl.when(tile == 2 * (line.length - k))
                def _():
                    scatter.relay(k)

            @pl.when(tile == 5)
            def _():
                relay()
        else:
            back_ref, dweights_ref, dtable_ref, dv_acc, dt_acc, dpre = refs

        @pl.when(tile == 0)
        def _():
            dv_acc[...] = jnp.zeros_like(dv_acc)
            dt_acc[...] = jnp.zeros_like(dt_acc)

        def scored(span, number):
            parts = [nn(acts_ref[:, span], table_ref[b, span, :]) for b in range(number)]
            return jnp.concatenate(parts, axis=1)

        def spread(span, dscores, number):
            total = 0.0
            for b in range(number):
                part = dscores[:, b * columns : (b + 1) * columns]
                dt_acc[b, span, :] += nn(acts_t_ref[span, :], part)
                total += nt(part, table_ref[b, span, :])
            return total

        def keep(parts):
            slopes = slope_ref[...].astype(F32)
            rows = pl.ds(pl.multiple_of(tile * TILE, TILE), TILE)
            dpre[rows, :] = (slopes * jnp.concatenate(parts, axis=1)).astype(BF16)

        @pl.when(tile < tiles)
        def _():
            parts = []
            up_t = up_ref[...].T
            spans = [slice(head * HD, (head + 1) * HD) for head in range(heads)]

            def made(span):
                return scored(span, blocks), nn(up_ref[:, span], values_t_ref[span, 0:MOST])

            ahead = made(spans[0])
            for head in range(heads):
                span = spans[head]
                scores, dsoft = ahead
                if head + 1 < heads:
                    ahead = made(spans[head + 1])
                soft = jnp.exp(scores - lse_ref[:, head : head + 1])
                dv_acc[span, 0:MOST] += nn(up_t[span, :], soft.astype(BF16))
                weighed = soft * dsoft
                centre = jnp.sum(weighed, axis=1, keepdims=True)
                parts.append(spread(span, (soft * (dsoft - centre)).astype(BF16), blocks))
            keep(parts)

        @pl.when(tile == tiles)
        def _():
            early, inside, shift, _ = small_masks(first_ref[0, 0], size)
            parts = []
            up_t = up_ref[...].T
            for head in range(heads):
                span = slice(head * HD, (head + 1) * HD)
                soft = masked_soft(scored(span, size // columns), inside)
                here = values_t_ref[span, MOST:tokens]
                moved = nt(here, shift).astype(BF16)
                dsoft = jnp.where(early, nn(up_ref[:, span], here), nn(up_ref[:, span], moved))
                dv_acc[span, MOST:tokens] = nn(up_t[span, :], by_token(soft, early, shift))
                centre = jnp.sum(soft * dsoft, axis=1, keepdims=True)
                parts.append(spread(span, (soft * (dsoft - centre)).astype(BF16), size // columns))
            keep(parts)
            dvalues_t = dv_acc[...].astype(BF16)
            back_ref[:, 0:width] = dvalues_t.T
            back_ref[:, width:] = dpre[...]
            value_grad = nn(dvalues_t, normed_ref[...])
            first_grad = nn(dpre[...].T, normed_ref[...])
            dweights_ref[:, 0:width] = value_grad.T.astype(BF16)
            dweights_ref[:, width:] = first_grad.T.astype(BF16)
            dtable_ref[...] = dt_acc[...].astype(BF16)
            if busy:
                scatter.end()
                end()

    whole = lambda t: (0, 0)
    rows = lambda t: (t, 0)
    return pl.pallas_call(
        kernel,
        grid=(tiles + 1,),
        in_specs=[
            pl.BlockSpec(memory_space=pltpu.SMEM),
            pl.BlockSpec((TILE, width), rows),
            pl.BlockSpec((width, TILE), lambda t: (0, t)),
            pl.BlockSpec((width, tokens), whole),
            pl.BlockSpec((TILE, width), rows),
            pl.BlockSpec(table.shape, lambda t: (0, 0, 0)),
            pl.BlockSpec((TILE, 128), rows),
            pl.BlockSpec((TILE, width), rows),
            pl.BlockSpec((tokens, model), whole),
        ]
        + [INTO, ANY] * busy,
        out_specs=[
            pl.BlockSpec((tokens, 2 * width), whole),
            pl.BlockSpec((model, 2 * width), whole),
            pl.BlockSpec(table.shape, lambda t: (0, 0, 0)),
        ]
        + [INTO, ANY] * busy,
        out_shape=[
            jax.ShapeDtypeStruct((tokens, 2 * width), BF16),
            jax.ShapeDtypeStruct((model, 2 * width), BF16),
            jax.ShapeDtypeStruct(table.shape, BF16),
        ]
        + (
            [
                jax.ShapeDtypeStruct(parts.shape[1:], F32),
                jax.ShapeDtypeStruct((n_mp,) + give.shape, give.dtype),
            ]
            if busy
            else []
        ),
        scratch_shapes=[
            pltpu.VMEM((width, tokens), F32),
            pltpu.VMEM(table.shape, F32),
            pltpu.VMEM((tokens, width), BF16),
        ]
        + ([DMA((n_mp,)), DMA((n_mp,)), DMA] + scatter_scratch(n, parts.shape[1:]) if busy else []),
        compiler_params=comm_params(9) if busy else pltpu.CompilerParams(vmem_limit_bytes=VMEM),
        cost_estimate=pl.CostEstimate(flops=24 * tokens * tokens * width, bytes_accessed=16 * tokens * width, transcendentals=0),
        name="dense_backward",
    )(first, acts, acts_t, values_t, upstream, table, lse, slope, normed, *([parts, give] if busy else []))


def random_forward(table, values_t):
    heads, rows, _ = table.shape
    slots, width, _ = values_t.shape

    def kernel(table_ref, values_ref, out_ref, lse_ref):
        scores = table_ref[0, :, 0:MOST].astype(F32)
        top = jnp.max(scores, axis=1, keepdims=True)
        powers = jnp.exp(scores - top)
        total = jnp.sum(powers, axis=1, keepdims=True)
        soft = (powers / total).astype(BF16)
        values = values_ref[...].reshape(slots * HD, MOST)
        out_ref[...] = nt(values, soft).astype(BF16).reshape(slots, HD, rows)
        lse_ref[...] = jnp.broadcast_to(top + jnp.log(total), (1, rows, 128))

    return pl.pallas_call(
        kernel,
        grid=(heads,),
        in_specs=[
            pl.BlockSpec((1, rows, table.shape[2]), lambda h: (h, 0, 0)),
            pl.BlockSpec((slots, HD, MOST), lambda h: (0, h, 0)),
        ],
        out_specs=[
            pl.BlockSpec((slots, HD, rows), lambda h: (0, h, 0)),
            pl.BlockSpec((1, rows, 128), lambda h: (h, 0, 0)),
        ],
        out_shape=[
            jax.ShapeDtypeStruct((slots, width, rows), BF16),
            jax.ShapeDtypeStruct((heads, rows, 128), F32),
        ],
        compiler_params=pltpu.CompilerParams(vmem_limit_bytes=VMEM),
        name="random_forward",
    )(table, values_t)


def random_backward(valid, table, lse, values_t, upstream_t):
    heads, rows, columns = table.shape
    slots, width, _ = values_t.shape
    buffers = pl.Buffered(2 if slots <= 16 else 1)

    def kernel(valid_ref, table_ref, lse_ref, values_ref, up_ref, dtable_ref, dvalues_ref):
        soft = jnp.exp(table_ref[0, :, 0:MOST].astype(F32) - lse_ref[0, :, 0:1])
        up = up_ref[...].reshape(slots * HD, rows) * valid_ref[0, 0].astype(BF16)
        values = values_ref[...].reshape(slots * HD, MOST)
        dsoft = tn(up, values)
        weighed = soft * dsoft
        centre = jnp.sum(weighed, axis=1, keepdims=True)
        dtable_ref[0, :, 0:MOST] = weighed - soft * centre
        dtable_ref[0, :, MOST:columns] = jnp.zeros((rows, columns - MOST), F32)
        dvalues_ref[...] = nn(up, soft.astype(BF16)).astype(BF16).reshape(slots, HD, MOST)

    return pl.pallas_call(
        kernel,
        grid=(heads,),
        in_specs=[
            pl.BlockSpec(memory_space=pltpu.SMEM),
            pl.BlockSpec((1, rows, columns), lambda h: (h, 0, 0)),
            pl.BlockSpec((1, rows, 128), lambda h: (h, 0, 0)),
            pl.BlockSpec((slots, HD, MOST), lambda h: (0, h, 0), pipeline_mode=buffers),
            pl.BlockSpec((slots, HD, rows), lambda h: (0, h, 0)),
        ],
        out_specs=[
            pl.BlockSpec((1, rows, columns), lambda h: (h, 0, 0)),
            pl.BlockSpec((slots, HD, MOST), lambda h: (0, h, 0)),
        ],
        out_shape=[
            jax.ShapeDtypeStruct((heads, rows, columns), F32),
            jax.ShapeDtypeStruct((slots, width, MOST), BF16),
        ],
        compiler_params=pltpu.CompilerParams(vmem_limit_bytes=VMEM),
        name="random_backward",
    )(valid, table, lse, values_t, upstream_t)


def short_forward(first, corner, values_t):
    heads, size, _ = corner.shape
    width = values_t.shape[0]

    def kernel(first_ref, corner_ref, values_ref, out_ref):
        early, inside, shift, rows = small_masks(first_ref[0, 0], size)
        for head in range(heads):
            span = slice(head * HD, (head + 1) * HD)
            soft = by_token(masked_soft(nn(rows, corner_ref[head]), inside), early, shift)
            out_ref[span, :] = nt(values_ref[span, :], soft).astype(BF16)

    return pl.pallas_call(
        kernel,
        in_specs=[
            pl.BlockSpec(memory_space=pltpu.SMEM),
            pl.BlockSpec(memory_space=pltpu.VMEM),
            pl.BlockSpec(memory_space=pltpu.VMEM),
        ],
        out_specs=pl.BlockSpec(memory_space=pltpu.VMEM),
        out_shape=jax.ShapeDtypeStruct((width, size), BF16),
        name="short_forward",
    )(first, corner, values_t)


def short_backward(first, corner, values_t, upstream_t):
    heads, size, _ = corner.shape
    width = values_t.shape[0]

    def kernel(first_ref, corner_ref, values_ref, up_ref, dcorner_ref, dvalues_ref):
        early, inside, shift, rows = small_masks(first_ref[0, 0], size)
        for head in range(heads):
            span = slice(head * HD, (head + 1) * HD)
            soft = masked_soft(nn(rows, corner_ref[head]), inside)
            here, up = values_ref[span, :], up_ref[span, :]
            moved = nt(here, shift).astype(BF16)
            dsoft = jnp.where(early, tn(up, here), tn(up, moved))
            dvalues_ref[span, :] = nn(up, by_token(soft, early, shift)).astype(BF16)
            centre = jnp.sum(soft * dsoft, axis=1, keepdims=True)
            dscores = (soft * (dsoft - centre)).astype(BF16)
            dcorner_ref[head] = tn(rows, dscores).astype(BF16)

    return pl.pallas_call(
        kernel,
        in_specs=[
            pl.BlockSpec(memory_space=pltpu.SMEM),
            pl.BlockSpec(memory_space=pltpu.VMEM),
            pl.BlockSpec(memory_space=pltpu.VMEM),
            pl.BlockSpec(memory_space=pltpu.VMEM),
        ],
        out_specs=[
            pl.BlockSpec(memory_space=pltpu.VMEM),
            pl.BlockSpec(memory_space=pltpu.VMEM),
        ],
        out_shape=[
            jax.ShapeDtypeStruct((heads, size, size), BF16),
            jax.ShapeDtypeStruct((width, size), BF16),
        ],
        name="short_backward",
    )(first, corner, values_t, upstream_t)


def table_grad(table, lse, values_t, upstream_t, corner):
    heads, rows, columns = table.shape
    slots, size = values_t.shape[0], corner.shape[2]

    def kernel(table_ref, lse_ref, values_ref, up_ref, corner_ref, out_ref):
        weights = jnp.exp(table_ref[0, :, 0:MOST].astype(F32) - lse_ref[0, :, 0:1])
        up = up_ref[...].reshape(slots * HD, rows)
        dsoft = tn(up, values_ref[...].reshape(slots * HD, MOST))
        weighed = weights * dsoft
        centre = jnp.sum(weighed, axis=1, keepdims=True)
        out_ref[0, :, 0:MOST] = weighed - weights * centre
        out_ref[0, :, MOST:columns] = jnp.zeros((rows, columns - MOST), F32)
        out_ref[0, :, 0:size] += corner_ref[0].astype(F32)

    return pl.pallas_call(
        kernel,
        grid=(heads,),
        in_specs=[
            pl.BlockSpec((1, rows, columns), lambda h: (h, 0, 0)),
            pl.BlockSpec((1, rows, 128), lambda h: (h, 0, 0)),
            pl.BlockSpec((slots, HD, MOST), lambda h: (0, h, 0)),
            pl.BlockSpec((slots, HD, rows), lambda h: (0, h, 0)),
            pl.BlockSpec((1, rows, size), lambda h: (h, 0, 0)),
        ],
        out_specs=pl.BlockSpec((1, rows, columns), lambda h: (h, 0, 0)),
        out_shape=jax.ShapeDtypeStruct((heads, rows, columns), F32),
        compiler_params=pltpu.CompilerParams(vmem_limit_bytes=VMEM),
        name="table_grad",
    )(table, lse, values_t, upstream_t, corner)


EPS = 1e-06
CURVE = 0.7978845608028654


def root(x):
    return lax.rsqrt(jnp.mean(x * x, axis=-1, keepdims=True) + EPS)


def normalize(x, gain):
    return (x * root(x) * gain).astype(BF16)


def normalize_back(x, gain, grad):
    scale = root(x)
    weighed = grad * gain
    pull = jnp.mean(weighed * x, axis=-1, keepdims=True)
    return scale * weighed - x * (scale * scale * scale * pull), jnp.sum(grad * x * scale, axis=0, keepdims=True)


def gelu(x):
    square = x * x
    half = 0.5 * jnp.tanh(x * (CURVE + CURVE * 0.044715 * square)) + 0.5
    value = x * half
    return value, half + (value - value * half) * (2 * CURVE + 6 * CURVE * 0.044715 * square)


def turn(x, start, rows):
    total, model = x.shape

    def kernel(start_ref, x_ref, out_ref, wide):
        for i in range(model // 128):
            lanes = slice(i * 128, (i + 1) * 128)
            part = x_ref[:, lanes].astype(F32)
            wide[i % 2, 0:total] = part
            wide[i % 2, total : total + rows] = part[0:rows]
            out_ref[:, lanes] = wide[i % 2, pl.ds(start_ref[0, 0], rows), :].astype(x.dtype)

    return pl.pallas_call(
        kernel,
        in_specs=[SCALAR, INTO],
        out_specs=INTO,
        out_shape=jax.ShapeDtypeStruct((rows, model), x.dtype),
        scratch_shapes=[pltpu.VMEM((2, total + rows, 128), F32)],
        compiler_params=pltpu.CompilerParams(vmem_limit_bytes=VMEM),
        name="turn",
    )(start.astype(jnp.int32).reshape(1, 1), x)


def begin(inputs, weights, gain):
    total, model = inputs.shape
    width = weights.shape[1] // 2
    tile = 256

    def kernel(x_ref, w_ref, gain_ref, normed_ref, values_ref, values_t_ref, acts_ref, acts_t_ref, slope_ref):
        normed = normalize(x_ref[...].astype(F32), gain_ref[0:1, :])
        normed_ref[...] = normed
        both = nn(normed, w_ref[...])
        acts, slope = gelu(both[:, width:])
        values = both[:, :width]
        values_ref[...] = values.astype(BF16)
        values_t_ref[...] = values.T.astype(BF16)
        acts_ref[...] = acts.astype(BF16)
        acts_t_ref[...] = acts.T.astype(BF16)
        slope_ref[...] = slope.astype(BF16)

    rows = lambda i: (i, 0)
    columns = lambda i: (0, i)
    return pl.pallas_call(
        kernel,
        grid=(total // tile,),
        in_specs=[
            pl.BlockSpec((tile, model), rows),
            pl.BlockSpec(weights.shape, lambda i: (0, 0)),
            pl.BlockSpec(gain.shape, lambda i: (0, 0)),
        ],
        out_specs=[
            pl.BlockSpec((tile, model), rows),
            pl.BlockSpec((tile, width), rows),
            pl.BlockSpec((width, tile), columns),
            pl.BlockSpec((tile, width), rows),
            pl.BlockSpec((width, tile), columns),
            pl.BlockSpec((tile, width), rows),
        ],
        out_shape=[
            jax.ShapeDtypeStruct((total, model), BF16),
            jax.ShapeDtypeStruct((total, width), BF16),
            jax.ShapeDtypeStruct((width, total), BF16),
            jax.ShapeDtypeStruct((total, width), BF16),
            jax.ShapeDtypeStruct((width, total), BF16),
            jax.ShapeDtypeStruct((total, width), BF16),
        ],
        compiler_params=pltpu.CompilerParams(vmem_limit_bytes=VMEM),
        cost_estimate=pl.CostEstimate(flops=2 * total * model * 2 * width, bytes_accessed=6 * total * model, transcendentals=0),
        name="begin",
    )(inputs, weights, gain)


def by_rows(mixed):
    if len(mixed.shape) == 2:
        return mixed.T
    return jnp.concatenate([mixed[c].T for c in range(mixed.shape[0])], axis=0)


def ends(x, mixed, flat, weights, width, gain, row, more):
    share, model = x.shape
    groups = weights.shape[0]
    hidden = (weights.shape[2] - 2 * width) // 2

    def kernel(*refs):
        x_ref, mixed_ref, gain_ref, up_ref, down_ref, side_ref = refs[:6]
        refs = refs[6:]
        middle_ref, normed_ref, hidden_ref, slope_ref, y_ref = refs[:5]
        acc = refs[-1]
        group = pl.program_id(0)

        @pl.when(group == 0)
        def _():
            total = x_ref[...].astype(F32)
            for j in range(groups):
                block = mixed_ref[j] if flat else by_rows(mixed_ref[j])
                total += nt(block, side_ref[j, :, 0:width])
            middle_ref[...] = total
            normed_ref[...] = normalize(total, gain_ref[row : row + 1, :])
            acc[...] = total

        normed = normed_ref[...]
        part = 256 if hidden % 256 == 0 else hidden
        ahead = nn(normed, up_ref[0, :, 0:part])
        for spot in range(0, hidden, part):
            pre = ahead
            if spot + part < hidden:
                ahead = nn(normed, up_ref[0, :, spot + part : spot + 2 * part])
            value, slope = gelu(pre)
            hidden_ref[0, :, spot : spot + part] = value.astype(BF16)
            slope_ref[0, :, spot : spot + part] = slope.astype(BF16)
        acc[...] += nt(hidden_ref[0], down_ref[0])

        @pl.when(group == groups - 1)
        def _():
            y = acc[...]
            y_ref[...] = y.astype(y_ref.dtype)
            if more:
                normed = normalize(y, gain_ref[row + 1 : row + 2, :])
                refs[5][...] = normed
                for j in range(groups):
                    refs[6][j] = nn(normed, side_ref[j, :, width : 2 * width]).T.astype(BF16)

    whole2, whole3 = (lambda g: (0, 0)), (lambda g: (0, 0, 0))
    in_specs = [
        pl.BlockSpec(x.shape, whole2),
        pl.BlockSpec(mixed.shape, lambda g: (0,) * mixed.ndim),
        pl.BlockSpec(gain.shape, whole2),
        pl.BlockSpec((1, model, hidden), lambda g: (g, 0, 0)),
        pl.BlockSpec((1, model, hidden), lambda g: (g, 0, 1)),
        pl.BlockSpec((groups, model, 2 * width), lambda g: (0, 0, hidden // width)),
    ]
    out_specs = [
        pl.BlockSpec((share, model), whole2),
        pl.BlockSpec((share, model), whole2),
        pl.BlockSpec((1, share, hidden), lambda g: (g, 0, 0)),
        pl.BlockSpec((1, share, hidden), lambda g: (g, 0, 0)),
        pl.BlockSpec((share, model), whole2),
    ]
    out_shape = [
        jax.ShapeDtypeStruct((share, model), F32),
        jax.ShapeDtypeStruct((share, model), BF16),
        jax.ShapeDtypeStruct((groups, share, hidden), BF16),
        jax.ShapeDtypeStruct((groups, share, hidden), BF16),
        jax.ShapeDtypeStruct((share, model), F32 if more else BF16),
    ]
    if more:
        out_specs += [pl.BlockSpec((share, model), whole2), pl.BlockSpec((groups, width, share), whole3)]
        out_shape += [
            jax.ShapeDtypeStruct((share, model), BF16),
            jax.ShapeDtypeStruct((groups, width, share), BF16),
        ]
    return pl.pallas_call(
        kernel,
        grid=(groups,),
        in_specs=in_specs,
        out_specs=out_specs,
        out_shape=out_shape,
        scratch_shapes=[pltpu.VMEM((share, model), F32)],
        compiler_params=pltpu.CompilerParams(vmem_limit_bytes=VMEM),
        cost_estimate=pl.CostEstimate(flops=4 * share * model * groups * hidden, bytes_accessed=4 * groups * model * hidden, transcendentals=0),
        name="ends",
    )(x, mixed, gain, weights, weights, weights)


def ends_back(grad, mixed, flat, weights, width, gain, row, record, after=None):
    middle, normed, hid, slope = record
    share, model = middle.shape
    groups = weights.shape[0]
    hidden = hid.shape[2]
    more = after is not None
    columns = 2 * hidden + (2 if more else 1) * width

    def kernel(*refs):
        grad_ref, mixed_ref, gain_ref, up_ref, down_ref, side_ref, middle_ref, normed_ref, hidden_ref, slope_ref = refs[:10]
        refs = refs[10:]
        if more:
            next_ref, next_normed_ref, dvalues_ref = refs[:3]
            refs = refs[3:]
        out_ref, dmiddle_ref, dmixed_ref, dgain_ref, total, low, low_t, normed_t, dnormed, grads_ref, side_grads, sems = refs
        group = pl.program_id(0)

        def leave(g):
            return pltpu.make_async_copy(grads_ref.at[g], out_ref.at[g, :, pl.ds(0, 2 * hidden)], sems.at[g])

        side_leave = pltpu.make_async_copy(
            side_grads, out_ref.at[:, :, pl.ds(2 * hidden, columns - 2 * hidden)], sems.at[groups]
        )

        @pl.when(group == 0)
        def _():
            g = grad_ref[...].astype(F32)
            dgain_ref[...] = jnp.zeros_like(dgain_ref)
            if more:
                pull = jnp.zeros((share, model), F32)
                next_t = next_normed_ref[...].T
                for j in range(groups):
                    dvalues = dvalues_ref[j].T
                    side_grads[j, :, width : 2 * width] = nn(next_t, dvalues).astype(BF16)
                    pull += nt(dvalues, side_ref[j, :, width : 2 * width])
                dx, dg = normalize_back(next_ref[...], gain_ref[row + 1 : row + 2, :], pull)
                g += dx
                dgain_ref[1:2, :] = dg
            total[...] = g
            low[...] = g.astype(BF16)
            low_t[...] = g.astype(BF16).T
            normed_t[...] = normed_ref[...].T
            dnormed[...] = jnp.zeros_like(dnormed)

        dpre = (slope_ref[0].astype(F32) * nn(low[...], down_ref[0])).astype(BF16)
        grads_ref[group, :, 0:hidden] = nn(normed_t[...], dpre).astype(BF16)
        grads_ref[group, :, hidden : 2 * hidden] = nn(low_t[...], hidden_ref[0]).astype(BF16)
        leave(group).start()
        dnormed[...] += nt(dpre, up_ref[0])

        @pl.when(group == groups - 1)
        def _():
            dx, dg = normalize_back(middle_ref[...], gain_ref[row : row + 1, :], dnormed[...])
            dmiddle = total[...] + dx
            dgain_ref[0:1, :] = dg
            dmiddle_ref[...] = dmiddle
            down = dmiddle.astype(BF16)
            down_t = down.T
            for j in range(groups):
                block = mixed_ref[j] if flat else by_rows(mixed_ref[j])
                side_grads[j, :, 0:width] = nn(down_t, block).astype(BF16)
                dmixed = nn(down, side_ref[j, :, 0:width])
                if flat:
                    dmixed_ref[j] = dmixed.astype(BF16)
                elif len(mixed.shape) == 3:
                    dmixed_ref[j] = dmixed.T.astype(BF16)
                else:
                    rows = mixed.shape[3]
                    for c in range(mixed.shape[1]):
                        dmixed_ref[j, c] = dmixed[c * rows : (c + 1) * rows].T.astype(BF16)
            side_leave.start()
            side_leave.wait()
            for g in range(groups):
                leave(g).wait()

    whole2, whole3 = (lambda g: (0, 0)), (lambda g: (0, 0, 0))
    whole = lambda a: pl.BlockSpec(a.shape, lambda g: (0,) * a.ndim)
    in_specs = [
        whole(grad),
        whole(mixed),
        whole(gain),
        pl.BlockSpec((1, model, hidden), lambda g: (g, 0, 0)),
        pl.BlockSpec((1, model, hidden), lambda g: (g, 0, 1)),
        pl.BlockSpec((groups, model, 2 * width), lambda g: (0, 0, hidden // width)),
        whole(middle),
        whole(normed),
        pl.BlockSpec((1, share, hidden), lambda g: (g, 0, 0)),
        pl.BlockSpec((1, share, hidden), lambda g: (g, 0, 0)),
    ]
    operands = [grad, mixed, gain, weights, weights, weights, middle, normed, hid, slope]
    if more:
        in_specs += [whole(a) for a in after]
        operands += list(after)
    out_specs = [
        ANY,
        pl.BlockSpec((share, model), whole2),
        whole(mixed),
        pl.BlockSpec((8, model), whole2),
    ]
    out_shape = [
        jax.ShapeDtypeStruct((groups, model, columns), BF16),
        jax.ShapeDtypeStruct((share, model), F32),
        jax.ShapeDtypeStruct(mixed.shape, BF16),
        jax.ShapeDtypeStruct((8, model), F32),
    ]
    scratch = [
        pltpu.VMEM((share, model), F32),
        pltpu.VMEM((share, model), BF16),
        pltpu.VMEM((model, share), BF16),
        pltpu.VMEM((model, share), BF16),
        pltpu.VMEM((share, model), F32),
        pltpu.VMEM((groups, model, 2 * hidden), BF16),
        pltpu.VMEM((groups, model, columns - 2 * hidden), BF16),
        DMA((groups + 1,)),
    ]
    return pl.pallas_call(
        kernel,
        grid=(groups,),
        in_specs=in_specs,
        out_specs=out_specs,
        out_shape=out_shape,
        scratch_shapes=scratch,
        compiler_params=pltpu.CompilerParams(vmem_limit_bytes=VMEM),
        cost_estimate=pl.CostEstimate(flops=8 * share * model * groups * hidden, bytes_accessed=8 * groups * model * hidden, transcendentals=0),
        name="ends_back",
    )(*operands)


def finish(back, weights, first, x, gain, dmiddle, gains, n, n_mp):
    groups, share, both = back.shape
    model, width = first.shape[1:]
    spot = weights.shape[2] // (2 * width) - 1
    pairs = n_mp // 2
    chunks = 4
    tall = share // chunks

    def kernel(back_ref, side_ref, first_ref, x_ref, gain_ref, dmiddle_ref, gains_ref, all_ref, sum_ref, out, here, one,
               two, far_send, far_recv, near_send, near_recv, on_send, on_recv, own_sem, g_send, g_recv, h_send, h_recv):
        me, place = lax.axis_index("mp"), lax.axis_index("dp")
        pair, core = me // 2, lax.rem(me, 2)
        twin = pair * 2 + 1 - core
        greet([("dp", n), ("mp", n_mp)])

        def rows(c):
            return pl.ds(c * tall, tall)

        def far(step, c):
            to = lax.rem(pair + step, pairs) * 2 + core
            return remote(
                out.at[rows(c)], all_ref.at[me, rows(c)], far_send.at[step, c], far_recv.at[step, c], "mp", to
            )

        def near(c):
            return remote(out.at[rows(c)], all_ref.at[me, rows(c)], near_send.at[c], near_recv.at[c], "mp", twin)

        def onward(step, c):
            source = lax.rem(pair + pairs - step, pairs) * 2 + core
            block = all_ref.at[source, rows(c)]
            return remote(block, block, on_send.at[step, c], on_recv.at[step, c], "mp", twin)

        total = jnp.zeros((1, model), F32)
        for c in range(chunks):
            span = slice(c * tall, (c + 1) * tall)
            pull = jnp.zeros((tall, model), F32)
            for j in range(groups):
                pull += nt(back_ref[j, span, 0:width], side_ref[j, :, width : 2 * width])
                pull += nt(back_ref[j, span, width:both], first_ref[j])
            dx, dg = normalize_back(x_ref[span, :].astype(F32), gain_ref[0:1, :], pull)
            out[span, :] = (dmiddle_ref[span, :] + dx).astype(BF16)
            total += dg
            for step in range(1, pairs):
                far(step, c).start()
            near(c).start()
        own = pltpu.make_async_copy(out, all_ref.at[me], own_sem)
        own.start()
        here[...] = gains_ref[...]
        here[0:1, :] = total
        one[me] = here[...]
        firsts = []
        for step in range(1, n_mp):
            to = lax.rem(me + step, n_mp)
            firsts.append(remote(here, one.at[me], g_send.at[step], g_recv.at[step], "mp", to))
            firsts[-1].start()
        for copy in firsts:
            copy.wait()
        total = one[0]
        for j in range(1, n_mp):
            total += one[j]
        two[place] = total

        def spread(step, there):
            return remote(two.at[place], two.at[there], h_send.at[step], h_recv.at[step], "dp", lax.rem(place + step, n))

        @pl.loop(1, n)
        def _(step):
            spread(step, place).start()

        for c in range(chunks):
            for step in range(1, pairs):
                far(step, c).wait_recv()
                onward(step, c).start()

        @pl.loop(1, n)
        def _(step):
            spread(step, place).wait_send()
            spread(step, lax.rem(place + n - step, n)).wait_recv()

        total = two[0]
        for j in range(1, n):
            total += two[j]
        sum_ref[...] = total
        for c in range(chunks):
            near(c).wait()
            for step in range(1, pairs):
                far(step, c).wait_send()
                onward(step, c).wait()
        own.wait()

    return pl.pallas_call(
        kernel,
        grid=(1,),
        in_specs=[
            pl.BlockSpec(back.shape, lambda i: (0, 0, 0)),
            pl.BlockSpec((groups, model, 2 * width), lambda i: (0, 0, spot)),
            pl.BlockSpec(first.shape, lambda i: (0, 0, 0)),
            pl.BlockSpec(x.shape, lambda i: (0, 0)),
            pl.BlockSpec(gain.shape, lambda i: (0, 0)),
            pl.BlockSpec(dmiddle.shape, lambda i: (0, 0)),
            pl.BlockSpec(gains.shape, lambda i: (0, 0)),
        ],
        out_specs=[ANY, pl.BlockSpec(gains.shape, lambda i: (0, 0))],
        out_shape=[
            jax.ShapeDtypeStruct((n_mp, share, model), BF16),
            jax.ShapeDtypeStruct(gains.shape, F32),
        ],
        scratch_shapes=[
            pltpu.VMEM((share, model), BF16),
            pltpu.VMEM(gains.shape, F32),
            pltpu.VMEM((n_mp,) + gains.shape, F32),
            pltpu.VMEM((n,) + gains.shape, F32),
            DMA((pairs, chunks)),
            DMA((pairs, chunks)),
            DMA((chunks,)),
            DMA((chunks,)),
            DMA((pairs, chunks)),
            DMA((pairs, chunks)),
            DMA,
            DMA((n_mp,)),
            DMA((n_mp,)),
            DMA((n,)),
            DMA((n,)),
        ],
        compiler_params=comm_params(4),
        name="finish",
    )(back, weights, first, x, gain, dmiddle, gains)


def per_device(
    n_dp,
    n_mp,
    tokens,
    lengths,
    norm_gain,
    w_value,
    w_out,
    w_up,
    w_down,
    synth_first,
    synth_second,
    random_table,
    cotangent,
):
    both = ("mp", "dp")
    place, rank = lax.axis_index("dp"), lax.axis_index("mp")
    total, model = tokens.shape
    share = total // n_mp
    size = total - MOST
    depth, width = w_value.shape[1], w_value.shape[2]
    hidden = w_up.shape[2]
    heads, rows, columns = random_table.shape
    near = rows == size and share % rows == 0 and n_dp in (2, 4, 6, 8)

    item_lengths = lengths[0]
    longest = jnp.argmax(item_lengths)
    start = (jnp.cumsum(item_lengths) - item_lengths)[longest]
    first = item_lengths[(longest + 1) % item_lengths.shape[0]].astype(jnp.int32).reshape(1, 1)

    gains = jnp.pad(norm_gain.reshape(4, depth).T, ((0, 0), (0, 124)))
    pack = jnp.concatenate([w_value[0], synth_first, gains], axis=1)
    table = synth_second.reshape(width, -1)
    corner = random_table[:, :, :size]
    if near:
        pack, table, corner = gather_weights([pack, table], corner.reshape(n_dp, -1, size), n_dp)
    else:
        begins = jnp.minimum(place * rows, size - rows)
        inside = (place * rows < size).astype(BF16)
        corner = lax.dynamic_update_slice(jnp.zeros((heads, size, size), BF16), corner * inside, (0, begins, 0))
        corner = lax.psum(corner, "dp")
        pack, table = lax.all_gather(pack, "dp"), lax.all_gather(table, "dp")
        table = table.transpose(1, 0, 2).reshape(width, total // size, size).transpose(1, 0, 2)
    pack = pack.reshape(model, -1)
    gain = jnp.pad(pack[:, 2 * width : 2 * width + 4].T.astype(F32), ((0, 4), (0, 0)))

    def whole(parts):
        joined = lax.all_gather(jnp.concatenate(parts, axis=1), both)
        return joined.reshape(n_mp, model, -1)

    weights_one = whole([w_up[0], w_down[0].T, w_out[0].T, w_value[1]])
    weights_two = [w_up[1], w_down[1].T, w_out[1].T, w_value[0]]

    inputs = turn(tokens, start, total)
    normed_one, values, values_t, acts, acts_t, slope = begin(inputs, pack[:, : 2 * width], gain)
    if near:
        mixed_one, lse, corner = dense_forward(first, acts, values, table, corner, n_dp, n_mp)
        corner = corner.reshape(heads, size, size)
    else:
        mixed, lse = dense_forward(first, acts, values, table)
        mixed_one = swap(mixed.reshape(n_mp, share, width), n_mp, 5)
    inputs = lax.dynamic_slice_in_dim(inputs, rank * share, share)
    *record_one, between, normed_two, parts = ends(
        inputs, mixed_one, True, weights_one, width, gain, 1, True
    )

    if near:
        values_all, mixed_two, short_t, table_lse, weights_two = table_forward(
            first, random_table, corner, parts, jnp.concatenate(weights_two, axis=1), n_dp, n_mp
        )
        weights_two = weights_two.reshape(n_mp, model, -1)
    else:
        weights_two = whole(weights_two)
        values_two = swap(parts, n_mp, 6, lanes_out=True)
        short_t = values_two[:, MOST:]
        values_all = lax.all_gather(values_two[:, :MOST], "dp")
        mixed, table_lse = random_forward(random_table, values_all)
        mixed = lax.all_to_all(mixed, "dp", 0, 0, tiled=True).transpose(1, 0, 2).reshape(width, total)
        mixed = jnp.concatenate([mixed[:, :MOST], short_forward(first, corner, short_t)], axis=1)
        mixed_two = swap(mixed, n_mp, 7, lanes_in=True)
    *record_two, result = ends(between, mixed_two, False, weights_two, width, gain, 3, False)
    early_first, _ = lax.optimization_barrier((synth_first, mixed_two))
    first_all = whole([early_first])

    grad = turn(cotangent, lax.rem(start + rank * share, total), share)
    grads_two, dmiddle, parts, dgain_two = ends_back(
        grad, mixed_two, False, weights_two, width, gain, 3, record_two
    )

    def scattered(grads, axes):
        grads = grads.reshape(-1, depth, grads.shape[-1])
        return lax.psum_scatter(grads, axes, scatter_dimension=0).astype(F32)

    if near:
        rows_upstream, dvalues, dcorner, grads_two = table_backward(
            first, random_table, corner, table_lse, short_t, parts, grads_two, n_dp, n_mp
        )
    else:
        upstream = swap(parts, n_mp, 8, lanes_out=True)
        dcorner, dshort = short_backward(first, corner, short_t, upstream[:, MOST:])
        dcorner = lax.dynamic_slice_in_dim(lax.psum(dcorner, "dp"), begins, rows, axis=1) * inside
        upstream = upstream.reshape(width, n_dp, rows).transpose(1, 0, 2)
        upstream = lax.all_to_all(upstream, "dp", 0, 0, tiled=True)
        valid = (place * rows < MOST).astype(F32).reshape(1, 1)
        dtable, dvalues = random_backward(valid, random_table, table_lse, values_all, upstream)
        dvalues = lax.psum_scatter(dvalues, "dp", scatter_dimension=0)
        dvalues = swap(jnp.concatenate([dvalues, dshort], axis=1), n_mp, 9, lanes_in=True)
        result = lax.all_gather(result, "mp")
        grads_two = scattered(grads_two, both)

    grads_one, dmiddle, parts, dgain_one = ends_back(
        dmiddle, mixed_one, True, weights_one, width, gain, 1, record_one, (between, normed_two, dvalues)
    )
    grads_one = scattered(grads_one, both)
    upstream = swap(parts, n_mp, 10).reshape(total, width)
    back_one = partial(dense_backward, first, acts, acts_t, values_t, upstream, table, lse, slope, normed_one)
    if near:
        back, entry_grad, second_grad, grads_two, result = back_one(
            grads_two.reshape(n_dp, depth, -1), result, n_dp, n_mp
        )
    else:
        back, entry_grad, second_grad = back_one()
    result = turn(result.reshape(total, model), total - start, total)
    back = back.reshape(n_mp, share, 2 * width)
    entry_grad = entry_grad.reshape(n_dp, depth, 2 * width)
    if near:
        back, entry_grad, second_grad, dcorner = last_exchange(
            back, [entry_grad, second_grad, dcorner.reshape(n_dp, -1, size)], n_dp, n_mp
        )
        dcorner = dcorner.reshape(heads, size, size)
    else:
        back = swap(back, n_mp, 11)
        entry_grad = lax.psum_scatter(entry_grad, "dp", scatter_dimension=0).astype(F32)
        second_grad = second_grad.transpose(1, 0, 2).reshape(width, n_dp, -1).transpose(1, 0, 2)
        second_grad = lax.psum_scatter(second_grad, "dp", scatter_dimension=0).astype(F32)
    gain_grad = jnp.concatenate([dgain_one[:1], dgain_one[:2], dgain_two[:1], jnp.zeros((4, model), F32)])
    input_grad, gain_grad = finish(back, weights_two, first_all, inputs, gain, dmiddle, gain_grad, n_dp, n_mp)
    input_grad = turn(input_grad.reshape(total, model), total - start, total)
    if near:
        upstream_last, _ = lax.optimization_barrier((rows_upstream, gain_grad))
        dtable = table_grad(random_table, table_lse, values_all, upstream_last, dcorner)
    else:
        dtable = dtable.at[:, :, :size].add(dcorner.astype(F32))

    gain_grad = lax.dynamic_slice_in_dim(gain_grad[:4], place * depth, depth, axis=1)
    out_at = slice(2 * hidden, 2 * hidden + width)
    return (
        result,
        input_grad,
        gain_grad.reshape(2, 2, depth),
        jnp.stack([entry_grad[:, :width], grads_one[:, 2 * hidden + width :]]),
        jnp.stack([grads_one[:, out_at].T, grads_two[:, out_at].T]),
        jnp.stack([grads_one[:, :hidden], grads_two[:, :hidden]]),
        jnp.stack([grads_one[:, hidden : 2 * hidden].T, grads_two[:, hidden : 2 * hidden].T]),
        entry_grad[:, width:],
        second_grad.reshape(heads, HD, -1),
        dtable,
    )


def solution(mesh):
    in_specs = (
        P("dp", None),
        P("dp", None),
        P(None, None, "dp"),
        P(None, "dp", "mp"),
        P(None, "mp", "dp"),
        P(None, "dp", "mp"),
        P(None, "mp", "dp"),
        P("dp", "mp"),
        P("mp", None, "dp"),
        P("mp", "dp", None),
        P("dp", None),
    )
    out_specs = (
        P("dp", None),
        P("dp", None),
        P(None, None, "dp"),
        P(None, "dp", "mp"),
        P(None, "mp", "dp"),
        P(None, "dp", "mp"),
        P(None, "mp", "dp"),
        P("dp", "mp"),
        P("mp", None, "dp"),
        P("mp", "dp", None),
    )
    return jax.shard_map(
        partial(per_device, mesh.shape["dp"], mesh.shape["mp"]),
        mesh=mesh,
        in_specs=in_specs,
        out_specs=out_specs,
        check_vma=False,
    )
```

```python
from functools import partial

import jax
import jax.numpy as jnp
from jax import lax
from jax.experimental import pallas as pl
from jax.experimental.pallas import tpu as pltpu
from jax.sharding import PartitionSpec as P

F32, BF16 = jnp.float32, jnp.bfloat16
HD = 64
MOST = 1792
TILE = 256
VMEM = 58 * 1024 * 1024


MESH = pl.DeviceIdType.MESH
ANY = pl.BlockSpec(memory_space=pl.ANY)
INTO = pl.BlockSpec(memory_space=pltpu.VMEM)
SCALAR = pl.BlockSpec(memory_space=pltpu.SMEM)
DMA = pltpu.SemaphoreType.DMA


def remote(source, target, send, recv, axis, index):
    return pltpu.make_async_remote_copy(
        src_ref=source, dst_ref=target, send_sem=send, recv_sem=recv, device_id={axis: index}, device_id_type=MESH
    )


def greet(groups):
    barrier = pltpu.get_barrier_semaphore()
    for axis, size in groups:
        me = lax.axis_index(axis)
        for step in range(1, size):
            pl.semaphore_signal(
                barrier, inc=1, device_id={axis: lax.rem(me + step, size)}, device_id_type=MESH
            )
    pl.semaphore_wait(barrier, sum(size - 1 for _, size in groups))


def greet_all(n, n_mp):
    barrier = pltpu.get_barrier_semaphore()
    me = lax.axis_index("dp") * n_mp + lax.axis_index("mp")

    @pl.loop(1, n * n_mp)
    def _(step):
        there = lax.rem(me + step, n * n_mp)
        where = {"dp": there // n_mp, "mp": lax.rem(there, n_mp)}
        pl.semaphore_signal(barrier, inc=1, device_id=where, device_id_type=MESH)

    pl.semaphore_wait(barrier, n * n_mp - 1)


def remote_to(source, target, send, recv, place, rank):
    return pltpu.make_async_remote_copy(
        src_ref=source,
        dst_ref=target,
        send_sem=send,
        recv_sem=recv,
        device_id={"dp": place, "mp": rank},
        device_id_type=MESH,
    )


def comm_params(number):
    return pltpu.CompilerParams(collective_id=number, has_side_effects=True, vmem_limit_bytes=VMEM)


class Line:
    def __init__(self, size):
        self.size, self.length = size, size // 2
        self.place = lax.axis_index("dp")
        self.at, self.side = self.place // 2, lax.rem(self.place, 2)
        self.partner = self.at * 2 + 1 - self.side
        self.right, self.left = self.place + 2, self.place - 2
        self.has_right, self.has_left = self.at + 1 < self.length, self.at > 0


class Gather:
    def __init__(self, line, pieces, use, even=False):
        self.line, self.pieces, self.use = line, pieces, use
        self.even = even and line.length == 4

    def block(self, slots, s, half=None):
        if half is None:
            return slots.at[s]
        rows = slots.shape[1] // 2
        return slots.at[s, pl.ds(half * rows, rows)]

    def push(self, piece, s, to, send, fresh=False, half=None, recv=None):
        own, slots = piece[:2]
        target = self.block(slots, s, half)
        remote(own if fresh else target, target, send, piece[4].at[s] if recv is None else recv, "dp", to).start()

    def arrived(self, piece, s, half=None, recv=None):
        target = self.block(piece[1], s, half)
        recv = piece[4].at[s] if recv is None else recv
        remote(target, target, piece[2].at[0], recv, "dp", self.line.partner).wait_recv()

    def sent(self, which, half=None):
        for piece in self.pieces:
            target = self.block(piece[1], 0, half)
            remote(target, target, which(piece), piece[4].at[0], "dp", self.line.partner).wait_send()

    def start(self, piece):
        line = self.line

        @pl.when(line.has_right)
        def _():
            self.push(piece, line.place, line.right, piece[3].at[0, line.at], fresh=True)

        @pl.when(line.has_left)
        def _():
            self.push(piece, line.place, line.left, piece[3].at[1, line.at], fresh=True)

        self.push(piece, line.place, line.partner, piece[2].at[line.at], fresh=True)

    def spared(self, a):
        at = self.line.at
        half = jnp.logical_or(jnp.logical_and(at == 0, a == 3), jnp.logical_and(at == 3, a == 0))
        none = jnp.logical_or(jnp.logical_and(at == 1, a == 0), jnp.logical_and(at == 2, a == 3))
        return jnp.logical_not(jnp.logical_or(half, none)), half

    def arrive(self, a, way):
        line = self.line
        s = a * 2 + line.side
        on, to = ((line.has_right, line.right), (line.has_left, line.left))[way]
        for piece in self.pieces:
            self.arrived(piece, s)

            @pl.when(on)
            def _():
                self.push(piece, s, to, piece[3].at[way, a])

            if self.even:
                whole, half = self.spared(a)

                @pl.when(whole)
                def _():
                    self.push(piece, s, line.partner, piece[2].at[a])

                @pl.when(half)
                def _():
                    self.push(piece, s, line.partner, piece[2].at[a], half=0)
            else:
                self.push(piece, s, line.partner, piece[2].at[a])
            piece[6](s)

    def crossed(self, a):
        line = self.line
        at = line.at
        s = a * 2 + 1 - line.side
        for piece in self.pieces:
            if self.even:
                _, half = self.spared(a)
                send, recv = piece[5].at[0], piece[5].at[1]

                @pl.when(half)
                def _():
                    self.arrived(piece, s, half=0)
                    self.arrived(piece, s, half=1, recv=recv)

                @pl.when(jnp.logical_not(half))
                def _():
                    self.arrived(piece, s)

                @pl.when(jnp.logical_and(at == 0, a == 0))
                def _():
                    self.push(piece, s, line.right, send)

                @pl.when(jnp.logical_and(at == 3, a == 3))
                def _():
                    self.push(piece, s, line.left, send)

                @pl.when(jnp.logical_and(at == 1, a == 3))
                def _():
                    self.push(piece, s, line.left, send, half=1, recv=recv)

                @pl.when(jnp.logical_and(at == 2, a == 0))
                def _():
                    self.push(piece, s, line.right, send, half=1, recv=recv)
            else:
                self.arrived(piece, s)
            piece[6](s)
        self.use(s)

    def step(self, k):
        line = self.line
        low, high = line.at - k, line.at + k

        @pl.when(low >= 0)
        def _():
            self.arrive(low, 0)

        @pl.when(high < line.length)
        def _():
            self.arrive(high, 1)

        @pl.when(low >= 0)
        def _():
            self.use(low * 2 + line.side)

        @pl.when(high < line.length)
        def _():
            self.use(high * 2 + line.side)

        @pl.when(low + 1 >= 0)
        def _():
            self.crossed(low + 1)

        @pl.when(jnp.logical_and(k > 1, high - 1 < line.length))
        def _():
            self.crossed(high - 1)

    def end(self):
        line = self.line

        @pl.loop(0, line.length)
        def _(a):
            if self.even:
                whole, half = self.spared(a)

                @pl.when(whole)
                def _():
                    self.sent(lambda piece: piece[2].at[a])

                @pl.when(half)
                def _():
                    self.sent(lambda piece: piece[2].at[a], half=0)
            else:
                self.sent(lambda piece: piece[2].at[a])

            @pl.when(jnp.logical_and(line.has_right, a <= line.at))
            def _():
                self.sent(lambda piece: piece[3].at[0, a])

            @pl.when(jnp.logical_and(line.has_left, a >= line.at))
            def _():
                self.sent(lambda piece: piece[3].at[1, a])

        if self.even:
            outer = jnp.logical_or(line.at == 0, line.at == 3)

            @pl.when(outer)
            def _():
                self.sent(lambda piece: piece[5].at[0])

            @pl.when(jnp.logical_not(outer))
            def _():
                self.sent(lambda piece: piece[5].at[0], half=1)


def line_gather(line, early, late, begin, more, use, even=False):
    gather = Gather(line, early + late, use, even)
    for piece in early:
        gather.start(piece)
    begin()
    for piece in late:
        gather.start(piece)
    more()

    @pl.loop(1, line.length + 1)
    def _(k):
        gather.step(k)

    gather.end()


def nothing(*_):
    pass


def gather_scratch(n):
    return [DMA((n // 2,)), DMA((2, n // 2)), DMA((n,)), DMA((2,))]


class Scatter:
    def __init__(self, line, items):
        self.line, self.items = line, items

    def over_x(self, item, a):
        _, _, x_out, x_in, _, _, _, send_x, recv_x = item[:9]
        return remote(x_out.at[a], x_in.at[a], send_x.at[a], recv_x.at[a], "dp", self.line.partner)

    def over_z(self, item, a, way, to=None):
        z_out, into, send, recv = item[4], item[5 + way], item[9], item[10 + way]
        return remote(z_out.at[a], into.at[a], send.at[a], recv.at[a], "dp", self.line.partner if to is None else to)

    def cross(self):
        length, at, side = self.line.length, self.line.at, self.line.side

        def one(a):
            for item in self.items:
                item[2][a] = item[0](a * 2 + 1 - side).astype(BF16)
                self.over_x(item, a).start()

        @pl.loop(0, length - 1)
        def _(step):
            k = length - 1 - step

            @pl.when(at + k < length)
            def _():
                one(at + k)

            @pl.when(at - k >= 0)
            def _():
                one(at - k)

        one(at)

    def relay(self, k):
        line = self.line
        length, at, side = line.length, line.at, line.side

        def one(a, way, behind, to):
            for item in self.items:
                make, _, _, x_in, z_out = item[:5]
                total = make(a * 2 + side)
                self.over_x(item, a).wait_recv()
                z_out[a] = (total + x_in[a].astype(F32)).astype(BF16)

                @pl.when(behind)
                def _():
                    self.over_z(item, a, way).wait_recv()
                    z_out[a] = (z_out[a].astype(F32) + item[5 + way][a].astype(F32)).astype(BF16)

                self.over_z(item, a, way, to).start()

        @pl.when(at + k < length)
        def _():
            one(at + k, 0, line.has_left, line.right)

        @pl.when(at - k >= 0)
        def _():
            one(at - k, 1, line.has_right, line.left)

    def end(self):
        line = self.line
        at = line.at
        for item in self.items:
            make, out, _, x_in, _, l_in, r_in = item[:7]
            total = make(line.place)
            self.over_x(item, at).wait_recv()
            out[...] = total + x_in[at].astype(F32)

            @pl.when(line.has_left)
            def _():
                self.over_z(item, at, 0).wait_recv()
                out[...] += l_in[at].astype(F32)

            @pl.when(line.has_right)
            def _():
                self.over_z(item, at, 1).wait_recv()
                out[...] += r_in[at].astype(F32)

        @pl.loop(0, line.length)
        def _(a):
            for item in self.items:
                self.over_x(item, a).wait_send()

            @pl.when(a != at)
            def _():
                for item in self.items:
                    self.over_z(item, a, 0).wait_send()


def line_scatter(line, items, middle):
    scatter = Scatter(line, items)
    scatter.cross()
    middle()

    @pl.loop(0, line.length - 1)
    def _(step):
        scatter.relay(line.length - 1 - step)

    scatter.end()


def scatter_scratch(n, shape):
    return [pltpu.VMEM((n // 2,) + shape, BF16)] * 5 + [DMA((n // 2,))] * 5


def gather_weights(arrays, corner, n):
    count = len(arrays)

    def kernel(*refs):
        owns, corner_ref, alls, part_ref = refs[:count], refs[count], refs[count + 1 : 2 * count + 1], refs[2 * count + 1]
        send, recv, kept_sem = refs[2 * count + 2 : 2 * count + 5]
        rest = refs[2 * count + 5 :]
        line = Line(n)
        place = line.place
        greet([("dp", n)])
        kept = [pltpu.make_async_copy(owns[i], alls[i].at[place], kept_sem.at[i]) for i in range(count)]

        def deal(s):
            return remote(corner_ref.at[s], part_ref, send.at[s], recv, "dp", s)

        def begin():
            for copy in kept:
                copy.start()

            @pl.when(place == 0)
            def _():
                @pl.loop(1, n)
                def _(s):
                    deal(s).start()

                part_ref[...] = corner_ref[0]

        pieces = [(owns[i], alls[i], *rest[4 * i : 4 * i + 4], nothing) for i in range(count)]
        line_gather(line, pieces, [], begin, nothing, nothing)
        for copy in kept:
            copy.wait()

        @pl.when(place != 0)
        def _():
            deal(0).wait_recv()

        @pl.when(place == 0)
        def _():
            @pl.loop(1, n)
            def _(s):
                deal(s).wait_send()

    return pl.pallas_call(
        kernel,
        in_specs=[ANY] * count + [INTO],
        out_specs=[ANY] * count + [INTO],
        out_shape=[jax.ShapeDtypeStruct((n,) + a.shape, a.dtype) for a in arrays]
        + [jax.ShapeDtypeStruct(corner.shape[1:], corner.dtype)],
        scratch_shapes=[DMA((n,)), DMA, DMA((count,))] + gather_scratch(n) * count,
        compiler_params=comm_params(0),
        name="gather_weights",
    )(*arrays, corner)


def swap(x, n, number, lanes_in=False, lanes_out=False):
    if lanes_in:
        block = (x.shape[0], x.shape[1] // n)
    else:
        block = x.shape[1:]
    shape = (block[0], n * block[1]) if lanes_out else (n,) + block

    def at(ref, lanes, j):
        if lanes:
            return ref.at[:, pl.ds(pl.multiple_of(j * block[1], block[1]), block[1])]
        return ref.at[j]

    def kernel(x_ref, out_ref, send, recv, own_sem):
        greet([("mp", n)])
        me = lax.axis_index("mp")
        copies = []
        for step in range(1, n):
            peer = lax.rem(me + step, n)
            copies.append(
                remote(at(x_ref, lanes_in, peer), at(out_ref, lanes_out, me), send.at[step], recv.at[step], "mp", peer)
            )
            copies[-1].start()
        own = pltpu.make_async_copy(at(x_ref, lanes_in, me), at(out_ref, lanes_out, me), own_sem)
        own.start()
        own.wait()
        for copy in copies:
            copy.wait()

    return pl.pallas_call(
        kernel,
        in_specs=[ANY],
        out_specs=ANY,
        out_shape=jax.ShapeDtypeStruct(shape, x.dtype),
        scratch_shapes=[DMA((n,)), DMA((n,)), DMA],
        compiler_params=comm_params(number),
        name="swap",
    )(x)


def table_forward(first, table, corner, parts, weights, n, n_mp):
    heads, rows, columns = table.shape
    _, width, share = parts.shape
    tokens = share * n_mp
    size = tokens - MOST
    owners = MOST // rows
    chunks = share // rows
    pairs = n_mp // 2

    def kernel(first_ref, table_ref, corner_ref, parts_ref, weights_ref, values_ref, mixed_ref, short_ref, lse_ref,
               all_ref, own, soft, sums, short_sum, v_send, v_recv, send_x, send_z, recv, more, send_m, recv_m, send_s,
               w_send_x, w_send_z, w_recv, w_more, w_own, far_send, far_recv, near_send, near_recv, on_send, on_recv):
        line = Line(n)
        place, me = line.place, lax.axis_index("mp")
        pair, core = me // 2, lax.rem(me, 2)
        twin = pair * 2 + 1 - core
        owner = place < owners
        greet_all(n, n_mp)

        def lanes(j):
            return own.at[:, pl.ds(pl.multiple_of(j * share, share), share)]

        gets = []
        for step in range(1, n_mp):
            peer = lax.rem(me + step, n_mp)
            gets.append(remote(parts_ref.at[peer], lanes(me), v_send.at[step], v_recv.at[step], "mp", peer))
        keep = pltpu.make_async_copy(weights_ref, all_ref.at[me, place], w_own)

        def prepare():
            offer(place, weights_ref)
            keep.start()
            own[:, pl.ds(pl.multiple_of(me * share, share), share)] = parts_ref[me]
            for copy in gets:
                copy.wait()
            values_ref[place] = own[:, 0:MOST]

        def over(step, s, source):
            to = lax.rem(pair + step, pairs) * 2 + core
            return remote(source, all_ref.at[me, s], far_send.at[step, s], far_recv.at[step, s], "mp", to)

        def across(s, source):
            return remote(source, all_ref.at[me, s], near_send.at[s], near_recv.at[s], "mp", twin)

        def onward(step, s):
            block = lax.rem(pair + pairs - step, pairs) * 2 + core
            return remote(
                all_ref.at[block, s], all_ref.at[block, s], on_send.at[step, s], on_recv.at[step, s], "mp", twin
            )

        def offer(s, source):
            for step in range(1, pairs):
                over(step, s, source).start()
            across(s, source).start()

        def product(s):
            for head in range(heads):
                span = slice(head * HD, (head + 1) * HD)
                sums[s, span, :] = nt(values_ref[s, span, :], soft[head]).astype(BF16)

        here = jnp.logical_and(owner, place // chunks == me)

        def back(s):
            return remote_to(
                sums.at[s],
                mixed_ref.at[me, lax.rem(place, chunks)],
                send_m.at[s],
                recv_m.at[me, lax.rem(place, chunks)],
                s,
                place // chunks,
            )

        def short_back():
            return remote(
                short_sum,
                mixed_ref.at[me, owners % chunks],
                send_s,
                recv_m.at[me, owners % chunks],
                "mp",
                owners // chunks,
            )

        def begin():
            short_ref[...] = own[:, MOST:tokens]
            for head in range(heads):
                scores = table_ref[head, :, 0:MOST].astype(F32)
                top = jnp.max(scores, axis=1, keepdims=True)
                powers = jnp.exp(scores - top)
                total = jnp.sum(powers, axis=1, keepdims=True)
                soft[head] = (powers / total).astype(BF16)
                lse_ref[head] = jnp.broadcast_to(top + jnp.log(total), (rows, 128))
            early, inside, shift, at = small_masks(first_ref[0, 0], size)
            for head in range(heads):
                span = slice(head * HD, (head + 1) * HD)
                weighed = by_token(masked_soft(nn(at, corner_ref[head]), inside), early, shift)
                short_sum[span, :] = nt(own[span, MOST:tokens], weighed).astype(BF16)

            @pl.when(me == owners // chunks)
            def _():
                mixed_ref[me, owners % chunks] = short_sum[...]

            @pl.when(me != owners // chunks)
            def _():
                short_back().start()

            @pl.when(owner)
            def _():
                product(place)

            @pl.when(here)
            def _():
                mixed_ref[me, lax.rem(place, chunks)] = sums[place]

            @pl.when(jnp.logical_and(owner, jnp.logical_not(here)))
            def _():
                back(place).start()

        def use(s):
            @pl.when(owner)
            def _():
                product(s)
                back(s).start()

        for copy in gets:
            copy.start()
        line_gather(
            line,
            [(weights_ref, all_ref.at[me], w_send_x, w_send_z, w_recv, w_more, lambda s: offer(s, all_ref.at[me, s]))],
            [(values_ref.at[place], values_ref, send_x, send_z, recv, more, nothing)],
            prepare,
            begin,
            use,
            even=True,
        )

        @pl.loop(0, n)
        def _(s):
            for step in range(1, pairs):
                over(step, s, weights_ref).wait_recv()
                onward(step, s).start()

        @pl.loop(0, n)
        def _(s):
            @pl.when(jnp.logical_and(owner, jnp.logical_or(s != place, jnp.logical_not(here))))
            def _():
                back(s).wait_send()

            across(s, weights_ref).wait()
            for step in range(1, pairs):
                over(step, s, weights_ref).wait_send()
                onward(step, s).wait()

        @pl.when(me != owners // chunks)
        def _():
            short_back().wait_send()

        for c in range(chunks):
            d = me * chunks + c
            for g in range(n_mp):
                source = jnp.where(d < owners, d, place)

                @pl.when(jnp.logical_not(jnp.logical_and(source == place, g == me)))
                def _():
                    remote(short_sum, mixed_ref.at[g, c], send_s, recv_m.at[g, c], "mp", twin).wait_recv()

        keep.wait()

    return pl.pallas_call(
        kernel,
        in_specs=[SCALAR, INTO, INTO, INTO, ANY],
        out_specs=[INTO, INTO, INTO, INTO, ANY],
        out_shape=[
            jax.ShapeDtypeStruct((n, width, MOST), BF16),
            jax.ShapeDtypeStruct((n_mp, chunks, width, rows), BF16),
            jax.ShapeDtypeStruct((width, size), BF16),
            jax.ShapeDtypeStruct((heads, rows, 128), F32),
            jax.ShapeDtypeStruct((n_mp, n) + weights.shape, BF16),
        ],
        scratch_shapes=[
            pltpu.VMEM((width, tokens), BF16),
            pltpu.VMEM((heads, rows, MOST), BF16),
            pltpu.VMEM((n, width, rows), BF16),
            pltpu.VMEM((width, rows), BF16),
            DMA((n_mp,)),
            DMA((n_mp,)),
            *gather_scratch(n),
            DMA((n,)),
            DMA((n_mp, chunks)),
            DMA,
            *gather_scratch(n),
            DMA,
            DMA((pairs, n)),
            DMA((pairs, n)),
            DMA((n,)),
            DMA((n,)),
            DMA((pairs, n)),
            DMA((pairs, n)),
        ],
        compiler_params=comm_params(1),
        name="table_forward",
    )(first, table, corner, parts, weights)


def spread_mp(x_ref, all_ref, send, recv, own_sem, n):
    me, pairs = lax.axis_index("mp"), n // 2
    pair, core = me // 2, lax.rem(me, 2)
    twin = pair * 2 + 1 - core
    own = pltpu.make_async_copy(x_ref, all_ref.at[me], own_sem)
    near = remote(x_ref, all_ref.at[me], send.at[0], recv.at[0], "mp", twin)

    def far(step):
        to = lax.rem(pair + step, pairs) * 2 + core
        return remote(x_ref, all_ref.at[me], send.at[step], recv.at[step], "mp", to)

    def onward(step):
        source = lax.rem(pair + pairs - step, pairs) * 2 + core
        return remote(
            all_ref.at[source], all_ref.at[source], send.at[pairs + step], recv.at[pairs + step], "mp", twin
        )

    def start():
        for step in range(1, pairs):
            far(step).start()
        near.start()
        own.start()

    def relay():
        for step in range(1, pairs):
            far(step).wait_recv()
            onward(step).start()

    def end():
        for step in range(1, pairs):
            far(step).wait_send()
            onward(step).wait()
        near.wait()
        own.wait()

    return start, relay, end


def blend_mp(x_ref, out_refs, kept, twins, others, local, near_send, near_recv, far_send, far_recv, n):
    me, pairs = lax.axis_index("mp"), n // 2
    pair, core = me // 2, lax.rem(me, 2)
    twin = pair * 2 + 1 - core
    rows = x_ref.shape[1]
    chunk = rows // 6

    def keep(p):
        return pltpu.make_async_copy(x_ref.at[p * 2 + core], kept.at[p], local.at[p])

    def give(p):
        return remote(x_ref.at[p * 2 + 1 - core], twins.at[p], near_send.at[p], near_recv.at[p], "mp", twin)

    def pass_on(step):
        to = lax.rem(pair + step, pairs)
        return remote(
            kept.at[to], others.at[step - 1], far_send.at[step], far_recv.at[step], "mp", to * 2 + core
        )

    def over_rows(body):
        @pl.loop(0, rows // chunk)
        def _(i):
            body(pl.ds(pl.multiple_of(i * chunk, chunk), chunk))

    def start():
        for step in range(1, pairs + 1):
            p = lax.rem(pair + step, pairs)
            give(p).start()
            keep(p).start()

    def go_on():
        for step in range(1, pairs):
            p = lax.rem(pair + step, pairs)
            keep(p).wait()
            give(p).wait_recv()

            def body(at):
                kept[p, at, :] = (kept[p, at, :].astype(F32) + twins[p, at, :].astype(F32)).astype(BF16)

            over_rows(body)
            pass_on(step).start()

    def end():
        keep(pair).wait()
        give(pair).wait_recv()
        for step in range(1, pairs):
            pass_on(step).wait_recv()

        def body(at):
            total = kept[pair, at, :].astype(F32) + twins[pair, at, :].astype(F32)
            for j in range(pairs - 1):
                total += others[j, at, :].astype(F32)
            spot = 0
            for ref in out_refs:
                ref[at, :] = total[:, spot : spot + ref.shape[1]].astype(BF16)
                spot += ref.shape[1]

        over_rows(body)
        for p in range(pairs):
            give(p).wait_send()
        for step in range(1, pairs):
            pass_on(step).wait_send()

    return start, go_on, end


def blend_scratch(n, shape):
    pairs = n // 2
    return [
        pltpu.VMEM((pairs,) + shape, BF16),
        pltpu.VMEM((pairs,) + shape, BF16),
        pltpu.VMEM((pairs - 1,) + shape, BF16),
    ] + [DMA((pairs,))] * 5


def table_backward(first, table, corner, lse, short_t, parts, grads, n, n_mp):
    heads, rows, columns = table.shape
    width, size = short_t.shape
    owners = MOST // rows
    _, chunks, _, _ = parts.shape
    share = chunks * rows

    def kernel(first_ref, table_ref, corner_ref, lse_ref, short_ref, parts_ref, grads_ref, ups, got_ref, dcorner_ref,
               blended_ref, full, short_up, total, soft, send_u, recv_u, recv_s, v_send, v_recv, *rest):
        line = Line(n)
        place, me = line.place, lax.axis_index("mp")
        owner = place < owners
        greet_all(n, n_mp)
        blend, go_on, blended = blend_mp(grads_ref, [blended_ref], *rest[10:], n_mp)

        def hand(g, c):
            return remote_to(
                parts_ref.at[g, c], ups.at[place], send_u.at[g, c], recv_u.at[place], me * chunks + c, g
            )

        def hand_short(g, c):
            return remote_to(parts_ref.at[g, c], short_up, send_u.at[g, c], recv_s, place, g)

        def each_hand(act):
            for c in range(chunks):
                d = me * chunks + c
                for g in range(n_mp):
                    @pl.when(jnp.logical_and(d < owners, jnp.logical_not(jnp.logical_and(d == place, g == me))))
                    def _():
                        act(hand(g, c))

                    @pl.when(jnp.logical_and(d == owners, g != me))
                    def _():
                        act(hand_short(g, c))

        each_hand(lambda copy: copy.start())
        blend()

        @pl.when(jnp.logical_and(owner, place // chunks == me))
        def _():
            ups[place] = parts_ref[me, lax.rem(place, chunks)]

        @pl.when(me == owners // chunks)
        def _():
            short_up[...] = parts_ref[me, owners % chunks]

        for head in range(heads):
            soft[head] = jnp.exp(table_ref[head, :, 0:MOST].astype(F32) - lse_ref[head, :, 0:1]).astype(BF16)

        @pl.when(me != owners // chunks)
        def _():
            hand_short(0, 0).wait_recv()

        early, inside, shift, at = small_masks(first_ref[0, 0], size)
        for head in range(heads):
            span = slice(head * HD, (head + 1) * HD)
            weights = masked_soft(nn(at, corner_ref[head]), inside)
            here, up = short_ref[span, :], short_up[span, :]
            moved = nt(here, shift).astype(BF16)
            dsoft = jnp.where(early, tn(up, here), tn(up, moved))
            full[span, MOST : MOST + size] = nn(up, by_token(weights, early, shift)).astype(BF16)
            centre = jnp.sum(weights * dsoft, axis=1, keepdims=True)
            dcorner_ref[head] = tn(at, (weights * (dsoft - centre)).astype(BF16)).astype(BF16)

        def make(s):
            @pl.when(jnp.logical_and(owner, jnp.logical_not(jnp.logical_and(s == place, place // chunks == me))))
            def _():
                remote(short_up, ups.at[s], send_u.at[0, 0], recv_u.at[s], "dp", line.partner).wait_recv()

            @pl.when(jnp.logical_not(owner))
            def _():
                ups[s] = jnp.zeros((width, rows), BF16)

            return jnp.concatenate(
                [nn(ups[s, head * HD : (head + 1) * HD, :], soft[head]) for head in range(heads)], axis=0
            )

        line_scatter(line, [(make, total, *rest[:10])], go_on)
        full[:, 0:MOST] = total[...].astype(BF16)

        def lanes(j):
            return full.at[:, pl.ds(pl.multiple_of(j * share, share), share)]

        gives = []
        for step in range(1, n_mp):
            peer = lax.rem(me + step, n_mp)
            gives.append(remote(lanes(peer), got_ref.at[me], v_send.at[step], v_recv.at[step], "mp", peer))
            gives[-1].start()
        got_ref[me] = full[:, pl.ds(pl.multiple_of(me * share, share), share)]
        blended()
        each_hand(lambda copy: copy.wait_send())
        for copy in gives:
            copy.wait()

    return pl.pallas_call(
        kernel,
        in_specs=[SCALAR] + [INTO] * 5 + [ANY],
        out_specs=[INTO] * 4,
        out_shape=[
            jax.ShapeDtypeStruct((n, width, rows), BF16),
            jax.ShapeDtypeStruct((n_mp, width, share), BF16),
            jax.ShapeDtypeStruct((heads, size, size), BF16),
            jax.ShapeDtypeStruct(grads.shape[1:], BF16),
        ],
        scratch_shapes=[
            pltpu.VMEM((width, share * n_mp), BF16),
            pltpu.VMEM((width, rows), BF16),
            pltpu.VMEM((width, MOST), F32),
            pltpu.VMEM((heads, rows, MOST), BF16),
            DMA((n_mp, chunks)),
            DMA((n,)),
            DMA,
            DMA((n_mp,)),
            DMA((n_mp,)),
        ]
        + scatter_scratch(n, (width, MOST))
        + blend_scratch(n_mp, grads.shape[1:]),
        compiler_params=comm_params(2),
        name="table_backward",
    )(first, table, corner, lse, short_t, parts, grads)


def last_exchange(back, grads, n, n_mp):
    count = len(grads)

    def kernel(*refs):
        back_ref, grad_refs = refs[0], refs[1 : 1 + count]
        got_ref, out_refs = refs[1 + count], refs[2 + count : 2 + 2 * count]
        send, recv, own_sem, part, part_send, part_recv, last = refs[2 + 2 * count : 9 + 2 * count]
        rest = refs[9 + 2 * count :]
        line = Line(n)
        place, me = line.place, lax.axis_index("mp")
        greet([("dp", n), ("mp", n_mp)])
        copies = []
        for step in range(1, n_mp):
            peer = lax.rem(me + step, n_mp)
            copies.append(
                remote(back_ref.at[peer], got_ref.at[me], send.at[step], recv.at[step], "mp", peer)
            )
            copies[-1].start()
        own = pltpu.make_async_copy(back_ref.at[me], got_ref.at[me], own_sem)
        own.start()
        outs = [*out_refs[: count - 1], last]
        items = [
            (lambda s, ref=grad_refs[i]: ref[s].astype(F32), outs[i], *rest[10 * i : 10 * i + 10])
            for i in range(count)
        ]
        line_scatter(line, items, nothing)
        part[...] = last[...].astype(BF16)

        def hand(s):
            return remote(part, out_refs[-1].at[s], part_send, part_recv.at[s], "dp", 0)

        @pl.when(place != 0)
        def _():
            hand(place).start()
            hand(place).wait_send()

        @pl.when(place == 0)
        def _():
            out_refs[-1][0] = part[...]

            @pl.loop(1, n)
            def _(s):
                hand(s).wait_recv()

        @pl.when(place != 0)
        def _():
            out_refs[-1][...] = jnp.zeros_like(out_refs[-1])

        own.wait()
        for copy in copies:
            copy.wait()

    return pl.pallas_call(
        kernel,
        in_specs=[ANY] + [INTO] * count,
        out_specs=[ANY] + [INTO] * count,
        out_shape=[jax.ShapeDtypeStruct(back.shape, BF16)]
        + [jax.ShapeDtypeStruct(g.shape[1:], F32) for g in grads[:-1]]
        + [jax.ShapeDtypeStruct(grads[-1].shape, BF16)],
        scratch_shapes=[DMA((n_mp,)), DMA((n_mp,)), DMA]
        + [pltpu.VMEM(grads[-1].shape[1:], BF16), DMA, DMA((n,)), pltpu.VMEM(grads[-1].shape[1:], F32)]
        + [each for g in grads for each in scatter_scratch(n, g.shape[1:])],
        compiler_params=comm_params(3),
        name="last_exchange",
    )(back, *grads)


def nn(a, b):
    return lax.dot_general(a, b, (((1,), (0,)), ((), ())), preferred_element_type=F32)


def nt(a, b):
    return lax.dot_general(a, b, (((1,), (1,)), ((), ())), preferred_element_type=F32)


def tn(a, b):
    return lax.dot_general(a, b, (((0,), (0,)), ((), ())), preferred_element_type=F32)


def small_masks(first, size):
    row = lax.broadcasted_iota(jnp.int32, (size, size), 0)
    col = lax.broadcasted_iota(jnp.int32, (size, size), 1)
    early = row < first
    inside = col < jnp.where(early, first, size - first)
    shift = jnp.where(col == row + first, 1.0, 0.0).astype(BF16)
    rows = jnp.where(col == jnp.where(early, row, row - first), 1.0, 0.0).astype(BF16)
    return early, inside, shift, rows


def masked_soft(scores, inside):
    masked = jnp.where(inside, scores, -1e30)
    powers = jnp.where(inside, jnp.exp(masked - jnp.max(masked, axis=1, keepdims=True)), 0.0)
    return powers / jnp.sum(powers, axis=1, keepdims=True)


def by_token(soft, early, shift):
    low = soft.astype(BF16)
    zero = jnp.zeros_like(low)
    late = nn(jnp.where(early, zero, low), shift).astype(BF16)
    return jnp.where(early, low, zero) + late


def dense_forward(first, acts, values, table, part=None, n=None, n_mp=None):
    busy = part is not None
    tokens, width = acts.shape
    heads = width // HD
    tiles = MOST // TILE
    size = tokens - MOST
    columns = table.shape[2]
    blocks = MOST // columns

    def kernel(first_ref, acts_ref, values_ref, table_ref, *refs):
        tile = pl.program_id(0)
        if busy:
            part_ref, got_ref, lse_ref, all_ref, out_ref, give_send, give_recv, own_sem, *rest = refs
            line = Line(n)
            me = lax.axis_index("mp")
            share = tokens // n_mp
            piece = (part_ref, all_ref, *rest, nothing)
            gather = Gather(line, [piece], nothing)

            @pl.when(tile == 0)
            def _():
                pltpu.make_async_copy(part_ref, all_ref.at[line.place], own_sem.at[0]).start()
                greet([("dp", n), ("mp", n_mp)])
                gather.start(piece)

            for k in range(1, line.length + 1):
                @pl.when(tile == min(2 * k, tiles))
                def _():
                    gather.step(k)

            def give(j):
                rows = out_ref.at[pl.ds(j * share, share)]
                return remote(rows, got_ref.at[me], give_send.at[j], give_recv.at[me], "mp", j)

            def keep():
                rows = out_ref.at[pl.ds(pl.multiple_of(me * share, share), share)]
                return pltpu.make_async_copy(rows, got_ref.at[me], own_sem.at[1])

            def put(rows):
                out_ref[pl.ds(pl.multiple_of(tile * TILE, TILE), TILE), :] = rows
                for j in range(n_mp):
                    done = tile == (j + 1) * share // TILE - 1

                    @pl.when(jnp.logical_and(done, me == j))
                    def _():
                        keep().start()

                    @pl.when(jnp.logical_and(done, me != j))
                    def _():
                        give(j).start()
        else:
            out_ref, lse_ref = refs

            def put(rows):
                out_ref[...] = rows
        lane = lax.broadcasted_iota(jnp.int32, (TILE, 128), 1)

        def scored(span, number):
            parts = [nn(acts_ref[:, span], table_ref[b, span, :]) for b in range(number)]
            return jnp.concatenate(parts, axis=1)

        @pl.when(tile < tiles)
        def _():
            lse = jnp.zeros((TILE, 128), F32)
            parts = []
            spans = [slice(head * HD, (head + 1) * HD) for head in range(heads)]
            ahead = scored(spans[0], blocks)
            for head in range(heads):
                scores = ahead
                if head + 1 < heads:
                    ahead = scored(spans[head + 1], blocks)
                top = jnp.max(scores, axis=1, keepdims=True)
                powers = jnp.exp(scores - top)
                total = jnp.sum(powers, axis=1, keepdims=True)
                mixed = nn(powers.astype(BF16), values_ref[0:MOST, spans[head]])
                parts.append((mixed / total).astype(BF16))
                lse = jnp.where(lane == head, top + jnp.log(total), lse)
            put(jnp.concatenate(parts, axis=1))
            lse_ref[...] = lse

        @pl.when(tile == tiles)
        def _():
            early, inside, shift, _ = small_masks(first_ref[0, 0], size)
            parts = []
            for head in range(heads):
                span = slice(head * HD, (head + 1) * HD)
                soft = by_token(masked_soft(scored(span, size // columns), inside), early, shift)
                parts.append(nn(soft, values_ref[MOST:tokens, span]).astype(BF16))
            put(jnp.concatenate(parts, axis=1))
            lse_ref[...] = jnp.zeros((TILE, 128), F32)
            if busy:
                gather.end()
                keep().wait()
                pltpu.make_async_copy(part_ref, all_ref.at[line.place], own_sem.at[0]).wait()
                for j in range(n_mp):
                    @pl.when(me != j)
                    def _():
                        give(j).wait_send()
                        remote(out_ref.at[0:share], got_ref.at[j], give_send.at[j], give_recv.at[j], "mp", j).wait_recv()

    return pl.pallas_call(
        kernel,
        grid=(tiles + 1,),
        in_specs=[
            pl.BlockSpec(memory_space=pltpu.SMEM),
            pl.BlockSpec((TILE, width), lambda t: (t, 0)),
            pl.BlockSpec((tokens, width), lambda t: (0, 0)),
            pl.BlockSpec(table.shape, lambda t: (0, 0, 0)),
        ]
        + [ANY] * busy,
        out_specs=[
            ANY if busy else pl.BlockSpec((TILE, width), lambda t: (t, 0)),
            pl.BlockSpec((TILE, 128), lambda t: (t, 0)),
        ]
        + [ANY] * busy,
        out_shape=[
            jax.ShapeDtypeStruct((n_mp, tokens // n_mp, width) if busy else (tokens, width), BF16),
            jax.ShapeDtypeStruct((tokens, 128), F32),
        ]
        + ([jax.ShapeDtypeStruct((n,) + part.shape, part.dtype)] if busy else []),
        scratch_shapes=[pltpu.VMEM((tokens, width), BF16), DMA((n_mp,)), DMA((n_mp,)), DMA((2,))] + gather_scratch(n) if busy else [],
        compiler_params=comm_params(8) if busy else pltpu.CompilerParams(vmem_limit_bytes=VMEM),
        cost_estimate=pl.CostEstimate(flops=12 * tokens * tokens * width, bytes_accessed=8 * tokens * width, transcendentals=0),
        name="dense_forward",
    )(first, acts, values, table, *([part] if busy else []))


def dense_backward(first, acts, acts_t, values_t, upstream, table, lse, slope, normed, parts=None, give=None, n=None, n_mp=None):
    busy = parts is not None
    tokens, width = acts.shape
    model = normed.shape[1]
    heads = width // HD
    tiles = MOST // TILE
    size = tokens - MOST
    columns = table.shape[2]
    blocks = MOST // columns

    def kernel(first_ref, acts_ref, acts_t_ref, values_t_ref, up_ref, table_ref, lse_ref, slope_ref, normed_ref, *refs):
        tile = pl.program_id(0)
        if busy:
            parts_ref, give_ref, back_ref, dweights_ref, dtable_ref, part_ref, all_ref = refs[:7]
            dv_acc, dt_acc, dpre, send, recv, own_sem, *rest = refs[7:]
            line = Line(n)
            scatter = Scatter(line, [(lambda s: parts_ref[s].astype(F32), part_ref, *rest)])
            start, relay, end = spread_mp(give_ref, all_ref, send, recv, own_sem, n_mp)

            @pl.when(tile == 0)
            def _():
                greet([("dp", n), ("mp", n_mp)])
                start()
                scatter.cross()

            for k in range(line.length - 1, 0, -1):
                @pl.when(tile == 2 * (line.length - k))
                def _():
                    scatter.relay(k)

            @pl.when(tile == 5)
            def _():
                relay()
        else:
            back_ref, dweights_ref, dtable_ref, dv_acc, dt_acc, dpre = refs

        @pl.when(tile == 0)
        def _():
            dv_acc[...] = jnp.zeros_like(dv_acc)
            dt_acc[...] = jnp.zeros_like(dt_acc)

        def scored(span, number):
            parts = [nn(acts_ref[:, span], table_ref[b, span, :]) for b in range(number)]
            return jnp.concatenate(parts, axis=1)

        def spread(span, dscores, number):
            total = 0.0
            for b in range(number):
                part = dscores[:, b * columns : (b + 1) * columns]
                dt_acc[b, span, :] += nn(acts_t_ref[span, :], part)
                total += nt(part, table_ref[b, span, :])
            return total

        def keep(parts):
            slopes = slope_ref[...].astype(F32)
            rows = pl.ds(pl.multiple_of(tile * TILE, TILE), TILE)
            dpre[rows, :] = (slopes * jnp.concatenate(parts, axis=1)).astype(BF16)

        @pl.when(tile < tiles)
        def _():
            parts = []
            up_t = up_ref[...].T
            spans = [slice(head * HD, (head + 1) * HD) for head in range(heads)]

            def made(span):
                return scored(span, blocks), nn(up_ref[:, span], values_t_ref[span, 0:MOST])

            ahead = made(spans[0])
            for head in range(heads):
                span = spans[head]
                scores, dsoft = ahead
                if head + 1 < heads:
                    ahead = made(spans[head + 1])
                soft = jnp.exp(scores - lse_ref[:, head : head + 1])
                dv_acc[span, 0:MOST] += nn(up_t[span, :], soft.astype(BF16))
                weighed = soft * dsoft
                centre = jnp.sum(weighed, axis=1, keepdims=True)
                parts.append(spread(span, (soft * (dsoft - centre)).astype(BF16), blocks))
            keep(parts)

        @pl.when(tile == tiles)
        def _():
            early, inside, shift, _ = small_masks(first_ref[0, 0], size)
            parts = []
            up_t = up_ref[...].T
            for head in range(heads):
                span = slice(head * HD, (head + 1) * HD)
                soft = masked_soft(scored(span, size // columns), inside)
                here = values_t_ref[span, MOST:tokens]
                moved = nt(here, shift).astype(BF16)
                dsoft = jnp.where(early, nn(up_ref[:, span], here), nn(up_ref[:, span], moved))
                dv_acc[span, MOST:tokens] = nn(up_t[span, :], by_token(soft, early, shift))
                centre = jnp.sum(soft * dsoft, axis=1, keepdims=True)
                parts.append(spread(span, (soft * (dsoft - centre)).astype(BF16), size // columns))
            keep(parts)
            dvalues_t = dv_acc[...].astype(BF16)
            back_ref[:, 0:width] = dvalues_t.T
            back_ref[:, width:] = dpre[...]
            value_grad = nn(dvalues_t, normed_ref[...])
            first_grad = nn(dpre[...].T, normed_ref[...])
            dweights_ref[:, 0:width] = value_grad.T.astype(BF16)
            dweights_ref[:, width:] = first_grad.T.astype(BF16)
            dtable_ref[...] = dt_acc[...].astype(BF16)
            if busy:
                scatter.end()
                end()

    whole = lambda t: (0, 0)
    rows = lambda t: (t, 0)
    return pl.pallas_call(
        kernel,
        grid=(tiles + 1,),
        in_specs=[
            pl.BlockSpec(memory_space=pltpu.SMEM),
            pl.BlockSpec((TILE, width), rows),
            pl.BlockSpec((width, TILE), lambda t: (0, t)),
            pl.BlockSpec((width, tokens), whole),
            pl.BlockSpec((TILE, width), rows),
            pl.BlockSpec(table.shape, lambda t: (0, 0, 0)),
            pl.BlockSpec((TILE, 128), rows),
            pl.BlockSpec((TILE, width), rows),
            pl.BlockSpec((tokens, model), whole),
        ]
        + [INTO, ANY] * busy,
        out_specs=[
            pl.BlockSpec((tokens, 2 * width), whole),
            pl.BlockSpec((model, 2 * width), whole),
            pl.BlockSpec(table.shape, lambda t: (0, 0, 0)),
        ]
        + [INTO, ANY] * busy,
        out_shape=[
            jax.ShapeDtypeStruct((tokens, 2 * width), BF16),
            jax.ShapeDtypeStruct((model, 2 * width), BF16),
            jax.ShapeDtypeStruct(table.shape, BF16),
        ]
        + (
            [
                jax.ShapeDtypeStruct(parts.shape[1:], F32),
                jax.ShapeDtypeStruct((n_mp,) + give.shape, give.dtype),
            ]
            if busy
            else []
        ),
        scratch_shapes=[
            pltpu.VMEM((width, tokens), F32),
            pltpu.VMEM(table.shape, F32),
            pltpu.VMEM((tokens, width), BF16),
        ]
        + ([DMA((n_mp,)), DMA((n_mp,)), DMA] + scatter_scratch(n, parts.shape[1:]) if busy else []),
        compiler_params=comm_params(9) if busy else pltpu.CompilerParams(vmem_limit_bytes=VMEM),
        cost_estimate=pl.CostEstimate(flops=24 * tokens * tokens * width, bytes_accessed=16 * tokens * width, transcendentals=0),
        name="dense_backward",
    )(first, acts, acts_t, values_t, upstream, table, lse, slope, normed, *([parts, give] if busy else []))


def random_forward(table, values_t):
    heads, rows, _ = table.shape
    slots, width, _ = values_t.shape

    def kernel(table_ref, values_ref, out_ref, lse_ref):
        scores = table_ref[0, :, 0:MOST].astype(F32)
        top = jnp.max(scores, axis=1, keepdims=True)
        powers = jnp.exp(scores - top)
        total = jnp.sum(powers, axis=1, keepdims=True)
        soft = (powers / total).astype(BF16)
        values = values_ref[...].reshape(slots * HD, MOST)
        out_ref[...] = nt(values, soft).astype(BF16).reshape(slots, HD, rows)
        lse_ref[...] = jnp.broadcast_to(top + jnp.log(total), (1, rows, 128))

    return pl.pallas_call(
        kernel,
        grid=(heads,),
        in_specs=[
            pl.BlockSpec((1, rows, table.shape[2]), lambda h: (h, 0, 0)),
            pl.BlockSpec((slots, HD, MOST), lambda h: (0, h, 0)),
        ],
        out_specs=[
            pl.BlockSpec((slots, HD, rows), lambda h: (0, h, 0)),
            pl.BlockSpec((1, rows, 128), lambda h: (h, 0, 0)),
        ],
        out_shape=[
            jax.ShapeDtypeStruct((slots, width, rows), BF16),
            jax.ShapeDtypeStruct((heads, rows, 128), F32),
        ],
        compiler_params=pltpu.CompilerParams(vmem_limit_bytes=VMEM),
        name="random_forward",
    )(table, values_t)


def random_backward(valid, table, lse, values_t, upstream_t):
    heads, rows, columns = table.shape
    slots, width, _ = values_t.shape
    buffers = pl.Buffered(2 if slots <= 16 else 1)

    def kernel(valid_ref, table_ref, lse_ref, values_ref, up_ref, dtable_ref, dvalues_ref):
        soft = jnp.exp(table_ref[0, :, 0:MOST].astype(F32) - lse_ref[0, :, 0:1])
        up = up_ref[...].reshape(slots * HD, rows) * valid_ref[0, 0].astype(BF16)
        values = values_ref[...].reshape(slots * HD, MOST)
        dsoft = tn(up, values)
        weighed = soft * dsoft
        centre = jnp.sum(weighed, axis=1, keepdims=True)
        dtable_ref[0, :, 0:MOST] = weighed - soft * centre
        dtable_ref[0, :, MOST:columns] = jnp.zeros((rows, columns - MOST), F32)
        dvalues_ref[...] = nn(up, soft.astype(BF16)).astype(BF16).reshape(slots, HD, MOST)

    return pl.pallas_call(
        kernel,
        grid=(heads,),
        in_specs=[
            pl.BlockSpec(memory_space=pltpu.SMEM),
            pl.BlockSpec((1, rows, columns), lambda h: (h, 0, 0)),
            pl.BlockSpec((1, rows, 128), lambda h: (h, 0, 0)),
            pl.BlockSpec((slots, HD, MOST), lambda h: (0, h, 0), pipeline_mode=buffers),
            pl.BlockSpec((slots, HD, rows), lambda h: (0, h, 0)),
        ],
        out_specs=[
            pl.BlockSpec((1, rows, columns), lambda h: (h, 0, 0)),
            pl.BlockSpec((slots, HD, MOST), lambda h: (0, h, 0)),
        ],
        out_shape=[
            jax.ShapeDtypeStruct((heads, rows, columns), F32),
            jax.ShapeDtypeStruct((slots, width, MOST), BF16),
        ],
        compiler_params=pltpu.CompilerParams(vmem_limit_bytes=VMEM),
        name="random_backward",
    )(valid, table, lse, values_t, upstream_t)


def short_forward(first, corner, values_t):
    heads, size, _ = corner.shape
    width = values_t.shape[0]

    def kernel(first_ref, corner_ref, values_ref, out_ref):
        early, inside, shift, rows = small_masks(first_ref[0, 0], size)
        for head in range(heads):
            span = slice(head * HD, (head + 1) * HD)
            soft = by_token(masked_soft(nn(rows, corner_ref[head]), inside), early, shift)
            out_ref[span, :] = nt(values_ref[span, :], soft).astype(BF16)

    return pl.pallas_call(
        kernel,
        in_specs=[
            pl.BlockSpec(memory_space=pltpu.SMEM),
            pl.BlockSpec(memory_space=pltpu.VMEM),
            pl.BlockSpec(memory_space=pltpu.VMEM),
        ],
        out_specs=pl.BlockSpec(memory_space=pltpu.VMEM),
        out_shape=jax.ShapeDtypeStruct((width, size), BF16),
        name="short_forward",
    )(first, corner, values_t)


def short_backward(first, corner, values_t, upstream_t):
    heads, size, _ = corner.shape
    width = values_t.shape[0]

    def kernel(first_ref, corner_ref, values_ref, up_ref, dcorner_ref, dvalues_ref):
        early, inside, shift, rows = small_masks(first_ref[0, 0], size)
        for head in range(heads):
            span = slice(head * HD, (head + 1) * HD)
            soft = masked_soft(nn(rows, corner_ref[head]), inside)
            here, up = values_ref[span, :], up_ref[span, :]
            moved = nt(here, shift).astype(BF16)
            dsoft = jnp.where(early, tn(up, here), tn(up, moved))
            dvalues_ref[span, :] = nn(up, by_token(soft, early, shift)).astype(BF16)
            centre = jnp.sum(soft * dsoft, axis=1, keepdims=True)
            dscores = (soft * (dsoft - centre)).astype(BF16)
            dcorner_ref[head] = tn(rows, dscores).astype(BF16)

    return pl.pallas_call(
        kernel,
        in_specs=[
            pl.BlockSpec(memory_space=pltpu.SMEM),
            pl.BlockSpec(memory_space=pltpu.VMEM),
            pl.BlockSpec(memory_space=pltpu.VMEM),
            pl.BlockSpec(memory_space=pltpu.VMEM),
        ],
        out_specs=[
            pl.BlockSpec(memory_space=pltpu.VMEM),
            pl.BlockSpec(memory_space=pltpu.VMEM),
        ],
        out_shape=[
            jax.ShapeDtypeStruct((heads, size, size), BF16),
            jax.ShapeDtypeStruct((width, size), BF16),
        ],
        name="short_backward",
    )(first, corner, values_t, upstream_t)


def table_grad(table, lse, values_t, upstream_t, corner):
    heads, rows, columns = table.shape
    slots, size = values_t.shape[0], corner.shape[2]

    def kernel(table_ref, lse_ref, values_ref, up_ref, corner_ref, out_ref):
        weights = jnp.exp(table_ref[0, :, 0:MOST].astype(F32) - lse_ref[0, :, 0:1])
        up = up_ref[...].reshape(slots * HD, rows)
        dsoft = tn(up, values_ref[...].reshape(slots * HD, MOST))
        weighed = weights * dsoft
        centre = jnp.sum(weighed, axis=1, keepdims=True)
        out_ref[0, :, 0:MOST] = weighed - weights * centre
        out_ref[0, :, MOST:columns] = jnp.zeros((rows, columns - MOST), F32)
        out_ref[0, :, 0:size] += corner_ref[0].astype(F32)

    return pl.pallas_call(
        kernel,
        grid=(heads,),
        in_specs=[
            pl.BlockSpec((1, rows, columns), lambda h: (h, 0, 0)),
            pl.BlockSpec((1, rows, 128), lambda h: (h, 0, 0)),
            pl.BlockSpec((slots, HD, MOST), lambda h: (0, h, 0)),
            pl.BlockSpec((slots, HD, rows), lambda h: (0, h, 0)),
            pl.BlockSpec((1, rows, size), lambda h: (h, 0, 0)),
        ],
        out_specs=pl.BlockSpec((1, rows, columns), lambda h: (h, 0, 0)),
        out_shape=jax.ShapeDtypeStruct((heads, rows, columns), F32),
        compiler_params=pltpu.CompilerParams(vmem_limit_bytes=VMEM),
        name="table_grad",
    )(table, lse, values_t, upstream_t, corner)


EPS = 1e-06
CURVE = 0.7978845608028654


def root(x):
    return lax.rsqrt(jnp.mean(x * x, axis=-1, keepdims=True) + EPS)


def normalize(x, gain):
    return (x * root(x) * gain).astype(BF16)


def normalize_back(x, gain, grad):
    scale = root(x)
    weighed = grad * gain
    pull = jnp.mean(weighed * x, axis=-1, keepdims=True)
    return scale * weighed - x * (scale * scale * scale * pull), jnp.sum(grad * x * scale, axis=0, keepdims=True)


def gelu(x):
    square = x * x
    half = 0.5 * jnp.tanh(x * (CURVE + CURVE * 0.044715 * square)) + 0.5
    value = x * half
    return value, half + (value - value * half) * (2 * CURVE + 6 * CURVE * 0.044715 * square)


def turn(x, start, rows):
    total, model = x.shape

    def kernel(start_ref, x_ref, out_ref, wide):
        for i in range(model // 128):
            lanes = slice(i * 128, (i + 1) * 128)
            part = x_ref[:, lanes].astype(F32)
            wide[i % 2, 0:total] = part
            wide[i % 2, total : total + rows] = part[0:rows]
            out_ref[:, lanes] = wide[i % 2, pl.ds(start_ref[0, 0], rows), :].astype(x.dtype)

    return pl.pallas_call(
        kernel,
        in_specs=[SCALAR, INTO],
        out_specs=INTO,
        out_shape=jax.ShapeDtypeStruct((rows, model), x.dtype),
        scratch_shapes=[pltpu.VMEM((2, total + rows, 128), F32)],
        compiler_params=pltpu.CompilerParams(vmem_limit_bytes=VMEM),
        name="turn",
    )(start.astype(jnp.int32).reshape(1, 1), x)


def begin(inputs, weights, gain):
    total, model = inputs.shape
    width = weights.shape[1] // 2
    tile = 256

    def kernel(x_ref, w_ref, gain_ref, normed_ref, values_ref, values_t_ref, acts_ref, acts_t_ref, slope_ref):
        normed = normalize(x_ref[...].astype(F32), gain_ref[0:1, :])
        normed_ref[...] = normed
        both = nn(normed, w_ref[...])
        acts, slope = gelu(both[:, width:])
        values = both[:, :width]
        values, acts = values.astype(BF16), acts.astype(BF16)
        values_ref[...] = values
        values_t_ref[...] = values.T
        acts_ref[...] = acts
        acts_t_ref[...] = acts.T
        slope_ref[...] = slope.astype(BF16)

    rows = lambda i: (i, 0)
    columns = lambda i: (0, i)
    return pl.pallas_call(
        kernel,
        grid=(total // tile,),
        in_specs=[
            pl.BlockSpec((tile, model), rows),
            pl.BlockSpec(weights.shape, lambda i: (0, 0)),
            pl.BlockSpec(gain.shape, lambda i: (0, 0)),
        ],
        out_specs=[
            pl.BlockSpec((tile, model), rows),
            pl.BlockSpec((tile, width), rows),
            pl.BlockSpec((width, tile), columns),
            pl.BlockSpec((tile, width), rows),
            pl.BlockSpec((width, tile), columns),
            pl.BlockSpec((tile, width), rows),
        ],
        out_shape=[
            jax.ShapeDtypeStruct((total, model), BF16),
            jax.ShapeDtypeStruct((total, width), BF16),
            jax.ShapeDtypeStruct((width, total), BF16),
            jax.ShapeDtypeStruct((total, width), BF16),
            jax.ShapeDtypeStruct((width, total), BF16),
            jax.ShapeDtypeStruct((total, width), BF16),
        ],
        compiler_params=pltpu.CompilerParams(vmem_limit_bytes=VMEM),
        cost_estimate=pl.CostEstimate(flops=2 * total * model * 2 * width, bytes_accessed=6 * total * model, transcendentals=0),
        name="begin",
    )(inputs, weights, gain)


def by_rows(mixed):
    if len(mixed.shape) == 2:
        return mixed.T
    return jnp.concatenate([mixed[c].T for c in range(mixed.shape[0])], axis=0)


def ends(x, mixed, flat, weights, width, gain, row, more):
    share, model = x.shape
    groups = weights.shape[0]
    hidden = (weights.shape[2] - 2 * width) // 2

    def kernel(*refs):
        x_ref, mixed_ref, gain_ref, up_ref, down_ref, side_ref = refs[:6]
        refs = refs[6:]
        middle_ref, normed_ref, hidden_ref, slope_ref, y_ref = refs[:5]
        acc = refs[-1]
        group = pl.program_id(0)

        @pl.when(group == 0)
        def _():
            total = x_ref[...].astype(F32)
            for j in range(groups):
                block = mixed_ref[j] if flat else by_rows(mixed_ref[j])
                total += nt(block, side_ref[j, :, 0:width])
            middle_ref[...] = total
            normed_ref[...] = normalize(total, gain_ref[row : row + 1, :])
            acc[...] = total

        normed = normed_ref[...]
        part = 256 if hidden % 256 == 0 else hidden
        ahead = nn(normed, up_ref[0, :, 0:part])
        for spot in range(0, hidden, part):
            pre = ahead
            if spot + part < hidden:
                ahead = nn(normed, up_ref[0, :, spot + part : spot + 2 * part])
            value, slope = gelu(pre)
            hidden_ref[0, :, spot : spot + part] = value.astype(BF16)
            slope_ref[0, :, spot : spot + part] = slope.astype(BF16)
        acc[...] += nt(hidden_ref[0], down_ref[0])

        @pl.when(group == groups - 1)
        def _():
            y = acc[...]
            y_ref[...] = y.astype(y_ref.dtype)
            if more:
                normed = normalize(y, gain_ref[row + 1 : row + 2, :])
                refs[5][...] = normed
                for j in range(groups):
                    refs[6][j] = nn(normed, side_ref[j, :, width : 2 * width]).T.astype(BF16)

    whole2, whole3 = (lambda g: (0, 0)), (lambda g: (0, 0, 0))
    in_specs = [
        pl.BlockSpec(x.shape, whole2),
        pl.BlockSpec(mixed.shape, lambda g: (0,) * mixed.ndim),
        pl.BlockSpec(gain.shape, whole2),
        pl.BlockSpec((1, model, hidden), lambda g: (g, 0, 0)),
        pl.BlockSpec((1, model, hidden), lambda g: (g, 0, 1)),
        pl.BlockSpec((groups, model, 2 * width), lambda g: (0, 0, hidden // width)),
    ]
    out_specs = [
        pl.BlockSpec((share, model), whole2),
        pl.BlockSpec((share, model), whole2),
        pl.BlockSpec((1, share, hidden), lambda g: (g, 0, 0)),
        pl.BlockSpec((1, share, hidden), lambda g: (g, 0, 0)),
        pl.BlockSpec((share, model), whole2),
    ]
    out_shape = [
        jax.ShapeDtypeStruct((share, model), F32),
        jax.ShapeDtypeStruct((share, model), BF16),
        jax.ShapeDtypeStruct((groups, share, hidden), BF16),
        jax.ShapeDtypeStruct((groups, share, hidden), BF16),
        jax.ShapeDtypeStruct((share, model), F32 if more else BF16),
    ]
    if more:
        out_specs += [pl.BlockSpec((share, model), whole2), pl.BlockSpec((groups, width, share), whole3)]
        out_shape += [
            jax.ShapeDtypeStruct((share, model), BF16),
            jax.ShapeDtypeStruct((groups, width, share), BF16),
        ]
    return pl.pallas_call(
        kernel,
        grid=(groups,),
        in_specs=in_specs,
        out_specs=out_specs,
        out_shape=out_shape,
        scratch_shapes=[pltpu.VMEM((share, model), F32)],
        compiler_params=pltpu.CompilerParams(vmem_limit_bytes=VMEM),
        cost_estimate=pl.CostEstimate(flops=4 * share * model * groups * hidden, bytes_accessed=4 * groups * model * hidden, transcendentals=0),
        name="ends",
    )(x, mixed, gain, weights, weights, weights)


def ends_back(grad, mixed, flat, weights, width, gain, row, record, after=None):
    middle, normed, hid, slope = record
    share, model = middle.shape
    groups = weights.shape[0]
    hidden = hid.shape[2]
    more = after is not None
    columns = 2 * hidden + (2 if more else 1) * width

    def kernel(*refs):
        grad_ref, mixed_ref, gain_ref, up_ref, down_ref, side_ref, middle_ref, normed_ref, hidden_ref, slope_ref = refs[:10]
        refs = refs[10:]
        if more:
            next_ref, next_normed_ref, dvalues_ref = refs[:3]
            refs = refs[3:]
        out_ref, dmiddle_ref, dmixed_ref, dgain_ref, total, low, low_t, normed_t, dnormed, grads_ref, side_grads, sems = refs
        group = pl.program_id(0)

        def leave(g):
            return pltpu.make_async_copy(grads_ref.at[g], out_ref.at[g, :, pl.ds(0, 2 * hidden)], sems.at[g])

        side_leave = pltpu.make_async_copy(
            side_grads, out_ref.at[:, :, pl.ds(2 * hidden, columns - 2 * hidden)], sems.at[groups]
        )

        @pl.when(group == 0)
        def _():
            g = grad_ref[...].astype(F32)
            dgain_ref[...] = jnp.zeros_like(dgain_ref)
            if more:
                pull = jnp.zeros((share, model), F32)
                next_t = next_normed_ref[...].T
                for j in range(groups):
                    dvalues = dvalues_ref[j].T
                    side_grads[j, :, width : 2 * width] = nn(next_t, dvalues).astype(BF16)
                    pull += nt(dvalues, side_ref[j, :, width : 2 * width])
                dx, dg = normalize_back(next_ref[...], gain_ref[row + 1 : row + 2, :], pull)
                g += dx
                dgain_ref[1:2, :] = dg
            total[...] = g
            low[...] = g.astype(BF16)
            low_t[...] = g.astype(BF16).T
            normed_t[...] = normed_ref[...].T
            dnormed[...] = jnp.zeros_like(dnormed)

        dpre = (slope_ref[0].astype(F32) * nn(low[...], down_ref[0])).astype(BF16)
        grads_ref[group, :, 0:hidden] = nn(normed_t[...], dpre).astype(BF16)
        grads_ref[group, :, hidden : 2 * hidden] = nn(low_t[...], hidden_ref[0]).astype(BF16)
        leave(group).start()
        dnormed[...] += nt(dpre, up_ref[0])

        @pl.when(group == groups - 1)
        def _():
            dx, dg = normalize_back(middle_ref[...], gain_ref[row : row + 1, :], dnormed[...])
            dmiddle = total[...] + dx
            dgain_ref[0:1, :] = dg
            dmiddle_ref[...] = dmiddle
            down = dmiddle.astype(BF16)
            down_t = down.T
            for j in range(groups):
                block = mixed_ref[j] if flat else by_rows(mixed_ref[j])
                side_grads[j, :, 0:width] = nn(down_t, block).astype(BF16)
                dmixed = nn(down, side_ref[j, :, 0:width])
                if flat:
                    dmixed_ref[j] = dmixed.astype(BF16)
                elif len(mixed.shape) == 3:
                    dmixed_ref[j] = dmixed.T.astype(BF16)
                else:
                    rows = mixed.shape[3]
                    for c in range(mixed.shape[1]):
                        dmixed_ref[j, c] = dmixed[c * rows : (c + 1) * rows].T.astype(BF16)
            side_leave.start()
            side_leave.wait()
            for g in range(groups):
                leave(g).wait()

    whole2, whole3 = (lambda g: (0, 0)), (lambda g: (0, 0, 0))
    whole = lambda a: pl.BlockSpec(a.shape, lambda g: (0,) * a.ndim)
    in_specs = [
        whole(grad),
        whole(mixed),
        whole(gain),
        pl.BlockSpec((1, model, hidden), lambda g: (g, 0, 0)),
        pl.BlockSpec((1, model, hidden), lambda g: (g, 0, 1)),
        pl.BlockSpec((groups, model, 2 * width), lambda g: (0, 0, hidden // width)),
        whole(middle),
        whole(normed),
        pl.BlockSpec((1, share, hidden), lambda g: (g, 0, 0)),
        pl.BlockSpec((1, share, hidden), lambda g: (g, 0, 0)),
    ]
    operands = [grad, mixed, gain, weights, weights, weights, middle, normed, hid, slope]
    if more:
        in_specs += [whole(a) for a in after]
        operands += list(after)
    out_specs = [
        ANY,
        pl.BlockSpec((share, model), whole2),
        whole(mixed),
        pl.BlockSpec((8, model), whole2),
    ]
    out_shape = [
        jax.ShapeDtypeStruct((groups, model, columns), BF16),
        jax.ShapeDtypeStruct((share, model), F32),
        jax.ShapeDtypeStruct(mixed.shape, BF16),
        jax.ShapeDtypeStruct((8, model), F32),
    ]
    scratch = [
        pltpu.VMEM((share, model), F32),
        pltpu.VMEM((share, model), BF16),
        pltpu.VMEM((model, share), BF16),
        pltpu.VMEM((model, share), BF16),
        pltpu.VMEM((share, model), F32),
        pltpu.VMEM((groups, model, 2 * hidden), BF16),
        pltpu.VMEM((groups, model, columns - 2 * hidden), BF16),
        DMA((groups + 1,)),
    ]
    return pl.pallas_call(
        kernel,
        grid=(groups,),
        in_specs=in_specs,
        out_specs=out_specs,
        out_shape=out_shape,
        scratch_shapes=scratch,
        compiler_params=pltpu.CompilerParams(vmem_limit_bytes=VMEM),
        cost_estimate=pl.CostEstimate(flops=8 * share * model * groups * hidden, bytes_accessed=8 * groups * model * hidden, transcendentals=0),
        name="ends_back",
    )(*operands)


def finish(back, weights, first, x, gain, dmiddle, gains, n, n_mp):
    groups, share, both = back.shape
    model, width = first.shape[1:]
    spot = weights.shape[2] // (2 * width) - 1
    pairs = n_mp // 2
    chunks = 4
    tall = share // chunks

    def kernel(back_ref, side_ref, first_ref, x_ref, gain_ref, dmiddle_ref, gains_ref, all_ref, sum_ref, out, here, one,
               two, far_send, far_recv, near_send, near_recv, on_send, on_recv, own_sem, g_send, g_recv, h_send, h_recv):
        me, place = lax.axis_index("mp"), lax.axis_index("dp")
        pair, core = me // 2, lax.rem(me, 2)
        twin = pair * 2 + 1 - core
        greet([("dp", n), ("mp", n_mp)])

        def rows(c):
            return pl.ds(c * tall, tall)

        def far(step, c):
            to = lax.rem(pair + step, pairs) * 2 + core
            return remote(
                out.at[rows(c)], all_ref.at[me, rows(c)], far_send.at[step, c], far_recv.at[step, c], "mp", to
            )

        def near(c):
            return remote(out.at[rows(c)], all_ref.at[me, rows(c)], near_send.at[c], near_recv.at[c], "mp", twin)

        def onward(step, c):
            source = lax.rem(pair + pairs - step, pairs) * 2 + core
            block = all_ref.at[source, rows(c)]
            return remote(block, block, on_send.at[step, c], on_recv.at[step, c], "mp", twin)

        total = jnp.zeros((1, model), F32)
        for c in range(chunks):
            span = slice(c * tall, (c + 1) * tall)
            pull = jnp.zeros((tall, model), F32)
            for j in range(groups):
                pull += nt(back_ref[j, span, 0:width], side_ref[j, :, width : 2 * width])
                pull += nt(back_ref[j, span, width:both], first_ref[j])
            dx, dg = normalize_back(x_ref[span, :].astype(F32), gain_ref[0:1, :], pull)
            out[span, :] = (dmiddle_ref[span, :] + dx).astype(BF16)
            total += dg
            for step in range(1, pairs):
                far(step, c).start()
            near(c).start()
        own = pltpu.make_async_copy(out, all_ref.at[me], own_sem)
        own.start()
        here[...] = gains_ref[...]
        here[0:1, :] = total
        one[me] = here[...]
        firsts = []
        for step in range(1, n_mp):
            to = lax.rem(me + step, n_mp)
            firsts.append(remote(here, one.at[me], g_send.at[step], g_recv.at[step], "mp", to))
            firsts[-1].start()
        for copy in firsts:
            copy.wait()
        total = one[0]
        for j in range(1, n_mp):
            total += one[j]
        two[place] = total

        def spread(step, there):
            return remote(two.at[place], two.at[there], h_send.at[step], h_recv.at[step], "dp", lax.rem(place + step, n))

        @pl.loop(1, n)
        def _(step):
            spread(step, place).start()

        for c in range(chunks):
            for step in range(1, pairs):
                far(step, c).wait_recv()
                onward(step, c).start()

        @pl.loop(1, n)
        def _(step):
            spread(step, place).wait_send()
            spread(step, lax.rem(place + n - step, n)).wait_recv()

        total = two[0]
        for j in range(1, n):
            total += two[j]
        sum_ref[...] = total
        for c in range(chunks):
            near(c).wait()
            for step in range(1, pairs):
                far(step, c).wait_send()
                onward(step, c).wait()
        own.wait()

    return pl.pallas_call(
        kernel,
        grid=(1,),
        in_specs=[
            pl.BlockSpec(back.shape, lambda i: (0, 0, 0)),
            pl.BlockSpec((groups, model, 2 * width), lambda i: (0, 0, spot)),
            pl.BlockSpec(first.shape, lambda i: (0, 0, 0)),
            pl.BlockSpec(x.shape, lambda i: (0, 0)),
            pl.BlockSpec(gain.shape, lambda i: (0, 0)),
            pl.BlockSpec(dmiddle.shape, lambda i: (0, 0)),
            pl.BlockSpec(gains.shape, lambda i: (0, 0)),
        ],
        out_specs=[ANY, pl.BlockSpec(gains.shape, lambda i: (0, 0))],
        out_shape=[
            jax.ShapeDtypeStruct((n_mp, share, model), BF16),
            jax.ShapeDtypeStruct(gains.shape, F32),
        ],
        scratch_shapes=[
            pltpu.VMEM((share, model), BF16),
            pltpu.VMEM(gains.shape, F32),
            pltpu.VMEM((n_mp,) + gains.shape, F32),
            pltpu.VMEM((n,) + gains.shape, F32),
            DMA((pairs, chunks)),
            DMA((pairs, chunks)),
            DMA((chunks,)),
            DMA((chunks,)),
            DMA((pairs, chunks)),
            DMA((pairs, chunks)),
            DMA,
            DMA((n_mp,)),
            DMA((n_mp,)),
            DMA((n,)),
            DMA((n,)),
        ],
        compiler_params=comm_params(4),
        name="finish",
    )(back, weights, first, x, gain, dmiddle, gains)


def per_device(
    n_dp,
    n_mp,
    tokens,
    lengths,
    norm_gain,
    w_value,
    w_out,
    w_up,
    w_down,
    synth_first,
    synth_second,
    random_table,
    cotangent,
):
    both = ("mp", "dp")
    place, rank = lax.axis_index("dp"), lax.axis_index("mp")
    total, model = tokens.shape
    share = total // n_mp
    size = total - MOST
    depth, width = w_value.shape[1], w_value.shape[2]
    hidden = w_up.shape[2]
    heads, rows, columns = random_table.shape
    near = rows == size and share % rows == 0 and n_dp in (2, 4, 6, 8)

    item_lengths = lengths[0]
    longest = jnp.argmax(item_lengths)
    start = (jnp.cumsum(item_lengths) - item_lengths)[longest]
    first = item_lengths[(longest + 1) % item_lengths.shape[0]].astype(jnp.int32).reshape(1, 1)

    gains = jnp.pad(norm_gain.reshape(4, depth).T, ((0, 0), (0, 124)))
    pack = jnp.concatenate([w_value[0], synth_first, gains], axis=1)
    table = synth_second.reshape(width, -1)
    corner = random_table[:, :, :size]
    if near:
        pack, table, corner = gather_weights([pack, table], corner.reshape(n_dp, -1, size), n_dp)
    else:
        begins = jnp.minimum(place * rows, size - rows)
        inside = (place * rows < size).astype(BF16)
        corner = lax.dynamic_update_slice(jnp.zeros((heads, size, size), BF16), corner * inside, (0, begins, 0))
        corner = lax.psum(corner, "dp")
        pack, table = lax.all_gather(pack, "dp"), lax.all_gather(table, "dp")
        table = table.transpose(1, 0, 2).reshape(width, total // size, size).transpose(1, 0, 2)
    pack = pack.reshape(model, -1)
    gain = jnp.pad(pack[:, 2 * width : 2 * width + 4].T.astype(F32), ((0, 4), (0, 0)))

    def whole(parts):
        joined = lax.all_gather(jnp.concatenate(parts, axis=1), both)
        return joined.reshape(n_mp, model, -1)

    weights_one = whole([w_up[0], w_down[0].T, w_out[0].T, w_value[1]])
    weights_two = [w_up[1], w_down[1].T, w_out[1].T, w_value[0]]

    inputs = turn(tokens, start, total)
    normed_one, values, values_t, acts, acts_t, slope = begin(inputs, pack[:, : 2 * width], gain)
    if near:
        mixed_one, lse, corner = dense_forward(first, acts, values, table, corner, n_dp, n_mp)
        corner = corner.reshape(heads, size, size)
    else:
        mixed, lse = dense_forward(first, acts, values, table)
        mixed_one = swap(mixed.reshape(n_mp, share, width), n_mp, 5)
    inputs = lax.dynamic_slice_in_dim(inputs, rank * share, share)
    *record_one, between, normed_two, parts = ends(
        inputs, mixed_one, True, weights_one, width, gain, 1, True
    )

    if near:
        values_all, mixed_two, short_t, table_lse, weights_two = table_forward(
            first, random_table, corner, parts, jnp.concatenate(weights_two, axis=1), n_dp, n_mp
        )
        weights_two = weights_two.reshape(n_mp, model, -1)
    else:
        weights_two = whole(weights_two)
        values_two = swap(parts, n_mp, 6, lanes_out=True)
        short_t = values_two[:, MOST:]
        values_all = lax.all_gather(values_two[:, :MOST], "dp")
        mixed, table_lse = random_forward(random_table, values_all)
        mixed = lax.all_to_all(mixed, "dp", 0, 0, tiled=True).transpose(1, 0, 2).reshape(width, total)
        mixed = jnp.concatenate([mixed[:, :MOST], short_forward(first, corner, short_t)], axis=1)
        mixed_two = swap(mixed, n_mp, 7, lanes_in=True)
    *record_two, result = ends(between, mixed_two, False, weights_two, width, gain, 3, False)
    early_first, _ = lax.optimization_barrier((synth_first, mixed_two))
    first_all = whole([early_first])

    grad = turn(cotangent, lax.rem(start + rank * share, total), share)
    grads_two, dmiddle, parts, dgain_two = ends_back(
        grad, mixed_two, False, weights_two, width, gain, 3, record_two
    )

    def scattered(grads, axes):
        grads = grads.reshape(-1, depth, grads.shape[-1])
        return lax.psum_scatter(grads, axes, scatter_dimension=0).astype(F32)

    if near:
        rows_upstream, dvalues, dcorner, grads_two = table_backward(
            first, random_table, corner, table_lse, short_t, parts, grads_two, n_dp, n_mp
        )
    else:
        upstream = swap(parts, n_mp, 8, lanes_out=True)
        dcorner, dshort = short_backward(first, corner, short_t, upstream[:, MOST:])
        dcorner = lax.dynamic_slice_in_dim(lax.psum(dcorner, "dp"), begins, rows, axis=1) * inside
        upstream = upstream.reshape(width, n_dp, rows).transpose(1, 0, 2)
        upstream = lax.all_to_all(upstream, "dp", 0, 0, tiled=True)
        valid = (place * rows < MOST).astype(F32).reshape(1, 1)
        dtable, dvalues = random_backward(valid, random_table, table_lse, values_all, upstream)
        dvalues = lax.psum_scatter(dvalues, "dp", scatter_dimension=0)
        dvalues = swap(jnp.concatenate([dvalues, dshort], axis=1), n_mp, 9, lanes_in=True)
        result = lax.all_gather(result, "mp")
        grads_two = scattered(grads_two, both)

    grads_one, dmiddle, parts, dgain_one = ends_back(
        dmiddle, mixed_one, True, weights_one, width, gain, 1, record_one, (between, normed_two, dvalues)
    )
    grads_one = scattered(grads_one, both)
    upstream = swap(parts, n_mp, 10).reshape(total, width)
    back_one = partial(dense_backward, first, acts, acts_t, values_t, upstream, table, lse, slope, normed_one)
    if near:
        back, entry_grad, second_grad, grads_two, result = back_one(
            grads_two.reshape(n_dp, depth, -1), result, n_dp, n_mp
        )
    else:
        back, entry_grad, second_grad = back_one()
    result = turn(result.reshape(total, model), total - start, total)
    back = back.reshape(n_mp, share, 2 * width)
    entry_grad = entry_grad.reshape(n_dp, depth, 2 * width)
    if near:
        back, entry_grad, second_grad, dcorner = last_exchange(
            back, [entry_grad, second_grad, dcorner.reshape(n_dp, -1, size)], n_dp, n_mp
        )
        dcorner = dcorner.reshape(heads, size, size)
    else:
        back = swap(back, n_mp, 11)
        entry_grad = lax.psum_scatter(entry_grad, "dp", scatter_dimension=0).astype(F32)
        second_grad = second_grad.transpose(1, 0, 2).reshape(width, n_dp, -1).transpose(1, 0, 2)
        second_grad = lax.psum_scatter(second_grad, "dp", scatter_dimension=0).astype(F32)
    gain_grad = jnp.concatenate([dgain_one[:1], dgain_one[:2], dgain_two[:1], jnp.zeros((4, model), F32)])
    input_grad, gain_grad = finish(back, weights_two, first_all, inputs, gain, dmiddle, gain_grad, n_dp, n_mp)
    input_grad = turn(input_grad.reshape(total, model), total - start, total)
    if near:
        upstream_last, _ = lax.optimization_barrier((rows_upstream, gain_grad))
        dtable = table_grad(random_table, table_lse, values_all, upstream_last, dcorner)
    else:
        dtable = dtable.at[:, :, :size].add(dcorner.astype(F32))

    gain_grad = lax.dynamic_slice_in_dim(gain_grad[:4], place * depth, depth, axis=1)
    out_at = slice(2 * hidden, 2 * hidden + width)
    return (
        result,
        input_grad,
        gain_grad.reshape(2, 2, depth),
        jnp.stack([entry_grad[:, :width], grads_one[:, 2 * hidden + width :]]),
        jnp.stack([grads_one[:, out_at].T, grads_two[:, out_at].T]),
        jnp.stack([grads_one[:, :hidden], grads_two[:, :hidden]]),
        jnp.stack([grads_one[:, hidden : 2 * hidden].T, grads_two[:, hidden : 2 * hidden].T]),
        entry_grad[:, width:],
        second_grad.reshape(heads, HD, -1),
        dtable,
    )


def solution(mesh):
    in_specs = (
        P("dp", None),
        P("dp", None),
        P(None, None, "dp"),
        P(None, "dp", "mp"),
        P(None, "mp", "dp"),
        P(None, "dp", "mp"),
        P(None, "mp", "dp"),
        P("dp", "mp"),
        P("mp", None, "dp"),
        P("mp", "dp", None),
        P("dp", None),
    )
    out_specs = (
        P("dp", None),
        P("dp", None),
        P(None, None, "dp"),
        P(None, "dp", "mp"),
        P(None, "mp", "dp"),
        P(None, "dp", "mp"),
        P(None, "mp", "dp"),
        P("dp", "mp"),
        P("mp", None, "dp"),
        P("mp", "dp", None),
    )
    return jax.shard_map(
        partial(per_device, mesh.shape["dp"], mesh.shape["mp"]),
        mesh=mesh,
        in_specs=in_specs,
        out_specs=out_specs,
        check_vma=False,
    )
```
